32 devices in a mesh: row: 4 (over z), seq: 8 (over y, x, core).
Axes of the slice: x: 2, y: 2, z: 4, core: 2. Of those that a mesh axis runs over, the one named last changes fastest.
Arguments:
- tokens: bfloat16 [8, 1024, 1024], P('row', 'seq'), may hold values from -6 to 6
- lengths: int32 [8, 2], P('row'), may hold values from 0 to 1024, as said below
- mixer_gain: bfloat16 [1024], replicated, may hold values from 0.5 to 1.5
- mixer_input: bfloat16 [1024, 3072], replicated, may hold values from -0.1875 to 0.1875
- mixer_kernel: bfloat16 [3, 1024], replicated, may hold values from -3.5 to 3.5
- mixer_output: bfloat16 [1024, 1024], replicated, may hold values from -0.1875 to 0.1875
- first_gain: bfloat16 [1024], replicated, may hold values from 0.5 to 1.5
- first_gate: bfloat16 [1024, 4608], replicated, may hold values from -0.1875 to 0.1875
- first_up: bfloat16 [1024, 4608], replicated, may hold values from -0.1875 to 0.1875
- first_down: bfloat16 [4608, 1024], replicated, may hold values from -0.09375 to 0.09375
- attend_gain: bfloat16 [1024], replicated, may hold values from 0.5 to 1.5
- query_weight: bfloat16 [1024, 1024], replicated, may hold values from -0.1875 to 0.1875
- key_weight: bfloat16 [1024, 512], replicated, may hold values from -0.1875 to 0.1875
- value_weight: bfloat16 [1024, 512], replicated, may hold values from -0.1875 to 0.1875
- query_gain: bfloat16 [64], replicated, may hold values from 0.5 to 1.5
- key_gain: bfloat16 [64], replicated, may hold values from 0.5 to 1.5
- attend_output: bfloat16 [1024, 1024], replicated, may hold values from -2 to 2
- second_gain: bfloat16 [1024], replicated, may hold values from 0.5 to 1.5
- second_gate: bfloat16 [1024, 4608], replicated, may hold values from -0.1875 to 0.1875
- second_up: bfloat16 [1024, 4608], replicated, may hold values from -0.1875 to 0.1875
- second_down: bfloat16 [4608, 1024], replicated, may hold values from -0.09375 to 0.09375
- cotangent: bfloat16 [8, 1024, 1024], P('row', 'seq'), may hold values from -6 to 6
Outputs:
- mixed: bfloat16 [8, 1024, 1024], P('row', 'seq')
- token_grad: bfloat16 [8, 1024, 1024], P('row', 'seq')
- mixer_gain_grad: float32 [1024], P('seq')
- mixer_input_grad: float32 [1024, 3072], P('seq')
- mixer_kernel_grad: float32 [3, 1024], P(None, 'seq')
- mixer_output_grad: float32 [1024, 1024], P('seq')
- first_gain_grad: float32 [1024], P('seq')
- first_gate_grad: float32 [1024, 4608], P('seq')
- first_up_grad: float32 [1024, 4608], P('seq')
- first_down_grad: float32 [4608, 1024], P('seq')
- attend_gain_grad: float32 [1024], P('seq')
- query_weight_grad: float32 [1024, 1024], P('seq')
- key_weight_grad: float32 [1024, 512], P('seq')
- value_weight_grad: float32 [1024, 512], P('seq')
- query_gain_grad: float32 [64], P('seq')
- key_gain_grad: float32 [64], P('seq')
- attend_output_grad: float32 [1024, 1024], P('seq')
- second_gain_grad: float32 [1024], P('seq')
- second_gate_grad: float32 [1024, 4608], P('seq')
- second_up_grad: float32 [1024, 4608], P('seq')
- second_down_grad: float32 [4608, 1024], P('seq')
The draws below stay inside these ranges and needn't reach their ends.
Inputs may be any that keep to these rules, and one draw needn't show every extreme that they name: Each row's lengths are multiples of 512 that sum to 1024, the nonzero ones first and zeros after them. Of each device's 2 rows, exactly one holds a single sequence of 1024, and every other row holds two or more sequences.
All inputs are finite; a program needn't handle non-finite values.
Results may differ from the reference program's by a relative error of at most 0.029.
Values may be sent and summed in bfloat16 or wider, within the bound.
A program may use at most 384 MiB of HBM per device.

```python
import jax
import jax.numpy as jnp
from jax import lax

D = 1024
FF = 4608
HEADS = 16
KV_HEADS = 8
HEAD_DIM = 64
ROWS_DEV = 2
GROUP = 2
ROWS = 8
SEQ = 1024
UNIT = 512
PIECES = 2


def draw_lengths(key, part):
    key = jax.random.fold_in(key, 7)
    cut_key, whole_key, forced_key = jax.random.split(key, 3)
    slots = jnp.arange(PIECES, dtype=jnp.int32)
    cuts = jax.random.randint(cut_key, (ROWS, PIECES), 0, 2)
    forced = jax.random.randint(forced_key, (ROWS, 1), 1, PIECES)
    cuts = jnp.maximum(cuts, (slots[None, :] == forced).astype(jnp.int32))
    cuts = cuts * (slots > 0).astype(jnp.int32)[None, :]
    chosen = jax.random.randint(whole_key, (ROWS // ROWS_DEV, 1), 0, ROWS_DEV)
    within = jnp.arange(ROWS_DEV, dtype=jnp.int32)[None, :]
    single = (within == chosen).reshape(ROWS)
    cuts = jnp.where(single[:, None], 0, cuts)
    piece_segment = jnp.cumsum(cuts, axis=1).astype(jnp.int32)
    counts = jnp.sum((piece_segment[:, None, :] == slots[None, :, None]).astype(jnp.int32), axis=-1)
    return (counts * UNIT).astype(jnp.int32)


def block_levels(own_key, dims, shards, smallest, top_value):
    level = 1.0
    for axis_at, shards_of in shards:
        steps = jax.random.uniform(jax.random.fold_in(jax.random.fold_in(own_key, 6), axis_at), (shards_of,), jnp.float32, smallest / len(shards), top_value / len(shards))
        level = level * jnp.repeat(jnp.exp(steps), dims[axis_at] // shards_of).reshape((-1,) + (1,) * (len(dims) - 1 - axis_at))
    return level


def scatter_about(own_key, extent, deviation, most, cuts=(), kind=jnp.bfloat16):
    level = block_levels(own_key, extent, cuts, -0.22, 0.18) if cuts else 1.0
    array = jax.random.normal(own_key, extent, jnp.float32) * deviation * level
    return jnp.minimum(jnp.maximum(array, -most), most).astype(kind)


def setup_inputs(seed: int = 0) -> dict:
    arg_keys = jax.random.split(jax.random.key(seed), 23)
    return {
        "tokens": scatter_about(arg_keys[0], (ROWS, SEQ, D), 1.0, 6.0, ((0, 4), (1, 8))),
        "lengths": draw_lengths(jax.random.fold_in(arg_keys[22], 71), 0),
        "mixer_gain": jnp.clip(1.0 + 0.1 * jax.random.normal(arg_keys[2], (D,), jnp.float32), 0.5, 1.5).astype(jnp.bfloat16),
        "mixer_input": scatter_about(arg_keys[3], (D, 3 * D), D ** -0.5, 0.1875),
        "mixer_kernel": scatter_about(arg_keys[4], (3, D), 3 ** -0.5, 3.5),
        "mixer_output": scatter_about(arg_keys[5], (D, D), D ** -0.5, 0.1875),
        "first_gain": jnp.clip(1.0 + 0.1 * jax.random.normal(arg_keys[6], (D,), jnp.float32), 0.5, 1.5).astype(jnp.bfloat16),
        "first_gate": scatter_about(arg_keys[7], (D, FF), D ** -0.5, 0.1875),
        "first_up": scatter_about(arg_keys[8], (D, FF), D ** -0.5, 0.1875),
        "first_down": scatter_about(arg_keys[9], (FF, D), FF ** -0.5, 0.09375),
        "attend_gain": jnp.clip(1.0 + 0.1 * jax.random.normal(arg_keys[10], (D,), jnp.float32), 0.5, 1.5).astype(jnp.bfloat16),
        "query_weight": scatter_about(arg_keys[11], (D, HEADS * HEAD_DIM), D ** -0.5, 0.1875),
        "key_weight": scatter_about(arg_keys[12], (D, KV_HEADS * HEAD_DIM), D ** -0.5, 0.1875),
        "value_weight": scatter_about(arg_keys[13], (D, KV_HEADS * HEAD_DIM), D ** -0.5, 0.1875),
        "query_gain": jnp.clip(1.0 + 0.1 * jax.random.normal(arg_keys[14], (HEAD_DIM,), jnp.float32), 0.5, 1.5).astype(jnp.bfloat16),
        "key_gain": jnp.clip(1.0 + 0.1 * jax.random.normal(arg_keys[15], (HEAD_DIM,), jnp.float32), 0.5, 1.5).astype(jnp.bfloat16),
        "attend_output": scatter_about(arg_keys[16], (HEADS * HEAD_DIM, D), 8 ** -0.5, 2.0),
        "second_gain": jnp.clip(1.0 + 0.1 * jax.random.normal(arg_keys[17], (D,), jnp.float32), 0.5, 1.5).astype(jnp.bfloat16),
        "second_gate": scatter_about(arg_keys[18], (D, FF), D ** -0.5, 0.1875),
        "second_up": scatter_about(arg_keys[19], (D, FF), D ** -0.5, 0.1875),
        "second_down": scatter_about(arg_keys[20], (FF, D), FF ** -0.5, 0.09375),
        "cotangent": scatter_about(arg_keys[21], (ROWS, SEQ, D), 1.0, 6.0, ((0, 4), (1, 8))),
    }


EPS = 1e-05
THETA = 1000000.0
NEGATIVE = -1e+30
HIGHEST = lax.Precision.HIGHEST

@jax.custom_vjp
def reduced_precision(v):
    return lax.optimization_barrier(v.astype(jnp.bfloat16)).astype(jnp.float32)

@jax.custom_vjp
def low_back(v):
    return v

def low_keep(v):
    return (reduced_precision(v), None)

def low_pass(kept, grad):
    return (grad,)

def back_keep(v):
    return (v, None)

def back_low(kept, grad):
    return (reduced_precision(grad),)
reduced_precision.defvjp(low_keep, low_pass)
low_back.defvjp(back_keep, back_low)

def segment_info(lengths, positions):
    boundary = jnp.cumsum(lengths, axis=-1).astype(jnp.int32)
    passed = boundary[:, None, :] <= positions[None, :, None]
    segment = lax.optimization_barrier(jnp.sum(passed.astype(jnp.int32), axis=-1)).astype(jnp.int32)
    seg_start = lax.optimization_barrier(jnp.max(jnp.where(passed, boundary[:, None, :], 0), axis=-1)).astype(jnp.int32)
    return (segment, seg_start)

def norm_rows(values, norm_gain):
    return values * lax.rsqrt(lax.optimization_barrier(jnp.mean(values * values, axis=-1, keepdims=True)) + EPS) * norm_gain

def rotate(values, offsets):
    half_dim = values.shape[-1] // 2
    inverse = THETA ** (-2.0 * jnp.arange(half_dim, dtype=jnp.float32) / values.shape[-1])
    angles = offsets.astype(jnp.float32)[:, :, None, None] * inverse
    cosine = jnp.cos(angles)
    sine_table = jnp.sin(angles)
    leading = values[..., :half_dim]
    trailing = values[..., half_dim:]
    return jnp.concatenate([leading * cosine - trailing * sine_table, trailing * cosine + leading * sine_table], axis=-1)

def swiglu(gate_value, upward):
    return gate_value / (1.0 + jnp.exp(-gate_value)) * upward

def dense(inputs, matrix):
    return jnp.einsum('rtd,df->rtf', inputs, matrix, precision=HIGHEST)

def mixer_layer(hidden, norm_gain, input_matrix, kernel, output_matrix, seg_start, positions):
    feature_columns = hidden.shape[-1]
    normed = reduced_precision(norm_rows(hidden, norm_gain))
    projected_rows = low_back(dense(normed, input_matrix))
    input_gate_value = projected_rows[..., :feature_columns]
    exit_gate = projected_rows[..., feature_columns:2 * feature_columns]
    carry_value = projected_rows[..., 2 * feature_columns:]
    gated_product = reduced_precision(input_gate_value * carry_value)
    one_back = jnp.pad(gated_product, ((0, 0), (1, 0), (0, 0)))[:, :-1]
    two_back = jnp.pad(gated_product, ((0, 0), (2, 0), (0, 0)))[:, :-2]
    keep_one = (positions[None, :] - 1 >= seg_start).astype(jnp.float32)[..., None]
    keep_two = (positions[None, :] - 2 >= seg_start).astype(jnp.float32)[..., None]
    convolved = kernel[2] * gated_product + kernel[1] * keep_one * one_back + kernel[0] * keep_two * two_back
    gated = reduced_precision(exit_gate * convolved)
    return hidden + low_back(dense(gated, output_matrix))

def feed_layer(hidden, norm_gain, gate_matrix, up_matrix, down_matrix):
    normed = reduced_precision(norm_rows(hidden, norm_gain))
    gate_value = low_back(dense(normed, gate_matrix))
    upward = low_back(dense(normed, up_matrix))
    active = reduced_precision(swiglu(gate_value, upward))
    return hidden + low_back(dense(active, down_matrix))

def attend_row(queries, keys, values, segment, positions):
    length = queries.shape[0]
    block_size = min(512, length)
    block_count = length // block_size
    query_blocks = queries.reshape(block_count, block_size, KV_HEADS, GROUP, HEAD_DIM)
    segment_blocks = segment.reshape(block_count, block_size)
    position_blocks = positions.reshape(block_count, block_size)
    score_scale = HEAD_DIM ** (-0.5)

    def one_block(pieces):
        query_block, segment_block, position_block = pieces
        scores = low_back(jnp.einsum('tkgh,skh->kgts', query_block, keys, precision=HIGHEST) * score_scale)
        allowed = (segment_block[:, None] == segment[None, :]) & (position_block[:, None] >= positions[None, :])
        scores = jnp.where(allowed[None, None], scores, NEGATIVE)
        peak_score = lax.optimization_barrier(jnp.max(scores, axis=-1, keepdims=True))
        exponent = jnp.exp(scores - peak_score)
        weights = reduced_precision(exponent / lax.optimization_barrier(jnp.sum(exponent, axis=-1, keepdims=True)))
        return jnp.einsum('kgts,skh->tkgh', weights, values, precision=HIGHEST)
    attended = lax.map(jax.checkpoint(one_block), (query_blocks, segment_blocks, position_blocks))
    return attended.reshape(length, KV_HEADS * GROUP * HEAD_DIM)

def attend_layer(hidden, norm_gain, query_matrix, key_matrix, value_matrix, query_norm, key_norm, output_matrix, segment, offsets):
    row_count, length, feature_columns = hidden.shape
    normed = reduced_precision(norm_rows(hidden, norm_gain))
    queries = low_back(dense(normed, query_matrix)).reshape(row_count, length, HEADS, HEAD_DIM)
    keys_raw = low_back(dense(normed, key_matrix)).reshape(row_count, length, KV_HEADS, HEAD_DIM)
    value_low = reduced_precision(low_back(dense(normed, value_matrix))).reshape(row_count, length, KV_HEADS, HEAD_DIM)
    query_low = reduced_precision(rotate(norm_rows(queries, query_norm), offsets)).reshape(row_count, length, KV_HEADS, GROUP, HEAD_DIM)
    key_low = reduced_precision(rotate(norm_rows(keys_raw, key_norm), offsets))
    positions = jnp.arange(length, dtype=jnp.int32)

    def one_row(pieces):
        return attend_row(pieces[0], pieces[1], pieces[2], pieces[3], positions)
    attended = lax.map(one_row, (query_low, key_low, value_low, segment))
    attended_low = reduced_precision(low_back(attended))
    return hidden + low_back(dense(attended_low, output_matrix))

def reference(tokens, lengths, mixer_gain, mixer_input, mixer_kernel, mixer_output, first_gain, first_gate, first_up, first_down, attend_gain, query_weight, key_weight, value_weight, query_gain, key_gain, attend_output, second_gain, second_gate, second_up, second_down, cotangent):
    length = tokens.shape[1]
    positions = jnp.arange(length, dtype=jnp.int32)
    segment, seg_start = segment_info(lengths, positions)
    offsets = (positions[None, :] - seg_start).astype(jnp.int32)
    params = tuple((item.astype(jnp.float32) for item in (tokens, mixer_gain, mixer_input, mixer_kernel, mixer_output, first_gain, first_gate, first_up, first_down, attend_gain, query_weight, key_weight, value_weight, query_gain, key_gain, attend_output, second_gain, second_gate, second_up, second_down)))

    def model(*weights):
        hidden = mixer_layer(weights[0], weights[1], weights[2], weights[3], weights[4], seg_start, positions)
        hidden = feed_layer(hidden, weights[5], weights[6], weights[7], weights[8])
        hidden = attend_layer(hidden, weights[9], weights[10], weights[11], weights[12], weights[13], weights[14], weights[15], segment, offsets)
        return feed_layer(hidden, weights[16], weights[17], weights[18], weights[19])
    result, pullback = jax.vjp(model, *params)
    grads = pullback(cotangent.astype(jnp.float32))
    return (result.astype(jnp.bfloat16), grads[0].astype(jnp.bfloat16), grads[1], grads[2], grads[3], grads[4], grads[5], grads[6], grads[7], grads[8], grads[9], grads[10], grads[11], grads[12], grads[13], grads[14], grads[15], grads[16], grads[17], grads[18], grads[19])
```

```python
import functools
import math

import jax
import jax.numpy as jnp
from jax import lax
from jax.experimental import pallas as pl
from jax.experimental.pallas import tpu as pltpu
from jax.sharding import PartitionSpec as P

HEADS = 16
KV_HEADS = 8
HEAD_DIM = 64
GROUP = 2


EPS = 1e-05
THETA = 1000000.0
NEGATIVE = -1e30
HIGHEST = lax.Precision.HIGHEST
MESH = pl.DeviceIdType.MESH
COLS = 512
SLOTS = 4
ZSLOTS = 8


def passed_along(value, axis, steps):
    count = lax.axis_size(axis)
    initial, last = (max(0, -steps), min(count, count - steps))
    return lax.ppermute(value, axis, [(source, source + steps) for source in range(initial, last)])


def segment_info(lengths, positions):
    boundary = jnp.cumsum(lengths, axis=-1)
    passed = boundary[:, None, :] <= positions[None, :, None]
    segment = jnp.sum(passed.astype(jnp.int32), axis=-1)
    seg_start = jnp.max(jnp.where(passed, boundary[:, None, :], 0), axis=-1)
    return (segment, seg_start)


def norm_rows(values, norm_gain):
    return values * lax.rsqrt(jnp.mean(values * values, axis=-1, keepdims=True) + EPS) * norm_gain


def rotate(values, offsets):
    half_dim = values.shape[-1] // 2
    inverse = THETA ** (-2.0 * jnp.arange(half_dim, dtype=jnp.float32) / values.shape[-1])
    angles = offsets.astype(jnp.float32)[:, :, None, None] * inverse
    cosine = jnp.cos(angles)
    sine_table = jnp.sin(angles)
    leading = values[..., :half_dim]
    trailing = values[..., half_dim:]
    return jnp.concatenate(
        [leading * cosine - trailing * sine_table, trailing * cosine + leading * sine_table],
        axis=-1,
    )


def swiglu(gate_value, upward):
    return gate_value / (1.0 + jnp.exp(-gate_value)) * upward


def dense(inputs, matrix):
    return jnp.einsum("rtd,df->rtf", inputs, matrix, preferred_element_type=jnp.float32)


def weight_grad(inputs, gradient):
    return (inputs, gradient)


def back_dense(gradient, matrix):
    return jnp.einsum("rtf,df->rtd", gradient, matrix, preferred_element_type=jnp.float32)


def mixer_block(hidden, norm_gain, input_matrix, kernel, output_matrix, seg_start, positions):
    feature_columns = hidden.shape[-1]
    length = hidden.shape[1]
    normed, norm_back = jax.vjp(norm_rows, hidden, norm_gain.astype(jnp.float32))
    normed_low = normed.astype(jnp.bfloat16)
    projected_rows = dense(normed_low, input_matrix)
    input_gate_value = projected_rows[..., :feature_columns]
    exit_gate = projected_rows[..., feature_columns : 2 * feature_columns]
    carry_value = projected_rows[..., 2 * feature_columns :]
    gated_product_reduced = (input_gate_value * carry_value).astype(jnp.bfloat16)
    previous = passed_along(gated_product_reduced[:, length - 2 :, :], "seq", 1)
    extended = jnp.concatenate([previous, gated_product_reduced], axis=1).astype(jnp.float32)
    keep_one = (positions[None, :] - 1 >= seg_start).astype(jnp.float32)[..., None]
    keep_two = (positions[None, :] - 2 >= seg_start).astype(jnp.float32)[..., None]
    kernel_taps = kernel.astype(jnp.float32)
    two_back = extended[:, :length]
    one_back = extended[:, 1 : length + 1]
    current = extended[:, 2:]
    convolved = (
        kernel_taps[2] * current
        + kernel_taps[1] * keep_one * one_back
        + kernel_taps[0] * keep_two * two_back
    )
    gated_low = (exit_gate * convolved).astype(jnp.bfloat16)
    result = hidden + dense(gated_low, output_matrix)

    def mixer_backward(gradient):
        gradient_low = gradient.astype(jnp.bfloat16)
        grad_output = weight_grad(gated_low, gradient_low)
        grad_gated = back_dense(gradient_low, output_matrix)
        output_gate_gradient = grad_gated * convolved
        grad_conv = grad_gated * exit_gate
        grad_kernel = jnp.stack(
            [
                jnp.sum(grad_conv * keep_two * two_back, axis=(0, 1)),
                jnp.sum(grad_conv * keep_one * one_back, axis=(0, 1)),
                jnp.sum(grad_conv * current, axis=(0, 1)),
            ]
        )
        grad_extended = jnp.pad(kernel_taps[0] * keep_two * grad_conv, ((0, 0), (0, 2), (0, 0)))
        grad_extended = grad_extended + jnp.pad(
            kernel_taps[1] * keep_one * grad_conv, ((0, 0), (1, 1), (0, 0))
        )
        grad_extended = grad_extended + jnp.pad(
            kernel_taps[2] * grad_conv, ((0, 0), (2, 0), (0, 0))
        )
        returned = passed_along(grad_extended[:, :2, :], "seq", -1)
        gated_product_gradient = grad_extended[:, 2:] + jnp.pad(
            returned, ((0, 0), (length - 2, 0), (0, 0))
        )
        grad_projected = jnp.concatenate(
            [
                gated_product_gradient * carry_value,
                output_gate_gradient,
                gated_product_gradient * input_gate_value,
            ],
            axis=-1,
        ).astype(jnp.bfloat16)
        grad_input = weight_grad(normed_low, grad_projected)
        grad_normed = back_dense(grad_projected, input_matrix)
        grad_hidden, grad_gain = norm_back(grad_normed)
        return (gradient + grad_hidden, (grad_gain, grad_input, grad_kernel, grad_output))

    return (result, mixer_backward)


def feed_block(hidden, norm_gain, gate_matrix, up_matrix, down_matrix):
    normed, norm_back = jax.vjp(norm_rows, hidden, norm_gain.astype(jnp.float32))
    normed_low = normed.astype(jnp.bfloat16)
    gate_value = dense(normed_low, gate_matrix)
    upward = dense(normed_low, up_matrix)
    active, active_back = jax.vjp(swiglu, gate_value, upward)
    active_low = active.astype(jnp.bfloat16)
    result = hidden + dense(active_low, down_matrix)

    def feed_backward(gradient):
        gradient_low = gradient.astype(jnp.bfloat16)
        grad_down = weight_grad(active_low, gradient_low)
        grad_gate, grad_upward = active_back(back_dense(gradient_low, down_matrix))
        gate_low = grad_gate.astype(jnp.bfloat16)
        upward_low = grad_upward.astype(jnp.bfloat16)
        grad_normed = back_dense(gate_low, gate_matrix) + back_dense(upward_low, up_matrix)
        grad_hidden, grad_gain = norm_back(grad_normed)
        return (
            gradient + grad_hidden,
            (
                grad_gain,
                weight_grad(normed_low, jnp.concatenate([gate_low, upward_low], axis=-1)),
                grad_down,
            ),
        )

    return (result, feed_backward)


def attend_block(
    hidden,
    lengths,
    norm_gain,
    query_matrix,
    key_matrix,
    value_matrix,
    query_norm,
    key_norm,
    output_matrix,
    segment,
    positions,
    offsets,
):
    row_count, length, feature_columns = hidden.shape
    score_scale = HEAD_DIM ** (-0.5)
    normed, norm_back = jax.vjp(norm_rows, hidden, norm_gain.astype(jnp.float32))
    normed_low = normed.astype(jnp.bfloat16)

    def head_path(projected_rows, head_gain):
        return rotate(norm_rows(projected_rows, head_gain), offsets)

    queries = dense(normed_low, query_matrix).reshape(row_count, length, HEADS, HEAD_DIM)
    keys_raw = dense(normed_low, key_matrix).reshape(row_count, length, KV_HEADS, HEAD_DIM)
    values_raw = dense(normed_low, value_matrix)
    query_rot, query_back = jax.vjp(head_path, queries, query_norm.astype(jnp.float32))
    key_rot, key_back = jax.vjp(head_path, keys_raw, key_norm.astype(jnp.float32))
    query_low = query_rot.astype(jnp.bfloat16).reshape(row_count, length, KV_HEADS, GROUP, HEAD_DIM)
    key_low = key_rot.astype(jnp.bfloat16)
    value_low = values_raw.astype(jnp.bfloat16).reshape(row_count, length, KV_HEADS, HEAD_DIM)
    all_keys, all_values = (
        lax.all_gather(key_low, "seq", axis=1, tiled=True),
        lax.all_gather(value_low, "seq", axis=1, tiled=True),
    )
    total_length = all_keys.shape[1]
    key_block = min(512, total_length)
    block_count = (positions[length - 1] + key_block) // key_block

    def block_scores(number, key_source, value_source):
        first_key = number * key_block
        keys_here = lax.dynamic_slice_in_dim(key_source, first_key, key_block, 1)
        values_here = lax.dynamic_slice_in_dim(value_source, first_key, key_block, 1)
        key_positions = first_key + jnp.arange(key_block, dtype=jnp.int32)
        key_segment, unused = segment_info(lengths, key_positions)
        scores = (
            jnp.einsum(
                "rtkgh,rskh->rkgts", query_low, keys_here, preferred_element_type=jnp.float32
            )
            * score_scale
        )
        allowed = (segment[:, :, None] == key_segment[:, None, :]) & (
            positions[None, :, None] >= key_positions[None, None, :]
        )
        allowed = allowed[:, None, None]
        return (jnp.where(allowed, scores, NEGATIVE), allowed, keys_here, values_here)

    stat_shape = (row_count, KV_HEADS, GROUP, length)

    def stats_step(number, carried):
        peak_score, running_sum = carried
        scores, allowed, unused_keys, unused_values = block_scores(number, all_keys, all_values)
        new_peak = jnp.maximum(peak_score, jnp.max(scores, axis=-1))
        fresh = jnp.sum(jnp.where(allowed, jnp.exp(scores - new_peak[..., None]), 0.0), axis=-1)
        return (new_peak, running_sum * jnp.exp(peak_score - new_peak) + fresh)

    peak_score, running_sum = lax.fori_loop(
        0,
        block_count,
        stats_step,
        (jnp.full(stat_shape, NEGATIVE, jnp.float32), jnp.zeros(stat_shape, jnp.float32)),
    )
    log_total = peak_score + jnp.log(running_sum)

    def probabilities(scores, allowed):
        return jnp.where(allowed, jnp.exp(scores - log_total[..., None]), 0.0)

    out_shape = (row_count, length, KV_HEADS, GROUP, HEAD_DIM)

    def output_step(number, carried):
        rounded, exact_sum = carried
        scores, allowed, keys_here, values_here = block_scores(number, all_keys, all_values)
        weights = probabilities(scores, allowed)
        rounded = rounded + jnp.einsum(
            "rkgts,rskh->rtkgh",
            weights.astype(jnp.bfloat16),
            values_here,
            preferred_element_type=jnp.float32,
        )
        exact_sum = exact_sum + jnp.einsum(
            "rkgts,rskh->rtkgh", weights, values_here.astype(jnp.float32), precision=HIGHEST
        )
        return (rounded, exact_sum)

    rounded, exact_sum = lax.fori_loop(
        0,
        block_count,
        output_step,
        (jnp.zeros(out_shape, jnp.float32), jnp.zeros(out_shape, jnp.float32)),
    )
    attended_low = rounded.reshape(row_count, length, HEADS * HEAD_DIM).astype(jnp.bfloat16)
    result = hidden + dense(attended_low, output_matrix)

    def attend_backward(gradient):
        gradient_low = gradient.astype(jnp.bfloat16)
        grad_output = weight_grad(attended_low, gradient_low)
        grad_attended = (
            back_dense(gradient_low, output_matrix).astype(jnp.bfloat16).reshape(out_shape)
        )
        row_delta = jnp.einsum(
            "rtkgh,rtkgh->rkgt", grad_attended.astype(jnp.float32), exact_sum, precision=HIGHEST
        )
        key_source, value_source = (all_keys, all_values)

        def grad_step(number, carried):
            grad_query, grad_keys, grad_values = carried
            scores, allowed, keys_here, values_here = block_scores(number, key_source, value_source)
            weights = probabilities(scores, allowed)
            grad_weights = jnp.einsum(
                "rtkgh,rskh->rkgts", grad_attended, values_here, preferred_element_type=jnp.float32
            )
            grad_scores = (weights * (grad_weights - row_delta[..., None])).astype(jnp.bfloat16)
            grad_query = (
                grad_query
                + jnp.einsum(
                    "rkgts,rskh->rtkgh", grad_scores, keys_here, preferred_element_type=jnp.float32
                )
                * score_scale
            )
            key_part = (
                jnp.einsum(
                    "rkgts,rtkgh->rskh", grad_scores, query_low, preferred_element_type=jnp.float32
                )
                * score_scale
            )
            value_part = jnp.einsum(
                "rkgts,rtkgh->rskh",
                weights.astype(jnp.bfloat16),
                grad_attended,
                preferred_element_type=jnp.float32,
            )
            grad_keys = lax.dynamic_update_slice_in_dim(grad_keys, key_part, number * key_block, 1)
            grad_values = lax.dynamic_update_slice_in_dim(
                grad_values, value_part, number * key_block, 1
            )
            return (grad_query, grad_keys, grad_values)

        key_shape = (row_count, total_length, KV_HEADS, HEAD_DIM)
        grad_query, grad_keys, grad_values = lax.fori_loop(
            0,
            block_count,
            grad_step,
            (
                jnp.zeros(out_shape, jnp.float32),
                jnp.zeros(key_shape, jnp.float32),
                jnp.zeros(key_shape, jnp.float32),
            ),
        )
        local_keys, local_values = (
            lax.psum_scatter(
                grad_keys.astype(jnp.bfloat16), "seq", scatter_dimension=1, tiled=True
            ).astype(jnp.float32),
            lax.psum_scatter(
                grad_values.astype(jnp.bfloat16), "seq", scatter_dimension=1, tiled=True
            ).astype(jnp.float32),
        )
        grad_queries, grad_query_norm = query_back(
            grad_query.reshape(row_count, length, HEADS, HEAD_DIM)
        )
        grad_keys_raw, grad_key_norm = key_back(local_keys)
        query_grad_low = grad_queries.reshape(row_count, length, HEADS * HEAD_DIM).astype(
            jnp.bfloat16
        )
        key_grad_low = grad_keys_raw.reshape(row_count, length, KV_HEADS * HEAD_DIM).astype(
            jnp.bfloat16
        )
        value_grad_low = local_values.reshape(row_count, length, KV_HEADS * HEAD_DIM).astype(
            jnp.bfloat16
        )
        grad_normed = (
            back_dense(query_grad_low, query_matrix)
            + back_dense(key_grad_low, key_matrix)
            + back_dense(value_grad_low, value_matrix)
        )
        grad_hidden, grad_gain = norm_back(grad_normed)
        return (
            gradient + grad_hidden,
            (
                grad_gain,
                weight_grad(
                    normed_low,
                    jnp.concatenate([query_grad_low, key_grad_low, value_grad_low], axis=-1),
                ),
                grad_query_norm,
                grad_key_norm,
                grad_output,
            ),
        )

    return (result, attend_backward)


def reduce_entries(pairs, shards, rows, block_rows):
    entries = []
    x_first = g_first = chunk = 0
    for x, g in pairs:
        x_count = x.shape[2]
        g_count = g.shape[1] // COLS
        entries.append((x_first, x_count, g_first, g_count, chunk))
        x_first += x_count
        g_first += g_count
        chunk += x_count * g_count
    return entries, x_first, g_first, chunk


def locate(entries, q):
    x_block, g_block = jnp.int32(0), jnp.int32(0)
    for x_first, x_count, g_first, g_count, chunk in entries:
        here = q - chunk
        inside = here >= 0
        x_block = jnp.where(inside, x_first + lax.rem(jnp.maximum(here, 0), x_count), x_block)
        g_block = jnp.where(inside, g_first + jnp.maximum(here, 0) // x_count, g_block)
    return x_block, g_block


def seq_steps(bits):
    upper = list(range(1, bits))
    middle = (len(upper) + 1) // 2
    kinds = []
    for order in (upper, upper[middle:] + upper[:middle]):
        held = sorted(upper, reverse=True)
        steps = []
        for bit in order:
            place = held.index(bit)
            steps.append((bit, 2**place, 2 ** (len(held) - 1 - place)))
            held.remove(bit)
        kinds.append(steps)
    return kinds


def reduce_kernel(entries, row_count, shards, chunks, *refs):
    count = len(entries)
    xs, gs = refs[:count], refs[count : 2 * count]
    out = refs[2 * count]
    (load_x, load_g, x_all, g_all, send_zero, recv_zero, *rest) = refs[2 * count + 1 :]
    bits = shards.bit_length() - 1
    kinds = seq_steps(bits)
    held, received = [[], []], [[], []]
    for kind in range(2):
        for _ in kinds[kind]:
            held[kind].append(rest.pop(0))
            received[kind].append(rest.pop(0))
    z_own, z_in, z_part, z_cross, z_total = rest[:5]
    seq_send, seq_recv, z_send, z_recv, out_sem = rest[5:]
    row, seq = lax.axis_index("row"), lax.axis_index("seq")
    bit_value = [lax.rem(seq // (1 << bit), 2) for bit in range(bits)]
    partner = [seq + (1 << bit) * (1 - 2 * bit_value[bit]) for bit in range(bits)]
    pairs = chunks // 2

    for at, (x_first, x_count, g_first, g_count, _) in enumerate(entries):
        pltpu.make_async_copy(
            xs[at], x_all.at[:, :, pl.ds(x_first, x_count)], load_x.at[at]
        ).start()
        pltpu.make_async_copy(
            gs[at], g_all.at[:, pl.ds(g_first * COLS, g_count * COLS)], load_g.at[at]
        ).start()

    barrier = pltpu.get_barrier_semaphore()
    for bit in range(bits):
        pl.semaphore_signal(barrier, inc=1, device_id=(row, partner[bit]), device_id_type=MESH)
    for step in (1, row_count - 1):
        pl.semaphore_signal(
            barrier, inc=1, device_id=(lax.rem(row + step, row_count), seq), device_id_type=MESH
        )
    pl.semaphore_wait(barrier, bits + 2)

    for at, (x_first, x_count, g_first, g_count, _) in enumerate(entries):
        pltpu.make_async_copy(
            xs[at], x_all.at[:, :, pl.ds(x_first, x_count)], load_x.at[at]
        ).wait()
        pltpu.make_async_copy(
            gs[at], g_all.at[:, pl.ds(g_first * COLS, g_count * COLS)], load_g.at[at]
        ).wait()

    def product(q, side):
        x_block, g_block = locate(entries, q)
        left = x_all[:, side, x_block]
        columns = pl.ds(pl.multiple_of(g_block * COLS, COLS), COLS)
        return jnp.dot(
            left.reshape(left.shape[0] * left.shape[1], left.shape[2]),
            g_all[:, columns],
            preferred_element_type=jnp.float32,
        )

    def seq_copy(kind, step, slot):
        if step == 0:
            bit = 0
            source, target = send_zero.at[kind, slot], recv_zero.at[kind, slot]
        else:
            bit = kinds[kind][step - 1][0]
            source = held[kind][step - 1].at[slot, :, 1 - bit_value[bit]]
            target = received[kind][step - 1].at[slot]
        return pltpu.make_async_remote_copy(
            src_ref=source,
            dst_ref=target,
            send_sem=seq_send.at[kind, step, slot],
            recv_sem=seq_recv.at[kind, step, slot],
            device_id=(row, partner[bit]),
            device_id_type=MESH,
        )

    def seq_sum(kind, step, slot, q):
        if step == 1:
            mine = product(q, bit_value[0])
            other = recv_zero[kind, slot].astype(jnp.float32)
            return mine + other.reshape(mine.shape)
        bit = kinds[kind][step - 2][0]
        mine = held[kind][step - 2][slot, :, bit_value[bit]].astype(jnp.float32)
        return mine + received[kind][step - 2][slot].astype(jnp.float32)

    half = row_count // 2
    depth = half - 1
    lower = row < half
    level = jnp.where(lower, row, row_count - 1 - row)
    toward = jnp.where(lower, row + 1, row - 1)
    away = jnp.where(lower, row - 1, row + 1)

    def z_copy(kind, step, slot):
        if step < depth:
            source = z_own if step == 0 else z_part
            target, where = z_in, toward
        elif step == depth:
            source = z_own if depth == 0 else z_part
            target, where = z_cross, toward
        else:
            source, target, where = z_total, z_total, away
        return pltpu.make_async_remote_copy(
            src_ref=source.at[kind, slot],
            dst_ref=target.at[kind, slot],
            send_sem=z_send.at[kind, step, slot],
            recv_sem=z_recv.at[kind, step, slot],
            device_id=(where, seq),
            device_id_type=MESH,
        )

    def out_copy(kind, slot, q):
        return pltpu.make_async_copy(z_total.at[kind, slot], out.at[q], out_sem.at[kind, slot])

    def each(stage, i, run):
        index = i - stage

        @pl.when(jnp.logical_and(index >= 0, index < pairs))
        def _():
            for kind in range(2):
                run(kind, index, 2 * index + kind)

    def first(kind, index, q):
        slot = lax.rem(index, SLOTS)
        send_zero[kind, slot] = product(q, 1 - bit_value[0]).astype(jnp.bfloat16).reshape(
            send_zero.shape[2:]
        )
        seq_copy(kind, 0, slot).start()

    def middle(step):
        def run(kind, index, q):
            slot = lax.rem(index, SLOTS)
            seq_copy(kind, step - 1, slot).wait()
            total = seq_sum(kind, step, slot, q)
            target = held[kind][step - 1]
            target[slot] = total.astype(jnp.bfloat16).reshape(target.shape[1:])
            seq_copy(kind, step, slot).start()

        return run

    def last(kind, index, q):
        slot, z_slot = lax.rem(index, SLOTS), lax.rem(index, ZSLOTS)
        seq_copy(kind, bits - 1, slot).wait()
        total = seq_sum(kind, bits, slot, q)
        z_own[kind, z_slot] = total.astype(jnp.bfloat16).reshape(z_own.shape[2:])

        @pl.when(level == 0)
        def _():
            z_copy(kind, 0, z_slot).start()

    def z_stage(step):
        def run(kind, index, q):
            slot = lax.rem(index, ZSLOTS)
            if step <= depth:

                @pl.when(level == step)
                def _():
                    z_copy(kind, step - 1, slot).wait_recv()
                    z_part[kind, slot] = (
                        z_own[kind, slot].astype(jnp.float32) + z_in[kind, slot].astype(jnp.float32)
                    ).astype(jnp.bfloat16)
                    z_copy(kind, step, slot).start()

                @pl.when(level == step - 1)
                def _():
                    z_copy(kind, step - 1, slot).wait_send()

            elif step == depth + 1:

                @pl.when(level == depth)
                def _():
                    z_copy(kind, depth, slot).wait()
                    own = z_own if depth == 0 else z_part
                    z_total[kind, slot] = (
                        own[kind, slot].astype(jnp.float32) + z_cross[kind, slot].astype(jnp.float32)
                    ).astype(jnp.bfloat16)
                    if depth > 0:
                        z_copy(kind, step, slot).start()
                    out_copy(kind, slot, q).start()

            else:
                receiver = 2 * depth + 1 - step

                @pl.when(level == receiver)
                def _():
                    z_copy(kind, step - 1, slot).wait_recv()
                    if receiver > 0:
                        z_copy(kind, step, slot).start()
                    out_copy(kind, slot, q).start()

                @pl.when(level == receiver + 1)
                def _():
                    z_copy(kind, step - 1, slot).wait_send()

        return run

    def finish(kind, index, q):
        out_copy(kind, lax.rem(index, ZSLOTS), q).wait()

    stages = [first]
    stages += [middle(step) for step in range(1, bits)]
    stages += [last]
    stages += [z_stage(step) for step in range(1, 2 * depth + 2)]
    stages += [finish]

    def iteration(i, carried):
        for stage, run in enumerate(stages):
            each(stage, i, run)
        return carried

    lax.fori_loop(0, pairs + len(stages) - 1, iteration, 0)


def reduce_gradients(pairs, row_count, shards, collective_id):
    block_rows, tokens = pairs[0][0].shape[3:]
    entries, x_blocks, g_blocks, chunks = reduce_entries(pairs, shards, row_count, block_rows)
    bits = shards.bit_length() - 1
    block = (block_rows, COLS)
    comm = []
    for steps in seq_steps(bits):
        for _, above, below in steps:
            comm.append(pltpu.VMEM((SLOTS, above, 2, below) + block, jnp.bfloat16))
            comm.append(pltpu.VMEM((SLOTS, above, below) + block, jnp.bfloat16))
    z_steps = row_count - 1
    result = pl.pallas_call(
        functools.partial(reduce_kernel, entries, row_count, shards, chunks),
        out_shape=jax.ShapeDtypeStruct((chunks,) + block, jnp.bfloat16),
        in_specs=[pl.BlockSpec(memory_space=pl.ANY)] * (2 * len(pairs)),
        out_specs=pl.BlockSpec(memory_space=pl.ANY),
        scratch_shapes=[
            pltpu.SemaphoreType.DMA((len(pairs),)),
            pltpu.SemaphoreType.DMA((len(pairs),)),
            pltpu.VMEM((shards // 2, 2, x_blocks, block_rows, tokens), jnp.bfloat16),
            pltpu.VMEM((tokens, g_blocks * COLS), jnp.bfloat16),
            pltpu.VMEM((2, SLOTS, shards // 2) + block, jnp.bfloat16),
            pltpu.VMEM((2, SLOTS, shards // 2) + block, jnp.bfloat16),
            *comm,
            *[pltpu.VMEM((2, ZSLOTS) + block, jnp.bfloat16) for _ in range(5)],
            pltpu.SemaphoreType.DMA((2, bits, SLOTS)),
            pltpu.SemaphoreType.DMA((2, bits, SLOTS)),
            pltpu.SemaphoreType.DMA((2, z_steps, ZSLOTS)),
            pltpu.SemaphoreType.DMA((2, z_steps, ZSLOTS)),
            pltpu.SemaphoreType.DMA((2, ZSLOTS)),
        ],
        compiler_params=pltpu.CompilerParams(
            collective_id=collective_id, has_side_effects=True, vmem_limit_bytes=52 * 2**20
        ),
        cost_estimate=pl.CostEstimate(
            flops=2 * chunks * shards * block_rows * COLS * tokens,
            bytes_accessed=2 * chunks * block_rows * COLS,
            transcendentals=0,
        ),
    )(*[x for x, _ in pairs], *[g for _, g in pairs])
    pieces = []
    for _, x_count, _, g_count, chunk in entries:
        piece = result[chunk : chunk + x_count * g_count].reshape((g_count, x_count) + block)
        pieces.append(
            piece.transpose(1, 2, 0, 3).reshape(x_count * block_rows, g_count * COLS)
        )
    return pieces


def body(
    tokens,
    lengths,
    mixer_gain,
    mixer_input,
    mixer_kernel,
    mixer_output,
    first_gain,
    first_gate,
    first_up,
    first_down,
    attend_gain,
    query_weight,
    key_weight,
    value_weight,
    query_gain,
    key_gain,
    attend_output,
    second_gain,
    second_gate,
    second_up,
    second_down,
    cotangent,
):
    length = tokens.shape[1]
    positions = lax.axis_index("seq") * length + jnp.arange(length, dtype=jnp.int32)
    segment, seg_start = segment_info(lengths, positions)
    offsets = positions[None, :] - seg_start
    hidden = tokens.astype(jnp.float32)
    hidden, mixer_back = mixer_block(
        hidden, mixer_gain, mixer_input, mixer_kernel, mixer_output, seg_start, positions
    )
    hidden, first_back = feed_block(hidden, first_gain, first_gate, first_up, first_down)
    hidden, attend_back = attend_block(
        hidden,
        lengths,
        attend_gain,
        query_weight,
        key_weight,
        value_weight,
        query_gain,
        key_gain,
        attend_output,
        segment,
        positions,
        offsets,
    )
    hidden, second_back = feed_block(hidden, second_gain, second_gate, second_up, second_down)
    gradient = cotangent.astype(jnp.float32)
    gradient, second_grads = second_back(gradient)
    gradient, attend_grads = attend_back(gradient)
    gradient, first_grads = first_back(gradient)
    gradient, mixer_grads = mixer_back(gradient)
    second_gain_sum, second_wide, second_down_pair = second_grads
    attend_gain_sum, attend_wide, query_gain_sum, key_gain_sum, attend_output_pair = attend_grads
    first_gain_sum, first_wide, first_down_pair = first_grads
    mixer_gain_sum, mixer_input_pair, mixer_kernel_sum, mixer_output_pair = mixer_grads
    row_count, shards = lax.axis_size("row"), lax.axis_size("seq")
    block_rows = math.gcd(tokens.shape[2] // shards, first_down.shape[0] // shards)

    def operands(pair):
        inputs, gradient_low = pair
        token_count = inputs.shape[0] * inputs.shape[1]
        inputs = inputs.reshape(token_count, -1).T
        blocks = inputs.shape[0] // shards // block_rows
        return (
            inputs.reshape(shards // 2, 2, blocks, block_rows, token_count),
            gradient_low.reshape(token_count, -1),
        )

    wide_vectors = jnp.concatenate(
        [
            mixer_kernel_sum,
            jnp.stack([mixer_gain_sum, first_gain_sum, attend_gain_sum, second_gain_sum]),
        ]
    )
    vector_count = wide_vectors.shape[0]
    vectors = jnp.concatenate(
        [
            part.reshape(-1, shards, part.shape[-1] // shards)
            .transpose(1, 0, 2)
            .reshape(shards, -1)
            for part in (wide_vectors, jnp.stack([query_gain_sum, key_gain_sum]))
        ],
        axis=1,
    )
    vector_rows = -(-vectors.shape[1] // COLS)
    token_count = tokens.shape[0] * tokens.shape[1]
    vectors = jnp.pad(vectors, ((0, 0), (0, vector_rows * COLS - vectors.shape[1])))
    vectors = vectors.reshape(shards * vector_rows, COLS).astype(jnp.bfloat16)
    vectors = jnp.pad(vectors, ((0, token_count - shards * vector_rows), (0, 0)))
    shard_at = lax.broadcasted_iota(jnp.int32, (shards, 2 * block_rows, token_count), 0)
    row_at = lax.broadcasted_iota(jnp.int32, (shards, 2 * block_rows, token_count), 1)
    token_at = lax.broadcasted_iota(jnp.int32, (shards, 2 * block_rows, token_count), 2)
    picks = (row_at < vector_rows) & (token_at == shard_at * vector_rows + row_at)
    picks = picks.astype(jnp.bfloat16).reshape(shards // 2, 2, 2, block_rows, token_count)
    (
        grad_second_down,
        second_both,
        grad_attend_output,
        attend_three,
        grad_first_down,
        first_both,
        grad_mixer_output,
        grad_mixer_input,
        vector_sums,
    ) = reduce_gradients(
        [
            operands(second_down_pair),
            operands(second_wide),
            operands(attend_output_pair),
            operands(attend_wide),
            operands(first_down_pair),
            operands(first_wide),
            operands(mixer_output_pair),
            operands(mixer_input_pair),
            (picks, vectors),
        ],
        row_count,
        shards,
        0,
    )

    def single(value):
        return value.astype(jnp.float32)

    hidden_columns = first_gate.shape[1]
    query_columns, key_columns = query_weight.shape[1], key_weight.shape[1]
    vector_sums = single(vector_sums[:vector_rows]).reshape(-1)
    width = tokens.shape[2] // shards
    wide_sums = vector_sums[: vector_count * width].reshape(vector_count, width)
    head_width = HEAD_DIM // shards
    head_sums = vector_sums[vector_count * width :][: 2 * head_width].reshape(2, head_width)
    return (
        hidden.astype(jnp.bfloat16),
        gradient.astype(jnp.bfloat16),
        wide_sums[3],
        single(grad_mixer_input),
        wide_sums[:3],
        single(grad_mixer_output),
        wide_sums[4],
        single(first_both[:, :hidden_columns]),
        single(first_both[:, hidden_columns:]),
        single(grad_first_down),
        wide_sums[5],
        single(attend_three[:, :query_columns]),
        single(attend_three[:, query_columns : query_columns + key_columns]),
        single(attend_three[:, query_columns + key_columns :]),
        head_sums[0],
        head_sums[1],
        single(grad_attend_output),
        wide_sums[6],
        single(second_both[:, :hidden_columns]),
        single(second_both[:, hidden_columns:]),
        single(grad_second_down),
    )


def solution(mesh):
    in_specs = (
        P("row", "seq", None),
        P("row", None),
        P(),
        P(),
        P(),
        P(),
        P(),
        P(),
        P(),
        P(),
        P(),
        P(),
        P(),
        P(),
        P(),
        P(),
        P(),
        P(),
        P(),
        P(),
        P(),
        P("row", "seq", None),
    )
    out_specs = (
        P("row", "seq", None),
        P("row", "seq", None),
        P("seq"),
        P("seq", None),
        P(None, "seq"),
        P("seq", None),
        P("seq"),
        P("seq", None),
        P("seq", None),
        P("seq", None),
        P("seq"),
        P("seq", None),
        P("seq", None),
        P("seq", None),
        P("seq"),
        P("seq"),
        P("seq", None),
        P("seq"),
        P("seq", None),
        P("seq", None),
        P("seq", None),
    )
    return jax.shard_map(body, mesh=mesh, in_specs=in_specs, out_specs=out_specs, check_vma=False)
```

```python
import functools
import math
import types

import jax
import jax.numpy as jnp
from jax import lax
from jax.experimental import pallas as pl
from jax.experimental.pallas import tpu as pltpu
from jax.sharding import PartitionSpec as P

HEADS = 16
KV_HEADS = 8
HEAD_DIM = 64
GROUP = 2


EPS = 1e-05
THETA = 1000000.0
NEGATIVE = -1e30
HIGHEST = lax.Precision.HIGHEST
MESH = pl.DeviceIdType.MESH
COLS = 512
SLOTS = 4
ZSLOTS = 6


def passed_along(value, axis, steps):
    count = lax.axis_size(axis)
    initial, last = (max(0, -steps), min(count, count - steps))
    return lax.ppermute(value, axis, [(source, source + steps) for source in range(initial, last)])


def segment_info(lengths, positions):
    boundary = jnp.cumsum(lengths, axis=-1)
    passed = boundary[:, None, :] <= positions[None, :, None]
    segment = jnp.sum(passed.astype(jnp.int32), axis=-1)
    seg_start = jnp.max(jnp.where(passed, boundary[:, None, :], 0), axis=-1)
    return (segment, seg_start)


def norm_rows(values, norm_gain):
    return values * lax.rsqrt(jnp.mean(values * values, axis=-1, keepdims=True) + EPS) * norm_gain


def rotate(values, offsets):
    half_dim = values.shape[-1] // 2
    inverse = THETA ** (-2.0 * jnp.arange(half_dim, dtype=jnp.float32) / values.shape[-1])
    angles = offsets.astype(jnp.float32)[:, :, None, None] * inverse
    cosine = jnp.cos(angles)
    sine_table = jnp.sin(angles)
    leading = values[..., :half_dim]
    trailing = values[..., half_dim:]
    return jnp.concatenate(
        [leading * cosine - trailing * sine_table, trailing * cosine + leading * sine_table],
        axis=-1,
    )


def swiglu(gate_value, upward):
    return gate_value / (1.0 + jnp.exp(-gate_value)) * upward


def dense(inputs, matrix):
    return jnp.einsum("rtd,df->rtf", inputs, matrix, preferred_element_type=jnp.float32)


def weight_grad(inputs, gradient):
    return (inputs, gradient)


def back_dense(gradient, matrix):
    return jnp.einsum("rtf,df->rtd", gradient, matrix, preferred_element_type=jnp.float32)


def mixer_block(hidden, norm_gain, input_matrix, kernel, output_matrix, seg_start, positions):
    feature_columns = hidden.shape[-1]
    length = hidden.shape[1]
    normed, norm_back = jax.vjp(norm_rows, hidden, norm_gain.astype(jnp.float32))
    normed_low = normed.astype(jnp.bfloat16)
    projected_rows = dense(normed_low, input_matrix)
    input_gate_value = projected_rows[..., :feature_columns]
    exit_gate = projected_rows[..., feature_columns : 2 * feature_columns]
    carry_value = projected_rows[..., 2 * feature_columns :]
    gated_product_reduced = (input_gate_value * carry_value).astype(jnp.bfloat16)
    previous = passed_along(gated_product_reduced[:, length - 2 :, :], "seq", 1)
    extended = jnp.concatenate([previous, gated_product_reduced], axis=1).astype(jnp.float32)
    keep_one = (positions[None, :] - 1 >= seg_start).astype(jnp.float32)[..., None]
    keep_two = (positions[None, :] - 2 >= seg_start).astype(jnp.float32)[..., None]
    kernel_taps = kernel.astype(jnp.float32)
    two_back = extended[:, :length]
    one_back = extended[:, 1 : length + 1]
    current = extended[:, 2:]
    convolved = (
        kernel_taps[2] * current
        + kernel_taps[1] * keep_one * one_back
        + kernel_taps[0] * keep_two * two_back
    )
    gated_low = (exit_gate * convolved).astype(jnp.bfloat16)
    result = hidden + dense(gated_low, output_matrix)

    def mixer_backward(gradient):
        gradient_low = gradient.astype(jnp.bfloat16)
        grad_output = weight_grad(gated_low, gradient_low)
        grad_gated = back_dense(gradient_low, output_matrix)
        output_gate_gradient = grad_gated * convolved
        grad_conv = grad_gated * exit_gate
        grad_kernel = jnp.stack(
            [
                jnp.sum(grad_conv * keep_two * two_back, axis=(0, 1)),
                jnp.sum(grad_conv * keep_one * one_back, axis=(0, 1)),
                jnp.sum(grad_conv * current, axis=(0, 1)),
            ]
        )
        grad_extended = jnp.pad(kernel_taps[0] * keep_two * grad_conv, ((0, 0), (0, 2), (0, 0)))
        grad_extended = grad_extended + jnp.pad(
            kernel_taps[1] * keep_one * grad_conv, ((0, 0), (1, 1), (0, 0))
        )
        grad_extended = grad_extended + jnp.pad(
            kernel_taps[2] * grad_conv, ((0, 0), (2, 0), (0, 0))
        )
        returned = passed_along(grad_extended[:, :2, :], "seq", -1)
        gated_product_gradient = grad_extended[:, 2:] + jnp.pad(
            returned, ((0, 0), (length - 2, 0), (0, 0))
        )
        grad_projected = jnp.concatenate(
            [
                gated_product_gradient * carry_value,
                output_gate_gradient,
                gated_product_gradient * input_gate_value,
            ],
            axis=-1,
        ).astype(jnp.bfloat16)
        grad_input = weight_grad(normed_low, grad_projected)
        grad_normed = back_dense(grad_projected, input_matrix)
        grad_hidden, grad_gain = norm_back(grad_normed)
        return (gradient + grad_hidden, (grad_gain, grad_input, grad_kernel, grad_output))

    return (result, mixer_backward)


def feed_block(hidden, norm_gain, gate_matrix, up_matrix, down_matrix):
    normed, norm_back = jax.vjp(norm_rows, hidden, norm_gain.astype(jnp.float32))
    normed_low = normed.astype(jnp.bfloat16)
    gate_value = dense(normed_low, gate_matrix)
    upward = dense(normed_low, up_matrix)
    active, active_back = jax.vjp(swiglu, gate_value, upward)
    active_low = active.astype(jnp.bfloat16)
    result = hidden + dense(active_low, down_matrix)

    def feed_backward(gradient):
        gradient_low = gradient.astype(jnp.bfloat16)
        grad_down = weight_grad(active_low, gradient_low)
        grad_gate, grad_upward = active_back(back_dense(gradient_low, down_matrix))
        gate_low = grad_gate.astype(jnp.bfloat16)
        upward_low = grad_upward.astype(jnp.bfloat16)
        grad_normed = back_dense(gate_low, gate_matrix) + back_dense(upward_low, up_matrix)
        grad_hidden, grad_gain = norm_back(grad_normed)
        return (
            gradient + grad_hidden,
            (
                grad_gain,
                weight_grad(normed_low, jnp.concatenate([gate_low, upward_low], axis=-1)),
                grad_down,
            ),
        )

    return (result, feed_backward)


def attend_block(
    hidden,
    lengths,
    norm_gain,
    query_matrix,
    key_matrix,
    value_matrix,
    query_norm,
    key_norm,
    output_matrix,
    segment,
    positions,
    offsets,
):
    row_count, length, feature_columns = hidden.shape
    score_scale = HEAD_DIM ** (-0.5)
    normed, norm_back = jax.vjp(norm_rows, hidden, norm_gain.astype(jnp.float32))
    normed_low = normed.astype(jnp.bfloat16)

    def head_path(projected_rows, head_gain):
        return rotate(norm_rows(projected_rows, head_gain), offsets)

    queries = dense(normed_low, query_matrix).reshape(row_count, length, HEADS, HEAD_DIM)
    keys_raw = dense(normed_low, key_matrix).reshape(row_count, length, KV_HEADS, HEAD_DIM)
    values_raw = dense(normed_low, value_matrix)
    query_rot, query_back = jax.vjp(head_path, queries, query_norm.astype(jnp.float32))
    key_rot, key_back = jax.vjp(head_path, keys_raw, key_norm.astype(jnp.float32))
    query_low = query_rot.astype(jnp.bfloat16).reshape(row_count, length, KV_HEADS, GROUP, HEAD_DIM)
    key_low = key_rot.astype(jnp.bfloat16)
    value_low = values_raw.astype(jnp.bfloat16).reshape(row_count, length, KV_HEADS, HEAD_DIM)
    all_keys, all_values = (
        lax.all_gather(key_low, "seq", axis=1, tiled=True),
        lax.all_gather(value_low, "seq", axis=1, tiled=True),
    )
    total_length = all_keys.shape[1]
    key_block = min(512, total_length)
    block_count = (positions[length - 1] + key_block) // key_block

    def block_scores(number, key_source, value_source):
        first_key = number * key_block
        keys_here = lax.dynamic_slice_in_dim(key_source, first_key, key_block, 1)
        values_here = lax.dynamic_slice_in_dim(value_source, first_key, key_block, 1)
        key_positions = first_key + jnp.arange(key_block, dtype=jnp.int32)
        key_segment, unused = segment_info(lengths, key_positions)
        scores = (
            jnp.einsum(
                "rtkgh,rskh->rkgts", query_low, keys_here, preferred_element_type=jnp.float32
            )
            * score_scale
        )
        allowed = (segment[:, :, None] == key_segment[:, None, :]) & (
            positions[None, :, None] >= key_positions[None, None, :]
        )
        allowed = allowed[:, None, None]
        return (jnp.where(allowed, scores, NEGATIVE), allowed, keys_here, values_here)

    stat_shape = (row_count, KV_HEADS, GROUP, length)

    def stats_step(number, carried):
        peak_score, running_sum = carried
        scores, allowed, unused_keys, unused_values = block_scores(number, all_keys, all_values)
        new_peak = jnp.maximum(peak_score, jnp.max(scores, axis=-1))
        fresh = jnp.sum(jnp.where(allowed, jnp.exp(scores - new_peak[..., None]), 0.0), axis=-1)
        return (new_peak, running_sum * jnp.exp(peak_score - new_peak) + fresh)

    peak_score, running_sum = lax.fori_loop(
        0,
        block_count,
        stats_step,
        (jnp.full(stat_shape, NEGATIVE, jnp.float32), jnp.zeros(stat_shape, jnp.float32)),
    )
    log_total = peak_score + jnp.log(running_sum)

    def probabilities(scores, allowed):
        return jnp.where(allowed, jnp.exp(scores - log_total[..., None]), 0.0)

    out_shape = (row_count, length, KV_HEADS, GROUP, HEAD_DIM)

    def output_step(number, carried):
        rounded, exact_sum = carried
        scores, allowed, keys_here, values_here = block_scores(number, all_keys, all_values)
        weights = probabilities(scores, allowed)
        rounded = rounded + jnp.einsum(
            "rkgts,rskh->rtkgh",
            weights.astype(jnp.bfloat16),
            values_here,
            preferred_element_type=jnp.float32,
        )
        exact_sum = exact_sum + jnp.einsum(
            "rkgts,rskh->rtkgh", weights, values_here.astype(jnp.float32), precision=HIGHEST
        )
        return (rounded, exact_sum)

    rounded, exact_sum = lax.fori_loop(
        0,
        block_count,
        output_step,
        (jnp.zeros(out_shape, jnp.float32), jnp.zeros(out_shape, jnp.float32)),
    )
    attended_low = rounded.reshape(row_count, length, HEADS * HEAD_DIM).astype(jnp.bfloat16)
    result = hidden + dense(attended_low, output_matrix)

    def attend_backward(gradient):
        gradient_low = gradient.astype(jnp.bfloat16)
        grad_output = weight_grad(attended_low, gradient_low)
        grad_attended = (
            back_dense(gradient_low, output_matrix).astype(jnp.bfloat16).reshape(out_shape)
        )
        row_delta = jnp.einsum(
            "rtkgh,rtkgh->rkgt", grad_attended.astype(jnp.float32), exact_sum, precision=HIGHEST
        )
        key_source, value_source = (all_keys, all_values)

        def grad_step(number, carried):
            grad_query, grad_keys, grad_values = carried
            scores, allowed, keys_here, values_here = block_scores(number, key_source, value_source)
            weights = probabilities(scores, allowed)
            grad_weights = jnp.einsum(
                "rtkgh,rskh->rkgts", grad_attended, values_here, preferred_element_type=jnp.float32
            )
            grad_scores = (weights * (grad_weights - row_delta[..., None])).astype(jnp.bfloat16)
            grad_query = (
                grad_query
                + jnp.einsum(
                    "rkgts,rskh->rtkgh", grad_scores, keys_here, preferred_element_type=jnp.float32
                )
                * score_scale
            )
            key_part = (
                jnp.einsum(
                    "rkgts,rtkgh->rskh", grad_scores, query_low, preferred_element_type=jnp.float32
                )
                * score_scale
            )
            value_part = jnp.einsum(
                "rkgts,rtkgh->rskh",
                weights.astype(jnp.bfloat16),
                grad_attended,
                preferred_element_type=jnp.float32,
            )
            grad_keys = lax.dynamic_update_slice_in_dim(grad_keys, key_part, number * key_block, 1)
            grad_values = lax.dynamic_update_slice_in_dim(
                grad_values, value_part, number * key_block, 1
            )
            return (grad_query, grad_keys, grad_values)

        key_shape = (row_count, total_length, KV_HEADS, HEAD_DIM)
        grad_query, grad_keys, grad_values = lax.fori_loop(
            0,
            block_count,
            grad_step,
            (
                jnp.zeros(out_shape, jnp.float32),
                jnp.zeros(key_shape, jnp.float32),
                jnp.zeros(key_shape, jnp.float32),
            ),
        )
        local_keys, local_values = (
            lax.psum_scatter(
                grad_keys.astype(jnp.bfloat16), "seq", scatter_dimension=1, tiled=True
            ).astype(jnp.float32),
            lax.psum_scatter(
                grad_values.astype(jnp.bfloat16), "seq", scatter_dimension=1, tiled=True
            ).astype(jnp.float32),
        )
        grad_queries, grad_query_norm = query_back(
            grad_query.reshape(row_count, length, HEADS, HEAD_DIM)
        )
        grad_keys_raw, grad_key_norm = key_back(local_keys)
        query_grad_low = grad_queries.reshape(row_count, length, HEADS * HEAD_DIM).astype(
            jnp.bfloat16
        )
        key_grad_low = grad_keys_raw.reshape(row_count, length, KV_HEADS * HEAD_DIM).astype(
            jnp.bfloat16
        )
        value_grad_low = local_values.reshape(row_count, length, KV_HEADS * HEAD_DIM).astype(
            jnp.bfloat16
        )
        grad_normed = (
            back_dense(query_grad_low, query_matrix)
            + back_dense(key_grad_low, key_matrix)
            + back_dense(value_grad_low, value_matrix)
        )
        grad_hidden, grad_gain = norm_back(grad_normed)
        return (
            gradient + grad_hidden,
            (
                grad_gain,
                weight_grad(
                    normed_low,
                    jnp.concatenate([query_grad_low, key_grad_low, value_grad_low], axis=-1),
                ),
                grad_query_norm,
                grad_key_norm,
                grad_output,
            ),
        )

    return (result, attend_backward)


def reduce_entries(pairs):
    entries = []
    x_first = g_first = chunk = 0
    for x_count, g_count in pairs:
        entries.append((x_first, x_count, g_first, g_count, chunk))
        x_first += x_count
        g_first += g_count
        chunk += x_count * g_count
    return entries, x_first, g_first, chunk


def locate(entries, q):
    x_block, g_block = jnp.int32(0), jnp.int32(0)
    for x_first, x_count, g_first, g_count, chunk in entries:
        here = q - chunk
        inside = here >= 0
        x_block = jnp.where(inside, x_first + lax.rem(jnp.maximum(here, 0), x_count), x_block)
        g_block = jnp.where(inside, g_first + jnp.maximum(here, 0) // x_count, g_block)
    return x_block, g_block


def seq_steps(bits):
    upper = list(range(1, bits))
    middle = (len(upper) + 1) // 2
    kinds = []
    for order in (upper, upper[middle:] + upper[:middle]):
        held = sorted(upper, reverse=True)
        steps = []
        for bit in order:
            place = held.index(bit)
            steps.append((bit, 2**place, 2 ** (len(held) - 1 - place)))
            held.remove(bit)
        kinds.append(steps)
    return kinds


def exchange_scratch(row_count, shards, block_rows, x_blocks, g_blocks, tokens):
    bits = shards.bit_length() - 1
    block = (block_rows, COLS)
    comm = []
    for steps in seq_steps(bits):
        for _, above, below in steps:
            comm.append(pltpu.VMEM((SLOTS, above, 2, below) + block, jnp.bfloat16))
            comm.append(pltpu.VMEM((SLOTS, above, below) + block, jnp.bfloat16))
    z_steps = row_count - 1
    return [
        pltpu.VMEM((shards // 2, 2, x_blocks, block_rows, tokens), jnp.bfloat16),
        pltpu.VMEM((tokens, g_blocks * COLS), jnp.bfloat16),
        pltpu.VMEM((2, SLOTS, shards // 2) + block, jnp.bfloat16),
        pltpu.VMEM((2, SLOTS, shards // 2) + block, jnp.bfloat16),
        *comm,
        *[pltpu.VMEM((2, ZSLOTS) + block, jnp.bfloat16) for _ in range(5)],
        pltpu.SemaphoreType.DMA((2, bits, SLOTS)),
        pltpu.SemaphoreType.DMA((2, bits, SLOTS)),
        pltpu.SemaphoreType.DMA((2, z_steps, ZSLOTS)),
        pltpu.SemaphoreType.DMA((2, z_steps, ZSLOTS)),
        pltpu.SemaphoreType.DMA((2, ZSLOTS)),
    ]


class Exchange:
    def __init__(self, entries, row_count, shards, outs, scratch, locals_at=(), local=None):
        self.entries, self.outs = entries, outs
        self.locals_at, self.local = locals_at, local
        self.bits = bits = shards.bit_length() - 1
        self.kinds = seq_steps(bits)
        (self.x_all, self.g_all, self.send_zero, self.recv_zero, *rest) = scratch
        self.held, self.received = [[], []], [[], []]
        for kind in range(2):
            for _ in self.kinds[kind]:
                self.held[kind].append(rest.pop(0))
                self.received[kind].append(rest.pop(0))
        self.z_own, self.z_in, self.z_part, self.z_cross, self.z_total = rest[:5]
        self.seq_send, self.seq_recv, self.z_send, self.z_recv, self.out_sem = rest[5:]
        self.row, self.seq = lax.axis_index("row"), lax.axis_index("seq")
        self.row_count, self.shards = row_count, shards
        self.value = [lax.rem(self.seq // (1 << bit), 2) for bit in range(bits)]
        self.partner = [self.seq + (1 << bit) * (1 - 2 * self.value[bit]) for bit in range(bits)]
        last = entries[-1]
        self.pairs = (last[4] + last[1] * last[3]) // 2 + len(locals_at)
        half = row_count // 2
        self.depth = half - 1
        lower = self.row < half
        self.level = jnp.where(lower, self.row, row_count - 1 - self.row)
        self.toward = jnp.where(lower, self.row + 1, self.row - 1)
        self.away = jnp.where(lower, self.row - 1, self.row + 1)

    def meet(self):
        barrier = pltpu.get_barrier_semaphore()
        others = [(self.row, partner) for partner in self.partner]
        for step in (1, self.row_count - 1):
            others.append((lax.rem(self.row + step, self.row_count), self.seq))
        for step in (1, self.shards - 1):
            others.append((self.row, lax.rem(self.seq + step, self.shards)))
        for other in others:
            pl.semaphore_signal(barrier, inc=1, device_id=other, device_id_type=MESH)
        pl.semaphore_wait(barrier, len(others))

    def is_local(self, index):
        found = index < 0
        for at in self.locals_at:
            found = jnp.logical_or(found, index == at)
        return found

    def chunk(self, kind, index):
        before = sum([jnp.where(index > at, 1, 0) for at in self.locals_at], 0)
        return 2 * (index - before) + kind

    def product(self, kind, index, side):
        x_block, g_block = locate(self.entries, self.chunk(kind, index))
        left = self.x_all[:, side, x_block]
        columns = pl.ds(pl.multiple_of(g_block * COLS, COLS), COLS)
        return jnp.dot(
            left.reshape(left.shape[0] * left.shape[1], left.shape[2]),
            self.g_all[:, columns],
            preferred_element_type=jnp.float32,
        )

    def seq_copy(self, kind, step, slot):
        if step == 0:
            bit = 0
            source, target = self.send_zero.at[kind, slot], self.recv_zero.at[kind, slot]
        else:
            bit = self.kinds[kind][step - 1][0]
            source = self.held[kind][step - 1].at[slot, :, 1 - self.value[bit]]
            target = self.received[kind][step - 1].at[slot]
        return pltpu.make_async_remote_copy(
            src_ref=source,
            dst_ref=target,
            send_sem=self.seq_send.at[kind, step, slot],
            recv_sem=self.seq_recv.at[kind, step, slot],
            device_id=(self.row, self.partner[bit]),
            device_id_type=MESH,
        )

    def seq_sum(self, kind, step, slot):
        bit = self.kinds[kind][step - 2][0]
        mine = self.held[kind][step - 2][slot, :, self.value[bit]].astype(jnp.float32)
        return mine + self.received[kind][step - 2][slot].astype(jnp.float32)

    def z_copy(self, kind, step, slot):
        if step < self.depth:
            source = self.z_own if step == 0 else self.z_part
            target, where = self.z_in, self.toward
        elif step == self.depth:
            source = self.z_own if self.depth == 0 else self.z_part
            target, where = self.z_cross, self.toward
        else:
            source, target, where = self.z_total, self.z_total, self.away
        return pltpu.make_async_remote_copy(
            src_ref=source.at[kind, slot],
            dst_ref=target.at[kind, slot],
            send_sem=self.z_send.at[kind, step, slot],
            recv_sem=self.z_recv.at[kind, step, slot],
            device_id=(where, self.seq),
            device_id_type=MESH,
        )

    def start_out(self, kind, slot, index):
        q = self.chunk(kind, index)
        rows = self.z_total.shape[2]
        for out, (_, x_count, _, g_count, chunk) in zip(self.outs, self.entries):
            here = q - chunk

            @pl.when(jnp.logical_and(here >= 0, here < x_count * g_count))
            def _():
                row_at = pl.multiple_of(lax.rem(here, x_count) * rows, rows)
                column_at = pl.multiple_of(here // x_count * COLS, COLS)
                pltpu.make_async_copy(
                    self.z_total.at[kind, slot],
                    out.at[pl.ds(row_at, rows), pl.ds(column_at, COLS)],
                    self.out_sem.at[kind, slot],
                ).start()

    def first(self, kind, index):
        slot = lax.rem(index, SLOTS)
        target = self.send_zero

        def put():
            target[kind, slot] = (
                self.product(kind, index, 1 - self.value[0])
                .astype(jnp.bfloat16)
                .reshape(target.shape[2:])
            )

        if self.local is None:
            put()
        else:
            pl.when(jnp.logical_not(self.is_local(index)))(put)

            @pl.when(self.is_local(index))
            def _():
                target[kind, slot] = self.local.part(kind, index, 1 - self.value[0])

        self.seq_copy(kind, 0, slot).start()

    def second(self, kind, index):
        slot = lax.rem(index, SLOTS)
        self.seq_copy(kind, 0, slot).wait()
        target = self.held[kind][0]

        def put():
            mine = self.product(kind, index, self.value[0])
            total = mine + self.recv_zero[kind, slot].astype(jnp.float32).reshape(mine.shape)
            target[slot] = total.astype(jnp.bfloat16).reshape(target.shape[1:])

        if self.local is None:
            put()
        else:
            pl.when(jnp.logical_not(self.is_local(index)))(put)

            @pl.when(self.is_local(index))
            def _():
                mine = self.local.part(kind, index, self.value[0]).astype(jnp.float32)
                total = mine + self.recv_zero[kind, slot].astype(jnp.float32)
                target[slot] = total.astype(jnp.bfloat16).reshape(target.shape[1:])

        self.seq_copy(kind, 1, slot).start()

    def middle(self, step):
        def run(kind, index):
            slot = lax.rem(index, SLOTS)
            self.seq_copy(kind, step - 1, slot).wait()
            total = self.seq_sum(kind, step, slot)
            target = self.held[kind][step - 1]
            target[slot] = total.astype(jnp.bfloat16).reshape(target.shape[1:])
            self.seq_copy(kind, step, slot).start()

        return run

    def last(self, kind, index):
        slot, z_slot = lax.rem(index, SLOTS), lax.rem(index, ZSLOTS)
        self.seq_copy(kind, self.bits - 1, slot).wait()
        total = self.seq_sum(kind, self.bits, slot).reshape(self.z_own.shape[2:])

        def put():
            self.z_own[kind, z_slot] = total.astype(jnp.bfloat16)

            @pl.when(self.level == 0)
            def _():
                self.z_copy(kind, 0, z_slot).start()

        if self.local is None:
            put()
        else:
            pl.when(jnp.logical_not(self.is_local(index)))(put)

            @pl.when(self.is_local(index))
            def _():
                self.local.take(kind, index, total)

    def z_stage(self, step):
        level, depth = self.level, self.depth

        def run(kind, index):
            slot = lax.rem(index, ZSLOTS)
            if step <= depth:

                @pl.when(level == step)
                def _():
                    self.z_copy(kind, step - 1, slot).wait_recv()
                    self.z_part[kind, slot] = (
                        self.z_own[kind, slot].astype(jnp.float32)
                        + self.z_in[kind, slot].astype(jnp.float32)
                    ).astype(jnp.bfloat16)
                    self.z_copy(kind, step, slot).start()

                @pl.when(level == step - 1)
                def _():
                    self.z_copy(kind, step - 1, slot).wait_send()

            elif step == depth + 1:

                @pl.when(level == depth)
                def _():
                    self.z_copy(kind, depth, slot).wait()
                    own = self.z_own if depth == 0 else self.z_part
                    self.z_total[kind, slot] = (
                        own[kind, slot].astype(jnp.float32)
                        + self.z_cross[kind, slot].astype(jnp.float32)
                    ).astype(jnp.bfloat16)
                    if depth > 0:
                        self.z_copy(kind, step, slot).start()
                    self.start_out(kind, slot, index)

            else:
                receiver = 2 * depth + 1 - step

                @pl.when(level == receiver)
                def _():
                    self.z_copy(kind, step - 1, slot).wait_recv()
                    if receiver > 0:
                        self.z_copy(kind, step, slot).start()
                    self.start_out(kind, slot, index)

                @pl.when(level == receiver + 1)
                def _():
                    self.z_copy(kind, step - 1, slot).wait_send()

        return run

    def finish(self, kind, index):
        slot = lax.rem(index, ZSLOTS)
        rows = self.z_total.shape[2]
        pltpu.make_async_copy(
            self.z_total.at[kind, slot],
            self.outs[0].at[pl.ds(0, rows), pl.ds(0, COLS)],
            self.out_sem.at[kind, slot],
        ).wait()

    def run(self, task):
        stages = [(self.first, False), (self.second, False)]
        stages += [(self.middle(step), False) for step in range(2, self.bits)]
        stages += [(self.last, False)]
        stages += [(self.z_stage(step), True) for step in range(1, 2 * self.depth + 2)]
        stages += [(self.finish, True)]

        def iteration(i, carried):
            for at, (stage, summed_only) in enumerate(stages):
                index = i - at
                here = jnp.logical_and(index >= 0, index < self.pairs)
                if summed_only and self.locals_at:
                    here = jnp.logical_and(here, jnp.logical_not(self.is_local(index)))

                @pl.when(here)
                def _():
                    for kind in range(2):
                        stage(kind, index)

            if task is not None:
                task(i)
            return carried

        lax.fori_loop(0, self.pairs + len(stages) - 1, iteration, 0)


def reduce_kernel(entries, row_count, shards, *refs):
    count = len(entries)
    xs, gs, outs = refs[:count], refs[count : 2 * count], refs[2 * count : 3 * count]
    load_x, load_g, *scratch = refs[3 * count :]
    exchange = Exchange(entries, row_count, shards, outs, scratch)
    copies = []
    for at, (x_first, x_count, g_first, g_count, _) in enumerate(entries):
        x_part = exchange.x_all.at[:, :, pl.ds(x_first, x_count)]
        g_part = exchange.g_all.at[:, pl.ds(g_first * COLS, g_count * COLS)]
        copies.append(pltpu.make_async_copy(xs[at], x_part, load_x.at[at]))
        copies.append(pltpu.make_async_copy(gs[at], g_part, load_g.at[at]))
    for copy in copies:
        copy.start()
    exchange.meet()
    for copy in copies:
        copy.wait()
    exchange.run(None)


def reduce_gradients(pairs, row_count, shards, collective_id):
    block_rows, tokens = pairs[0][0].shape[3:]
    entries, x_blocks, g_blocks, chunks = reduce_entries(
        [(x.shape[2], g.shape[1] // COLS) for x, g in pairs]
    )
    return pl.pallas_call(
        functools.partial(reduce_kernel, entries, row_count, shards),
        out_shape=[
            jax.ShapeDtypeStruct((x_count * block_rows, g_count * COLS), jnp.bfloat16)
            for _, x_count, _, g_count, _ in entries
        ],
        in_specs=[pl.BlockSpec(memory_space=pl.ANY)] * (2 * len(pairs)),
        out_specs=[pl.BlockSpec(memory_space=pl.ANY)] * len(pairs),
        scratch_shapes=[
            pltpu.SemaphoreType.DMA((len(pairs),)),
            pltpu.SemaphoreType.DMA((len(pairs),)),
            *exchange_scratch(row_count, shards, block_rows, x_blocks, g_blocks, tokens),
        ],
        compiler_params=pltpu.CompilerParams(
            collective_id=collective_id, has_side_effects=True, vmem_limit_bytes=52 * 2**20
        ),
        cost_estimate=pl.CostEstimate(
            flops=2 * chunks * shards * block_rows * COLS * tokens,
            bytes_accessed=2 * chunks * block_rows * COLS,
            transcendentals=0,
        ),
    )(*[x for x, _ in pairs], *[g for _, g in pairs])


def body(
    tokens,
    lengths,
    mixer_gain,
    mixer_input,
    mixer_kernel,
    mixer_output,
    first_gain,
    first_gate,
    first_up,
    first_down,
    attend_gain,
    query_weight,
    key_weight,
    value_weight,
    query_gain,
    key_gain,
    attend_output,
    second_gain,
    second_gate,
    second_up,
    second_down,
    cotangent,
):
    length = tokens.shape[1]
    positions = lax.axis_index("seq") * length + jnp.arange(length, dtype=jnp.int32)
    segment, seg_start = segment_info(lengths, positions)
    offsets = positions[None, :] - seg_start
    hidden = tokens.astype(jnp.float32)
    hidden, mixer_back = mixer_block(
        hidden, mixer_gain, mixer_input, mixer_kernel, mixer_output, seg_start, positions
    )
    hidden, first_back = feed_block(hidden, first_gain, first_gate, first_up, first_down)
    hidden, attend_back = attend_block(
        hidden,
        lengths,
        attend_gain,
        query_weight,
        key_weight,
        value_weight,
        query_gain,
        key_gain,
        attend_output,
        segment,
        positions,
        offsets,
    )
    hidden, second_back = feed_block(hidden, second_gain, second_gate, second_up, second_down)
    gradient = cotangent.astype(jnp.float32)
    gradient, second_grads = second_back(gradient)
    gradient, attend_grads = attend_back(gradient)
    gradient, first_grads = first_back(gradient)
    gradient, mixer_grads = mixer_back(gradient)
    second_gain_sum, second_wide, second_down_pair = second_grads
    attend_gain_sum, attend_wide, query_gain_sum, key_gain_sum, attend_output_pair = attend_grads
    first_gain_sum, first_wide, first_down_pair = first_grads
    mixer_gain_sum, mixer_input_pair, mixer_kernel_sum, mixer_output_pair = mixer_grads
    row_count, shards = lax.axis_size("row"), lax.axis_size("seq")
    block_rows = math.gcd(tokens.shape[2] // shards, first_down.shape[0] // shards)

    def operands(pair):
        inputs, gradient_low = pair
        token_count = inputs.shape[0] * inputs.shape[1]
        inputs = inputs.reshape(token_count, -1).T
        blocks = inputs.shape[0] // shards // block_rows
        return (
            inputs.reshape(shards // 2, 2, blocks, block_rows, token_count),
            gradient_low.reshape(token_count, -1),
        )

    wide_vectors = jnp.concatenate(
        [
            mixer_kernel_sum,
            jnp.stack([mixer_gain_sum, first_gain_sum, attend_gain_sum, second_gain_sum]),
        ]
    )
    vector_count = wide_vectors.shape[0]
    vectors = jnp.concatenate(
        [
            part.reshape(-1, shards, part.shape[-1] // shards)
            .transpose(1, 0, 2)
            .reshape(shards, -1)
            for part in (wide_vectors, jnp.stack([query_gain_sum, key_gain_sum]))
        ],
        axis=1,
    )
    vector_rows = -(-vectors.shape[1] // COLS)
    token_count = tokens.shape[0] * tokens.shape[1]
    vectors = jnp.pad(vectors, ((0, 0), (0, vector_rows * COLS - vectors.shape[1])))
    vectors = vectors.reshape(shards * vector_rows, COLS).astype(jnp.bfloat16)
    vectors = jnp.pad(vectors, ((0, token_count - shards * vector_rows), (0, 0)))
    shard_at = lax.broadcasted_iota(jnp.int32, (shards, 2 * block_rows, token_count), 0)
    row_at = lax.broadcasted_iota(jnp.int32, (shards, 2 * block_rows, token_count), 1)
    token_at = lax.broadcasted_iota(jnp.int32, (shards, 2 * block_rows, token_count), 2)
    picks = (row_at < vector_rows) & (token_at == shard_at * vector_rows + row_at)
    picks = picks.astype(jnp.bfloat16).reshape(shards // 2, 2, 2, block_rows, token_count)
    (
        grad_second_down,
        second_both,
        grad_attend_output,
        attend_three,
        grad_first_down,
        first_both,
        grad_mixer_output,
        grad_mixer_input,
        vector_sums,
    ) = reduce_gradients(
        [
            operands(second_down_pair),
            operands(second_wide),
            operands(attend_output_pair),
            operands(attend_wide),
            operands(first_down_pair),
            operands(first_wide),
            operands(mixer_output_pair),
            operands(mixer_input_pair),
            (picks, vectors),
        ],
        row_count,
        shards,
        0,
    )

    def single(value):
        return value.astype(jnp.float32)

    hidden_columns = first_gate.shape[1]
    query_columns, key_columns = query_weight.shape[1], key_weight.shape[1]
    vector_sums = single(vector_sums[:vector_rows]).reshape(-1)
    width = tokens.shape[2] // shards
    wide_sums = vector_sums[: vector_count * width].reshape(vector_count, width)
    head_width = HEAD_DIM // shards
    head_sums = vector_sums[vector_count * width :][: 2 * head_width].reshape(2, head_width)
    return (
        hidden.astype(jnp.bfloat16),
        gradient.astype(jnp.bfloat16),
        wide_sums[3],
        single(grad_mixer_input),
        wide_sums[:3],
        single(grad_mixer_output),
        wide_sums[4],
        single(first_both[:, :hidden_columns]),
        single(first_both[:, hidden_columns:]),
        single(grad_first_down),
        wide_sums[5],
        single(attend_three[:, :query_columns]),
        single(attend_three[:, query_columns : query_columns + key_columns]),
        single(attend_three[:, query_columns + key_columns :]),
        head_sums[0],
        head_sums[1],
        single(grad_attend_output),
        wide_sums[6],
        single(second_both[:, :hidden_columns]),
        single(second_both[:, hidden_columns:]),
        single(grad_second_down),
    )


def dot_nt(left, right):
    return lax.dot_general(
        left, right, (((1,), (1,)), ((), ())), preferred_element_type=jnp.float32
    )


def dot_tn(left, right):
    return lax.dot_general(
        left, right, (((0,), (0,)), ((), ())), preferred_element_type=jnp.float32
    )


def lanes_below(shape, bound, period):
    return lax.rem(lax.broadcasted_iota(jnp.int32, shape, len(shape) - 1), period) < bound


def two_heads(pair, low):
    pair = pair.astype(jnp.float32)
    turned = pltpu.roll(pair, HEAD_DIM, 1)
    first = lanes_below(pair.shape, HEAD_DIM, 2 * HEAD_DIM)
    if low:
        parts = [jnp.where(first, pair, 0.0), jnp.where(first, turned, 0.0)]
    else:
        parts = [jnp.where(first, 0.0, turned), jnp.where(first, 0.0, pair)]
    return jnp.concatenate(parts, axis=0).astype(jnp.bfloat16)


BACKWARD_STARTS = {
    "second": 0,
    "attend_output": 9,
    "attention": 11,
    "queries": 19,
    "keys": 24,
    "first": 25,
    "mixer_output": 34,
    "halo": 36,
    "mixer_input": 37,
    "close": 40,
}
LOCAL_PAIRS = (15, 16, 19, 20)


def backward_kernel(names, entries, row_count, shards, *refs):
    at = types.SimpleNamespace(**dict(zip(names, refs)))
    outs = refs[len(names) : len(names) + len(entries)]
    token_out = refs[len(names) + len(entries)]
    scratch = refs[len(names) + len(entries) + 1 :]
    (
        tiles_a,
        tiles_b,
        tiles_c,
        saved,
        keys_values,
        key_grads,
        key_sums,
        queries,
        attended_grad,
        wide,
        mask,
        queries_raw,
        keys_raw,
        gradient,
        normed_grad,
        hidden,
        halo_out,
        halo_in,
        small,
        tile_sem,
        load_sem,
        halo_sem,
        *scratch,
    ) = scratch
    local = types.SimpleNamespace()
    exchange = Exchange(entries, row_count, shards, outs, scratch, LOCAL_PAIRS, local)
    x_all, g_all = exchange.x_all, exchange.g_all
    seq, row = exchange.seq, exchange.row
    tokens, width = gradient.shape
    rows = keys_values.shape[0]
    length = tokens // rows
    hidden_blocks = at.first_gate.shape[1] // COLS
    blocks = width // COLS
    g_at = [entry[2] * COLS for entry in entries]
    second_down, second_wide, output_at, heads_at, first_down, first_wide = g_at[:6]
    mixer_out_at, mixer_in_at, small_at = g_at[6:]
    starts = BACKWARD_STARTS

    def local_place(kind, index):
        first, second, third, fourth = LOCAL_PAIRS
        row_at = jnp.where(index >= third, 1, 0)
        quad = jnp.where(jnp.logical_or(index == second, index == fourth), 1, 0)
        return row_at, pl.ds(pl.multiple_of(quad * COLS, COLS), COLS)

    def part(kind, index, side):
        row_at, columns = local_place(kind, index)
        return key_grads[row_at, :, side, kind, :, columns]

    def take(kind, index, total):
        row_at, columns = local_place(kind, index)
        key_sums[row_at, kind, :, columns] = total

    local.part, local.take = part, take

    def tile_copies(name, j, slot):
        columns = pl.ds(pl.multiple_of(j * COLS, COLS), COLS)
        a, b, c = tiles_a.at[slot], tiles_b.at[slot], tiles_c.at[slot]
        if name in ("second", "first"):
            down, gate, up, gate_value, up_value = (
                (at.second_down, at.second_gate, at.second_up, at.gate_two, at.up_two)
                if name == "second"
                else (at.first_down, at.first_gate, at.first_up, at.gate_one, at.up_one)
            )
            moves = [
                (down.at[columns], a),
                (gate.at[:, columns], b),
                (up.at[:, columns], c),
                (gate_value.at[:, columns], saved.at[slot, 0]),
                (up_value.at[:, columns], saved.at[slot, 1]),
            ]
        elif name == "attend_output":
            moves = [(at.attend_output.at[columns], a)]
        elif name == "mixer_output":
            moves = [(at.mixer_output.at[columns], a)]
        elif name == "queries":
            moves = [
                (at.query_weight.at[:, pl.ds(0, COLS)], b),
                (at.query_weight.at[:, pl.ds(COLS, COLS)], c),
            ]
        elif name == "keys":
            moves = [(at.key_weight, b), (at.value_weight, c)]
        else:
            even = pl.multiple_of(2 * j * COLS, COLS)
            odd = pl.multiple_of((2 * j + 1) * COLS, COLS)
            moves = [
                (at.mixer_input.at[:, pl.ds(even, COLS)], b),
                (at.mixer_input.at[:, pl.ds(odd, COLS)], c),
            ]
        return [
            pltpu.make_async_copy(source, target, tile_sem.at[slot, place])
            for place, (source, target) in enumerate(moves)
        ]

    steps = [
        ("second", hidden_blocks),
        ("attend_output", blocks),
        ("queries", 1),
        ("keys", 1),
        ("first", hidden_blocks),
        ("mixer_output", blocks),
        ("mixer_input", 3 * blocks // 2),
    ]
    first_step, total = {}, 0
    for name, number in steps:
        first_step[name] = total
        total += number
    order = [name for name, _ in steps]
    numbers = dict(steps)

    def tile_step(name, j):
        slot = lax.rem(first_step[name] + j, 2)
        for copy in tile_copies(name, j, slot):
            copy.wait()

        @pl.when(j + 1 < numbers[name])
        def _():
            for copy in tile_copies(name, j + 1, 1 - slot):
                copy.start()

        if name != order[-1]:
            following = order[order.index(name) + 1]

            @pl.when(j + 1 == numbers[name])
            def _():
                for copy in tile_copies(following, 0, 1 - slot):
                    copy.start()

        return slot

    def load(place, source, target):
        return pltpu.make_async_copy(source, target, load_sem.at[place])

    count = len(entries)
    x_loads = [
        load(number, at.xs[number], x_all.at[:, :, pl.ds(x_first, x_count)])
        for number, (x_first, x_count, _, _, _) in enumerate(entries)
    ]
    cotangent_load = load(count, at.cotangent, g_all.at[:, pl.ds(second_down, width)])
    middle_loads = [
        load(count + 1, at.queries_low, queries),
        load(count + 2, at.keys_values, keys_values),
        load(count + 3, at.mask, mask),
        load(count + 4, at.queries_raw, queries_raw),
        load(count + 5, at.keys_raw, keys_raw),
    ]
    late_loads = [
        load(count + 6, at.mixer_saved, keys_values.at[0]),
        load(count + 7, at.projected, keys_values.at[1, pl.ds(0, 3 * tokens)]),
    ]
    hidden_loads = [
        load(count + 8, source, hidden)
        for source in (at.hidden_three, at.hidden_two, at.hidden_one, at.hidden_zero)
    ]
    out_copy = load(count + 9, attended_grad, token_out)

    x_loads[0].start()
    cotangent_load.start()
    for copy in tile_copies("second", 0, 0):
        copy.start()
    for copy in x_loads[1:] + middle_loads + hidden_loads[:1]:
        copy.start()
    normed_grad[...] = jnp.zeros_like(normed_grad)
    small[...] = jnp.zeros_like(small)
    g_all[:, pl.ds(small_at, COLS)] = jnp.zeros((tokens, COLS), jnp.bfloat16)
    exchange.meet()
    x_loads[0].wait()
    cotangent_load.wait()
    gradient[...] = g_all[:, pl.ds(second_down, width)].astype(jnp.float32)

    def low_gradient(place):
        g_all[:, pl.ds(place, width)] = gradient[...].astype(jnp.bfloat16)

    def norm_back(number):
        hidden_loads[number].wait()
        gain = at.gains[number : number + 1, :]
        sums = jnp.zeros((1, width), jnp.float32)
        piece = 64
        for first in range(0, tokens, piece):
            span = pl.ds(first, piece)
            value, upper = hidden[span], normed_grad[span]
            inverse = lax.rsqrt(jnp.mean(value * value, axis=-1, keepdims=True) + EPS)
            value = value * inverse
            sums = sums + jnp.sum(upper * value, axis=0, keepdims=True)
            upper = upper * gain
            shift = jnp.mean(upper * value, axis=-1, keepdims=True)
            gradient[span] = gradient[span] + inverse * (upper - value * shift)
        for block in range(blocks):
            place = blocks * number + block
            small[place : place + 1, :] = sums[:, block * COLS : (block + 1) * COLS]
        normed_grad[...] = jnp.zeros_like(normed_grad)
        if number + 1 < len(hidden_loads):
            hidden_loads[number + 1].start()

    def feed_tile(name, j, gradient_at, wide_at):
        slot = tile_step(name, j)
        low = g_all[:, pl.ds(gradient_at, width)]
        active_grad = dot_nt(low, tiles_a[slot])
        gate_value = saved[slot, 0].astype(jnp.float32)
        up_value = saved[slot, 1].astype(jnp.float32)
        share = 1.0 / (1.0 + jnp.exp(-gate_value))
        up_grad = (active_grad * gate_value * share).astype(jnp.bfloat16)
        gate_grad = active_grad * up_value * share * (1.0 + gate_value * (1.0 - share))
        gate_grad = gate_grad.astype(jnp.bfloat16)
        gate_place = pl.multiple_of(wide_at + j * COLS, COLS)
        up_place = pl.multiple_of(wide_at + (hidden_blocks + j) * COLS, COLS)
        g_all[:, pl.ds(gate_place, COLS)] = gate_grad
        g_all[:, pl.ds(up_place, COLS)] = up_grad
        normed_grad[...] += dot_nt(gate_grad, tiles_b[slot]) + dot_nt(up_grad, tiles_c[slot])

    def output_tile(name, j, gradient_at, target):
        slot = tile_step(name, j)
        low = g_all[:, pl.ds(gradient_at, width)]
        value = dot_nt(low, tiles_a[slot])
        target[:, j * COLS : (j + 1) * COLS] = value.astype(target.dtype)

    def attention_head(row_at, head):
        span = pl.ds(pl.multiple_of(row_at * length, length), length)
        columns = pl.ds(pl.multiple_of(head * 2 * HEAD_DIM, 2 * HEAD_DIM), 2 * HEAD_DIM)
        query = two_heads(queries[span, columns], True)
        upper = two_heads(attended_grad[span, columns], False)
        both = keys_values[row_at, :, columns]
        weights = jnp.exp(dot_nt(both, query)) * mask[row_at].astype(jnp.float32)
        weights = weights * (1.0 / jnp.sum(weights, axis=0, keepdims=True))
        weight_grad_value = dot_nt(both, upper)
        delta = jnp.sum(weights * weight_grad_value, axis=0, keepdims=True)
        score_grad = (weights * (weight_grad_value - delta)).astype(jnp.bfloat16)
        both_grad = jnp.dot(score_grad, query, preferred_element_type=jnp.float32)
        both_grad += jnp.dot(
            weights.astype(jnp.bfloat16), upper, preferred_element_type=jnp.float32
        )
        shape = key_grads.shape[1:5] + (2 * HEAD_DIM,)
        key_grads[row_at, :, :, :, :, columns] = both_grad.astype(jnp.bfloat16).reshape(shape)
        query_grad = dot_tn(score_grad, both) * HEAD_DIM ** (-0.5)
        first = lanes_below((length, 2 * HEAD_DIM), HEAD_DIM, 2 * HEAD_DIM)
        wide[span, columns] = jnp.where(
            first, query_grad[:length], pltpu.roll(query_grad[length:], HEAD_DIM, 1)
        )

    lane = 2 * HEAD_DIM
    head_of = lax.broadcasted_iota(jnp.int32, (lane, lane), 0) // HEAD_DIM
    ones = head_of == lax.broadcasted_iota(jnp.int32, (lane, lane), 1) // HEAD_DIM
    ones = ones.astype(jnp.float32).astype(jnp.bfloat16)

    def head_mean(value):
        total = jnp.dot(value.astype(jnp.bfloat16), ones, preferred_element_type=jnp.float32)
        return total * (1.0 / HEAD_DIM)

    def head_back(value, raw, gain):
        half = HEAD_DIM // 2
        first = lanes_below(value.shape, half, HEAD_DIM)
        turned = jnp.where(first, pltpu.roll(value, lane - half, 1), pltpu.roll(value, half, 1))
        value = value * at.cosine[...] - turned * at.sine[...]
        raw = raw.astype(jnp.float32)
        inverse = lax.rsqrt(head_mean(raw * raw) + EPS)
        raw = raw * inverse
        sums = jnp.sum(value * raw, axis=0, keepdims=True)
        value = value * gain
        return inverse * (value - raw * head_mean(value * raw)), sums

    def both_halves(sums):
        return sums + pltpu.roll(sums, HEAD_DIM, 1)

    head_row = 7 * blocks

    def query_heads():
        sums = jnp.zeros((8, lane), jnp.float32)
        for part_at in range(0, width, lane):
            columns = pl.ds(part_at, lane)
            value, more = head_back(wide[:, columns], queries_raw[:, columns], at.head_gains[0:1])
            g_all[:, pl.ds(heads_at + part_at, lane)] = value.astype(jnp.bfloat16)
            sums = sums + more
        small[head_row : head_row + 1, 0:lane] = both_halves(sums)[0:1]

    def key_heads():
        sums = jnp.zeros((8, lane), jnp.float32)
        first = lanes_below((tokens, lane), HEAD_DIM, lane)
        for pair in range(width // lane // 2):
            even, odd = [
                key_sums[:, :, :, pl.ds((2 * pair + which) * lane, lane)].reshape(tokens, lane)
                for which in range(2)
            ]
            key_value = jnp.where(first, even, pltpu.roll(odd, HEAD_DIM, 1))
            value_value = jnp.where(first, pltpu.roll(even, HEAD_DIM, 1), odd)
            columns = pl.ds(pair * lane, lane)
            value, more = head_back(key_value, keys_raw[:, columns], at.head_gains[1:2])
            place = heads_at + width + pair * lane
            g_all[:, pl.ds(place, lane)] = value.astype(jnp.bfloat16)
            place += width // 2
            g_all[:, pl.ds(place, lane)] = value_value.astype(jnp.bfloat16)
            sums = sums + more
        small[head_row : head_row + 1, lane : 2 * lane] = both_halves(sums)[0:1]

    def project_back(name, j, even_at, odd_at):
        slot = tile_step(name, j)
        normed_grad[...] += dot_nt(g_all[:, pl.ds(even_at, COLS)], tiles_b[slot]) + dot_nt(
            g_all[:, pl.ds(odd_at, COLS)], tiles_c[slot]
        )

    def halo_copy():
        return pltpu.make_async_remote_copy(
            src_ref=halo_out,
            dst_ref=halo_in,
            send_sem=halo_sem.at[0],
            recv_sem=halo_sem.at[1],
            device_id=(row, jnp.maximum(seq - 1, 0)),
            device_id_type=MESH,
        )

    def saved_part(number, columns):
        return keys_values[0, pl.ds(number * tokens, tokens), columns].astype(jnp.float32)

    def projected_part(number, columns):
        return keys_values[1, pl.ds(number * tokens, tokens), columns].astype(jnp.float32)

    def convolution_back():
        within = lax.rem(lax.broadcasted_iota(jnp.int32, (tokens, lane), 0), length)
        edge = lax.broadcasted_iota(jnp.int32, (8, lane), 0)
        for part_at in range(0, width, lane):
            columns = pl.ds(part_at, lane)
            gated_grad = wide[:, columns]
            exit_grad = gated_grad * saved_part(0, columns)
            place = mixer_in_at + width + part_at
            g_all[:, pl.ds(place, lane)] = exit_grad.astype(jnp.bfloat16)
            conv_grad = gated_grad * projected_part(1, columns)
            block, inside = part_at // COLS, part_at % COLS
            for tap in range(3):
                sums = jnp.sum(conv_grad * saved_part(1 + tap, columns), axis=0, keepdims=True)
                place = blocks * (4 + tap) + block
                small[place : place + 1, inside : inside + lane] = sums
            two = at.taps[0:1, columns] * at.keep[1] * conv_grad
            one = at.taps[1:2, columns] * at.keep[0] * conv_grad
            here = at.taps[2:3, columns] * conv_grad
            here += jnp.where(within < length - 1, pltpu.roll(one, tokens - 1, 0), 0.0)
            here += jnp.where(within < length - 2, pltpu.roll(two, tokens - 2, 0), 0.0)
            normed_grad[:, columns] = here
            for which in range(rows):
                span = slice(which * length, which * length + 8)
                sent = two[span] + jnp.where(edge == 1, pltpu.roll(one[span], 1, 0), 0.0)
                halo_out[which, :, columns] = jnp.where(edge < 2, sent, 0.0)

        @pl.when(seq > 0)
        def _():
            halo_copy().start()

    def product_back():
        @pl.when(seq < shards - 1)
        def _():
            halo_copy().wait_recv()
            for which in range(rows):
                span = pl.ds((which + 1) * length - 8, 8)
                normed_grad[span] = normed_grad[span] + pltpu.roll(halo_in[which], 6, 0)

        @pl.when(seq > 0)
        def _():
            halo_copy().wait_send()

        for part_at in range(0, width, lane):
            columns = pl.ds(part_at, lane)
            product_grad = normed_grad[:, columns]
            entry_grad = product_grad * projected_part(2, columns)
            carrier_grad = product_grad * projected_part(0, columns)
            g_all[:, pl.ds(mixer_in_at + part_at, lane)] = entry_grad.astype(jnp.bfloat16)
            place = mixer_in_at + 2 * width + part_at
            g_all[:, pl.ds(place, lane)] = carrier_grad.astype(jnp.bfloat16)
        normed_grad[...] = jnp.zeros_like(normed_grad)

    def task(i):
        def when(name, run, after=0, number=1):
            j = i - (starts[name] + after)

            @pl.when(jnp.logical_and(j >= 0, j < number))
            def _():
                run(j)

        when("second", lambda j: feed_tile("second", j, second_down, second_wide), 0, hidden_blocks)

        def waits(j):
            for copy in x_loads[1:] + middle_loads:
                copy.wait()

        when("second", waits, hidden_blocks - 1)

        def to_attended(j):
            norm_back(0)
            low_gradient(output_at)
            output_tile("attend_output", 0, output_at, attended_grad)

        when("attend_output", to_attended)
        when("attend_output", lambda j: output_tile("attend_output", 1, output_at, attended_grad), 1)

        def attention(j):
            pairs = KV_HEADS // 2
            for which in range(2):
                attention_head(j // pairs, 2 * lax.rem(j, pairs) + which)

        when("attention", attention, 0, rows * KV_HEADS // 2)

        def to_queries(j):
            for copy in late_loads:
                copy.start()
            query_heads()

        when("queries", to_queries)
        when("queries", lambda j: project_back("queries", 0, heads_at, heads_at + COLS), 1)

        def to_keys(j):
            key_heads()
            project_back("keys", 0, heads_at + width, heads_at + width + COLS)
            norm_back(1)
            low_gradient(first_down)

        when("keys", to_keys)
        when("first", lambda j: feed_tile("first", j, first_down, first_wide), 0, hidden_blocks)

        def to_gated(j):
            norm_back(2)
            low_gradient(mixer_out_at)
            output_tile("mixer_output", 0, mixer_out_at, wide)
            for copy in late_loads:
                copy.wait()

        when("mixer_output", to_gated)

        def to_convolved(j):
            output_tile("mixer_output", 1, mixer_out_at, wide)
            convolution_back()

        when("mixer_output", to_convolved, 1)
        when("halo", lambda j: product_back())

        def mixer_tile(j):
            even = pl.multiple_of(mixer_in_at + 2 * j * COLS, COLS)
            project_back("mixer_input", j, even, pl.multiple_of(even + COLS, COLS))

        when("mixer_input", mixer_tile, 0, numbers["mixer_input"])

        def close(j):
            norm_back(3)
            attended_grad[...] = gradient[...].astype(jnp.bfloat16)
            out_copy.start()
            g_all[pl.ds(0, small.shape[0]), pl.ds(small_at, COLS)] = small[...].astype(jnp.bfloat16)

        when("close", close)
        when("close", lambda j: out_copy.wait(), 1)

    exchange.run(task)


def backward(groups, arrays, resident, row_count, shards, collective_id):
    xs = [x for x, _ in groups]
    block_rows, tokens = xs[0].shape[3:]
    width = arrays["cotangent"].shape[1]
    entries, x_blocks, g_blocks, chunks = reduce_entries(
        [(x.shape[2], columns // COLS) for x, columns in groups]
    )
    names = ["xs_%d" % number for number in range(len(xs))] + list(arrays)
    values = list(xs) + list(arrays.values())
    rows, total_length = arrays["keys_values"].shape[:2]
    any_space = pl.BlockSpec(memory_space=pl.ANY)
    vmem_space = pl.BlockSpec(memory_space=pltpu.VMEM)
    key_blocks = total_length // shards // block_rows

    def kernel(*refs):
        xs_refs, others = refs[: len(xs)], refs[len(xs) : len(values)]
        named = [("xs", xs_refs)] + list(zip(arrays, others))
        backward_kernel(
            [name for name, _ in named],
            entries,
            row_count,
            shards,
            *[ref for _, ref in named],
            *refs[len(values) :],
        )

    low, full = jnp.bfloat16, jnp.float32
    return pl.pallas_call(
        kernel,
        out_shape=[
            jax.ShapeDtypeStruct((x_count * block_rows, g_count * COLS), low)
            for _, x_count, _, g_count, _ in entries
        ]
        + [jax.ShapeDtypeStruct((tokens, width), low)],
        in_specs=[vmem_space if name in resident else any_space for name in names],
        out_specs=[any_space] * (len(entries) + 1),
        scratch_shapes=[
            pltpu.VMEM((2, COLS, width), low),
            pltpu.VMEM((2, width, COLS), low),
            pltpu.VMEM((2, width, COLS), low),
            pltpu.VMEM((2, 2, tokens, COLS), low),
            pltpu.VMEM((rows, total_length, width), low),
            pltpu.VMEM((rows, shards // 2, 2, key_blocks, block_rows, width), low),
            pltpu.VMEM((rows, key_blocks, block_rows, width), full),
            pltpu.VMEM((tokens, width), low),
            pltpu.VMEM((tokens, width), low),
            pltpu.VMEM((tokens, width), full),
            pltpu.VMEM((rows, total_length, 2 * tokens // rows), low),
            pltpu.VMEM((tokens, width), low),
            pltpu.VMEM((tokens, width // 2), low),
            pltpu.VMEM((tokens, width), full),
            pltpu.VMEM((tokens, width), full),
            pltpu.VMEM((tokens, width), full),
            pltpu.VMEM((rows, 8, width), full),
            pltpu.VMEM((rows, 8, width), full),
            pltpu.VMEM((16, COLS), full),
            pltpu.SemaphoreType.DMA((2, 5)),
            pltpu.SemaphoreType.DMA((len(entries) + 10,)),
            pltpu.SemaphoreType.DMA((2,)),
            *exchange_scratch(row_count, shards, block_rows, x_blocks, g_blocks, tokens),
        ],
        compiler_params=pltpu.CompilerParams(
            collective_id=collective_id, has_side_effects=True, vmem_limit_bytes=63 * 2**20
        ),
        cost_estimate=pl.CostEstimate(
            flops=4 * chunks * shards * block_rows * COLS * tokens,
            bytes_accessed=2 * chunks * shards * block_rows * COLS,
            transcendentals=0,
        ),
    )(*values)


def attention_kernel(query_ref, both_ref, mask_ref, out_ref):
    query = two_heads(query_ref[...], True)
    both = both_ref[0]
    allowed = mask_ref[0].astype(jnp.float32)
    weights = jnp.exp(dot_nt(query, both)) * jnp.concatenate([allowed, allowed], axis=0)
    weights = weights * (1.0 / jnp.sum(weights, axis=-1, keepdims=True))
    value = jnp.dot(weights.astype(jnp.bfloat16), both, preferred_element_type=jnp.float32)
    length = out_ref.shape[0]
    first = lanes_below((length, 2 * HEAD_DIM), HEAD_DIM, 2 * HEAD_DIM)
    out_ref[...] = jnp.where(
        first, pltpu.roll(value[:length], HEAD_DIM, 1), value[length:]
    ).astype(out_ref.dtype)


def attention(queries, keys_values, mask):
    rows, total_length, width = keys_values.shape
    length = queries.shape[0] // rows
    lane = 2 * HEAD_DIM
    return pl.pallas_call(
        attention_kernel,
        grid=(rows, width // lane),
        in_specs=[
            pl.BlockSpec((length, lane), lambda r, h: (r, h)),
            pl.BlockSpec((1, total_length, lane), lambda r, h: (r, 0, h)),
            pl.BlockSpec((1, length, total_length), lambda r, h: (r, 0, 0)),
        ],
        out_specs=pl.BlockSpec((length, lane), lambda r, h: (r, h)),
        out_shape=jax.ShapeDtypeStruct(queries.shape, jnp.bfloat16),
        compiler_params=pltpu.CompilerParams(vmem_limit_bytes=32 * 2**20),
        cost_estimate=pl.CostEstimate(
            flops=8 * queries.shape[0] * total_length * width,
            bytes_accessed=4 * keys_values.size,
            transcendentals=2 * queries.shape[0] * total_length * KV_HEADS,
        ),
    )(queries, keys_values, mask)


def fused_body(
    tokens,
    lengths,
    mixer_gain,
    mixer_input,
    mixer_kernel,
    mixer_output,
    first_gain,
    first_gate,
    first_up,
    first_down,
    attend_gain,
    query_weight,
    key_weight,
    value_weight,
    query_gain,
    key_gain,
    attend_output,
    second_gain,
    second_gate,
    second_up,
    second_down,
    cotangent,
):
    full, low = jnp.float32, jnp.bfloat16
    rows, length, width = tokens.shape
    token_count = rows * length
    row_count, shards = lax.axis_size("row"), lax.axis_size("seq")
    seq = lax.axis_index("seq")
    positions = seq * length + jnp.arange(length, dtype=jnp.int32)
    segment, seg_start = segment_info(lengths, positions)
    offsets = positions[None, :] - seg_start

    def flat(value):
        return value.reshape(token_count, -1)

    hidden_zero = tokens.astype(full)
    mixer_in = norm_rows(hidden_zero, mixer_gain.astype(full)).astype(low)
    projected = dense(mixer_in, mixer_input)
    entry, exit_gate, carrier = [
        projected[..., number * width : (number + 1) * width] for number in range(3)
    ]
    product = (entry * carrier).astype(low)
    previous = passed_along(product[:, length - 2 :, :], "seq", 1)
    extended = jnp.concatenate([previous, product], axis=1).astype(full)
    keep_one = (positions[None, :] - 1 >= seg_start).astype(full)[..., None]
    keep_two = (positions[None, :] - 2 >= seg_start).astype(full)[..., None]
    taps = mixer_kernel.astype(full)
    two_back = keep_two * extended[:, :length]
    one_back = keep_one * extended[:, 1 : length + 1]
    current = extended[:, 2:]
    convolved = taps[2] * current + taps[1] * one_back + taps[0] * two_back
    gated = (exit_gate * convolved).astype(low)
    hidden_one = hidden_zero + dense(gated, mixer_output)
    mixer_saved = jnp.concatenate(
        [flat(part).astype(low) for part in (convolved, two_back, one_back, current)]
    )
    projected_saved = jnp.concatenate(
        [flat(part).astype(low) for part in (entry, exit_gate, carrier)]
    )

    def feed(hidden, gain, gate_matrix, up_matrix, down_matrix):
        normed = norm_rows(hidden, gain.astype(full)).astype(low)
        gate_value, upward = dense(normed, gate_matrix), dense(normed, up_matrix)
        active = swiglu(gate_value, upward).astype(low)
        saved = (normed, active, flat(gate_value.astype(low)), flat(upward.astype(low)))
        return hidden + dense(active, down_matrix), saved

    hidden_two, first_saved = feed(hidden_one, first_gain, first_gate, first_up, first_down)

    attend_in = norm_rows(hidden_two, attend_gain.astype(full)).astype(low)
    queries_raw, keys_raw = dense(attend_in, query_weight), dense(attend_in, key_weight)
    values = dense(attend_in, value_weight)

    def head_path(value, heads, gain):
        value = value.reshape(rows, length, heads, HEAD_DIM)
        return rotate(norm_rows(value, gain.astype(full)), offsets)

    queries_low = flat(
        (head_path(queries_raw, HEADS, query_gain).astype(low) * low(HEAD_DIM**-0.5))
    )
    keys_low = head_path(keys_raw, KV_HEADS, key_gain).astype(low)
    values_low = values.astype(low).reshape(keys_low.shape)
    both = jnp.stack([keys_low, values_low], axis=3).reshape(rows, length, width)
    keys_values = lax.all_gather(both, "seq", axis=1, tiled=True)
    total_length = keys_values.shape[1]
    key_positions = jnp.arange(total_length, dtype=jnp.int32)
    key_segment, _ = segment_info(lengths, key_positions)
    allowed = (segment[:, :, None] == key_segment[:, None, :]) & (
        positions[None, :, None] >= key_positions[None, None, :]
    )
    allowed_turned = (segment[:, None, :] == key_segment[:, :, None]) & (
        positions[None, None, :] >= key_positions[None, :, None]
    )
    mask_turned = jnp.concatenate([allowed_turned, allowed_turned], axis=-1).astype(low)
    attended = attention(queries_low, keys_values, allowed.astype(low))
    hidden_three = hidden_two + dense(attended.reshape(tokens.shape), attend_output)
    mixed, second_saved = feed(hidden_three, second_gain, second_gate, second_up, second_down)

    half = HEAD_DIM // 2
    inverse = THETA ** (-2.0 * jnp.arange(half, dtype=full) / HEAD_DIM)
    angles = offsets.astype(full).reshape(token_count, 1) * inverse
    cosine, sine = jnp.cos(angles), jnp.sin(angles)
    block_rows = math.gcd(width // shards, first_down.shape[0] // shards)

    def turned(inputs):
        inputs = flat(inputs).T
        blocks = inputs.shape[0] // shards // block_rows
        return inputs.reshape(shards // 2, 2, blocks, block_rows, token_count)

    blocks = width // COLS
    shape = (shards, 2 * block_rows, token_count)
    shard_at, row_at, token_at = [lax.broadcasted_iota(jnp.int32, shape, dim) for dim in range(3)]
    wanted = blocks * row_at + jnp.where(row_at < 7, shard_at * blocks // shards, 0)
    picks = ((row_at < 8) & (token_at == wanted)).astype(low)
    picks = picks.reshape(shards // 2, 2, 2, block_rows, token_count)

    def padded(value):
        return jnp.pad(value.astype(full), ((0, 8 - value.shape[0]), (0, 0)))

    lane = 2 * HEAD_DIM
    arrays = dict(
        cotangent=flat(cotangent),
        gate_two=second_saved[2],
        up_two=second_saved[3],
        gate_one=first_saved[2],
        up_one=first_saved[3],
        hidden_three=flat(hidden_three),
        hidden_two=flat(hidden_two),
        hidden_one=flat(hidden_one),
        hidden_zero=flat(hidden_zero),
        queries_low=queries_low,
        keys_values=keys_values,
        mask=mask_turned,
        queries_raw=flat(queries_raw).astype(low),
        keys_raw=flat(keys_raw).astype(low),
        mixer_saved=mixer_saved,
        projected=projected_saved,
        cosine=jnp.concatenate([cosine] * 4, axis=1),
        sine=jnp.concatenate([-sine, sine] * 2, axis=1),
        keep=jnp.broadcast_to(
            jnp.stack([keep_one, keep_two]).reshape(2, token_count, 1), (2, token_count, lane)
        ),
        gains=padded(jnp.stack([second_gain, attend_gain, first_gain, mixer_gain])),
        taps=padded(mixer_kernel),
        head_gains=padded(jnp.tile(jnp.stack([query_gain, key_gain]), (1, 2))),
        second_down=second_down,
        second_gate=second_gate,
        second_up=second_up,
        attend_output=attend_output,
        query_weight=query_weight,
        key_weight=key_weight,
        value_weight=value_weight,
        first_down=first_down,
        first_gate=first_gate,
        first_up=first_up,
        mixer_output=mixer_output,
        mixer_input=mixer_input,
    )
    resident = ("cosine", "sine", "keep", "gains", "taps", "head_gains")
    hidden_columns = first_gate.shape[1]
    head_columns = width + 2 * key_weight.shape[1]
    groups = [
        (turned(second_saved[1]), width),
        (turned(second_saved[0]), 2 * hidden_columns),
        (turned(attended), width),
        (turned(attend_in), head_columns),
        (turned(first_saved[1]), width),
        (turned(first_saved[0]), 2 * hidden_columns),
        (turned(gated), width),
        (turned(mixer_in), 3 * width),
        (picks, COLS),
    ]
    (
        grad_second_down,
        second_both,
        grad_attend_output,
        attend_three,
        grad_first_down,
        first_both,
        grad_mixer_output,
        grad_mixer_input,
        sums,
        token_grad,
    ) = backward(groups, arrays, resident, row_count, shards, 1)

    def single(value):
        return value.astype(full)

    share = width // shards
    vectors = single(
        lax.dynamic_slice(sums, (0, lax.rem(seq, COLS // share) * share), (7, share))
    )
    head_share = HEAD_DIM // shards
    heads = [
        single(lax.dynamic_slice(sums, (7, which * lane + seq * head_share), (1, head_share)))[0]
        for which in range(2)
    ]
    key_columns = key_weight.shape[1]
    return (
        mixed.astype(low),
        token_grad.reshape(tokens.shape),
        vectors[3],
        single(grad_mixer_input),
        vectors[4:7],
        single(grad_mixer_output),
        vectors[2],
        single(first_both[:, :hidden_columns]),
        single(first_both[:, hidden_columns:]),
        single(grad_first_down),
        vectors[1],
        single(attend_three[:, :width]),
        single(attend_three[:, width : width + key_columns]),
        single(attend_three[:, width + key_columns :]),
        heads[0],
        heads[1],
        single(grad_attend_output),
        vectors[0],
        single(second_both[:, :hidden_columns]),
        single(second_both[:, hidden_columns:]),
        single(grad_second_down),
    )


def fused_or_general(*args):
    tokens = args[0]
    rows, length, width = tokens.shape
    row_count, shards = lax.axis_size("row"), lax.axis_size("seq")
    key_bytes = 2 * rows * length * shards * width
    if key_bytes <= 4 * 2**20 and shards == 8 and 4 * rows == shards and row_count == 4:
        return fused_body(*args)
    return body(*args)


def solution(mesh):
    in_specs = (
        P("row", "seq", None),
        P("row", None),
        P(),
        P(),
        P(),
        P(),
        P(),
        P(),
        P(),
        P(),
        P(),
        P(),
        P(),
        P(),
        P(),
        P(),
        P(),
        P(),
        P(),
        P(),
        P(),
        P("row", "seq", None),
    )
    out_specs = (
        P("row", "seq", None),
        P("row", "seq", None),
        P("seq"),
        P("seq", None),
        P(None, "seq"),
        P("seq", None),
        P("seq"),
        P("seq", None),
        P("seq", None),
        P("seq", None),
        P("seq"),
        P("seq", None),
        P("seq", None),
        P("seq", None),
        P("seq"),
        P("seq"),
        P("seq", None),
        P("seq"),
        P("seq", None),
        P("seq", None),
        P("seq", None),
    )
    return jax.shard_map(fused_or_general, mesh=mesh, in_specs=in_specs, out_specs=out_specs, check_vma=False)
```

```python
import functools
import math
import types

import jax
import jax.numpy as jnp
from jax import lax
from jax.experimental import pallas as pl
from jax.experimental.pallas import tpu as pltpu
from jax.sharding import PartitionSpec as P

HEADS = 16
KV_HEADS = 8
HEAD_DIM = 64
GROUP = 2


EPS = 1e-05
THETA = 1000000.0
NEGATIVE = -1e30
HIGHEST = lax.Precision.HIGHEST
MESH = pl.DeviceIdType.MESH
COLS = 512
SLOTS = 4
ZSLOTS = 6


def passed_along(value, axis, steps):
    count = lax.axis_size(axis)
    initial, last = (max(0, -steps), min(count, count - steps))
    return lax.ppermute(value, axis, [(source, source + steps) for source in range(initial, last)])


def segment_info(lengths, positions):
    boundary = jnp.cumsum(lengths, axis=-1)
    passed = boundary[:, None, :] <= positions[None, :, None]
    segment = jnp.sum(passed.astype(jnp.int32), axis=-1)
    seg_start = jnp.max(jnp.where(passed, boundary[:, None, :], 0), axis=-1)
    return (segment, seg_start)


def norm_rows(values, norm_gain):
    return values * lax.rsqrt(jnp.mean(values * values, axis=-1, keepdims=True) + EPS) * norm_gain


def rotate(values, offsets):
    half_dim = values.shape[-1] // 2
    inverse = THETA ** (-2.0 * jnp.arange(half_dim, dtype=jnp.float32) / values.shape[-1])
    angles = offsets.astype(jnp.float32)[:, :, None, None] * inverse
    cosine = jnp.cos(angles)
    sine_table = jnp.sin(angles)
    leading = values[..., :half_dim]
    trailing = values[..., half_dim:]
    return jnp.concatenate(
        [leading * cosine - trailing * sine_table, trailing * cosine + leading * sine_table],
        axis=-1,
    )


def swiglu(gate_value, upward):
    return gate_value / (1.0 + jnp.exp(-gate_value)) * upward


def dense(inputs, matrix):
    return jnp.einsum("rtd,df->rtf", inputs, matrix, preferred_element_type=jnp.float32)


def weight_grad(inputs, gradient):
    return (inputs, gradient)


def back_dense(gradient, matrix):
    return jnp.einsum("rtf,df->rtd", gradient, matrix, preferred_element_type=jnp.float32)


def mixer_block(hidden, norm_gain, input_matrix, kernel, output_matrix, seg_start, positions):
    feature_columns = hidden.shape[-1]
    length = hidden.shape[1]
    normed, norm_back = jax.vjp(norm_rows, hidden, norm_gain.astype(jnp.float32))
    normed_low = normed.astype(jnp.bfloat16)
    projected_rows = dense(normed_low, input_matrix)
    input_gate_value = projected_rows[..., :feature_columns]
    exit_gate = projected_rows[..., feature_columns : 2 * feature_columns]
    carry_value = projected_rows[..., 2 * feature_columns :]
    gated_product_reduced = (input_gate_value * carry_value).astype(jnp.bfloat16)
    previous = passed_along(gated_product_reduced[:, length - 2 :, :], "seq", 1)
    extended = jnp.concatenate([previous, gated_product_reduced], axis=1).astype(jnp.float32)
    keep_one = (positions[None, :] - 1 >= seg_start).astype(jnp.float32)[..., None]
    keep_two = (positions[None, :] - 2 >= seg_start).astype(jnp.float32)[..., None]
    kernel_taps = kernel.astype(jnp.float32)
    two_back = extended[:, :length]
    one_back = extended[:, 1 : length + 1]
    current = extended[:, 2:]
    convolved = (
        kernel_taps[2] * current
        + kernel_taps[1] * keep_one * one_back
        + kernel_taps[0] * keep_two * two_back
    )
    gated_low = (exit_gate * convolved).astype(jnp.bfloat16)
    result = hidden + dense(gated_low, output_matrix)

    def mixer_backward(gradient):
        gradient_low = gradient.astype(jnp.bfloat16)
        grad_output = weight_grad(gated_low, gradient_low)
        grad_gated = back_dense(gradient_low, output_matrix)
        output_gate_gradient = grad_gated * convolved
        grad_conv = grad_gated * exit_gate
        grad_kernel = jnp.stack(
            [
                jnp.sum(grad_conv * keep_two * two_back, axis=(0, 1)),
                jnp.sum(grad_conv * keep_one * one_back, axis=(0, 1)),
                jnp.sum(grad_conv * current, axis=(0, 1)),
            ]
        )
        grad_extended = jnp.pad(kernel_taps[0] * keep_two * grad_conv, ((0, 0), (0, 2), (0, 0)))
        grad_extended = grad_extended + jnp.pad(
            kernel_taps[1] * keep_one * grad_conv, ((0, 0), (1, 1), (0, 0))
        )
        grad_extended = grad_extended + jnp.pad(
            kernel_taps[2] * grad_conv, ((0, 0), (2, 0), (0, 0))
        )
        returned = passed_along(grad_extended[:, :2, :], "seq", -1)
        gated_product_gradient = grad_extended[:, 2:] + jnp.pad(
            returned, ((0, 0), (length - 2, 0), (0, 0))
        )
        grad_projected = jnp.concatenate(
            [
                gated_product_gradient * carry_value,
                output_gate_gradient,
                gated_product_gradient * input_gate_value,
            ],
            axis=-1,
        ).astype(jnp.bfloat16)
        grad_input = weight_grad(normed_low, grad_projected)
        grad_normed = back_dense(grad_projected, input_matrix)
        grad_hidden, grad_gain = norm_back(grad_normed)
        return (gradient + grad_hidden, (grad_gain, grad_input, grad_kernel, grad_output))

    return (result, mixer_backward)


def feed_block(hidden, norm_gain, gate_matrix, up_matrix, down_matrix):
    normed, norm_back = jax.vjp(norm_rows, hidden, norm_gain.astype(jnp.float32))
    normed_low = normed.astype(jnp.bfloat16)
    gate_value = dense(normed_low, gate_matrix)
    upward = dense(normed_low, up_matrix)
    active, active_back = jax.vjp(swiglu, gate_value, upward)
    active_low = active.astype(jnp.bfloat16)
    result = hidden + dense(active_low, down_matrix)

    def feed_backward(gradient):
        gradient_low = gradient.astype(jnp.bfloat16)
        grad_down = weight_grad(active_low, gradient_low)
        grad_gate, grad_upward = active_back(back_dense(gradient_low, down_matrix))
        gate_low = grad_gate.astype(jnp.bfloat16)
        upward_low = grad_upward.astype(jnp.bfloat16)
        grad_normed = back_dense(gate_low, gate_matrix) + back_dense(upward_low, up_matrix)
        grad_hidden, grad_gain = norm_back(grad_normed)
        return (
            gradient + grad_hidden,
            (
                grad_gain,
                weight_grad(normed_low, jnp.concatenate([gate_low, upward_low], axis=-1)),
                grad_down,
            ),
        )

    return (result, feed_backward)


def attend_block(
    hidden,
    lengths,
    norm_gain,
    query_matrix,
    key_matrix,
    value_matrix,
    query_norm,
    key_norm,
    output_matrix,
    segment,
    positions,
    offsets,
):
    row_count, length, feature_columns = hidden.shape
    score_scale = HEAD_DIM ** (-0.5)
    normed, norm_back = jax.vjp(norm_rows, hidden, norm_gain.astype(jnp.float32))
    normed_low = normed.astype(jnp.bfloat16)

    def head_path(projected_rows, head_gain):
        return rotate(norm_rows(projected_rows, head_gain), offsets)

    queries = dense(normed_low, query_matrix).reshape(row_count, length, HEADS, HEAD_DIM)
    keys_raw = dense(normed_low, key_matrix).reshape(row_count, length, KV_HEADS, HEAD_DIM)
    values_raw = dense(normed_low, value_matrix)
    query_rot, query_back = jax.vjp(head_path, queries, query_norm.astype(jnp.float32))
    key_rot, key_back = jax.vjp(head_path, keys_raw, key_norm.astype(jnp.float32))
    query_low = query_rot.astype(jnp.bfloat16).reshape(row_count, length, KV_HEADS, GROUP, HEAD_DIM)
    key_low = key_rot.astype(jnp.bfloat16)
    value_low = values_raw.astype(jnp.bfloat16).reshape(row_count, length, KV_HEADS, HEAD_DIM)
    all_keys, all_values = (
        lax.all_gather(key_low, "seq", axis=1, tiled=True),
        lax.all_gather(value_low, "seq", axis=1, tiled=True),
    )
    total_length = all_keys.shape[1]
    key_block = min(512, total_length)
    block_count = (positions[length - 1] + key_block) // key_block

    def block_scores(number, key_source, value_source):
        first_key = number * key_block
        keys_here = lax.dynamic_slice_in_dim(key_source, first_key, key_block, 1)
        values_here = lax.dynamic_slice_in_dim(value_source, first_key, key_block, 1)
        key_positions = first_key + jnp.arange(key_block, dtype=jnp.int32)
        key_segment, unused = segment_info(lengths, key_positions)
        scores = (
            jnp.einsum(
                "rtkgh,rskh->rkgts", query_low, keys_here, preferred_element_type=jnp.float32
            )
            * score_scale
        )
        allowed = (segment[:, :, None] == key_segment[:, None, :]) & (
            positions[None, :, None] >= key_positions[None, None, :]
        )
        allowed = allowed[:, None, None]
        return (jnp.where(allowed, scores, NEGATIVE), allowed, keys_here, values_here)

    stat_shape = (row_count, KV_HEADS, GROUP, length)

    def stats_step(number, carried):
        peak_score, running_sum = carried
        scores, allowed, unused_keys, unused_values = block_scores(number, all_keys, all_values)
        new_peak = jnp.maximum(peak_score, jnp.max(scores, axis=-1))
        fresh = jnp.sum(jnp.where(allowed, jnp.exp(scores - new_peak[..., None]), 0.0), axis=-1)
        return (new_peak, running_sum * jnp.exp(peak_score - new_peak) + fresh)

    peak_score, running_sum = lax.fori_loop(
        0,
        block_count,
        stats_step,
        (jnp.full(stat_shape, NEGATIVE, jnp.float32), jnp.zeros(stat_shape, jnp.float32)),
    )
    log_total = peak_score + jnp.log(running_sum)

    def probabilities(scores, allowed):
        return jnp.where(allowed, jnp.exp(scores - log_total[..., None]), 0.0)

    out_shape = (row_count, length, KV_HEADS, GROUP, HEAD_DIM)

    def output_step(number, carried):
        rounded, exact_sum = carried
        scores, allowed, keys_here, values_here = block_scores(number, all_keys, all_values)
        weights = probabilities(scores, allowed)
        rounded = rounded + jnp.einsum(
            "rkgts,rskh->rtkgh",
            weights.astype(jnp.bfloat16),
            values_here,
            preferred_element_type=jnp.float32,
        )
        exact_sum = exact_sum + jnp.einsum(
            "rkgts,rskh->rtkgh", weights, values_here.astype(jnp.float32), precision=HIGHEST
        )
        return (rounded, exact_sum)

    rounded, exact_sum = lax.fori_loop(
        0,
        block_count,
        output_step,
        (jnp.zeros(out_shape, jnp.float32), jnp.zeros(out_shape, jnp.float32)),
    )
    attended_low = rounded.reshape(row_count, length, HEADS * HEAD_DIM).astype(jnp.bfloat16)
    result = hidden + dense(attended_low, output_matrix)

    def attend_backward(gradient):
        gradient_low = gradient.astype(jnp.bfloat16)
        grad_output = weight_grad(attended_low, gradient_low)
        grad_attended = (
            back_dense(gradient_low, output_matrix).astype(jnp.bfloat16).reshape(out_shape)
        )
        row_delta = jnp.einsum(
            "rtkgh,rtkgh->rkgt", grad_attended.astype(jnp.float32), exact_sum, precision=HIGHEST
        )
        key_source, value_source = (all_keys, all_values)

        def grad_step(number, carried):
            grad_query, grad_keys, grad_values = carried
            scores, allowed, keys_here, values_here = block_scores(number, key_source, value_source)
            weights = probabilities(scores, allowed)
            grad_weights = jnp.einsum(
                "rtkgh,rskh->rkgts", grad_attended, values_here, preferred_element_type=jnp.float32
            )
            grad_scores = (weights * (grad_weights - row_delta[..., None])).astype(jnp.bfloat16)
            grad_query = (
                grad_query
                + jnp.einsum(
                    "rkgts,rskh->rtkgh", grad_scores, keys_here, preferred_element_type=jnp.float32
                )
                * score_scale
            )
            key_part = (
                jnp.einsum(
                    "rkgts,rtkgh->rskh", grad_scores, query_low, preferred_element_type=jnp.float32
                )
                * score_scale
            )
            value_part = jnp.einsum(
                "rkgts,rtkgh->rskh",
                weights.astype(jnp.bfloat16),
                grad_attended,
                preferred_element_type=jnp.float32,
            )
            grad_keys = lax.dynamic_update_slice_in_dim(grad_keys, key_part, number * key_block, 1)
            grad_values = lax.dynamic_update_slice_in_dim(
                grad_values, value_part, number * key_block, 1
            )
            return (grad_query, grad_keys, grad_values)

        key_shape = (row_count, total_length, KV_HEADS, HEAD_DIM)
        grad_query, grad_keys, grad_values = lax.fori_loop(
            0,
            block_count,
            grad_step,
            (
                jnp.zeros(out_shape, jnp.float32),
                jnp.zeros(key_shape, jnp.float32),
                jnp.zeros(key_shape, jnp.float32),
            ),
        )
        local_keys, local_values = (
            lax.psum_scatter(
                grad_keys.astype(jnp.bfloat16), "seq", scatter_dimension=1, tiled=True
            ).astype(jnp.float32),
            lax.psum_scatter(
                grad_values.astype(jnp.bfloat16), "seq", scatter_dimension=1, tiled=True
            ).astype(jnp.float32),
        )
        grad_queries, grad_query_norm = query_back(
            grad_query.reshape(row_count, length, HEADS, HEAD_DIM)
        )
        grad_keys_raw, grad_key_norm = key_back(local_keys)
        query_grad_low = grad_queries.reshape(row_count, length, HEADS * HEAD_DIM).astype(
            jnp.bfloat16
        )
        key_grad_low = grad_keys_raw.reshape(row_count, length, KV_HEADS * HEAD_DIM).astype(
            jnp.bfloat16
        )
        value_grad_low = local_values.reshape(row_count, length, KV_HEADS * HEAD_DIM).astype(
            jnp.bfloat16
        )
        grad_normed = (
            back_dense(query_grad_low, query_matrix)
            + back_dense(key_grad_low, key_matrix)
            + back_dense(value_grad_low, value_matrix)
        )
        grad_hidden, grad_gain = norm_back(grad_normed)
        return (
            gradient + grad_hidden,
            (
                grad_gain,
                weight_grad(
                    normed_low,
                    jnp.concatenate([query_grad_low, key_grad_low, value_grad_low], axis=-1),
                ),
                grad_query_norm,
                grad_key_norm,
                grad_output,
            ),
        )

    return (result, attend_backward)


def reduce_entries(pairs):
    entries = []
    x_first = g_first = chunk = 0
    for x_count, g_count in pairs:
        entries.append((x_first, x_count, g_first, g_count, chunk))
        x_first += x_count
        g_first += g_count
        chunk += x_count * g_count
    return entries, x_first, g_first, chunk


def locate(entries, q):
    x_block, g_block = jnp.int32(0), jnp.int32(0)
    for x_first, x_count, g_first, g_count, chunk in entries:
        here = q - chunk
        inside = here >= 0
        x_block = jnp.where(inside, x_first + lax.rem(jnp.maximum(here, 0), x_count), x_block)
        g_block = jnp.where(inside, g_first + jnp.maximum(here, 0) // x_count, g_block)
    return x_block, g_block


def seq_steps(bits):
    upper = list(range(1, bits))
    middle = (len(upper) + 1) // 2
    kinds = []
    for order in (upper, upper[middle:] + upper[:middle]):
        held = sorted(upper, reverse=True)
        steps = []
        for bit in order:
            place = held.index(bit)
            steps.append((bit, 2**place, 2 ** (len(held) - 1 - place)))
            held.remove(bit)
        kinds.append(steps)
    return kinds


def exchange_scratch(row_count, shards, block_rows, x_blocks, g_blocks, tokens):
    bits = shards.bit_length() - 1
    block = (block_rows, COLS)
    comm = []
    for steps in seq_steps(bits):
        for _, above, below in steps:
            comm.append(pltpu.VMEM((2, above, 2, below) + block, jnp.bfloat16))
            comm.append(pltpu.VMEM((SLOTS, above, below) + block, jnp.bfloat16))
    z_steps = row_count - 1
    return [
        pltpu.VMEM((shards // 2, 2, x_blocks, block_rows, tokens), jnp.bfloat16),
        pltpu.VMEM((tokens, g_blocks * COLS), jnp.bfloat16),
        pltpu.VMEM((2, 2, shards // 2) + block, jnp.bfloat16),
        pltpu.VMEM((2, SLOTS, shards // 2) + block, jnp.bfloat16),
        *comm,
        *[pltpu.VMEM((2, ZSLOTS) + block, jnp.bfloat16) for _ in range(5)],
        pltpu.SemaphoreType.DMA((2, bits, SLOTS)),
        pltpu.SemaphoreType.DMA((2, bits, SLOTS)),
        pltpu.SemaphoreType.DMA((2, z_steps, ZSLOTS)),
        pltpu.SemaphoreType.DMA((2, z_steps, ZSLOTS)),
        pltpu.SemaphoreType.DMA((2, ZSLOTS)),
    ]


class Exchange:
    def __init__(self, entries, row_count, shards, outs, scratch, locals_at=(), local=None):
        self.entries, self.outs = entries, outs
        self.locals_at, self.local = locals_at, local
        self.bits = bits = shards.bit_length() - 1
        self.kinds = seq_steps(bits)
        (self.x_all, self.g_all, self.send_zero, self.recv_zero, *rest) = scratch
        self.held, self.received = [[], []], [[], []]
        for kind in range(2):
            for _ in self.kinds[kind]:
                self.held[kind].append(rest.pop(0))
                self.received[kind].append(rest.pop(0))
        self.z_own, self.z_in, self.z_part, self.z_cross, self.z_total = rest[:5]
        self.seq_send, self.seq_recv, self.z_send, self.z_recv, self.out_sem = rest[5:]
        self.row, self.seq = lax.axis_index("row"), lax.axis_index("seq")
        self.row_count, self.shards = row_count, shards
        self.value = [lax.rem(self.seq // (1 << bit), 2) for bit in range(bits)]
        self.partner = [self.seq + (1 << bit) * (1 - 2 * self.value[bit]) for bit in range(bits)]
        last = entries[-1]
        self.pairs = (last[4] + last[1] * last[3]) // 2 + len(locals_at)
        half = row_count // 2
        self.depth = half - 1
        lower = self.row < half
        self.level = jnp.where(lower, self.row, row_count - 1 - self.row)
        self.toward = jnp.where(lower, self.row + 1, self.row - 1)
        self.away = jnp.where(lower, self.row - 1, self.row + 1)

    def meet(self):
        barrier = pltpu.get_barrier_semaphore()
        others = [(self.row, partner) for partner in self.partner]
        for step in (1, self.row_count - 1):
            others.append((lax.rem(self.row + step, self.row_count), self.seq))
        for step in (1, self.shards - 1):
            others.append((self.row, lax.rem(self.seq + step, self.shards)))
        for other in others:
            pl.semaphore_signal(barrier, inc=1, device_id=other, device_id_type=MESH)
        pl.semaphore_wait(barrier, len(others))

    def is_local(self, index):
        found = index < 0
        for at in self.locals_at:
            found = jnp.logical_or(found, index == at)
        return found

    def chunk(self, kind, index):
        before = sum([jnp.where(index > at, 1, 0) for at in self.locals_at], 0)
        return 2 * (index - before) + kind

    def product(self, kind, index, side):
        x_block, g_block = locate(self.entries, self.chunk(kind, index))
        left = self.x_all[:, side, x_block]
        columns = pl.ds(pl.multiple_of(g_block * COLS, COLS), COLS)
        return jnp.dot(
            left.reshape(left.shape[0] * left.shape[1], left.shape[2]),
            self.g_all[:, columns],
            preferred_element_type=jnp.float32,
        )

    def seq_copy(self, kind, step, slot):
        if step == 0:
            bit = 0
            source = self.send_zero.at[kind, lax.rem(slot, 2)]
            target = self.recv_zero.at[kind, slot]
        else:
            bit = self.kinds[kind][step - 1][0]
            source = self.held[kind][step - 1].at[lax.rem(slot, 2), :, 1 - self.value[bit]]
            target = self.received[kind][step - 1].at[slot]
        return pltpu.make_async_remote_copy(
            src_ref=source,
            dst_ref=target,
            send_sem=self.seq_send.at[kind, step, slot],
            recv_sem=self.seq_recv.at[kind, step, slot],
            device_id=(self.row, self.partner[bit]),
            device_id_type=MESH,
        )

    def seq_sum(self, kind, step, slot):
        bit = self.kinds[kind][step - 2][0]
        mine = self.held[kind][step - 2][lax.rem(slot, 2), :, self.value[bit]].astype(jnp.float32)
        return mine + self.received[kind][step - 2][slot].astype(jnp.float32)

    def z_copy(self, kind, step, slot):
        if step < self.depth:
            source = self.z_own if step == 0 else self.z_part
            target, where = self.z_in, self.toward
        elif step == self.depth:
            source = self.z_own if self.depth == 0 else self.z_part
            target, where = self.z_cross, self.toward
        else:
            source, target, where = self.z_total, self.z_total, self.away
        return pltpu.make_async_remote_copy(
            src_ref=source.at[kind, slot],
            dst_ref=target.at[kind, slot],
            send_sem=self.z_send.at[kind, step, slot],
            recv_sem=self.z_recv.at[kind, step, slot],
            device_id=(where, self.seq),
            device_id_type=MESH,
        )

    def start_out(self, kind, slot, index):
        q = self.chunk(kind, index)
        rows = self.z_total.shape[2]
        for out, (_, x_count, _, g_count, chunk) in zip(self.outs, self.entries):
            here = q - chunk

            @pl.when(jnp.logical_and(here >= 0, here < x_count * g_count))
            def _():
                row_at = pl.multiple_of(lax.rem(here, x_count) * rows, rows)
                column_at = pl.multiple_of(here // x_count * COLS, COLS)
                pltpu.make_async_copy(
                    self.z_total.at[kind, slot],
                    out.at[pl.ds(row_at, rows), pl.ds(column_at, COLS)],
                    self.out_sem.at[kind, slot],
                ).start()

    def first(self, kind, index):
        slot = lax.rem(index, SLOTS)
        target = self.send_zero

        def put():
            target[kind, lax.rem(slot, 2)] = (
                self.product(kind, index, 1 - self.value[0])
                .astype(jnp.bfloat16)
                .reshape(target.shape[2:])
            )

        if self.local is None:
            put()
        else:
            pl.when(jnp.logical_not(self.is_local(index)))(put)

            @pl.when(self.is_local(index))
            def _():
                target[kind, lax.rem(slot, 2)] = self.local.part(kind, index, 1 - self.value[0])

        self.seq_copy(kind, 0, slot).start()

    def second(self, kind, index):
        slot = lax.rem(index, SLOTS)
        self.seq_copy(kind, 0, slot).wait()
        target = self.held[kind][0]

        def put():
            mine = self.product(kind, index, self.value[0])
            total = mine + self.recv_zero[kind, slot].astype(jnp.float32).reshape(mine.shape)
            target[lax.rem(slot, 2)] = total.astype(jnp.bfloat16).reshape(target.shape[1:])

        if self.local is None:
            put()
        else:
            pl.when(jnp.logical_not(self.is_local(index)))(put)

            @pl.when(self.is_local(index))
            def _():
                mine = self.local.part(kind, index, self.value[0]).astype(jnp.float32)
                total = mine + self.recv_zero[kind, slot].astype(jnp.float32)
                target[lax.rem(slot, 2)] = total.astype(jnp.bfloat16).reshape(target.shape[1:])

        self.seq_copy(kind, 1, slot).start()

    def middle(self, step):
        def run(kind, index):
            slot = lax.rem(index, SLOTS)
            self.seq_copy(kind, step - 1, slot).wait()
            total = self.seq_sum(kind, step, slot)
            target = self.held[kind][step - 1]
            target[lax.rem(slot, 2)] = total.astype(jnp.bfloat16).reshape(target.shape[1:])
            self.seq_copy(kind, step, slot).start()

        return run

    def last(self, kind, index):
        slot, z_slot = lax.rem(index, SLOTS), lax.rem(index, ZSLOTS)
        self.seq_copy(kind, self.bits - 1, slot).wait()
        total = self.seq_sum(kind, self.bits, slot).reshape(self.z_own.shape[2:])

        def put():
            self.z_own[kind, z_slot] = total.astype(jnp.bfloat16)

            @pl.when(self.level == 0)
            def _():
                self.z_copy(kind, 0, z_slot).start()

        if self.local is None:
            put()
        else:
            pl.when(jnp.logical_not(self.is_local(index)))(put)

            @pl.when(self.is_local(index))
            def _():
                self.local.take(kind, index, total)

    def z_stage(self, step):
        level, depth = self.level, self.depth

        def run(kind, index):
            slot = lax.rem(index, ZSLOTS)
            if step <= depth:

                @pl.when(level == step)
                def _():
                    self.z_copy(kind, step - 1, slot).wait_recv()
                    self.z_part[kind, slot] = (
                        self.z_own[kind, slot].astype(jnp.float32)
                        + self.z_in[kind, slot].astype(jnp.float32)
                    ).astype(jnp.bfloat16)
                    self.z_copy(kind, step, slot).start()

                @pl.when(level == step - 1)
                def _():
                    self.z_copy(kind, step - 1, slot).wait_send()

            elif step == depth + 1:

                @pl.when(level == depth)
                def _():
                    self.z_copy(kind, depth, slot).wait()
                    own = self.z_own if depth == 0 else self.z_part
                    self.z_total[kind, slot] = (
                        own[kind, slot].astype(jnp.float32)
                        + self.z_cross[kind, slot].astype(jnp.float32)
                    ).astype(jnp.bfloat16)
                    if depth > 0:
                        self.z_copy(kind, step, slot).start()
                    self.start_out(kind, slot, index)

            else:
                receiver = 2 * depth + 1 - step

                @pl.when(level == receiver)
                def _():
                    self.z_copy(kind, step - 1, slot).wait_recv()
                    if receiver > 0:
                        self.z_copy(kind, step, slot).start()
                    self.start_out(kind, slot, index)

                @pl.when(level == receiver + 1)
                def _():
                    self.z_copy(kind, step - 1, slot).wait_send()

        return run

    def finish(self, kind, index):
        slot = lax.rem(index, ZSLOTS)
        rows = self.z_total.shape[2]
        pltpu.make_async_copy(
            self.z_total.at[kind, slot],
            self.outs[0].at[pl.ds(0, rows), pl.ds(0, COLS)],
            self.out_sem.at[kind, slot],
        ).wait()

    def run(self, task):
        stages = [(self.first, False), (self.second, False)]
        stages += [(self.middle(step), False) for step in range(2, self.bits)]
        stages += [(self.last, False)]
        stages += [(self.z_stage(step), True) for step in range(1, 2 * self.depth + 2)]
        stages += [(self.finish, True)]

        def iteration(i, carried):
            for at, (stage, summed_only) in enumerate(stages):
                index = i - at
                here = jnp.logical_and(index >= 0, index < self.pairs)
                if summed_only and self.locals_at:
                    here = jnp.logical_and(here, jnp.logical_not(self.is_local(index)))

                @pl.when(here)
                def _():
                    for kind in range(2):
                        stage(kind, index)

            if task is not None:
                task(i)
            return carried

        lax.fori_loop(0, self.pairs + len(stages) - 1, iteration, 0)


def reduce_kernel(entries, row_count, shards, *refs):
    count = len(entries)
    xs, gs, outs = refs[:count], refs[count : 2 * count], refs[2 * count : 3 * count]
    load_x, load_g, *scratch = refs[3 * count :]
    exchange = Exchange(entries, row_count, shards, outs, scratch)
    copies = []
    for at, (x_first, x_count, g_first, g_count, _) in enumerate(entries):
        x_part = exchange.x_all.at[:, :, pl.ds(x_first, x_count)]
        g_part = exchange.g_all.at[:, pl.ds(g_first * COLS, g_count * COLS)]
        copies.append(pltpu.make_async_copy(xs[at], x_part, load_x.at[at]))
        copies.append(pltpu.make_async_copy(gs[at], g_part, load_g.at[at]))
    for copy in copies:
        copy.start()
    exchange.meet()
    for copy in copies:
        copy.wait()
    exchange.run(None)


def reduce_gradients(pairs, row_count, shards, collective_id):
    block_rows, tokens = pairs[0][0].shape[3:]
    entries, x_blocks, g_blocks, chunks = reduce_entries(
        [(x.shape[2], g.shape[1] // COLS) for x, g in pairs]
    )
    return pl.pallas_call(
        functools.partial(reduce_kernel, entries, row_count, shards),
        out_shape=[
            jax.ShapeDtypeStruct((x_count * block_rows, g_count * COLS), jnp.bfloat16)
            for _, x_count, _, g_count, _ in entries
        ],
        in_specs=[pl.BlockSpec(memory_space=pl.ANY)] * (2 * len(pairs)),
        out_specs=[pl.BlockSpec(memory_space=pl.ANY)] * len(pairs),
        scratch_shapes=[
            pltpu.SemaphoreType.DMA((len(pairs),)),
            pltpu.SemaphoreType.DMA((len(pairs),)),
            *exchange_scratch(row_count, shards, block_rows, x_blocks, g_blocks, tokens),
        ],
        compiler_params=pltpu.CompilerParams(
            collective_id=collective_id, has_side_effects=True, vmem_limit_bytes=52 * 2**20
        ),
        cost_estimate=pl.CostEstimate(
            flops=2 * chunks * shards * block_rows * COLS * tokens,
            bytes_accessed=2 * chunks * block_rows * COLS,
            transcendentals=0,
        ),
    )(*[x for x, _ in pairs], *[g for _, g in pairs])


def body(
    tokens,
    lengths,
    mixer_gain,
    mixer_input,
    mixer_kernel,
    mixer_output,
    first_gain,
    first_gate,
    first_up,
    first_down,
    attend_gain,
    query_weight,
    key_weight,
    value_weight,
    query_gain,
    key_gain,
    attend_output,
    second_gain,
    second_gate,
    second_up,
    second_down,
    cotangent,
):
    length = tokens.shape[1]
    positions = lax.axis_index("seq") * length + jnp.arange(length, dtype=jnp.int32)
    segment, seg_start = segment_info(lengths, positions)
    offsets = positions[None, :] - seg_start
    hidden = tokens.astype(jnp.float32)
    hidden, mixer_back = mixer_block(
        hidden, mixer_gain, mixer_input, mixer_kernel, mixer_output, seg_start, positions
    )
    hidden, first_back = feed_block(hidden, first_gain, first_gate, first_up, first_down)
    hidden, attend_back = attend_block(
        hidden,
        lengths,
        attend_gain,
        query_weight,
        key_weight,
        value_weight,
        query_gain,
        key_gain,
        attend_output,
        segment,
        positions,
        offsets,
    )
    hidden, second_back = feed_block(hidden, second_gain, second_gate, second_up, second_down)
    gradient = cotangent.astype(jnp.float32)
    gradient, second_grads = second_back(gradient)
    gradient, attend_grads = attend_back(gradient)
    gradient, first_grads = first_back(gradient)
    gradient, mixer_grads = mixer_back(gradient)
    second_gain_sum, second_wide, second_down_pair = second_grads
    attend_gain_sum, attend_wide, query_gain_sum, key_gain_sum, attend_output_pair = attend_grads
    first_gain_sum, first_wide, first_down_pair = first_grads
    mixer_gain_sum, mixer_input_pair, mixer_kernel_sum, mixer_output_pair = mixer_grads
    row_count, shards = lax.axis_size("row"), lax.axis_size("seq")
    block_rows = math.gcd(tokens.shape[2] // shards, first_down.shape[0] // shards)

    def operands(pair):
        inputs, gradient_low = pair
        token_count = inputs.shape[0] * inputs.shape[1]
        inputs = inputs.reshape(token_count, -1).T
        blocks = inputs.shape[0] // shards // block_rows
        return (
            inputs.reshape(shards // 2, 2, blocks, block_rows, token_count),
            gradient_low.reshape(token_count, -1),
        )

    wide_vectors = jnp.concatenate(
        [
            mixer_kernel_sum,
            jnp.stack([mixer_gain_sum, first_gain_sum, attend_gain_sum, second_gain_sum]),
        ]
    )
    vector_count = wide_vectors.shape[0]
    vectors = jnp.concatenate(
        [
            part.reshape(-1, shards, part.shape[-1] // shards)
            .transpose(1, 0, 2)
            .reshape(shards, -1)
            for part in (wide_vectors, jnp.stack([query_gain_sum, key_gain_sum]))
        ],
        axis=1,
    )
    vector_rows = -(-vectors.shape[1] // COLS)
    token_count = tokens.shape[0] * tokens.shape[1]
    vectors = jnp.pad(vectors, ((0, 0), (0, vector_rows * COLS - vectors.shape[1])))
    vectors = vectors.reshape(shards * vector_rows, COLS).astype(jnp.bfloat16)
    vectors = jnp.pad(vectors, ((0, token_count - shards * vector_rows), (0, 0)))
    shard_at = lax.broadcasted_iota(jnp.int32, (shards, 2 * block_rows, token_count), 0)
    row_at = lax.broadcasted_iota(jnp.int32, (shards, 2 * block_rows, token_count), 1)
    token_at = lax.broadcasted_iota(jnp.int32, (shards, 2 * block_rows, token_count), 2)
    picks = (row_at < vector_rows) & (token_at == shard_at * vector_rows + row_at)
    picks = picks.astype(jnp.bfloat16).reshape(shards // 2, 2, 2, block_rows, token_count)
    (
        grad_second_down,
        second_both,
        grad_attend_output,
        attend_three,
        grad_first_down,
        first_both,
        grad_mixer_output,
        grad_mixer_input,
        vector_sums,
    ) = reduce_gradients(
        [
            operands(second_down_pair),
            operands(second_wide),
            operands(attend_output_pair),
            operands(attend_wide),
            operands(first_down_pair),
            operands(first_wide),
            operands(mixer_output_pair),
            operands(mixer_input_pair),
            (picks, vectors),
        ],
        row_count,
        shards,
        0,
    )

    def single(value):
        return value.astype(jnp.float32)

    hidden_columns = first_gate.shape[1]
    query_columns, key_columns = query_weight.shape[1], key_weight.shape[1]
    vector_sums = single(vector_sums[:vector_rows]).reshape(-1)
    width = tokens.shape[2] // shards
    wide_sums = vector_sums[: vector_count * width].reshape(vector_count, width)
    head_width = HEAD_DIM // shards
    head_sums = vector_sums[vector_count * width :][: 2 * head_width].reshape(2, head_width)
    return (
        hidden.astype(jnp.bfloat16),
        gradient.astype(jnp.bfloat16),
        wide_sums[3],
        single(grad_mixer_input),
        wide_sums[:3],
        single(grad_mixer_output),
        wide_sums[4],
        single(first_both[:, :hidden_columns]),
        single(first_both[:, hidden_columns:]),
        single(grad_first_down),
        wide_sums[5],
        single(attend_three[:, :query_columns]),
        single(attend_three[:, query_columns : query_columns + key_columns]),
        single(attend_three[:, query_columns + key_columns :]),
        head_sums[0],
        head_sums[1],
        single(grad_attend_output),
        wide_sums[6],
        single(second_both[:, :hidden_columns]),
        single(second_both[:, hidden_columns:]),
        single(grad_second_down),
    )


def dot_nt(left, right):
    return lax.dot_general(
        left, right, (((1,), (1,)), ((), ())), preferred_element_type=jnp.float32
    )


def dot_tn(left, right):
    return lax.dot_general(
        left, right, (((0,), (0,)), ((), ())), preferred_element_type=jnp.float32
    )


def lanes_below(shape, bound, period):
    return lax.rem(lax.broadcasted_iota(jnp.int32, shape, len(shape) - 1), period) < bound


def two_heads(pair, low):
    pair = pair.astype(jnp.float32)
    turned = pltpu.roll(pair, HEAD_DIM, 1)
    first = lanes_below(pair.shape, HEAD_DIM, 2 * HEAD_DIM)
    if low:
        parts = [jnp.where(first, pair, 0.0), jnp.where(first, turned, 0.0)]
    else:
        parts = [jnp.where(first, 0.0, turned), jnp.where(first, 0.0, pair)]
    return jnp.concatenate(parts, axis=0).astype(jnp.bfloat16)


BACKWARD_STARTS = {
    "second": 0,
    "attend_output": 8,
    "attention": 10,
    "queries": 26,
    "keys": 31,
    "first": 32,
    "mixer_output": 41,
    "halo": 43,
    "mixer_input": 44,
    "close": 47,
}
LOCAL_PAIRS = (18, 19, 26, 27)


def backward_kernel(names, entries, row_count, shards, *refs):
    at = types.SimpleNamespace(**dict(zip(names, refs)))
    outs = refs[len(names) : len(names) + len(entries)]
    token_out, mixed_out = refs[len(names) + len(entries) : len(names) + len(entries) + 2]
    scratch = refs[len(names) + len(entries) + 2 :]
    (
        tiles_a,
        tiles_b,
        tiles_c,
        saved,
        keys_values,
        key_grads,
        key_sums,
        queries,
        attended_grad,
        wide,
        mask,
        queries_raw,
        keys_raw,
        gradient,
        normed_grad,
        hidden,
        halo_out,
        halo_in,
        small,
        tile_sem,
        load_sem,
        halo_sem,
        *scratch,
    ) = scratch
    local = types.SimpleNamespace()
    exchange = Exchange(entries, row_count, shards, outs, scratch, LOCAL_PAIRS, local)
    x_all, g_all = exchange.x_all, exchange.g_all
    seq, row = exchange.seq, exchange.row
    tokens, width = gradient.shape
    rows = keys_values.shape[0]
    length = tokens // rows
    hidden_blocks = at.first_gate.shape[1] // COLS
    blocks = width // COLS
    g_at = [entry[2] * COLS for entry in entries]
    second_wide, second_down, output_at, heads_at, first_down, first_wide = g_at[:6]
    mixer_out_at, mixer_in_at, small_at = g_at[6:]
    starts = BACKWARD_STARTS

    def local_place(kind, index):
        first, second, third, fourth = LOCAL_PAIRS
        row_at = jnp.where(index >= third, 1, 0)
        quad = jnp.where(jnp.logical_or(index == second, index == fourth), 1, 0)
        return row_at, pl.ds(pl.multiple_of(quad * COLS, COLS), COLS)

    def part(kind, index, side):
        row_at, columns = local_place(kind, index)
        return key_grads[row_at, :, side, kind, :, columns]

    def take(kind, index, total):
        row_at, columns = local_place(kind, index)
        key_sums[row_at, kind, :, columns] = total.astype(jnp.bfloat16)

    local.part, local.take = part, take

    def tile_copies(name, j, slot):
        columns = pl.ds(pl.multiple_of(j * COLS, COLS), COLS)
        a, b, c = tiles_a.at[slot], tiles_b.at[slot], tiles_c.at[slot]
        if name == "second":
            moves = [
                (at.second_gate.at[:, columns], b),
                (at.second_up.at[:, columns], c),
                (at.second_down.at[columns], a),
            ]
        elif name == "first":
            moves = [
                (at.first_down.at[columns], a),
                (at.first_gate.at[:, columns], b),
                (at.first_up.at[:, columns], c),
                (at.gate_one.at[:, columns], saved.at[slot, 0]),
                (at.up_one.at[:, columns], saved.at[slot, 1]),
            ]
        elif name == "attend_output":
            moves = [(at.attend_output.at[columns], a)]
        elif name == "mixer_output":
            moves = [(at.mixer_output.at[columns], a)]
        elif name == "queries":
            moves = [
                (at.query_weight.at[:, pl.ds(0, COLS)], b),
                (at.query_weight.at[:, pl.ds(COLS, COLS)], c),
            ]
        elif name == "keys":
            moves = [(at.key_weight, b), (at.value_weight, c)]
        else:
            even = pl.multiple_of(2 * j * COLS, COLS)
            odd = pl.multiple_of((2 * j + 1) * COLS, COLS)
            moves = [
                (at.mixer_input.at[:, pl.ds(even, COLS)], b),
                (at.mixer_input.at[:, pl.ds(odd, COLS)], c),
            ]
        return [
            pltpu.make_async_copy(source, target, tile_sem.at[slot, place])
            for place, (source, target) in enumerate(moves)
        ]

    steps = [
        ("second", hidden_blocks),
        ("attend_output", blocks),
        ("queries", 1),
        ("keys", 1),
        ("first", hidden_blocks),
        ("mixer_output", blocks),
        ("mixer_input", 3 * blocks // 2),
    ]
    first_step, total = {}, 0
    for name, number in steps:
        first_step[name] = total
        total += number
    order = [name for name, _ in steps]
    numbers = dict(steps)

    def tile_step(name, j):
        slot = (first_step[name] + j) % 2 if isinstance(j, int) else lax.rem(first_step[name] + j, 2)
        for copy in tile_copies(name, j, slot):
            copy.wait()

        @pl.when(j + 1 < numbers[name])
        def _():
            for copy in tile_copies(name, j + 1, 1 - slot):
                copy.start()

        if name != order[-1]:
            following = order[order.index(name) + 1]

            @pl.when(j + 1 == numbers[name])
            def _():
                for copy in tile_copies(following, 0, 1 - slot):
                    copy.start()

        return slot

    def load(place, source, target):
        return pltpu.make_async_copy(source, target, load_sem.at[place])

    count = len(entries)
    x_loads = [
        load(number, at.xs[number - 2], x_all.at[:, :, pl.ds(x_first, x_count)])
        for number, (x_first, x_count, _, _, _) in enumerate(entries)
        if number >= 2
    ]
    cotangent_load = load(count, at.cotangent, g_all.at[:, pl.ds(second_down, width)])
    middle_loads = [
        load(count + 1, at.queries_low, queries),
        load(count + 2, at.keys_values, keys_values),
        load(count + 3, at.mask, mask),
        load(count + 5, at.keys_raw, keys_raw),
    ]
    raw_load = load(count + 4, at.queries_raw, queries_raw)
    staged = queries_raw
    late_loads = [
        load(count + 6, at.mixer_saved, keys_values.at[0]),
        load(count + 7, at.projected, keys_values.at[1, pl.ds(0, 3 * tokens)]),
    ]
    hidden_loads = [
        load(count + 8, source, hidden)
        for source in (at.hidden_three, at.hidden_two, at.hidden_one, at.hidden_zero)
    ]
    out_copy = load(count + 9, staged, token_out)
    mixed_copy = load(count + 9, staged, mixed_out)

    hidden_loads[0].start()
    cotangent_load.start()
    for copy in tile_copies("second", 0, 0):
        copy.start()
    for copy in middle_loads + x_loads:
        copy.start()
    normed_grad[...] = jnp.zeros_like(normed_grad)
    small[...] = jnp.zeros_like(small)
    g_all[:, pl.ds(small_at, COLS)] = jnp.zeros((tokens, COLS), jnp.bfloat16)
    wide[...] = jnp.zeros_like(wide)
    hidden_loads[0].wait()
    normed = attended_grad
    x_two = entries[0][0]
    for first in range(0, tokens, 128):
        span = pl.ds(first, 128)
        value = hidden[span]
        inverse = lax.rsqrt(jnp.mean(value * value, axis=-1, keepdims=True) + EPS)
        value = value * inverse * at.gains[0:1, :]
        normed[span] = value.astype(jnp.bfloat16)
        turned = value.T.astype(jnp.bfloat16)
        shape = x_all.shape[:2] + (2,) + x_all.shape[3:4] + (128,)
        x_all[:, :, x_two : x_two + 2, :, pl.ds(first, 128)] = turned.reshape(shape)
    cotangent_load.wait()
    gradient[...] = g_all[:, pl.ds(second_down, width)].astype(jnp.float32)

    def low_gradient(place):
        g_all[:, pl.ds(place, width)] = gradient[...].astype(jnp.bfloat16)

    def norm_back(number):
        if number > 0:
            hidden_loads[number].wait()
        gain = at.gains[number : number + 1, :]
        sums = jnp.zeros((1, width), jnp.float32)
        piece = 64
        for first in range(0, tokens, piece):
            span = pl.ds(first, piece)
            value, upper = hidden[span], normed_grad[span]
            inverse = lax.rsqrt(jnp.mean(value * value, axis=-1, keepdims=True) + EPS)
            value = value * inverse
            sums = sums + jnp.sum(upper * value, axis=0, keepdims=True)
            upper = upper * gain
            shift = jnp.mean(upper * value, axis=-1, keepdims=True)
            gradient[span] = gradient[span] + inverse * (upper - value * shift)
        for block in range(blocks):
            place = blocks * number + block
            small[place : place + 1, :] = sums[:, block * COLS : (block + 1) * COLS]
        normed_grad[...] = jnp.zeros_like(normed_grad)
        if number + 1 < len(hidden_loads):
            hidden_loads[number + 1].start()

    def feed_tile(name, j, gradient_at, wide_at):
        slot = tile_step(name, j)
        low = g_all[:, pl.ds(gradient_at, width)]
        active_grad = dot_nt(low, tiles_a[slot])
        if name == "second":
            gate_value = jnp.dot(normed[...], tiles_b[slot], preferred_element_type=jnp.float32)
            up_value = jnp.dot(normed[...], tiles_c[slot], preferred_element_type=jnp.float32)
        else:
            gate_value = saved[slot, 0].astype(jnp.float32)
            up_value = saved[slot, 1].astype(jnp.float32)
        share = 1.0 / (1.0 + jnp.exp(-gate_value))
        if name == "second":
            active = gate_value * share * up_value
            wide[...] += jnp.dot(
                active.astype(jnp.bfloat16), tiles_a[slot], preferred_element_type=jnp.float32
            )
            turned = active.T.astype(jnp.bfloat16)
            x_down, x_count = entries[1][:2]
            block_rows = x_all.shape[3]
            for block in range(COLS // block_rows):
                place = j * (COLS // block_rows) + block
                shard = place // x_count
                part = turned[block * block_rows : (block + 1) * block_rows]
                x_all[shard // 2, lax.rem(shard, 2), x_down + lax.rem(place, x_count)] = part
        up_grad = (active_grad * gate_value * share).astype(jnp.bfloat16)
        gate_grad = active_grad * up_value * share * (1.0 + gate_value * (1.0 - share))
        gate_grad = gate_grad.astype(jnp.bfloat16)
        gate_place = pl.multiple_of(wide_at + j * COLS, COLS)
        up_place = pl.multiple_of(wide_at + (hidden_blocks + j) * COLS, COLS)
        g_all[:, pl.ds(gate_place, COLS)] = gate_grad
        g_all[:, pl.ds(up_place, COLS)] = up_grad
        normed_grad[...] += dot_nt(gate_grad, tiles_b[slot]) + dot_nt(up_grad, tiles_c[slot])

    def output_tile(name, j, gradient_at, target):
        slot = tile_step(name, j)
        low = g_all[:, pl.ds(gradient_at, width)]
        value = dot_nt(low, tiles_a[slot])
        target[:, j * COLS : (j + 1) * COLS] = value.astype(target.dtype)

    def attention_head(row_at, head):
        span = pl.ds(pl.multiple_of(row_at * length, length), length)
        columns = pl.ds(pl.multiple_of(head * 2 * HEAD_DIM, 2 * HEAD_DIM), 2 * HEAD_DIM)
        query = two_heads(queries[span, columns], True)
        upper = two_heads(attended_grad[span, columns], False)
        both = keys_values[row_at, :, columns]
        allowed = mask[row_at].astype(jnp.float32)
        weights = jnp.exp(dot_nt(both, query)) * jnp.concatenate([allowed, allowed], axis=1)
        weights = weights * (1.0 / jnp.sum(weights, axis=0, keepdims=True))
        weight_grad_value = dot_nt(both, upper)
        delta = jnp.sum(weights * weight_grad_value, axis=0, keepdims=True)
        score_grad = (weights * (weight_grad_value - delta)).astype(jnp.bfloat16)
        both_grad = jnp.dot(score_grad, query, preferred_element_type=jnp.float32)
        both_grad += jnp.dot(
            weights.astype(jnp.bfloat16), upper, preferred_element_type=jnp.float32
        )
        shape = key_grads.shape[1:5] + (2 * HEAD_DIM,)
        key_grads[row_at, :, :, :, :, columns] = both_grad.astype(jnp.bfloat16).reshape(shape)
        query_grad = dot_tn(score_grad, both) * HEAD_DIM ** (-0.5)
        first = lanes_below((length, 2 * HEAD_DIM), HEAD_DIM, 2 * HEAD_DIM)
        wide[span, columns] = jnp.where(
            first, query_grad[:length], pltpu.roll(query_grad[length:], HEAD_DIM, 1)
        )

    lane = 2 * HEAD_DIM
    head_of = lax.broadcasted_iota(jnp.int32, (lane, lane), 0) // HEAD_DIM
    ones = head_of == lax.broadcasted_iota(jnp.int32, (lane, lane), 1) // HEAD_DIM
    ones = ones.astype(jnp.float32).astype(jnp.bfloat16)

    def head_mean(value):
        total = jnp.dot(value.astype(jnp.bfloat16), ones, preferred_element_type=jnp.float32)
        return total * (1.0 / HEAD_DIM)

    def head_back(value, raw, gain):
        half = HEAD_DIM // 2
        first = lanes_below(value.shape, half, HEAD_DIM)
        turned = jnp.where(first, pltpu.roll(value, lane - half, 1), pltpu.roll(value, half, 1))
        value = value * at.cosine[...] - turned * at.sine[...]
        raw = raw.astype(jnp.float32)
        inverse = lax.rsqrt(head_mean(raw * raw) + EPS)
        raw = raw * inverse
        sums = jnp.sum(value * raw, axis=0, keepdims=True)
        value = value * gain
        return inverse * (value - raw * head_mean(value * raw)), sums

    def both_halves(sums):
        return sums + pltpu.roll(sums, HEAD_DIM, 1)

    head_row = 7 * blocks

    def query_heads():
        sums = jnp.zeros((8, lane), jnp.float32)
        for part_at in range(0, width, lane):
            columns = pl.ds(part_at, lane)
            value, more = head_back(wide[:, columns], queries_raw[:, columns], at.head_gains[0:1])
            g_all[:, pl.ds(heads_at + part_at, lane)] = value.astype(jnp.bfloat16)
            sums = sums + more
        small[head_row : head_row + 1, 0:lane] = both_halves(sums)[0:1]

    def key_heads():
        sums = jnp.zeros((8, lane), jnp.float32)
        first = lanes_below((tokens, lane), HEAD_DIM, lane)
        for pair in range(width // lane // 2):
            even, odd = [
                key_sums[:, :, :, pl.ds((2 * pair + which) * lane, lane)]
                .astype(jnp.float32)
                .reshape(tokens, lane)
                for which in range(2)
            ]
            key_value = jnp.where(first, even, pltpu.roll(odd, HEAD_DIM, 1))
            value_value = jnp.where(first, pltpu.roll(even, HEAD_DIM, 1), odd)
            columns = pl.ds(pair * lane, lane)
            value, more = head_back(key_value, keys_raw[:, columns], at.head_gains[1:2])
            place = heads_at + width + pair * lane
            g_all[:, pl.ds(place, lane)] = value.astype(jnp.bfloat16)
            place += width // 2
            g_all[:, pl.ds(place, lane)] = value_value.astype(jnp.bfloat16)
            sums = sums + more
        small[head_row : head_row + 1, lane : 2 * lane] = both_halves(sums)[0:1]

    def project_back(name, j, even_at, odd_at):
        slot = tile_step(name, j)
        normed_grad[...] += dot_nt(g_all[:, pl.ds(even_at, COLS)], tiles_b[slot]) + dot_nt(
            g_all[:, pl.ds(odd_at, COLS)], tiles_c[slot]
        )

    def halo_copy():
        return pltpu.make_async_remote_copy(
            src_ref=halo_out,
            dst_ref=halo_in,
            send_sem=halo_sem.at[0],
            recv_sem=halo_sem.at[1],
            device_id=(row, jnp.maximum(seq - 1, 0)),
            device_id_type=MESH,
        )

    def saved_part(number, columns):
        return keys_values[0, pl.ds(number * tokens, tokens), columns].astype(jnp.float32)

    def projected_part(number, columns):
        return keys_values[1, pl.ds(number * tokens, tokens), columns].astype(jnp.float32)

    def convolution_back():
        within = lax.rem(lax.broadcasted_iota(jnp.int32, (tokens, lane), 0), length)
        edge = lax.broadcasted_iota(jnp.int32, (8, lane), 0)
        for part_at in range(0, width, lane):
            columns = pl.ds(part_at, lane)
            gated_grad = wide[:, columns]
            exit_grad = gated_grad * saved_part(0, columns)
            place = mixer_in_at + width + part_at
            g_all[:, pl.ds(place, lane)] = exit_grad.astype(jnp.bfloat16)
            conv_grad = gated_grad * projected_part(1, columns)
            block, inside = part_at // COLS, part_at % COLS
            for tap in range(3):
                sums = jnp.sum(conv_grad * saved_part(1 + tap, columns), axis=0, keepdims=True)
                place = blocks * (4 + tap) + block
                small[place : place + 1, inside : inside + lane] = sums
            two = at.taps[0:1, columns] * at.keep[1] * conv_grad
            one = at.taps[1:2, columns] * at.keep[0] * conv_grad
            here = at.taps[2:3, columns] * conv_grad
            here += jnp.where(within < length - 1, pltpu.roll(one, tokens - 1, 0), 0.0)
            here += jnp.where(within < length - 2, pltpu.roll(two, tokens - 2, 0), 0.0)
            normed_grad[:, columns] = here
            for which in range(rows):
                span = slice(which * length, which * length + 8)
                sent = two[span] + jnp.where(edge == 1, pltpu.roll(one[span], 1, 0), 0.0)
                halo_out[which, :, columns] = jnp.where(edge < 2, sent, 0.0)

        @pl.when(seq > 0)
        def _():
            halo_copy().start()

    def product_back():
        @pl.when(seq < shards - 1)
        def _():
            halo_copy().wait_recv()
            for which in range(rows):
                span = pl.ds((which + 1) * length - 8, 8)
                normed_grad[span] = normed_grad[span] + pltpu.roll(halo_in[which], 6, 0)

        @pl.when(seq > 0)
        def _():
            halo_copy().wait_send()

        for part_at in range(0, width, lane):
            columns = pl.ds(part_at, lane)
            product_grad = normed_grad[:, columns]
            entry_grad = product_grad * projected_part(2, columns)
            carrier_grad = product_grad * projected_part(0, columns)
            g_all[:, pl.ds(mixer_in_at + part_at, lane)] = entry_grad.astype(jnp.bfloat16)
            place = mixer_in_at + 2 * width + part_at
            g_all[:, pl.ds(place, lane)] = carrier_grad.astype(jnp.bfloat16)
        normed_grad[...] = jnp.zeros_like(normed_grad)

    def task(i):
        def when(name, run, after=0, number=1):
            j = i - (starts[name] + after)

            @pl.when(jnp.logical_and(j >= 0, j < number))
            def _():
                run(j)

        when(
            "second",
            lambda j: feed_tile("second", j + 1, second_down, second_wide),
            0,
            hidden_blocks - 1,
        )

        def waits(j):
            for copy in middle_loads + x_loads:
                copy.wait()

        when("attend_output", waits)

        def to_attended(j):
            staged[...] = (hidden[...] + wide[...]).astype(jnp.bfloat16)
            mixed_copy.start()
            norm_back(0)
            low_gradient(output_at)
            output_tile("attend_output", 0, output_at, attended_grad)

        when("attend_output", to_attended)
        when("attend_output", lambda j: output_tile("attend_output", 1, output_at, attended_grad), 1)

        def staged_free(j):
            mixed_copy.wait()
            raw_load.start()

        when("attention", staged_free)

        def attention(j):
            attention_head(j // KV_HEADS, lax.rem(j, KV_HEADS))

        when("attention", attention, 0, rows * KV_HEADS)

        def to_queries(j):
            raw_load.wait()
            for copy in late_loads:
                copy.start()
            query_heads()

        when("queries", to_queries)
        when("queries", lambda j: project_back("queries", 0, heads_at, heads_at + COLS), 1)

        def to_keys(j):
            key_heads()
            project_back("keys", 0, heads_at + width, heads_at + width + COLS)
            norm_back(1)
            low_gradient(first_down)

        when("keys", to_keys)
        when("first", lambda j: feed_tile("first", j, first_down, first_wide), 0, hidden_blocks)

        def to_gated(j):
            norm_back(2)
            low_gradient(mixer_out_at)
            output_tile("mixer_output", 0, mixer_out_at, wide)
            for copy in late_loads:
                copy.wait()

        when("mixer_output", to_gated)

        def to_convolved(j):
            output_tile("mixer_output", 1, mixer_out_at, wide)
            convolution_back()

        when("mixer_output", to_convolved, 1)
        when("halo", lambda j: product_back())

        def mixer_tile(j):
            even = pl.multiple_of(mixer_in_at + 2 * j * COLS, COLS)
            project_back("mixer_input", j, even, pl.multiple_of(even + COLS, COLS))

        when("mixer_input", mixer_tile, 0, numbers["mixer_input"])

        def close(j):
            norm_back(3)
            staged[...] = gradient[...].astype(jnp.bfloat16)
            out_copy.start()
            g_all[pl.ds(0, small.shape[0]), pl.ds(small_at, COLS)] = small[...].astype(jnp.bfloat16)

        when("close", close)
        when("close", lambda j: out_copy.wait(), 1)

    exchange.meet()
    feed_tile("second", 0, second_down, second_wide)
    exchange.run(task)


def backward(groups, arrays, resident, row_count, shards, collective_id):
    xs = [x for x, _ in groups if not isinstance(x, int)]
    block_rows, tokens = xs[0].shape[3:]
    width = arrays["cotangent"].shape[1]
    entries, x_blocks, g_blocks, chunks = reduce_entries(
        [(x if isinstance(x, int) else x.shape[2], columns // COLS) for x, columns in groups]
    )
    names = ["xs_%d" % number for number in range(len(xs))] + list(arrays)
    values = list(xs) + list(arrays.values())
    rows, total_length = arrays["keys_values"].shape[:2]
    any_space = pl.BlockSpec(memory_space=pl.ANY)
    vmem_space = pl.BlockSpec(memory_space=pltpu.VMEM)
    key_blocks = total_length // shards // block_rows

    def kernel(*refs):
        xs_refs, others = refs[: len(xs)], refs[len(xs) : len(values)]
        named = [("xs", xs_refs)] + list(zip(arrays, others))
        backward_kernel(
            [name for name, _ in named],
            entries,
            row_count,
            shards,
            *[ref for _, ref in named],
            *refs[len(values) :],
        )

    low, full = jnp.bfloat16, jnp.float32
    return pl.pallas_call(
        kernel,
        out_shape=[
            jax.ShapeDtypeStruct((x_count * block_rows, g_count * COLS), low)
            for _, x_count, _, g_count, _ in entries
        ]
        + [jax.ShapeDtypeStruct((tokens, width), low)] * 2,
        in_specs=[vmem_space if name in resident else any_space for name in names],
        out_specs=[any_space] * (len(entries) + 2),
        scratch_shapes=[
            pltpu.VMEM((2, COLS, width), low),
            pltpu.VMEM((2, width, COLS), low),
            pltpu.VMEM((2, width, COLS), low),
            pltpu.VMEM((2, 2, tokens, COLS), low),
            pltpu.VMEM((rows, total_length, width), low),
            pltpu.VMEM((rows, shards // 2, 2, key_blocks, block_rows, width), low),
            pltpu.VMEM((rows, key_blocks, block_rows, width), low),
            pltpu.VMEM((tokens, width), low),
            pltpu.VMEM((tokens, width), low),
            pltpu.VMEM((tokens, width), full),
            pltpu.VMEM((rows, total_length, tokens // rows), low),
            pltpu.VMEM((tokens, width), low),
            pltpu.VMEM((tokens, width // 2), low),
            pltpu.VMEM((tokens, width), full),
            pltpu.VMEM((tokens, width), full),
            pltpu.VMEM((tokens, width), full),
            pltpu.VMEM((rows, 8, width), full),
            pltpu.VMEM((rows, 8, width), full),
            pltpu.VMEM((16, COLS), full),
            pltpu.SemaphoreType.DMA((2, 5)),
            pltpu.SemaphoreType.DMA((len(entries) + 10,)),
            pltpu.SemaphoreType.DMA((2,)),
            *exchange_scratch(row_count, shards, block_rows, x_blocks, g_blocks, tokens),
        ],
        compiler_params=pltpu.CompilerParams(
            collective_id=collective_id, has_side_effects=True, vmem_limit_bytes=63 * 2**20
        ),
        cost_estimate=pl.CostEstimate(
            flops=4 * chunks * shards * block_rows * COLS * tokens,
            bytes_accessed=2 * chunks * shards * block_rows * COLS,
            transcendentals=0,
        ),
    )(*values)


def attention_kernel(query_ref, both_ref, mask_ref, out_ref):
    query = two_heads(query_ref[...], True)
    both = both_ref[0]
    allowed = mask_ref[0].astype(jnp.float32)
    weights = jnp.exp(dot_nt(query, both)) * jnp.concatenate([allowed, allowed], axis=0)
    weights = weights * (1.0 / jnp.sum(weights, axis=-1, keepdims=True))
    value = jnp.dot(weights.astype(jnp.bfloat16), both, preferred_element_type=jnp.float32)
    length = out_ref.shape[0]
    first = lanes_below((length, 2 * HEAD_DIM), HEAD_DIM, 2 * HEAD_DIM)
    out_ref[...] = jnp.where(
        first, pltpu.roll(value[:length], HEAD_DIM, 1), value[length:]
    ).astype(out_ref.dtype)


def attention(queries, keys_values, mask):
    rows, total_length, width = keys_values.shape
    length = queries.shape[0] // rows
    lane = 2 * HEAD_DIM
    return pl.pallas_call(
        attention_kernel,
        grid=(rows, width // lane),
        in_specs=[
            pl.BlockSpec((length, lane), lambda r, h: (r, h)),
            pl.BlockSpec((1, total_length, lane), lambda r, h: (r, 0, h)),
            pl.BlockSpec((1, length, total_length), lambda r, h: (r, 0, 0)),
        ],
        out_specs=pl.BlockSpec((length, lane), lambda r, h: (r, h)),
        out_shape=jax.ShapeDtypeStruct(queries.shape, jnp.bfloat16),
        compiler_params=pltpu.CompilerParams(vmem_limit_bytes=32 * 2**20),
        cost_estimate=pl.CostEstimate(
            flops=8 * queries.shape[0] * total_length * width,
            bytes_accessed=4 * keys_values.size,
            transcendentals=2 * queries.shape[0] * total_length * KV_HEADS,
        ),
    )(queries, keys_values, mask)


def fused_body(
    tokens,
    lengths,
    mixer_gain,
    mixer_input,
    mixer_kernel,
    mixer_output,
    first_gain,
    first_gate,
    first_up,
    first_down,
    attend_gain,
    query_weight,
    key_weight,
    value_weight,
    query_gain,
    key_gain,
    attend_output,
    second_gain,
    second_gate,
    second_up,
    second_down,
    cotangent,
):
    full, low = jnp.float32, jnp.bfloat16
    rows, length, width = tokens.shape
    token_count = rows * length
    row_count, shards = lax.axis_size("row"), lax.axis_size("seq")
    seq = lax.axis_index("seq")
    positions = seq * length + jnp.arange(length, dtype=jnp.int32)
    segment, seg_start = segment_info(lengths, positions)
    offsets = positions[None, :] - seg_start

    def flat(value):
        return value.reshape(token_count, -1)

    hidden_zero = tokens.astype(full)
    mixer_in = norm_rows(hidden_zero, mixer_gain.astype(full)).astype(low)
    projected = dense(mixer_in, mixer_input)
    entry, exit_gate, carrier = [
        projected[..., number * width : (number + 1) * width] for number in range(3)
    ]
    product = (entry * carrier).astype(low)
    previous = passed_along(product[:, length - 2 :, :], "seq", 1)
    extended = jnp.concatenate([previous, product], axis=1).astype(full)
    keep_one = (positions[None, :] - 1 >= seg_start).astype(full)[..., None]
    keep_two = (positions[None, :] - 2 >= seg_start).astype(full)[..., None]
    taps = mixer_kernel.astype(full)
    two_back = keep_two * extended[:, :length]
    one_back = keep_one * extended[:, 1 : length + 1]
    current = extended[:, 2:]
    convolved = taps[2] * current + taps[1] * one_back + taps[0] * two_back
    gated = (exit_gate * convolved).astype(low)
    hidden_one = hidden_zero + dense(gated, mixer_output)
    mixer_saved = jnp.concatenate(
        [flat(part).astype(low) for part in (convolved, two_back, one_back, current)]
    )
    projected_saved = jnp.concatenate(
        [flat(part).astype(low) for part in (entry, exit_gate, carrier)]
    )

    def feed(hidden, gain, gate_matrix, up_matrix, down_matrix):
        normed = norm_rows(hidden, gain.astype(full)).astype(low)
        gate_value, upward = dense(normed, gate_matrix), dense(normed, up_matrix)
        active = swiglu(gate_value, upward).astype(low)
        saved = (normed, active, flat(gate_value.astype(low)), flat(upward.astype(low)))
        return hidden + dense(active, down_matrix), saved

    hidden_two, first_saved = feed(hidden_one, first_gain, first_gate, first_up, first_down)

    attend_in = norm_rows(hidden_two, attend_gain.astype(full)).astype(low)
    queries_raw, keys_raw = dense(attend_in, query_weight), dense(attend_in, key_weight)
    values = dense(attend_in, value_weight)

    def head_path(value, heads, gain):
        value = value.reshape(rows, length, heads, HEAD_DIM)
        return rotate(norm_rows(value, gain.astype(full)), offsets)

    queries_low = flat(
        (head_path(queries_raw, HEADS, query_gain).astype(low) * low(HEAD_DIM**-0.5))
    )
    keys_low = head_path(keys_raw, KV_HEADS, key_gain).astype(low)
    values_low = values.astype(low).reshape(keys_low.shape)
    both = jnp.stack([keys_low, values_low], axis=3).reshape(rows, length, width)
    keys_values = lax.all_gather(both, "seq", axis=1, tiled=True)
    total_length = keys_values.shape[1]
    key_positions = jnp.arange(total_length, dtype=jnp.int32)
    key_segment, _ = segment_info(lengths, key_positions)
    allowed = (segment[:, :, None] == key_segment[:, None, :]) & (
        positions[None, :, None] >= key_positions[None, None, :]
    )
    allowed_turned = (segment[:, None, :] == key_segment[:, :, None]) & (
        positions[None, None, :] >= key_positions[None, :, None]
    )
    attended = attention(queries_low, keys_values, allowed.astype(low))
    hidden_three = hidden_two + dense(attended.reshape(tokens.shape), attend_output)

    half = HEAD_DIM // 2
    inverse = THETA ** (-2.0 * jnp.arange(half, dtype=full) / HEAD_DIM)
    angles = offsets.astype(full).reshape(token_count, 1) * inverse
    cosine, sine = jnp.cos(angles), jnp.sin(angles)
    block_rows = math.gcd(width // shards, first_down.shape[0] // shards)

    def turned(inputs):
        inputs = flat(inputs).T
        blocks = inputs.shape[0] // shards // block_rows
        return inputs.reshape(shards // 2, 2, blocks, block_rows, token_count)

    blocks = width // COLS
    shape = (shards, 2 * block_rows, token_count)
    shard_at, row_at, token_at = [lax.broadcasted_iota(jnp.int32, shape, dim) for dim in range(3)]
    wanted = blocks * row_at + jnp.where(row_at < 7, shard_at * blocks // shards, 0)
    picks = ((row_at < 8) & (token_at == wanted)).astype(low)
    picks = picks.reshape(shards // 2, 2, 2, block_rows, token_count)

    def padded(value):
        return jnp.pad(value.astype(full), ((0, 8 - value.shape[0]), (0, 0)))

    lane = 2 * HEAD_DIM
    arrays = dict(
        cotangent=flat(cotangent),
        gate_one=first_saved[2],
        up_one=first_saved[3],
        hidden_three=flat(hidden_three),
        hidden_two=flat(hidden_two),
        hidden_one=flat(hidden_one),
        hidden_zero=flat(hidden_zero),
        queries_low=queries_low,
        keys_values=keys_values,
        mask=allowed_turned.astype(low),
        queries_raw=flat(queries_raw).astype(low),
        keys_raw=flat(keys_raw).astype(low),
        mixer_saved=mixer_saved,
        projected=projected_saved,
        cosine=jnp.concatenate([cosine] * 4, axis=1),
        sine=jnp.concatenate([-sine, sine] * 2, axis=1),
        keep=jnp.broadcast_to(
            jnp.stack([keep_one, keep_two]).reshape(2, token_count, 1), (2, token_count, lane)
        ),
        gains=padded(jnp.stack([second_gain, attend_gain, first_gain, mixer_gain])),
        taps=padded(mixer_kernel),
        head_gains=padded(jnp.tile(jnp.stack([query_gain, key_gain]), (1, 2))),
        second_down=second_down,
        second_gate=second_gate,
        second_up=second_up,
        attend_output=attend_output,
        query_weight=query_weight,
        key_weight=key_weight,
        value_weight=value_weight,
        first_down=first_down,
        first_gate=first_gate,
        first_up=first_up,
        mixer_output=mixer_output,
        mixer_input=mixer_input,
    )
    resident = ("cosine", "sine", "keep", "gains", "taps", "head_gains")
    hidden_columns = first_gate.shape[1]
    head_columns = width + 2 * key_weight.shape[1]
    groups = [
        (width // shards // block_rows, 2 * hidden_columns),
        (hidden_columns // shards // block_rows, width),
        (turned(attended), width),
        (turned(attend_in), head_columns),
        (turned(first_saved[1]), width),
        (turned(first_saved[0]), 2 * hidden_columns),
        (turned(gated), width),
        (turned(mixer_in), 3 * width),
        (picks, COLS),
    ]
    (
        second_both,
        grad_second_down,
        grad_attend_output,
        attend_three,
        grad_first_down,
        first_both,
        grad_mixer_output,
        grad_mixer_input,
        sums,
        token_grad,
        mixed,
    ) = backward(groups, arrays, resident, row_count, shards, 1)

    def single(value):
        return value.astype(full)

    share = width // shards
    vectors = single(
        lax.dynamic_slice(sums, (0, lax.rem(seq, COLS // share) * share), (7, share))
    )
    head_share = HEAD_DIM // shards
    heads = [
        single(lax.dynamic_slice(sums, (7, which * lane + seq * head_share), (1, head_share)))[0]
        for which in range(2)
    ]
    key_columns = key_weight.shape[1]
    return (
        mixed.reshape(tokens.shape),
        token_grad.reshape(tokens.shape),
        vectors[3],
        single(grad_mixer_input),
        vectors[4:7],
        single(grad_mixer_output),
        vectors[2],
        single(first_both[:, :hidden_columns]),
        single(first_both[:, hidden_columns:]),
        single(grad_first_down),
        vectors[1],
        single(attend_three[:, :width]),
        single(attend_three[:, width : width + key_columns]),
        single(attend_three[:, width + key_columns :]),
        heads[0],
        heads[1],
        single(grad_attend_output),
        vectors[0],
        single(second_both[:, :hidden_columns]),
        single(second_both[:, hidden_columns:]),
        single(grad_second_down),
    )


def fused_or_general(*args):
    tokens = args[0]
    rows, length, width = tokens.shape
    row_count, shards = lax.axis_size("row"), lax.axis_size("seq")
    key_bytes = 2 * rows * length * shards * width
    if key_bytes <= 4 * 2**20 and shards == 8 and 4 * rows == shards and row_count == 4:
        return fused_body(*args)
    return body(*args)


def solution(mesh):
    in_specs = (
        P("row", "seq", None),
        P("row", None),
        P(),
        P(),
        P(),
        P(),
        P(),
        P(),
        P(),
        P(),
        P(),
        P(),
        P(),
        P(),
        P(),
        P(),
        P(),
        P(),
        P(),
        P(),
        P(),
        P("row", "seq", None),
    )
    out_specs = (
        P("row", "seq", None),
        P("row", "seq", None),
        P("seq"),
        P("seq", None),
        P(None, "seq"),
        P("seq", None),
        P("seq"),
        P("seq", None),
        P("seq", None),
        P("seq", None),
        P("seq"),
        P("seq", None),
        P("seq", None),
        P("seq", None),
        P("seq"),
        P("seq"),
        P("seq", None),
        P("seq"),
        P("seq", None),
        P("seq", None),
        P("seq", None),
    )
    return jax.shard_map(fused_or_general, mesh=mesh, in_specs=in_specs, out_specs=out_specs, check_vma=False)
```

```python
import functools
import math
import types

import jax
import jax.numpy as jnp
from jax import lax
from jax.experimental import pallas as pl
from jax.experimental.pallas import tpu as pltpu
from jax.sharding import PartitionSpec as P

HEADS = 16
KV_HEADS = 8
HEAD_DIM = 64
GROUP = 2


EPS = 1e-05
THETA = 1000000.0
NEGATIVE = -1e30
HIGHEST = lax.Precision.HIGHEST
MESH = pl.DeviceIdType.MESH
COLS = 512
SLOTS = 4
ZSLOTS = 6


def passed_along(value, axis, steps):
    count = lax.axis_size(axis)
    initial, last = (max(0, -steps), min(count, count - steps))
    return lax.ppermute(value, axis, [(source, source + steps) for source in range(initial, last)])


def segment_info(lengths, positions):
    boundary = jnp.cumsum(lengths, axis=-1)
    passed = boundary[:, None, :] <= positions[None, :, None]
    segment = jnp.sum(passed.astype(jnp.int32), axis=-1)
    seg_start = jnp.max(jnp.where(passed, boundary[:, None, :], 0), axis=-1)
    return (segment, seg_start)


def norm_rows(values, norm_gain):
    return values * lax.rsqrt(jnp.mean(values * values, axis=-1, keepdims=True) + EPS) * norm_gain


def rotate(values, offsets):
    half_dim = values.shape[-1] // 2
    inverse = THETA ** (-2.0 * jnp.arange(half_dim, dtype=jnp.float32) / values.shape[-1])
    angles = offsets.astype(jnp.float32)[:, :, None, None] * inverse
    cosine = jnp.cos(angles)
    sine_table = jnp.sin(angles)
    leading = values[..., :half_dim]
    trailing = values[..., half_dim:]
    return jnp.concatenate(
        [leading * cosine - trailing * sine_table, trailing * cosine + leading * sine_table],
        axis=-1,
    )


def swiglu(gate_value, upward):
    return gate_value / (1.0 + jnp.exp(-gate_value)) * upward


def dense(inputs, matrix):
    return jnp.einsum("rtd,df->rtf", inputs, matrix, preferred_element_type=jnp.float32)


def weight_grad(inputs, gradient):
    return (inputs, gradient)


def back_dense(gradient, matrix):
    return jnp.einsum("rtf,df->rtd", gradient, matrix, preferred_element_type=jnp.float32)


def mixer_block(hidden, norm_gain, input_matrix, kernel, output_matrix, seg_start, positions):
    feature_columns = hidden.shape[-1]
    length = hidden.shape[1]
    normed, norm_back = jax.vjp(norm_rows, hidden, norm_gain.astype(jnp.float32))
    normed_low = normed.astype(jnp.bfloat16)
    projected_rows = dense(normed_low, input_matrix)
    input_gate_value = projected_rows[..., :feature_columns]
    exit_gate = projected_rows[..., feature_columns : 2 * feature_columns]
    carry_value = projected_rows[..., 2 * feature_columns :]
    gated_product_reduced = (input_gate_value * carry_value).astype(jnp.bfloat16)
    previous = passed_along(gated_product_reduced[:, length - 2 :, :], "seq", 1)
    extended = jnp.concatenate([previous, gated_product_reduced], axis=1).astype(jnp.float32)
    keep_one = (positions[None, :] - 1 >= seg_start).astype(jnp.float32)[..., None]
    keep_two = (positions[None, :] - 2 >= seg_start).astype(jnp.float32)[..., None]
    kernel_taps = kernel.astype(jnp.float32)
    two_back = extended[:, :length]
    one_back = extended[:, 1 : length + 1]
    current = extended[:, 2:]
    convolved = (
        kernel_taps[2] * current
        + kernel_taps[1] * keep_one * one_back
        + kernel_taps[0] * keep_two * two_back
    )
    gated_low = (exit_gate * convolved).astype(jnp.bfloat16)
    result = hidden + dense(gated_low, output_matrix)

    def mixer_backward(gradient):
        gradient_low = gradient.astype(jnp.bfloat16)
        grad_output = weight_grad(gated_low, gradient_low)
        grad_gated = back_dense(gradient_low, output_matrix)
        output_gate_gradient = grad_gated * convolved
        grad_conv = grad_gated * exit_gate
        grad_kernel = jnp.stack(
            [
                jnp.sum(grad_conv * keep_two * two_back, axis=(0, 1)),
                jnp.sum(grad_conv * keep_one * one_back, axis=(0, 1)),
                jnp.sum(grad_conv * current, axis=(0, 1)),
            ]
        )
        grad_extended = jnp.pad(kernel_taps[0] * keep_two * grad_conv, ((0, 0), (0, 2), (0, 0)))
        grad_extended = grad_extended + jnp.pad(
            kernel_taps[1] * keep_one * grad_conv, ((0, 0), (1, 1), (0, 0))
        )
        grad_extended = grad_extended + jnp.pad(
            kernel_taps[2] * grad_conv, ((0, 0), (2, 0), (0, 0))
        )
        returned = passed_along(grad_extended[:, :2, :], "seq", -1)
        gated_product_gradient = grad_extended[:, 2:] + jnp.pad(
            returned, ((0, 0), (length - 2, 0), (0, 0))
        )
        grad_projected = jnp.concatenate(
            [
                gated_product_gradient * carry_value,
                output_gate_gradient,
                gated_product_gradient * input_gate_value,
            ],
            axis=-1,
        ).astype(jnp.bfloat16)
        grad_input = weight_grad(normed_low, grad_projected)
        grad_normed = back_dense(grad_projected, input_matrix)
        grad_hidden, grad_gain = norm_back(grad_normed)
        return (gradient + grad_hidden, (grad_gain, grad_input, grad_kernel, grad_output))

    return (result, mixer_backward)


def feed_block(hidden, norm_gain, gate_matrix, up_matrix, down_matrix):
    normed, norm_back = jax.vjp(norm_rows, hidden, norm_gain.astype(jnp.float32))
    normed_low = normed.astype(jnp.bfloat16)
    gate_value = dense(normed_low, gate_matrix)
    upward = dense(normed_low, up_matrix)
    active, active_back = jax.vjp(swiglu, gate_value, upward)
    active_low = active.astype(jnp.bfloat16)
    result = hidden + dense(active_low, down_matrix)

    def feed_backward(gradient):
        gradient_low = gradient.astype(jnp.bfloat16)
        grad_down = weight_grad(active_low, gradient_low)
        grad_gate, grad_upward = active_back(back_dense(gradient_low, down_matrix))
        gate_low = grad_gate.astype(jnp.bfloat16)
        upward_low = grad_upward.astype(jnp.bfloat16)
        grad_normed = back_dense(gate_low, gate_matrix) + back_dense(upward_low, up_matrix)
        grad_hidden, grad_gain = norm_back(grad_normed)
        return (
            gradient + grad_hidden,
            (
                grad_gain,
                weight_grad(normed_low, jnp.concatenate([gate_low, upward_low], axis=-1)),
                grad_down,
            ),
        )

    return (result, feed_backward)


def attend_block(
    hidden,
    lengths,
    norm_gain,
    query_matrix,
    key_matrix,
    value_matrix,
    query_norm,
    key_norm,
    output_matrix,
    segment,
    positions,
    offsets,
):
    row_count, length, feature_columns = hidden.shape
    score_scale = HEAD_DIM ** (-0.5)
    normed, norm_back = jax.vjp(norm_rows, hidden, norm_gain.astype(jnp.float32))
    normed_low = normed.astype(jnp.bfloat16)

    def head_path(projected_rows, head_gain):
        return rotate(norm_rows(projected_rows, head_gain), offsets)

    queries = dense(normed_low, query_matrix).reshape(row_count, length, HEADS, HEAD_DIM)
    keys_raw = dense(normed_low, key_matrix).reshape(row_count, length, KV_HEADS, HEAD_DIM)
    values_raw = dense(normed_low, value_matrix)
    query_rot, query_back = jax.vjp(head_path, queries, query_norm.astype(jnp.float32))
    key_rot, key_back = jax.vjp(head_path, keys_raw, key_norm.astype(jnp.float32))
    query_low = query_rot.astype(jnp.bfloat16).reshape(row_count, length, KV_HEADS, GROUP, HEAD_DIM)
    key_low = key_rot.astype(jnp.bfloat16)
    value_low = values_raw.astype(jnp.bfloat16).reshape(row_count, length, KV_HEADS, HEAD_DIM)
    all_keys, all_values = (
        lax.all_gather(key_low, "seq", axis=1, tiled=True),
        lax.all_gather(value_low, "seq", axis=1, tiled=True),
    )
    total_length = all_keys.shape[1]
    key_block = min(512, total_length)
    block_count = (positions[length - 1] + key_block) // key_block

    def block_scores(number, key_source, value_source):
        first_key = number * key_block
        keys_here = lax.dynamic_slice_in_dim(key_source, first_key, key_block, 1)
        values_here = lax.dynamic_slice_in_dim(value_source, first_key, key_block, 1)
        key_positions = first_key + jnp.arange(key_block, dtype=jnp.int32)
        key_segment, unused = segment_info(lengths, key_positions)
        scores = (
            jnp.einsum(
                "rtkgh,rskh->rkgts", query_low, keys_here, preferred_element_type=jnp.float32
            )
            * score_scale
        )
        allowed = (segment[:, :, None] == key_segment[:, None, :]) & (
            positions[None, :, None] >= key_positions[None, None, :]
        )
        allowed = allowed[:, None, None]
        return (jnp.where(allowed, scores, NEGATIVE), allowed, keys_here, values_here)

    stat_shape = (row_count, KV_HEADS, GROUP, length)

    def stats_step(number, carried):
        peak_score, running_sum = carried
        scores, allowed, unused_keys, unused_values = block_scores(number, all_keys, all_values)
        new_peak = jnp.maximum(peak_score, jnp.max(scores, axis=-1))
        fresh = jnp.sum(jnp.where(allowed, jnp.exp(scores - new_peak[..., None]), 0.0), axis=-1)
        return (new_peak, running_sum * jnp.exp(peak_score - new_peak) + fresh)

    peak_score, running_sum = lax.fori_loop(
        0,
        block_count,
        stats_step,
        (jnp.full(stat_shape, NEGATIVE, jnp.float32), jnp.zeros(stat_shape, jnp.float32)),
    )
    log_total = peak_score + jnp.log(running_sum)

    def probabilities(scores, allowed):
        return jnp.where(allowed, jnp.exp(scores - log_total[..., None]), 0.0)

    out_shape = (row_count, length, KV_HEADS, GROUP, HEAD_DIM)

    def output_step(number, carried):
        rounded, exact_sum = carried
        scores, allowed, keys_here, values_here = block_scores(number, all_keys, all_values)
        weights = probabilities(scores, allowed)
        rounded = rounded + jnp.einsum(
            "rkgts,rskh->rtkgh",
            weights.astype(jnp.bfloat16),
            values_here,
            preferred_element_type=jnp.float32,
        )
        exact_sum = exact_sum + jnp.einsum(
            "rkgts,rskh->rtkgh", weights, values_here.astype(jnp.float32), precision=HIGHEST
        )
        return (rounded, exact_sum)

    rounded, exact_sum = lax.fori_loop(
        0,
        block_count,
        output_step,
        (jnp.zeros(out_shape, jnp.float32), jnp.zeros(out_shape, jnp.float32)),
    )
    attended_low = rounded.reshape(row_count, length, HEADS * HEAD_DIM).astype(jnp.bfloat16)
    result = hidden + dense(attended_low, output_matrix)

    def attend_backward(gradient):
        gradient_low = gradient.astype(jnp.bfloat16)
        grad_output = weight_grad(attended_low, gradient_low)
        grad_attended = (
            back_dense(gradient_low, output_matrix).astype(jnp.bfloat16).reshape(out_shape)
        )
        row_delta = jnp.einsum(
            "rtkgh,rtkgh->rkgt", grad_attended.astype(jnp.float32), exact_sum, precision=HIGHEST
        )
        key_source, value_source = (all_keys, all_values)

        def grad_step(number, carried):
            grad_query, grad_keys, grad_values = carried
            scores, allowed, keys_here, values_here = block_scores(number, key_source, value_source)
            weights = probabilities(scores, allowed)
            grad_weights = jnp.einsum(
                "rtkgh,rskh->rkgts", grad_attended, values_here, preferred_element_type=jnp.float32
            )
            grad_scores = (weights * (grad_weights - row_delta[..., None])).astype(jnp.bfloat16)
            grad_query = (
                grad_query
                + jnp.einsum(
                    "rkgts,rskh->rtkgh", grad_scores, keys_here, preferred_element_type=jnp.float32
                )
                * score_scale
            )
            key_part = (
                jnp.einsum(
                    "rkgts,rtkgh->rskh", grad_scores, query_low, preferred_element_type=jnp.float32
                )
                * score_scale
            )
            value_part = jnp.einsum(
                "rkgts,rtkgh->rskh",
                weights.astype(jnp.bfloat16),
                grad_attended,
                preferred_element_type=jnp.float32,
            )
            grad_keys = lax.dynamic_update_slice_in_dim(grad_keys, key_part, number * key_block, 1)
            grad_values = lax.dynamic_update_slice_in_dim(
                grad_values, value_part, number * key_block, 1
            )
            return (grad_query, grad_keys, grad_values)

        key_shape = (row_count, total_length, KV_HEADS, HEAD_DIM)
        grad_query, grad_keys, grad_values = lax.fori_loop(
            0,
            block_count,
            grad_step,
            (
                jnp.zeros(out_shape, jnp.float32),
                jnp.zeros(key_shape, jnp.float32),
                jnp.zeros(key_shape, jnp.float32),
            ),
        )
        local_keys, local_values = (
            lax.psum_scatter(
                grad_keys.astype(jnp.bfloat16), "seq", scatter_dimension=1, tiled=True
            ).astype(jnp.float32),
            lax.psum_scatter(
                grad_values.astype(jnp.bfloat16), "seq", scatter_dimension=1, tiled=True
            ).astype(jnp.float32),
        )
        grad_queries, grad_query_norm = query_back(
            grad_query.reshape(row_count, length, HEADS, HEAD_DIM)
        )
        grad_keys_raw, grad_key_norm = key_back(local_keys)
        query_grad_low = grad_queries.reshape(row_count, length, HEADS * HEAD_DIM).astype(
            jnp.bfloat16
        )
        key_grad_low = grad_keys_raw.reshape(row_count, length, KV_HEADS * HEAD_DIM).astype(
            jnp.bfloat16
        )
        value_grad_low = local_values.reshape(row_count, length, KV_HEADS * HEAD_DIM).astype(
            jnp.bfloat16
        )
        grad_normed = (
            back_dense(query_grad_low, query_matrix)
            + back_dense(key_grad_low, key_matrix)
            + back_dense(value_grad_low, value_matrix)
        )
        grad_hidden, grad_gain = norm_back(grad_normed)
        return (
            gradient + grad_hidden,
            (
                grad_gain,
                weight_grad(
                    normed_low,
                    jnp.concatenate([query_grad_low, key_grad_low, value_grad_low], axis=-1),
                ),
                grad_query_norm,
                grad_key_norm,
                grad_output,
            ),
        )

    return (result, attend_backward)


def reduce_entries(pairs):
    entries = []
    x_first = g_first = chunk = 0
    for x_count, g_count in pairs:
        entries.append((x_first, x_count, g_first, g_count, chunk))
        x_first += x_count
        g_first += g_count
        chunk += x_count * g_count
    return entries, x_first, g_first, chunk


def locate(entries, q):
    x_block, g_block = jnp.int32(0), jnp.int32(0)
    for x_first, x_count, g_first, g_count, chunk in entries:
        here = q - chunk
        inside = here >= 0
        x_block = jnp.where(inside, x_first + lax.rem(jnp.maximum(here, 0), x_count), x_block)
        g_block = jnp.where(inside, g_first + jnp.maximum(here, 0) // x_count, g_block)
    return x_block, g_block


def seq_steps(bits):
    upper = list(range(1, bits))
    middle = (len(upper) + 1) // 2
    kinds = []
    for order in (upper, upper[middle:] + upper[:middle]):
        held = sorted(upper, reverse=True)
        steps = []
        for bit in order:
            place = held.index(bit)
            steps.append((bit, 2**place, 2 ** (len(held) - 1 - place)))
            held.remove(bit)
        kinds.append(steps)
    return kinds


def exchange_scratch(row_count, shards, block_rows, x_blocks, g_blocks, tokens):
    bits = shards.bit_length() - 1
    block = (block_rows, COLS)
    comm = []
    for steps in seq_steps(bits):
        for _, above, below in steps:
            comm.append(pltpu.VMEM((2, above, 2, below) + block, jnp.bfloat16))
            comm.append(pltpu.VMEM((SLOTS, above, below) + block, jnp.bfloat16))
    z_steps = row_count - 1
    return [
        pltpu.VMEM((shards // 2, 2, x_blocks, block_rows, tokens), jnp.bfloat16),
        pltpu.VMEM((tokens, g_blocks * COLS), jnp.bfloat16),
        pltpu.VMEM((2, 2, shards // 2) + block, jnp.bfloat16),
        pltpu.VMEM((2, SLOTS, shards // 2) + block, jnp.bfloat16),
        *comm,
        *[pltpu.VMEM((2, ZSLOTS) + block, jnp.bfloat16) for _ in range(5)],
        pltpu.SemaphoreType.DMA((2, bits, SLOTS)),
        pltpu.SemaphoreType.DMA((2, bits, SLOTS)),
        pltpu.SemaphoreType.DMA((2, z_steps, ZSLOTS)),
        pltpu.SemaphoreType.DMA((2, z_steps, ZSLOTS)),
        pltpu.SemaphoreType.DMA((2, ZSLOTS)),
    ]


class Exchange:
    def __init__(self, entries, row_count, shards, outs, scratch, locals_at=(), local=None):
        self.entries, self.outs = entries, outs
        self.locals_at, self.local = locals_at, local
        self.bits = bits = shards.bit_length() - 1
        self.kinds = seq_steps(bits)
        (self.x_all, self.g_all, self.send_zero, self.recv_zero, *rest) = scratch
        self.held, self.received = [[], []], [[], []]
        for kind in range(2):
            for _ in self.kinds[kind]:
                self.held[kind].append(rest.pop(0))
                self.received[kind].append(rest.pop(0))
        self.z_own, self.z_in, self.z_part, self.z_cross, self.z_total = rest[:5]
        self.seq_send, self.seq_recv, self.z_send, self.z_recv, self.out_sem = rest[5:]
        self.row, self.seq = lax.axis_index("row"), lax.axis_index("seq")
        self.row_count, self.shards = row_count, shards
        self.value = [lax.rem(self.seq // (1 << bit), 2) for bit in range(bits)]
        self.partner = [self.seq + (1 << bit) * (1 - 2 * self.value[bit]) for bit in range(bits)]
        last = entries[-1]
        self.pairs = (last[4] + last[1] * last[3]) // 2 + len(locals_at)
        half = row_count // 2
        self.depth = half - 1
        lower = self.row < half
        self.level = jnp.where(lower, self.row, row_count - 1 - self.row)
        self.toward = jnp.where(lower, self.row + 1, self.row - 1)
        self.away = jnp.where(lower, self.row - 1, self.row + 1)

    def meet(self):
        barrier = pltpu.get_barrier_semaphore()
        others = [(self.row, partner) for partner in self.partner]
        for step in (1, self.row_count - 1):
            others.append((lax.rem(self.row + step, self.row_count), self.seq))
        for step in (1, self.shards - 1):
            others.append((self.row, lax.rem(self.seq + step, self.shards)))
        for other in others:
            pl.semaphore_signal(barrier, inc=1, device_id=other, device_id_type=MESH)
        pl.semaphore_wait(barrier, len(others))

    def is_local(self, index):
        found = index < 0
        for at in self.locals_at:
            found = jnp.logical_or(found, index == at)
        return found

    def chunk(self, kind, index):
        before = sum([jnp.where(index > at, 1, 0) for at in self.locals_at], 0)
        return 2 * (index - before) + kind

    def product(self, kind, index, side):
        x_block, g_block = locate(self.entries, self.chunk(kind, index))
        left = self.x_all[:, side, x_block]
        columns = pl.ds(pl.multiple_of(g_block * COLS, COLS), COLS)
        return jnp.dot(
            left.reshape(left.shape[0] * left.shape[1], left.shape[2]),
            self.g_all[:, columns],
            preferred_element_type=jnp.float32,
        )

    def seq_copy(self, kind, step, slot):
        if step == 0:
            bit = 0
            source = self.send_zero.at[kind, lax.rem(slot, 2)]
            target = self.recv_zero.at[kind, slot]
        else:
            bit = self.kinds[kind][step - 1][0]
            source = self.held[kind][step - 1].at[lax.rem(slot, 2), :, 1 - self.value[bit]]
            target = self.received[kind][step - 1].at[slot]
        return pltpu.make_async_remote_copy(
            src_ref=source,
            dst_ref=target,
            send_sem=self.seq_send.at[kind, step, slot],
            recv_sem=self.seq_recv.at[kind, step, slot],
            device_id=(self.row, self.partner[bit]),
            device_id_type=MESH,
        )

    def seq_sum(self, kind, step, slot):
        bit = self.kinds[kind][step - 2][0]
        mine = self.held[kind][step - 2][lax.rem(slot, 2), :, self.value[bit]].astype(jnp.float32)
        return mine + self.received[kind][step - 2][slot].astype(jnp.float32)

    def z_copy(self, kind, step, slot):
        if step < self.depth:
            source = self.z_own if step == 0 else self.z_part
            target, where = self.z_in, self.toward
        elif step == self.depth:
            source = self.z_own if self.depth == 0 else self.z_part
            target, where = self.z_cross, self.toward
        else:
            source, target, where = self.z_total, self.z_total, self.away
        return pltpu.make_async_remote_copy(
            src_ref=source.at[kind, slot],
            dst_ref=target.at[kind, slot],
            send_sem=self.z_send.at[kind, step, slot],
            recv_sem=self.z_recv.at[kind, step, slot],
            device_id=(where, self.seq),
            device_id_type=MESH,
        )

    def start_out(self, kind, slot, index):
        q = self.chunk(kind, index)
        rows = self.z_total.shape[2]
        for out, (_, x_count, _, g_count, chunk) in zip(self.outs, self.entries):
            here = q - chunk

            @pl.when(jnp.logical_and(here >= 0, here < x_count * g_count))
            def _():
                row_at = pl.multiple_of(lax.rem(here, x_count) * rows, rows)
                column_at = pl.multiple_of(here // x_count * COLS, COLS)
                pltpu.make_async_copy(
                    self.z_total.at[kind, slot],
                    out.at[pl.ds(row_at, rows), pl.ds(column_at, COLS)],
                    self.out_sem.at[kind, slot],
                ).start()

    def first(self, kind, index):
        slot = lax.rem(index, SLOTS)
        target = self.send_zero

        def put():
            target[kind, lax.rem(slot, 2)] = (
                self.product(kind, index, 1 - self.value[0])
                .astype(jnp.bfloat16)
                .reshape(target.shape[2:])
            )

        if self.local is None:
            put()
        else:
            pl.when(jnp.logical_not(self.is_local(index)))(put)

            @pl.when(self.is_local(index))
            def _():
                target[kind, lax.rem(slot, 2)] = self.local.part(kind, index, 1 - self.value[0])

        self.seq_copy(kind, 0, slot).start()

    def second(self, kind, index):
        slot = lax.rem(index, SLOTS)
        self.seq_copy(kind, 0, slot).wait()
        target = self.held[kind][0]

        def put():
            mine = self.product(kind, index, self.value[0])
            total = mine + self.recv_zero[kind, slot].astype(jnp.float32).reshape(mine.shape)
            target[lax.rem(slot, 2)] = total.astype(jnp.bfloat16).reshape(target.shape[1:])

        if self.local is None:
            put()
        else:
            pl.when(jnp.logical_not(self.is_local(index)))(put)

            @pl.when(self.is_local(index))
            def _():
                mine = self.local.part(kind, index, self.value[0]).astype(jnp.float32)
                total = mine + self.recv_zero[kind, slot].astype(jnp.float32)
                target[lax.rem(slot, 2)] = total.astype(jnp.bfloat16).reshape(target.shape[1:])

        self.seq_copy(kind, 1, slot).start()

    def middle(self, step):
        def run(kind, index):
            slot = lax.rem(index, SLOTS)
            self.seq_copy(kind, step - 1, slot).wait()
            total = self.seq_sum(kind, step, slot)
            target = self.held[kind][step - 1]
            target[lax.rem(slot, 2)] = total.astype(jnp.bfloat16).reshape(target.shape[1:])
            self.seq_copy(kind, step, slot).start()

        return run

    def last(self, kind, index):
        slot, z_slot = lax.rem(index, SLOTS), lax.rem(index, ZSLOTS)
        self.seq_copy(kind, self.bits - 1, slot).wait()
        total = self.seq_sum(kind, self.bits, slot).reshape(self.z_own.shape[2:])

        def put():
            self.z_own[kind, z_slot] = total.astype(jnp.bfloat16)

            @pl.when(self.level == 0)
            def _():
                self.z_copy(kind, 0, z_slot).start()

        if self.local is None:
            put()
        else:
            pl.when(jnp.logical_not(self.is_local(index)))(put)

            @pl.when(self.is_local(index))
            def _():
                self.local.take(kind, index, total)

    def z_stage(self, step):
        level, depth = self.level, self.depth

        def run(kind, index):
            slot = lax.rem(index, ZSLOTS)
            if step <= depth:

                @pl.when(level == step)
                def _():
                    self.z_copy(kind, step - 1, slot).wait_recv()
                    self.z_part[kind, slot] = (
                        self.z_own[kind, slot].astype(jnp.float32)
                        + self.z_in[kind, slot].astype(jnp.float32)
                    ).astype(jnp.bfloat16)
                    self.z_copy(kind, step, slot).start()

                @pl.when(level == step - 1)
                def _():
                    self.z_copy(kind, step - 1, slot).wait_send()

            elif step == depth + 1:

                @pl.when(level == depth)
                def _():
                    self.z_copy(kind, depth, slot).wait()
                    own = self.z_own if depth == 0 else self.z_part
                    self.z_total[kind, slot] = (
                        own[kind, slot].astype(jnp.float32)
                        + self.z_cross[kind, slot].astype(jnp.float32)
                    ).astype(jnp.bfloat16)
                    if depth > 0:
                        self.z_copy(kind, step, slot).start()
                    self.start_out(kind, slot, index)

            else:
                receiver = 2 * depth + 1 - step

                @pl.when(level == receiver)
                def _():
                    self.z_copy(kind, step - 1, slot).wait_recv()
                    if receiver > 0:
                        self.z_copy(kind, step, slot).start()
                    self.start_out(kind, slot, index)

                @pl.when(level == receiver + 1)
                def _():
                    self.z_copy(kind, step - 1, slot).wait_send()

        return run

    def finish(self, kind, index):
        slot = lax.rem(index, ZSLOTS)
        rows = self.z_total.shape[2]
        pltpu.make_async_copy(
            self.z_total.at[kind, slot],
            self.outs[0].at[pl.ds(0, rows), pl.ds(0, COLS)],
            self.out_sem.at[kind, slot],
        ).wait()

    def run(self, task):
        stages = [(self.first, False), (self.second, False)]
        stages += [(self.middle(step), False) for step in range(2, self.bits)]
        stages += [(self.last, False)]
        stages += [(self.z_stage(step), True) for step in range(1, 2 * self.depth + 2)]
        stages += [(self.finish, True)]

        def iteration(i, carried):
            for at, (stage, summed_only) in enumerate(stages):
                index = i - at
                here = jnp.logical_and(index >= 0, index < self.pairs)
                if summed_only and self.locals_at:
                    here = jnp.logical_and(here, jnp.logical_not(self.is_local(index)))

                @pl.when(here)
                def _():
                    for kind in range(2):
                        stage(kind, index)

            if task is not None:
                task(i)
            return carried

        lax.fori_loop(0, self.pairs + len(stages) - 1, iteration, 0)


def reduce_kernel(entries, row_count, shards, *refs):
    count = len(entries)
    xs, gs, outs = refs[:count], refs[count : 2 * count], refs[2 * count : 3 * count]
    load_x, load_g, *scratch = refs[3 * count :]
    exchange = Exchange(entries, row_count, shards, outs, scratch)
    copies = []
    for at, (x_first, x_count, g_first, g_count, _) in enumerate(entries):
        x_part = exchange.x_all.at[:, :, pl.ds(x_first, x_count)]
        g_part = exchange.g_all.at[:, pl.ds(g_first * COLS, g_count * COLS)]
        copies.append(pltpu.make_async_copy(xs[at], x_part, load_x.at[at]))
        copies.append(pltpu.make_async_copy(gs[at], g_part, load_g.at[at]))
    for copy in copies:
        copy.start()
    exchange.meet()
    for copy in copies:
        copy.wait()
    exchange.run(None)


def reduce_gradients(pairs, row_count, shards, collective_id):
    block_rows, tokens = pairs[0][0].shape[3:]
    entries, x_blocks, g_blocks, chunks = reduce_entries(
        [(x.shape[2], g.shape[1] // COLS) for x, g in pairs]
    )
    return pl.pallas_call(
        functools.partial(reduce_kernel, entries, row_count, shards),
        out_shape=[
            jax.ShapeDtypeStruct((x_count * block_rows, g_count * COLS), jnp.bfloat16)
            for _, x_count, _, g_count, _ in entries
        ],
        in_specs=[pl.BlockSpec(memory_space=pl.ANY)] * (2 * len(pairs)),
        out_specs=[pl.BlockSpec(memory_space=pl.ANY)] * len(pairs),
        scratch_shapes=[
            pltpu.SemaphoreType.DMA((len(pairs),)),
            pltpu.SemaphoreType.DMA((len(pairs),)),
            *exchange_scratch(row_count, shards, block_rows, x_blocks, g_blocks, tokens),
        ],
        compiler_params=pltpu.CompilerParams(
            collective_id=collective_id, has_side_effects=True, vmem_limit_bytes=52 * 2**20
        ),
        cost_estimate=pl.CostEstimate(
            flops=2 * chunks * shards * block_rows * COLS * tokens,
            bytes_accessed=2 * chunks * block_rows * COLS,
            transcendentals=0,
        ),
    )(*[x for x, _ in pairs], *[g for _, g in pairs])


def body(
    tokens,
    lengths,
    mixer_gain,
    mixer_input,
    mixer_kernel,
    mixer_output,
    first_gain,
    first_gate,
    first_up,
    first_down,
    attend_gain,
    query_weight,
    key_weight,
    value_weight,
    query_gain,
    key_gain,
    attend_output,
    second_gain,
    second_gate,
    second_up,
    second_down,
    cotangent,
):
    length = tokens.shape[1]
    positions = lax.axis_index("seq") * length + jnp.arange(length, dtype=jnp.int32)
    segment, seg_start = segment_info(lengths, positions)
    offsets = positions[None, :] - seg_start
    hidden = tokens.astype(jnp.float32)
    hidden, mixer_back = mixer_block(
        hidden, mixer_gain, mixer_input, mixer_kernel, mixer_output, seg_start, positions
    )
    hidden, first_back = feed_block(hidden, first_gain, first_gate, first_up, first_down)
    hidden, attend_back = attend_block(
        hidden,
        lengths,
        attend_gain,
        query_weight,
        key_weight,
        value_weight,
        query_gain,
        key_gain,
        attend_output,
        segment,
        positions,
        offsets,
    )
    hidden, second_back = feed_block(hidden, second_gain, second_gate, second_up, second_down)
    gradient = cotangent.astype(jnp.float32)
    gradient, second_grads = second_back(gradient)
    gradient, attend_grads = attend_back(gradient)
    gradient, first_grads = first_back(gradient)
    gradient, mixer_grads = mixer_back(gradient)
    second_gain_sum, second_wide, second_down_pair = second_grads
    attend_gain_sum, attend_wide, query_gain_sum, key_gain_sum, attend_output_pair = attend_grads
    first_gain_sum, first_wide, first_down_pair = first_grads
    mixer_gain_sum, mixer_input_pair, mixer_kernel_sum, mixer_output_pair = mixer_grads
    row_count, shards = lax.axis_size("row"), lax.axis_size("seq")
    block_rows = math.gcd(tokens.shape[2] // shards, first_down.shape[0] // shards)

    def operands(pair):
        inputs, gradient_low = pair
        token_count = inputs.shape[0] * inputs.shape[1]
        inputs = inputs.reshape(token_count, -1).T
        blocks = inputs.shape[0] // shards // block_rows
        return (
            inputs.reshape(shards // 2, 2, blocks, block_rows, token_count),
            gradient_low.reshape(token_count, -1),
        )

    wide_vectors = jnp.concatenate(
        [
            mixer_kernel_sum,
            jnp.stack([mixer_gain_sum, first_gain_sum, attend_gain_sum, second_gain_sum]),
        ]
    )
    vector_count = wide_vectors.shape[0]
    vectors = jnp.concatenate(
        [
            part.reshape(-1, shards, part.shape[-1] // shards)
            .transpose(1, 0, 2)
            .reshape(shards, -1)
            for part in (wide_vectors, jnp.stack([query_gain_sum, key_gain_sum]))
        ],
        axis=1,
    )
    vector_rows = -(-vectors.shape[1] // COLS)
    token_count = tokens.shape[0] * tokens.shape[1]
    vectors = jnp.pad(vectors, ((0, 0), (0, vector_rows * COLS - vectors.shape[1])))
    vectors = vectors.reshape(shards * vector_rows, COLS).astype(jnp.bfloat16)
    vectors = jnp.pad(vectors, ((0, token_count - shards * vector_rows), (0, 0)))
    shard_at = lax.broadcasted_iota(jnp.int32, (shards, 2 * block_rows, token_count), 0)
    row_at = lax.broadcasted_iota(jnp.int32, (shards, 2 * block_rows, token_count), 1)
    token_at = lax.broadcasted_iota(jnp.int32, (shards, 2 * block_rows, token_count), 2)
    picks = (row_at < vector_rows) & (token_at == shard_at * vector_rows + row_at)
    picks = picks.astype(jnp.bfloat16).reshape(shards // 2, 2, 2, block_rows, token_count)
    (
        grad_second_down,
        second_both,
        grad_attend_output,
        attend_three,
        grad_first_down,
        first_both,
        grad_mixer_output,
        grad_mixer_input,
        vector_sums,
    ) = reduce_gradients(
        [
            operands(second_down_pair),
            operands(second_wide),
            operands(attend_output_pair),
            operands(attend_wide),
            operands(first_down_pair),
            operands(first_wide),
            operands(mixer_output_pair),
            operands(mixer_input_pair),
            (picks, vectors),
        ],
        row_count,
        shards,
        0,
    )

    def single(value):
        return value.astype(jnp.float32)

    hidden_columns = first_gate.shape[1]
    query_columns, key_columns = query_weight.shape[1], key_weight.shape[1]
    vector_sums = single(vector_sums[:vector_rows]).reshape(-1)
    width = tokens.shape[2] // shards
    wide_sums = vector_sums[: vector_count * width].reshape(vector_count, width)
    head_width = HEAD_DIM // shards
    head_sums = vector_sums[vector_count * width :][: 2 * head_width].reshape(2, head_width)
    return (
        hidden.astype(jnp.bfloat16),
        gradient.astype(jnp.bfloat16),
        wide_sums[3],
        single(grad_mixer_input),
        wide_sums[:3],
        single(grad_mixer_output),
        wide_sums[4],
        single(first_both[:, :hidden_columns]),
        single(first_both[:, hidden_columns:]),
        single(grad_first_down),
        wide_sums[5],
        single(attend_three[:, :query_columns]),
        single(attend_three[:, query_columns : query_columns + key_columns]),
        single(attend_three[:, query_columns + key_columns :]),
        head_sums[0],
        head_sums[1],
        single(grad_attend_output),
        wide_sums[6],
        single(second_both[:, :hidden_columns]),
        single(second_both[:, hidden_columns:]),
        single(grad_second_down),
    )


def dot_nt(left, right):
    return lax.dot_general(
        left, right, (((1,), (1,)), ((), ())), preferred_element_type=jnp.float32
    )


def dot_tn(left, right):
    return lax.dot_general(
        left, right, (((0,), (0,)), ((), ())), preferred_element_type=jnp.float32
    )


def lanes_below(shape, bound, period):
    return lax.rem(lax.broadcasted_iota(jnp.int32, shape, len(shape) - 1), period) < bound


def two_heads(pair, low):
    pair = pair.astype(jnp.float32)
    turned = pltpu.roll(pair, HEAD_DIM, 1)
    first = lanes_below(pair.shape, HEAD_DIM, 2 * HEAD_DIM)
    if low:
        parts = [jnp.where(first, pair, 0.0), jnp.where(first, turned, 0.0)]
    else:
        parts = [jnp.where(first, 0.0, turned), jnp.where(first, 0.0, pair)]
    return jnp.concatenate(parts, axis=0).astype(jnp.bfloat16)


def head_tools(lane):
    head_of = lax.broadcasted_iota(jnp.int32, (lane, lane), 0) // HEAD_DIM
    ones = head_of == lax.broadcasted_iota(jnp.int32, (lane, lane), 1) // HEAD_DIM
    ones = ones.astype(jnp.float32).astype(jnp.bfloat16)

    def head_mean(value):
        total = jnp.dot(value.astype(jnp.bfloat16), ones, preferred_element_type=jnp.float32)
        return total * (1.0 / HEAD_DIM)

    def turn(value):
        half = HEAD_DIM // 2
        first = lanes_below(value.shape, half, HEAD_DIM)
        return jnp.where(first, pltpu.roll(value, lane - half, 1), pltpu.roll(value, half, 1))

    return head_mean, turn


def forward_kernel(names, out_names, scratch_names, shards, *refs):
    at = types.SimpleNamespace(**dict(zip(names + out_names + scratch_names, refs)))
    row, seq = lax.axis_index("row"), lax.axis_index("seq")
    tokens, width = at.low_one.shape
    rows, total_length = at.both.shape[:2]
    length = tokens // rows
    lane = 2 * HEAD_DIM
    blocks = width // COLS
    hidden_blocks = at.first_gate.shape[1] // COLS
    bits = [lax.rem(seq // (1 << bit), 2) for bit in range(3)]
    partner = [seq + (1 << bit) * (1 - 2 * bits[bit]) for bit in range(3)]
    head_mean, turn = head_tools(lane)

    def tile_copies(step, slot):
        name, j = step
        b, c = at.tiles_b.at[slot], at.tiles_c.at[slot]

        def columns(block):
            return pl.ds(block * COLS if isinstance(block, int) else pl.multiple_of(block * COLS, COLS), COLS)

        if name == "mixer_input":
            first, second = ((0, 4), (1, 5), (2, 3))[j]
            moves = [
                (at.mixer_input.at[:, columns(first)], b),
                (at.mixer_input.at[:, columns(second)], c),
            ]
        elif name == "keys":
            moves = [(at.key_weight, b), (at.value_weight, c)]
        elif name == "first":
            moves = [
                (at.first_gate.at[:, columns(j)], b),
                (at.first_up.at[:, columns(j)], c),
                (at.first_down.at[columns(j)], at.tiles_a.at[slot]),
            ]
        else:
            matrix = {
                "mixer_output": at.mixer_output,
                "queries": at.query_weight,
                "attend_output": at.attend_output,
            }[name]
            moves = [(matrix.at[:, columns(0)], b), (matrix.at[:, columns(1)], c)]
        return [
            pltpu.make_async_copy(source, target, at.tile_sem.at[slot, place])
            for place, (source, target) in enumerate(moves)
        ]

    steps = [("mixer_input", 0), ("mixer_input", 1), ("mixer_input", 2), ("mixer_output", 0)]
    first_at = len(steps)
    steps += [("first", j) for j in range(hidden_blocks)]
    steps += [("keys", 0), ("queries", 0), ("attend_output", 0)]

    def begin(number):
        for copy in tile_copies(steps[number], number % 2):
            copy.wait()
        if number + 1 < len(steps):
            for copy in tile_copies(steps[number + 1], (number + 1) % 2):
                copy.start()
        return number % 2

    saves = []

    def save(source, target):
        copy = pltpu.make_async_copy(source, target, at.save_sem.at[len(saves)])
        copy.start()
        saves.append(copy)

    def normed(hidden, number, target):
        for first in range(0, tokens, 64):
            span = pl.ds(first, 64)
            value = hidden[span]
            inverse = lax.rsqrt(jnp.mean(value * value, axis=-1, keepdims=True) + EPS)
            value = value * inverse * at.vectors[number : number + 1, :]
            target[span] = value.astype(jnp.bfloat16)

    def times(left, tile):
        return jnp.dot(left[...], tile, preferred_element_type=jnp.float32)

    for copy in tile_copies(steps[0], 0):
        copy.start()
    token_load = pltpu.make_async_copy(at.tokens, at.attended, at.load_sem.at[0])
    token_load.start()
    at.halo_in[...] = jnp.zeros_like(at.halo_in)
    barrier = pltpu.get_barrier_semaphore()
    others = partner + [lax.rem(seq + step, shards) for step in (1, shards - 1)]
    for other in others:
        pl.semaphore_signal(barrier, inc=1, device_id=(row, other), device_id_type=MESH)
    token_load.wait()
    at.hidden_a[...] = at.attended[...].astype(jnp.float32)
    save(at.hidden_a, at.hidden_zero)
    normed(at.hidden_a, 3, at.low_one)
    pl.semaphore_wait(barrier, len(others))

    for number, (first, second) in enumerate(((0, 4), (1, 5))):
        slot = begin(number)
        entry = times(at.low_one, at.tiles_b[slot])
        carrier = times(at.low_one, at.tiles_c[slot])
        columns = pl.ds(number * COLS, COLS)
        product = (entry * carrier).astype(jnp.bfloat16)
        at.mixed_low[pl.ds(3 * tokens, tokens), columns] = product
        product = product.astype(jnp.float32)
        at.gates_low[pl.ds(0, tokens), columns] = entry.astype(jnp.bfloat16)
        at.gates_low[pl.ds(2 * tokens, tokens), columns] = carrier.astype(jnp.bfloat16)
        for which in range(rows):
            last = product[(which + 1) * length - 8 : (which + 1) * length]
            at.halo_out[which, :, columns] = last
    halo = pltpu.make_async_remote_copy(
        src_ref=at.halo_out,
        dst_ref=at.halo_in,
        send_sem=at.halo_sem.at[0],
        recv_sem=at.halo_sem.at[1],
        device_id=(row, jnp.minimum(seq + 1, shards - 1)),
        device_id_type=MESH,
    )

    @pl.when(seq < shards - 1)
    def _():
        halo.start()

    slot = begin(2)
    for block, tile in enumerate((at.tiles_b, at.tiles_c)):
        at.work[:, pl.ds(block * COLS, COLS)] = times(at.low_one, tile[slot])

    @pl.when(seq > 0)
    def _():
        halo.wait_recv()

    @pl.when(seq < shards - 1)
    def _():
        halo.wait_send()

    position = lax.rem(lax.broadcasted_iota(jnp.int32, (tokens, lane), 0), length) + seq * length
    keep_one = position - 1 >= at.seg_start[...]
    keep_two = position - 2 >= at.seg_start[...]
    edge = lax.broadcasted_iota(jnp.int32, (8, lane), 0)
    for part_at in range(0, width, lane):
        columns = pl.ds(part_at, lane)
        current = at.mixed_low[pl.ds(3 * tokens, tokens), columns].astype(jnp.float32)
        shifted = []
        for steps_back, keep in ((1, keep_one), (2, keep_two)):
            back = pltpu.roll(current, steps_back, 0)
            pieces = []
            for which in range(rows):
                before = pltpu.roll(at.halo_in[which, :, columns], steps_back, 0)
                start = which * length
                pieces.append(jnp.where(edge < steps_back, before, back[start : start + 8]))
                pieces.append(back[start + 8 : start + length])
            back = jnp.concatenate(pieces, axis=0)
            shifted.append(jnp.where(keep, back, 0.0))
        one, two = shifted
        convolved = at.vectors[6:7, columns] * current + at.vectors[5:6, columns] * one
        convolved += at.vectors[4:5, columns] * two
        exit_gate = at.work[:, columns]
        at.mixed_low[pl.ds(0, tokens), columns] = convolved.astype(jnp.bfloat16)
        at.mixed_low[pl.ds(tokens, tokens), columns] = two.astype(jnp.bfloat16)
        at.mixed_low[pl.ds(2 * tokens, tokens), columns] = one.astype(jnp.bfloat16)
        at.gates_low[pl.ds(tokens, tokens), columns] = exit_gate.astype(jnp.bfloat16)
        at.low_two[:, columns] = (exit_gate * convolved).astype(jnp.bfloat16)
    save(at.mixed_low, at.mixer_saved)
    save(at.gates_low, at.projected)

    def add_output(number, left, before, after):
        slot = begin(number)
        for block, tile in enumerate((at.tiles_b, at.tiles_c)):
            columns = pl.ds(block * COLS, COLS)
            after[:, columns] = before[:, columns] + times(left, tile[slot])

    add_output(3, at.low_two, at.hidden_a, at.hidden_b)
    save(at.hidden_b, at.hidden_one)
    normed(at.hidden_b, 2, at.low_three)
    at.hidden_c[...] = at.hidden_b[...]

    def feed_tile(j, carried):
        slot = lax.rem(first_at + j, 2)
        for copy in tile_copies(("first", j), slot):
            copy.wait()

        @pl.when(j + 1 < hidden_blocks)
        def _():
            for copy in tile_copies(("first", j + 1), 1 - slot):
                copy.start()

        @pl.when(j + 1 == hidden_blocks)
        def _():
            for copy in tile_copies(("keys", 0), 1 - slot):
                copy.start()

        gate_value = times(at.low_three, at.tiles_b[slot])
        up_value = times(at.low_three, at.tiles_c[slot])
        columns = pl.ds(pl.multiple_of(j * COLS, COLS), COLS)
        at.gate_low[:, columns] = gate_value.astype(jnp.bfloat16)
        at.up_low[:, columns] = up_value.astype(jnp.bfloat16)
        active = gate_value / (1.0 + jnp.exp(-gate_value)) * up_value
        active = active.astype(jnp.bfloat16)
        at.active_low[:, columns] = active
        at.hidden_c[...] += jnp.dot(
            active, at.tiles_a[slot], preferred_element_type=jnp.float32
        )
        return carried

    lax.fori_loop(0, hidden_blocks, feed_tile, 0)
    save(at.hidden_c, at.hidden_two)
    save(at.gate_low, at.gate_one)
    save(at.up_low, at.up_one)
    normed(at.hidden_c, 1, at.low_four)

    def head_path(raw, gain):
        value = raw * lax.rsqrt(head_mean(raw * raw) + EPS) * gain
        return value * at.cosine[...] + turn(value) * at.sine[...]

    keys_at = first_at + hidden_blocks
    slot = begin(keys_at)
    at.work[:, pl.ds(0, width // 2)] = times(at.low_four, at.tiles_b[slot])
    at.work[:, pl.ds(width // 2, width // 2)] = times(at.low_four, at.tiles_c[slot])
    at.keys_low[...] = at.work[:, pl.ds(0, width // 2)].astype(jnp.bfloat16)
    save(at.keys_low, at.keys_raw)
    first = lanes_below((tokens, lane), HEAD_DIM, lane)
    own = pl.ds(pl.multiple_of(seq * length, length), length)
    for pair in range(width // lane // 2):
        keys = head_path(at.work[:, pl.ds(pair * lane, lane)], at.vectors[8:9, pl.ds(0, lane)])
        values = at.work[:, pl.ds(width // 2 + pair * lane, lane)]
        even = jnp.where(first, keys, pltpu.roll(values, HEAD_DIM, 1)).astype(jnp.bfloat16)
        odd = jnp.where(first, pltpu.roll(keys, HEAD_DIM, 1), values).astype(jnp.bfloat16)
        for which, value in enumerate((even, odd)):
            columns = pl.ds((2 * pair + which) * lane, lane)
            at.both[:, own, columns] = value.reshape(rows, length, lane)

    def piece(owner, which=None):
        span = pl.ds(pl.multiple_of(owner * length, length), length)
        return at.both.at[:, span] if which is None else at.both.at[which, span]

    def send(number, part, bit):
        return pltpu.make_async_remote_copy(
            src_ref=part,
            dst_ref=part,
            send_sem=at.gather_send.at[number],
            recv_sem=at.gather_recv.at[number],
            device_id=(row, partner[bit]),
            device_id_type=MESH,
        )

    def flip(owner, bit):
        value = lax.rem(owner // (1 << bit), 2)
        return owner + (1 << bit) * (1 - 2 * value)

    across, along = partner[1], partner[2]
    corner = flip(across, 2)
    near_zero, far_one = send(0, piece(seq, 0), 1), send(1, piece(seq, 1), 2)
    near_one, far_zero = send(2, piece(seq, 1), 1), send(3, piece(seq, 0), 2)
    twin = send(4, piece(seq), 0)
    for copy in (near_zero, far_one, near_one, far_zero, twin):
        copy.start()

    slot = begin(keys_at + 1)
    for block, tile in enumerate((at.tiles_b, at.tiles_c)):
        at.work[:, pl.ds(block * COLS, COLS)] = times(at.low_four, tile[slot])
    at.queries_low[...] = at.work[...].astype(jnp.bfloat16)
    save(at.queries_low, at.queries_raw)
    for head in range(width // lane):
        columns = pl.ds(head * lane, lane)
        query = head_path(at.work[:, columns], at.vectors[7:8, pl.ds(0, lane)]).astype(jnp.bfloat16)
        query = query * jnp.bfloat16(HEAD_DIM**-0.5)
        at.scaled[:, columns] = query
        for which in range(rows):
            at.paired[which * (width // lane) + head] = two_heads(
                query[which * length : (which + 1) * length], True
            )
    save(at.scaled, at.queries_out)

    def transposed(low, target):
        for first in range(0, tokens, lane):
            span = pl.ds(first, lane)
            value = low[span].astype(jnp.float32).T.astype(jnp.bfloat16)
            target[:, :, :, :, span] = value.reshape(target.shape[:-1] + (lane,))

    transposed(at.low_one, at.turned_one)
    save(at.turned_one, at.mixer_in_x)
    near_zero.wait()
    far_one.wait()
    near_forward = send(5, piece(across, 0), 2)
    far_forward = send(6, piece(along, 1), 1)
    near_forward.start()
    far_forward.start()
    transposed(at.low_two, at.turned_two)
    save(at.turned_two, at.gated_x)

    at.sums[...] = jnp.zeros_like(at.sums)
    pairs_of = width // lane
    chip = seq // 2

    def attend(other):
        @pl.when(other <= chip)
        def _():
            span = pl.ds(pl.multiple_of(other * 2 * length, 2 * length), 2 * length)
            shape = (length, 2 * length)
            key_at = lax.broadcasted_iota(jnp.int32, shape, 1) + other * 2 * length
            query_at = lax.broadcasted_iota(jnp.int32, shape, 0) + seq * length
            first = lanes_below((2 * length, lane), HEAD_DIM, lane)
            for which in range(rows):
                start = at.seg_start[pl.ds(which * length, length)]
                start = jnp.concatenate([start, start], axis=1)
                allowed = jnp.logical_and(key_at >= start, key_at <= query_at)
                allowed = jnp.concatenate([allowed, allowed], axis=0)

                def one(head, carried):
                    columns = pl.ds(pl.multiple_of(head * lane, lane), lane)
                    both = at.both[which, span, columns]
                    place = which * pairs_of + head
                    weights = jnp.exp(dot_nt(at.paired[place], both))
                    weights = jnp.where(allowed, weights, 0.0).astype(jnp.bfloat16)
                    right = jnp.where(first, 1.0, both.astype(jnp.float32)).astype(jnp.bfloat16)
                    at.sums[place] += jnp.dot(
                        weights, right, preferred_element_type=jnp.float32
                    )
                    return carried

                lax.fori_loop(0, pairs_of, one, 0)

    twin.wait()
    attend(chip)
    near_one.wait()
    near_share = send(7, piece(across), 0)
    near_share.start()
    far_zero.wait()
    far_share = send(8, piece(along), 0)
    far_share.start()
    transposed(at.low_three, at.turned_three)
    save(at.turned_three, at.first_in_x)
    near_share.wait()
    attend(across // 2)
    transposed(at.low_four, at.turned_four)
    save(at.turned_four, at.attend_in_x)
    far_share.wait()
    attend(along // 2)

    block_rows = at.turned_active.shape[3]
    x_count = at.turned_active.shape[2]
    for j in range(hidden_blocks):
        for first in range(0, tokens, lane):
            span = pl.ds(first, lane)
            value = at.active_low[span, pl.ds(j * COLS, COLS)].astype(jnp.float32).T
            value = value.astype(jnp.bfloat16)
            for block in range(COLS // block_rows):
                place = j * (COLS // block_rows) + block
                shard = place // x_count
                at.turned_active[shard // 2, shard % 2, place % x_count, :, span] = value[
                    block * block_rows : (block + 1) * block_rows
                ]
    save(at.turned_active, at.active_x)
    near_forward.wait()
    far_forward.wait()
    corner_share = send(9, piece(corner), 0)
    corner_share.start()
    corner_share.wait()
    save(at.both, at.keys_values)
    attend(corner // 2)

    first = lanes_below((length, lane), HEAD_DIM, lane)
    for which in range(rows):
        span = pl.ds(which * length, length)
        for head in range(pairs_of):
            value = at.sums[which * pairs_of + head]
            value = value * (1.0 / pltpu.roll(value, HEAD_DIM, 1))
            value = jnp.where(first, pltpu.roll(value[:length], HEAD_DIM, 1), value[length:])
            at.attended[span, pl.ds(head * lane, lane)] = value.astype(jnp.bfloat16)
    add_output(keys_at + 2, at.attended, at.hidden_c, at.hidden_d)
    save(at.hidden_d, at.hidden_three)
    transposed(at.attended, at.turned_five)
    save(at.turned_five, at.attended_x)
    for copy in saves:
        copy.wait()


def forward(arrays, resident, rows, shards, collective_id):
    tokens, width = arrays["tokens"].shape
    hidden_columns = arrays["first_gate"].shape[1]
    length = tokens // rows
    total_length = length * shards
    block_rows = math.gcd(width // shards, hidden_columns // shards)
    low, full = jnp.bfloat16, jnp.float32

    def x_shape(columns):
        return (shards // 2, 2, columns // shards // block_rows, block_rows, tokens)

    outs = dict(
        hidden_zero=((tokens, width), full),
        hidden_one=((tokens, width), full),
        hidden_two=((tokens, width), full),
        hidden_three=((tokens, width), full),
        gate_one=((tokens, hidden_columns), low),
        up_one=((tokens, hidden_columns), low),
        queries_out=((tokens, width), low),
        queries_raw=((tokens, width), low),
        keys_raw=((tokens, width // 2), low),
        keys_values=((rows, total_length, width), low),
        mixer_saved=((4 * tokens, width), low),
        projected=((3 * tokens, width), low),
        mixer_in_x=(x_shape(width), low),
        gated_x=(x_shape(width), low),
        first_in_x=(x_shape(width), low),
        attend_in_x=(x_shape(width), low),
        attended_x=(x_shape(width), low),
        active_x=(x_shape(hidden_columns), low),
    )
    pairs = rows * width // (2 * HEAD_DIM)
    dma = pltpu.SemaphoreType.DMA
    scratch = dict(
        tiles_a=pltpu.VMEM((2, COLS, width), low),
        tiles_b=pltpu.VMEM((2, width, COLS), low),
        tiles_c=pltpu.VMEM((2, width, COLS), low),
        hidden_a=pltpu.VMEM((tokens, width), full),
        hidden_b=pltpu.VMEM((tokens, width), full),
        hidden_c=pltpu.VMEM((tokens, width), full),
        hidden_d=pltpu.VMEM((tokens, width), full),
        low_one=pltpu.VMEM((tokens, width), low),
        low_two=pltpu.VMEM((tokens, width), low),
        low_three=pltpu.VMEM((tokens, width), low),
        low_four=pltpu.VMEM((tokens, width), low),
        attended=pltpu.VMEM((tokens, width), low),
        work=pltpu.VMEM((tokens, width), full),
        mixed_low=pltpu.VMEM((4 * tokens, width), low),
        gates_low=pltpu.VMEM((3 * tokens, width), low),
        gate_low=pltpu.VMEM((tokens, hidden_columns), low),
        up_low=pltpu.VMEM((tokens, hidden_columns), low),
        active_low=pltpu.VMEM((tokens, hidden_columns), low),
        keys_low=pltpu.VMEM((tokens, width // 2), low),
        queries_low=pltpu.VMEM((tokens, width), low),
        scaled=pltpu.VMEM((tokens, width), low),
        both=pltpu.VMEM((rows, total_length, width), low),
        paired=pltpu.VMEM((pairs, 2 * length, 2 * HEAD_DIM), low),
        sums=pltpu.VMEM((pairs, 2 * length, 2 * HEAD_DIM), full),
        turned_one=pltpu.VMEM(x_shape(width), low),
        turned_two=pltpu.VMEM(x_shape(width), low),
        turned_three=pltpu.VMEM(x_shape(width), low),
        turned_four=pltpu.VMEM(x_shape(width), low),
        turned_five=pltpu.VMEM(x_shape(width), low),
        turned_active=pltpu.VMEM(x_shape(hidden_columns), low),
        halo_out=pltpu.VMEM((rows, 8, width), full),
        halo_in=pltpu.VMEM((rows, 8, width), full),
        tile_sem=dma((2, 3)),
        load_sem=dma((1,)),
        save_sem=dma((len(outs),)),
        halo_sem=dma((2,)),
        gather_send=dma((10,)),
        gather_recv=dma((10,)),
    )
    any_space = pl.BlockSpec(memory_space=pl.ANY)
    vmem_space = pl.BlockSpec(memory_space=pltpu.VMEM)
    weights = sum(value.size for value in arrays.values())
    results = pl.pallas_call(
        functools.partial(forward_kernel, list(arrays), list(outs), list(scratch), shards),
        out_shape=[jax.ShapeDtypeStruct(shape, kind) for shape, kind in outs.values()],
        in_specs=[vmem_space if name in resident else any_space for name in arrays],
        out_specs=[any_space] * len(outs),
        scratch_shapes=list(scratch.values()),
        compiler_params=pltpu.CompilerParams(
            collective_id=collective_id, has_side_effects=True, vmem_limit_bytes=60 * 2**20
        ),
        cost_estimate=pl.CostEstimate(
            flops=2 * weights * tokens, bytes_accessed=2 * weights, transcendentals=0
        ),
    )(*arrays.values())
    return dict(zip(outs, results))


BACKWARD_STARTS = {
    "second": 0,
    "attend_output": 8,
    "attention": 10,
    "queries": 26,
    "keys": 31,
    "first": 32,
    "mixer_output": 41,
    "halo": 43,
    "mixer_input": 44,
    "close": 47,
}
LOCAL_PAIRS = (18, 19, 26, 27)


def backward_kernel(names, entries, row_count, shards, *refs):
    at = types.SimpleNamespace(**dict(zip(names, refs)))
    outs = refs[len(names) : len(names) + len(entries)]
    token_out, mixed_out = refs[len(names) + len(entries) : len(names) + len(entries) + 2]
    scratch = refs[len(names) + len(entries) + 2 :]
    (
        tiles_a,
        tiles_b,
        tiles_c,
        saved,
        keys_values,
        key_grads,
        key_sums,
        queries,
        attended_grad,
        wide,
        queries_raw,
        keys_raw,
        gradient,
        normed_grad,
        hidden,
        halo_out,
        halo_in,
        small,
        tile_sem,
        load_sem,
        halo_sem,
        *scratch,
    ) = scratch
    local = types.SimpleNamespace()
    exchange = Exchange(entries, row_count, shards, outs, scratch, LOCAL_PAIRS, local)
    x_all, g_all = exchange.x_all, exchange.g_all
    seq, row = exchange.seq, exchange.row
    tokens, width = gradient.shape
    rows = keys_values.shape[0]
    length = tokens // rows
    hidden_blocks = at.first_gate.shape[1] // COLS
    blocks = width // COLS
    g_at = [entry[2] * COLS for entry in entries]
    second_wide, second_down, output_at, heads_at, first_down, first_wide = g_at[:6]
    mixer_out_at, mixer_in_at, small_at = g_at[6:]
    starts = BACKWARD_STARTS

    def local_place(kind, index):
        first, second, third, fourth = LOCAL_PAIRS
        row_at = jnp.where(index >= third, 1, 0)
        quad = jnp.where(jnp.logical_or(index == second, index == fourth), 1, 0)
        return row_at, pl.ds(pl.multiple_of(quad * COLS, COLS), COLS)

    def part(kind, index, side):
        row_at, columns = local_place(kind, index)
        return key_grads[row_at, :, side, kind, :, columns]

    def take(kind, index, total):
        row_at, columns = local_place(kind, index)
        key_sums[row_at, kind, :, columns] = total.astype(jnp.bfloat16)

    local.part, local.take = part, take

    def tile_copies(name, j, slot):
        columns = pl.ds(pl.multiple_of(j * COLS, COLS), COLS)
        a, b, c = tiles_a.at[slot], tiles_b.at[slot], tiles_c.at[slot]
        if name == "second":
            moves = [
                (at.second_gate.at[:, columns], b),
                (at.second_up.at[:, columns], c),
                (at.second_down.at[columns], a),
            ]
        elif name == "first":
            moves = [
                (at.first_down.at[columns], a),
                (at.first_gate.at[:, columns], b),
                (at.first_up.at[:, columns], c),
                (at.gate_one.at[:, columns], saved.at[slot, 0]),
                (at.up_one.at[:, columns], saved.at[slot, 1]),
            ]
        elif name == "attend_output":
            moves = [(at.attend_output.at[columns], a)]
        elif name == "mixer_output":
            moves = [(at.mixer_output.at[columns], a)]
        elif name == "queries":
            moves = [
                (at.query_weight.at[:, pl.ds(0, COLS)], b),
                (at.query_weight.at[:, pl.ds(COLS, COLS)], c),
            ]
        elif name == "keys":
            moves = [(at.key_weight, b), (at.value_weight, c)]
        else:
            even = pl.multiple_of(2 * j * COLS, COLS)
            odd = pl.multiple_of((2 * j + 1) * COLS, COLS)
            moves = [
                (at.mixer_input.at[:, pl.ds(even, COLS)], b),
                (at.mixer_input.at[:, pl.ds(odd, COLS)], c),
            ]
        return [
            pltpu.make_async_copy(source, target, tile_sem.at[slot, place])
            for place, (source, target) in enumerate(moves)
        ]

    steps = [
        ("second", hidden_blocks),
        ("attend_output", blocks),
        ("queries", 1),
        ("keys", 1),
        ("first", hidden_blocks),
        ("mixer_output", blocks),
        ("mixer_input", 3 * blocks // 2),
    ]
    first_step, total = {}, 0
    for name, number in steps:
        first_step[name] = total
        total += number
    order = [name for name, _ in steps]
    numbers = dict(steps)

    def tile_step(name, j):
        slot = (first_step[name] + j) % 2 if isinstance(j, int) else lax.rem(first_step[name] + j, 2)
        for copy in tile_copies(name, j, slot):
            copy.wait()

        @pl.when(j + 1 < numbers[name])
        def _():
            for copy in tile_copies(name, j + 1, 1 - slot):
                copy.start()

        if name != order[-1]:
            following = order[order.index(name) + 1]

            @pl.when(j + 1 == numbers[name])
            def _():
                for copy in tile_copies(following, 0, 1 - slot):
                    copy.start()

        return slot

    def load(place, source, target):
        return pltpu.make_async_copy(source, target, load_sem.at[place])

    count = len(entries)
    x_loads = [
        load(number, at.xs[number - 2], x_all.at[:, :, pl.ds(x_first, x_count)])
        for number, (x_first, x_count, _, _, _) in enumerate(entries)
        if 2 <= number < count - 1
    ]
    cotangent_load = load(count, at.cotangent, g_all.at[:, pl.ds(second_down, width)])
    middle_loads = [
        load(count + 1, at.queries_out, queries),
        load(count + 2, at.keys_values, keys_values),
        load(count + 5, at.keys_raw, keys_raw),
    ]
    raw_load = load(count + 4, at.queries_raw, queries_raw)
    staged = queries_raw
    late_loads = [
        load(count + 6, at.mixer_saved, keys_values.at[0]),
        load(count + 7, at.projected, keys_values.at[1, pl.ds(0, 3 * tokens)]),
    ]
    hidden_loads = [
        load(count + 8, source, hidden)
        for source in (at.hidden_three, at.hidden_two, at.hidden_one, at.hidden_zero)
    ]
    out_copy = load(count + 9, staged, token_out)
    mixed_copy = load(count + 9, staged, mixed_out)

    hidden_loads[0].start()
    cotangent_load.start()
    for copy in tile_copies("second", 0, 0):
        copy.start()
    for copy in middle_loads + x_loads:
        copy.start()
    normed_grad[...] = jnp.zeros_like(normed_grad)
    small[...] = jnp.zeros_like(small)
    g_all[:, pl.ds(small_at, COLS)] = jnp.zeros((tokens, COLS), jnp.bfloat16)
    wide[...] = jnp.zeros_like(wide)
    hidden_loads[0].wait()
    normed = attended_grad
    x_two = entries[0][0]
    for first in range(0, tokens, 128):
        span = pl.ds(first, 128)
        value = hidden[span]
        inverse = lax.rsqrt(jnp.mean(value * value, axis=-1, keepdims=True) + EPS)
        value = value * inverse * at.vectors[0:1, :]
        normed[span] = value.astype(jnp.bfloat16)
        turned = value.T.astype(jnp.bfloat16)
        shape = x_all.shape[:2] + (2,) + x_all.shape[3:4] + (128,)
        x_all[:, :, x_two : x_two + 2, :, pl.ds(first, 128)] = turned.reshape(shape)
    cotangent_load.wait()
    gradient[...] = g_all[:, pl.ds(second_down, width)].astype(jnp.float32)

    def low_gradient(place):
        g_all[:, pl.ds(place, width)] = gradient[...].astype(jnp.bfloat16)

    def norm_back(number):
        if number > 0:
            hidden_loads[number].wait()
        gain = at.vectors[number : number + 1, :]
        sums = jnp.zeros((1, width), jnp.float32)
        piece = 64
        for first in range(0, tokens, piece):
            span = pl.ds(first, piece)
            value, upper = hidden[span], normed_grad[span]
            inverse = lax.rsqrt(jnp.mean(value * value, axis=-1, keepdims=True) + EPS)
            value = value * inverse
            sums = sums + jnp.sum(upper * value, axis=0, keepdims=True)
            upper = upper * gain
            shift = jnp.mean(upper * value, axis=-1, keepdims=True)
            gradient[span] = gradient[span] + inverse * (upper - value * shift)
        for block in range(blocks):
            place = blocks * number + block
            small[place : place + 1, :] = sums[:, block * COLS : (block + 1) * COLS]
        normed_grad[...] = jnp.zeros_like(normed_grad)
        if number + 1 < len(hidden_loads):
            hidden_loads[number + 1].start()

    def feed_tile(name, j, gradient_at, wide_at):
        slot = tile_step(name, j)
        low = g_all[:, pl.ds(gradient_at, width)]
        active_grad = dot_nt(low, tiles_a[slot])
        if name == "second":
            gate_value = jnp.dot(normed[...], tiles_b[slot], preferred_element_type=jnp.float32)
            up_value = jnp.dot(normed[...], tiles_c[slot], preferred_element_type=jnp.float32)
        else:
            gate_value = saved[slot, 0].astype(jnp.float32)
            up_value = saved[slot, 1].astype(jnp.float32)
        share = 1.0 / (1.0 + jnp.exp(-gate_value))
        if name == "second":
            active = gate_value * share * up_value
            wide[...] += jnp.dot(
                active.astype(jnp.bfloat16), tiles_a[slot], preferred_element_type=jnp.float32
            )
            turned = active.T.astype(jnp.bfloat16)
            x_down, x_count = entries[1][:2]
            block_rows = x_all.shape[3]
            for block in range(COLS // block_rows):
                place = j * (COLS // block_rows) + block
                shard = place // x_count
                part = turned[block * block_rows : (block + 1) * block_rows]
                x_all[shard // 2, lax.rem(shard, 2), x_down + lax.rem(place, x_count)] = part
        up_grad = (active_grad * gate_value * share).astype(jnp.bfloat16)
        gate_grad = active_grad * up_value * share * (1.0 + gate_value * (1.0 - share))
        gate_grad = gate_grad.astype(jnp.bfloat16)
        gate_place = pl.multiple_of(wide_at + j * COLS, COLS)
        up_place = pl.multiple_of(wide_at + (hidden_blocks + j) * COLS, COLS)
        g_all[:, pl.ds(gate_place, COLS)] = gate_grad
        g_all[:, pl.ds(up_place, COLS)] = up_grad
        normed_grad[...] += dot_nt(gate_grad, tiles_b[slot]) + dot_nt(up_grad, tiles_c[slot])

    def output_tile(name, j, gradient_at, target):
        slot = tile_step(name, j)
        low = g_all[:, pl.ds(gradient_at, width)]
        value = dot_nt(low, tiles_a[slot])
        target[:, j * COLS : (j + 1) * COLS] = value.astype(target.dtype)

    def attention_head(row_at, head):
        span = pl.ds(pl.multiple_of(row_at * length, length), length)
        columns = pl.ds(pl.multiple_of(head * 2 * HEAD_DIM, 2 * HEAD_DIM), 2 * HEAD_DIM)
        query = two_heads(queries[span, columns], True)
        upper = two_heads(attended_grad[span, columns], False)
        both = keys_values[row_at, :, columns]
        key_at = lax.broadcasted_iota(jnp.int32, (both.shape[0], length), 0)
        query_at = lax.broadcasted_iota(jnp.int32, (both.shape[0], length), 1) + seq * length
        allowed = jnp.logical_and(key_at >= at.starts[row_at, 0:1], key_at <= query_at)
        weights = jnp.exp(dot_nt(both, query))
        weights = jnp.where(jnp.concatenate([allowed, allowed], axis=1), weights, 0.0)
        weights = weights * (1.0 / jnp.sum(weights, axis=0, keepdims=True))
        weight_grad_value = dot_nt(both, upper)
        delta = jnp.sum(weights * weight_grad_value, axis=0, keepdims=True)
        score_grad = (weights * (weight_grad_value - delta)).astype(jnp.bfloat16)
        both_grad = jnp.dot(score_grad, query, preferred_element_type=jnp.float32)
        both_grad += jnp.dot(
            weights.astype(jnp.bfloat16), upper, preferred_element_type=jnp.float32
        )
        shape = key_grads.shape[1:5] + (2 * HEAD_DIM,)
        key_grads[row_at, :, :, :, :, columns] = both_grad.astype(jnp.bfloat16).reshape(shape)
        query_grad = dot_tn(score_grad, both) * HEAD_DIM ** (-0.5)
        first = lanes_below((length, 2 * HEAD_DIM), HEAD_DIM, 2 * HEAD_DIM)
        wide[span, columns] = jnp.where(
            first, query_grad[:length], pltpu.roll(query_grad[length:], HEAD_DIM, 1)
        )

    lane = 2 * HEAD_DIM
    head_mean, turn = head_tools(lane)

    def head_back(value, raw, gain):
        value = value * at.cosine[...] - turn(value) * at.sine[...]
        raw = raw.astype(jnp.float32)
        inverse = lax.rsqrt(head_mean(raw * raw) + EPS)
        raw = raw * inverse
        sums = jnp.sum(value * raw, axis=0, keepdims=True)
        value = value * gain
        return inverse * (value - raw * head_mean(value * raw)), sums

    def both_halves(sums):
        return sums + pltpu.roll(sums, HEAD_DIM, 1)

    head_row = 7 * blocks

    def query_heads():
        sums = jnp.zeros((8, lane), jnp.float32)
        for part_at in range(0, width, lane):
            columns = pl.ds(part_at, lane)
            value, more = head_back(wide[:, columns], queries_raw[:, columns], at.vectors[7:8, pl.ds(0, lane)])
            g_all[:, pl.ds(heads_at + part_at, lane)] = value.astype(jnp.bfloat16)
            sums = sums + more
        small[head_row : head_row + 1, 0:lane] = both_halves(sums)[0:1]

    def key_heads():
        sums = jnp.zeros((8, lane), jnp.float32)
        first = lanes_below((tokens, lane), HEAD_DIM, lane)
        for pair in range(width // lane // 2):
            even, odd = [
                key_sums[:, :, :, pl.ds((2 * pair + which) * lane, lane)]
                .astype(jnp.float32)
                .reshape(tokens, lane)
                for which in range(2)
            ]
            key_value = jnp.where(first, even, pltpu.roll(odd, HEAD_DIM, 1))
            value_value = jnp.where(first, pltpu.roll(even, HEAD_DIM, 1), odd)
            columns = pl.ds(pair * lane, lane)
            value, more = head_back(key_value, keys_raw[:, columns], at.vectors[8:9, pl.ds(0, lane)])
            place = heads_at + width + pair * lane
            g_all[:, pl.ds(place, lane)] = value.astype(jnp.bfloat16)
            place += width // 2
            g_all[:, pl.ds(place, lane)] = value_value.astype(jnp.bfloat16)
            sums = sums + more
        small[head_row : head_row + 1, lane : 2 * lane] = both_halves(sums)[0:1]

    def project_back(name, j, even_at, odd_at):
        slot = tile_step(name, j)
        normed_grad[...] += dot_nt(g_all[:, pl.ds(even_at, COLS)], tiles_b[slot]) + dot_nt(
            g_all[:, pl.ds(odd_at, COLS)], tiles_c[slot]
        )

    def halo_copy():
        return pltpu.make_async_remote_copy(
            src_ref=halo_out,
            dst_ref=halo_in,
            send_sem=halo_sem.at[0],
            recv_sem=halo_sem.at[1],
            device_id=(row, jnp.maximum(seq - 1, 0)),
            device_id_type=MESH,
        )

    def saved_part(number, columns):
        return keys_values[0, pl.ds(number * tokens, tokens), columns].astype(jnp.float32)

    def projected_part(number, columns):
        return keys_values[1, pl.ds(number * tokens, tokens), columns].astype(jnp.float32)

    def convolution_back():
        within = lax.rem(lax.broadcasted_iota(jnp.int32, (tokens, lane), 0), length)
        position = within + seq * length
        keep_one = position - 1 >= at.seg_start[...]
        keep_two = position - 2 >= at.seg_start[...]
        edge = lax.broadcasted_iota(jnp.int32, (8, lane), 0)
        for part_at in range(0, width, lane):
            columns = pl.ds(part_at, lane)
            gated_grad = wide[:, columns]
            exit_grad = gated_grad * saved_part(0, columns)
            place = mixer_in_at + width + part_at
            g_all[:, pl.ds(place, lane)] = exit_grad.astype(jnp.bfloat16)
            conv_grad = gated_grad * projected_part(1, columns)
            block, inside = part_at // COLS, part_at % COLS
            for tap in range(3):
                sums = jnp.sum(conv_grad * saved_part(1 + tap, columns), axis=0, keepdims=True)
                place = blocks * (4 + tap) + block
                small[place : place + 1, inside : inside + lane] = sums
            two = jnp.where(keep_two, at.vectors[4:5, columns] * conv_grad, 0.0)
            one = jnp.where(keep_one, at.vectors[5:6, columns] * conv_grad, 0.0)
            here = at.vectors[6:7, columns] * conv_grad
            here += jnp.where(within < length - 1, pltpu.roll(one, tokens - 1, 0), 0.0)
            here += jnp.where(within < length - 2, pltpu.roll(two, tokens - 2, 0), 0.0)
            normed_grad[:, columns] = here
            for which in range(rows):
                span = slice(which * length, which * length + 8)
                sent = two[span] + jnp.where(edge == 1, pltpu.roll(one[span], 1, 0), 0.0)
                halo_out[which, :, columns] = jnp.where(edge < 2, sent, 0.0)

        @pl.when(seq > 0)
        def _():
            halo_copy().start()

    def product_back():
        @pl.when(seq < shards - 1)
        def _():
            halo_copy().wait_recv()
            for which in range(rows):
                span = pl.ds((which + 1) * length - 8, 8)
                normed_grad[span] = normed_grad[span] + pltpu.roll(halo_in[which], 6, 0)

        @pl.when(seq > 0)
        def _():
            halo_copy().wait_send()

        for part_at in range(0, width, lane):
            columns = pl.ds(part_at, lane)
            product_grad = normed_grad[:, columns]
            entry_grad = product_grad * projected_part(2, columns)
            carrier_grad = product_grad * projected_part(0, columns)
            g_all[:, pl.ds(mixer_in_at + part_at, lane)] = entry_grad.astype(jnp.bfloat16)
            place = mixer_in_at + 2 * width + part_at
            g_all[:, pl.ds(place, lane)] = carrier_grad.astype(jnp.bfloat16)
        normed_grad[...] = jnp.zeros_like(normed_grad)

    def task(i):
        def when(name, run, after=0, number=1):
            j = i - (starts[name] + after)

            @pl.when(jnp.logical_and(j >= 0, j < number))
            def _():
                run(j)

        when(
            "second",
            lambda j: feed_tile("second", j + 1, second_down, second_wide),
            0,
            hidden_blocks - 1,
        )

        def waits(j):
            for copy in middle_loads + x_loads:
                copy.wait()

        when("attend_output", waits)

        def to_attended(j):
            staged[...] = (hidden[...] + wide[...]).astype(jnp.bfloat16)
            mixed_copy.start()
            norm_back(0)
            low_gradient(output_at)
            output_tile("attend_output", 0, output_at, attended_grad)

        when("attend_output", to_attended)
        when("attend_output", lambda j: output_tile("attend_output", 1, output_at, attended_grad), 1)

        def staged_free(j):
            mixed_copy.wait()
            raw_load.start()

        when("attention", staged_free)

        def attention(j):
            attention_head(j // KV_HEADS, lax.rem(j, KV_HEADS))

        when("attention", attention, 0, rows * KV_HEADS)

        def to_queries(j):
            raw_load.wait()
            for copy in late_loads:
                copy.start()
            query_heads()

        when("queries", to_queries)
        def pick_rows(j):
            block_rows = x_all.shape[3]
            shape = (shards * 2 * block_rows, tokens)
            place = lax.broadcasted_iota(jnp.int32, shape, 0)
            vector, shard = lax.rem(place, 2 * block_rows), place // (2 * block_rows)
            wanted = blocks * vector + jnp.where(vector < 7, shard * blocks // shards, 0)
            found = lax.broadcasted_iota(jnp.int32, shape, 1) == wanted
            found = jnp.logical_and(found, vector < 8).astype(jnp.float32).astype(jnp.bfloat16)
            x_first = entries[-1][0]
            target = x_all.shape[:2] + (2, block_rows, tokens)
            x_all[:, :, x_first : x_first + 2] = found.reshape(target)

        when("queries", pick_rows, 2)
        when("queries", lambda j: project_back("queries", 0, heads_at, heads_at + COLS), 1)

        def to_keys(j):
            key_heads()
            project_back("keys", 0, heads_at + width, heads_at + width + COLS)
            norm_back(1)
            low_gradient(first_down)

        when("keys", to_keys)
        when("first", lambda j: feed_tile("first", j, first_down, first_wide), 0, hidden_blocks)

        def to_gated(j):
            norm_back(2)
            low_gradient(mixer_out_at)
            output_tile("mixer_output", 0, mixer_out_at, wide)
            for copy in late_loads:
                copy.wait()

        when("mixer_output", to_gated)

        def to_convolved(j):
            output_tile("mixer_output", 1, mixer_out_at, wide)
            convolution_back()

        when("mixer_output", to_convolved, 1)
        when("halo", lambda j: product_back())

        def mixer_tile(j):
            even = pl.multiple_of(mixer_in_at + 2 * j * COLS, COLS)
            project_back("mixer_input", j, even, pl.multiple_of(even + COLS, COLS))

        when("mixer_input", mixer_tile, 0, numbers["mixer_input"])

        def close(j):
            norm_back(3)
            staged[...] = gradient[...].astype(jnp.bfloat16)
            out_copy.start()
            g_all[pl.ds(0, small.shape[0]), pl.ds(small_at, COLS)] = small[...].astype(jnp.bfloat16)

        when("close", close)
        when("close", lambda j: out_copy.wait(), 1)

    exchange.meet()
    feed_tile("second", 0, second_down, second_wide)
    exchange.run(task)


def backward(groups, arrays, resident, row_count, shards, collective_id):
    xs = [x for x, _ in groups if not isinstance(x, int)]
    block_rows, tokens = xs[0].shape[3:]
    width = arrays["cotangent"].shape[1]
    entries, x_blocks, g_blocks, chunks = reduce_entries(
        [(x if isinstance(x, int) else x.shape[2], columns // COLS) for x, columns in groups]
    )
    names = ["xs_%d" % number for number in range(len(xs))] + list(arrays)
    values = list(xs) + list(arrays.values())
    rows, total_length = arrays["keys_values"].shape[:2]
    any_space = pl.BlockSpec(memory_space=pl.ANY)
    vmem_space = pl.BlockSpec(memory_space=pltpu.VMEM)
    key_blocks = total_length // shards // block_rows

    def kernel(*refs):
        xs_refs, others = refs[: len(xs)], refs[len(xs) : len(values)]
        named = [("xs", xs_refs)] + list(zip(arrays, others))
        backward_kernel(
            [name for name, _ in named],
            entries,
            row_count,
            shards,
            *[ref for _, ref in named],
            *refs[len(values) :],
        )

    low, full = jnp.bfloat16, jnp.float32
    return pl.pallas_call(
        kernel,
        out_shape=[
            jax.ShapeDtypeStruct((x_count * block_rows, g_count * COLS), low)
            for _, x_count, _, g_count, _ in entries
        ]
        + [jax.ShapeDtypeStruct((tokens, width), low)] * 2,
        in_specs=[vmem_space if name in resident else any_space for name in names],
        out_specs=[any_space] * (len(entries) + 2),
        scratch_shapes=[
            pltpu.VMEM((2, COLS, width), low),
            pltpu.VMEM((2, width, COLS), low),
            pltpu.VMEM((2, width, COLS), low),
            pltpu.VMEM((2, 2, tokens, COLS), low),
            pltpu.VMEM((rows, total_length, width), low),
            pltpu.VMEM((rows, shards // 2, 2, key_blocks, block_rows, width), low),
            pltpu.VMEM((rows, key_blocks, block_rows, width), low),
            pltpu.VMEM((tokens, width), low),
            pltpu.VMEM((tokens, width), low),
            pltpu.VMEM((tokens, width), full),
            pltpu.VMEM((tokens, width), low),
            pltpu.VMEM((tokens, width // 2), low),
            pltpu.VMEM((tokens, width), full),
            pltpu.VMEM((tokens, width), full),
            pltpu.VMEM((tokens, width), full),
            pltpu.VMEM((rows, 8, width), full),
            pltpu.VMEM((rows, 8, width), full),
            pltpu.VMEM((16, COLS), full),
            pltpu.SemaphoreType.DMA((2, 5)),
            pltpu.SemaphoreType.DMA((len(entries) + 10,)),
            pltpu.SemaphoreType.DMA((2,)),
            *exchange_scratch(row_count, shards, block_rows, x_blocks, g_blocks, tokens),
        ],
        compiler_params=pltpu.CompilerParams(
            collective_id=collective_id, has_side_effects=True, vmem_limit_bytes=63 * 2**20
        ),
        cost_estimate=pl.CostEstimate(
            flops=4 * chunks * shards * block_rows * COLS * tokens,
            bytes_accessed=2 * chunks * shards * block_rows * COLS,
            transcendentals=0,
        ),
    )(*values)


def fused_body(
    tokens,
    lengths,
    mixer_gain,
    mixer_input,
    mixer_kernel,
    mixer_output,
    first_gain,
    first_gate,
    first_up,
    first_down,
    attend_gain,
    query_weight,
    key_weight,
    value_weight,
    query_gain,
    key_gain,
    attend_output,
    second_gain,
    second_gate,
    second_up,
    second_down,
    cotangent,
):
    full, low = jnp.float32, jnp.bfloat16
    rows, length, width = tokens.shape
    token_count = rows * length
    lane = 2 * HEAD_DIM
    row_count, shards = lax.axis_size("row"), lax.axis_size("seq")
    seq = lax.axis_index("seq")
    positions = seq * length + jnp.arange(length, dtype=jnp.int32)
    _, seg_start = segment_info(lengths, positions)
    offsets = positions[None, :] - seg_start
    half = HEAD_DIM // 2
    inverse = THETA ** (-2.0 * jnp.arange(half, dtype=full) / HEAD_DIM)
    angles = offsets.astype(full).reshape(token_count, 1) * jnp.tile(inverse, 4)
    sign = jnp.tile(jnp.concatenate([-jnp.ones(half, full), jnp.ones(half, full)]), 2)
    vectors = jnp.concatenate(
        [
            jnp.stack([second_gain, attend_gain, first_gain, mixer_gain]),
            mixer_kernel,
            jnp.stack([jnp.tile(gain, width // HEAD_DIM) for gain in (query_gain, key_gain)]),
            jnp.zeros((7, width), low),
        ]
    ).astype(full)
    tables = dict(
        cosine=jnp.cos(angles),
        sine=jnp.sin(angles) * sign,
        seg_start=jnp.broadcast_to(seg_start.reshape(token_count, 1), (token_count, lane)),
        vectors=vectors,
    )
    arrays = dict(
        tokens=tokens.reshape(token_count, width),
        mixer_input=mixer_input,
        mixer_output=mixer_output,
        first_gate=first_gate,
        first_up=first_up,
        first_down=first_down,
        query_weight=query_weight,
        key_weight=key_weight,
        value_weight=value_weight,
        attend_output=attend_output,
        **tables,
    )
    saved = forward(arrays, tuple(tables), rows, shards, 2)
    block_rows = saved["attended_x"].shape[3]
    weights = dict(
        second_down=second_down,
        second_gate=second_gate,
        second_up=second_up,
        attend_output=attend_output,
        query_weight=query_weight,
        key_weight=key_weight,
        value_weight=value_weight,
        first_down=first_down,
        first_gate=first_gate,
        first_up=first_up,
        mixer_output=mixer_output,
        mixer_input=mixer_input,
    )
    names = ["gate_one", "up_one", "hidden_three", "hidden_two", "hidden_one", "hidden_zero"]
    names += ["queries_out", "keys_values", "queries_raw", "keys_raw", "mixer_saved", "projected"]
    starts = jnp.broadcast_to(seg_start[:, None, :], (rows, 8, length))
    arrays = dict(
        cotangent=cotangent.reshape(token_count, width),
        **{name: saved[name] for name in names},
        **tables,
        starts=starts,
        **weights,
    )
    hidden_columns = first_gate.shape[1]
    head_columns = width + 2 * key_weight.shape[1]
    groups = [
        (width // shards // block_rows, 2 * hidden_columns),
        (hidden_columns // shards // block_rows, width),
        (saved["attended_x"], width),
        (saved["attend_in_x"], head_columns),
        (saved["active_x"], width),
        (saved["first_in_x"], 2 * hidden_columns),
        (saved["gated_x"], width),
        (saved["mixer_in_x"], 3 * width),
        (2, COLS),
    ]
    (
        second_both,
        grad_second_down,
        grad_attend_output,
        attend_three,
        grad_first_down,
        first_both,
        grad_mixer_output,
        grad_mixer_input,
        sums,
        token_grad,
        mixed,
    ) = backward(groups, arrays, tuple(tables) + ("starts",), row_count, shards, 1)

    def single(value):
        return value.astype(full)

    share = width // shards
    vectors = single(
        lax.dynamic_slice(sums, (0, lax.rem(seq, COLS // share) * share), (7, share))
    )
    head_share = HEAD_DIM // shards
    heads = [
        single(lax.dynamic_slice(sums, (7, which * lane + seq * head_share), (1, head_share)))[0]
        for which in range(2)
    ]
    key_columns = key_weight.shape[1]
    return (
        mixed.reshape(tokens.shape),
        token_grad.reshape(tokens.shape),
        vectors[3],
        single(grad_mixer_input),
        vectors[4:7],
        single(grad_mixer_output),
        vectors[2],
        single(first_both[:, :hidden_columns]),
        single(first_both[:, hidden_columns:]),
        single(grad_first_down),
        vectors[1],
        single(attend_three[:, :width]),
        single(attend_three[:, width : width + key_columns]),
        single(attend_three[:, width + key_columns :]),
        heads[0],
        heads[1],
        single(grad_attend_output),
        vectors[0],
        single(second_both[:, :hidden_columns]),
        single(second_both[:, hidden_columns:]),
        single(grad_second_down),
    )


def fused_or_general(*args):
    tokens = args[0]
    rows, length, width = tokens.shape
    row_count, shards = lax.axis_size("row"), lax.axis_size("seq")
    key_bytes = 2 * rows * length * shards * width
    if key_bytes <= 4 * 2**20 and shards == 8 and 4 * rows == shards and row_count == 4:
        return fused_body(*args)
    return body(*args)


def solution(mesh):
    in_specs = (
        P("row", "seq", None),
        P("row", None),
        P(),
        P(),
        P(),
        P(),
        P(),
        P(),
        P(),
        P(),
        P(),
        P(),
        P(),
        P(),
        P(),
        P(),
        P(),
        P(),
        P(),
        P(),
        P(),
        P("row", "seq", None),
    )
    out_specs = (
        P("row", "seq", None),
        P("row", "seq", None),
        P("seq"),
        P("seq", None),
        P(None, "seq"),
        P("seq", None),
        P("seq"),
        P("seq", None),
        P("seq", None),
        P("seq", None),
        P("seq"),
        P("seq", None),
        P("seq", None),
        P("seq", None),
        P("seq"),
        P("seq"),
        P("seq", None),
        P("seq"),
        P("seq", None),
        P("seq", None),
        P("seq", None),
    )
    return jax.shard_map(fused_or_general, mesh=mesh, in_specs=in_specs, out_specs=out_specs, check_vma=False)
```

```python
import functools
import math
import types

import jax
import jax.numpy as jnp
from jax import lax
from jax.experimental import pallas as pl
from jax.experimental.pallas import tpu as pltpu
from jax.sharding import PartitionSpec as P

HEADS = 16
KV_HEADS = 8
HEAD_DIM = 64
GROUP = 2


EPS = 1e-05
THETA = 1000000.0
NEGATIVE = -1e30
HIGHEST = lax.Precision.HIGHEST
MESH = pl.DeviceIdType.MESH
COLS = 512
SLOTS = 4
ZSLOTS = 6


def passed_along(value, axis, steps):
    count = lax.axis_size(axis)
    initial, last = (max(0, -steps), min(count, count - steps))
    return lax.ppermute(value, axis, [(source, source + steps) for source in range(initial, last)])


def segment_info(lengths, positions):
    boundary = jnp.cumsum(lengths, axis=-1)
    passed = boundary[:, None, :] <= positions[None, :, None]
    segment = jnp.sum(passed.astype(jnp.int32), axis=-1)
    seg_start = jnp.max(jnp.where(passed, boundary[:, None, :], 0), axis=-1)
    return (segment, seg_start)


def norm_rows(values, norm_gain):
    return values * lax.rsqrt(jnp.mean(values * values, axis=-1, keepdims=True) + EPS) * norm_gain


def rotate(values, offsets):
    half_dim = values.shape[-1] // 2
    inverse = THETA ** (-2.0 * jnp.arange(half_dim, dtype=jnp.float32) / values.shape[-1])
    angles = offsets.astype(jnp.float32)[:, :, None, None] * inverse
    cosine = jnp.cos(angles)
    sine_table = jnp.sin(angles)
    leading = values[..., :half_dim]
    trailing = values[..., half_dim:]
    return jnp.concatenate(
        [leading * cosine - trailing * sine_table, trailing * cosine + leading * sine_table],
        axis=-1,
    )


def swiglu(gate_value, upward):
    return gate_value / (1.0 + jnp.exp(-gate_value)) * upward


def dense(inputs, matrix):
    return jnp.einsum("rtd,df->rtf", inputs, matrix, preferred_element_type=jnp.float32)


def weight_grad(inputs, gradient):
    return (inputs, gradient)


def back_dense(gradient, matrix):
    return jnp.einsum("rtf,df->rtd", gradient, matrix, preferred_element_type=jnp.float32)


def mixer_block(hidden, norm_gain, input_matrix, kernel, output_matrix, seg_start, positions):
    feature_columns = hidden.shape[-1]
    length = hidden.shape[1]
    normed, norm_back = jax.vjp(norm_rows, hidden, norm_gain.astype(jnp.float32))
    normed_low = normed.astype(jnp.bfloat16)
    projected_rows = dense(normed_low, input_matrix)
    input_gate_value = projected_rows[..., :feature_columns]
    exit_gate = projected_rows[..., feature_columns : 2 * feature_columns]
    carry_value = projected_rows[..., 2 * feature_columns :]
    gated_product_reduced = (input_gate_value * carry_value).astype(jnp.bfloat16)
    previous = passed_along(gated_product_reduced[:, length - 2 :, :], "seq", 1)
    extended = jnp.concatenate([previous, gated_product_reduced], axis=1).astype(jnp.float32)
    keep_one = (positions[None, :] - 1 >= seg_start).astype(jnp.float32)[..., None]
    keep_two = (positions[None, :] - 2 >= seg_start).astype(jnp.float32)[..., None]
    kernel_taps = kernel.astype(jnp.float32)
    two_back = extended[:, :length]
    one_back = extended[:, 1 : length + 1]
    current = extended[:, 2:]
    convolved = (
        kernel_taps[2] * current
        + kernel_taps[1] * keep_one * one_back
        + kernel_taps[0] * keep_two * two_back
    )
    gated_low = (exit_gate * convolved).astype(jnp.bfloat16)
    result = hidden + dense(gated_low, output_matrix)

    def mixer_backward(gradient):
        gradient_low = gradient.astype(jnp.bfloat16)
        grad_output = weight_grad(gated_low, gradient_low)
        grad_gated = back_dense(gradient_low, output_matrix)
        output_gate_gradient = grad_gated * convolved
        grad_conv = grad_gated * exit_gate
        grad_kernel = jnp.stack(
            [
                jnp.sum(grad_conv * keep_two * two_back, axis=(0, 1)),
                jnp.sum(grad_conv * keep_one * one_back, axis=(0, 1)),
                jnp.sum(grad_conv * current, axis=(0, 1)),
            ]
        )
        grad_extended = jnp.pad(kernel_taps[0] * keep_two * grad_conv, ((0, 0), (0, 2), (0, 0)))
        grad_extended = grad_extended + jnp.pad(
            kernel_taps[1] * keep_one * grad_conv, ((0, 0), (1, 1), (0, 0))
        )
        grad_extended = grad_extended + jnp.pad(
            kernel_taps[2] * grad_conv, ((0, 0), (2, 0), (0, 0))
        )
        returned = passed_along(grad_extended[:, :2, :], "seq", -1)
        gated_product_gradient = grad_extended[:, 2:] + jnp.pad(
            returned, ((0, 0), (length - 2, 0), (0, 0))
        )
        grad_projected = jnp.concatenate(
            [
                gated_product_gradient * carry_value,
                output_gate_gradient,
                gated_product_gradient * input_gate_value,
            ],
            axis=-1,
        ).astype(jnp.bfloat16)
        grad_input = weight_grad(normed_low, grad_projected)
        grad_normed = back_dense(grad_projected, input_matrix)
        grad_hidden, grad_gain = norm_back(grad_normed)
        return (gradient + grad_hidden, (grad_gain, grad_input, grad_kernel, grad_output))

    return (result, mixer_backward)


def feed_block(hidden, norm_gain, gate_matrix, up_matrix, down_matrix):
    normed, norm_back = jax.vjp(norm_rows, hidden, norm_gain.astype(jnp.float32))
    normed_low = normed.astype(jnp.bfloat16)
    gate_value = dense(normed_low, gate_matrix)
    upward = dense(normed_low, up_matrix)
    active, active_back = jax.vjp(swiglu, gate_value, upward)
    active_low = active.astype(jnp.bfloat16)
    result = hidden + dense(active_low, down_matrix)

    def feed_backward(gradient):
        gradient_low = gradient.astype(jnp.bfloat16)
        grad_down = weight_grad(active_low, gradient_low)
        grad_gate, grad_upward = active_back(back_dense(gradient_low, down_matrix))
        gate_low = grad_gate.astype(jnp.bfloat16)
        upward_low = grad_upward.astype(jnp.bfloat16)
        grad_normed = back_dense(gate_low, gate_matrix) + back_dense(upward_low, up_matrix)
        grad_hidden, grad_gain = norm_back(grad_normed)
        return (
            gradient + grad_hidden,
            (
                grad_gain,
                weight_grad(normed_low, jnp.concatenate([gate_low, upward_low], axis=-1)),
                grad_down,
            ),
        )

    return (result, feed_backward)


def attend_block(
    hidden,
    lengths,
    norm_gain,
    query_matrix,
    key_matrix,
    value_matrix,
    query_norm,
    key_norm,
    output_matrix,
    segment,
    positions,
    offsets,
):
    row_count, length, feature_columns = hidden.shape
    score_scale = HEAD_DIM ** (-0.5)
    normed, norm_back = jax.vjp(norm_rows, hidden, norm_gain.astype(jnp.float32))
    normed_low = normed.astype(jnp.bfloat16)

    def head_path(projected_rows, head_gain):
        return rotate(norm_rows(projected_rows, head_gain), offsets)

    queries = dense(normed_low, query_matrix).reshape(row_count, length, HEADS, HEAD_DIM)
    keys_raw = dense(normed_low, key_matrix).reshape(row_count, length, KV_HEADS, HEAD_DIM)
    values_raw = dense(normed_low, value_matrix)
    query_rot, query_back = jax.vjp(head_path, queries, query_norm.astype(jnp.float32))
    key_rot, key_back = jax.vjp(head_path, keys_raw, key_norm.astype(jnp.float32))
    query_low = query_rot.astype(jnp.bfloat16).reshape(row_count, length, KV_HEADS, GROUP, HEAD_DIM)
    key_low = key_rot.astype(jnp.bfloat16)
    value_low = values_raw.astype(jnp.bfloat16).reshape(row_count, length, KV_HEADS, HEAD_DIM)
    all_keys, all_values = (
        lax.all_gather(key_low, "seq", axis=1, tiled=True),
        lax.all_gather(value_low, "seq", axis=1, tiled=True),
    )
    total_length = all_keys.shape[1]
    key_block = min(512, total_length)
    block_count = (positions[length - 1] + key_block) // key_block

    def block_scores(number, key_source, value_source):
        first_key = number * key_block
        keys_here = lax.dynamic_slice_in_dim(key_source, first_key, key_block, 1)
        values_here = lax.dynamic_slice_in_dim(value_source, first_key, key_block, 1)
        key_positions = first_key + jnp.arange(key_block, dtype=jnp.int32)
        key_segment, unused = segment_info(lengths, key_positions)
        scores = (
            jnp.einsum(
                "rtkgh,rskh->rkgts", query_low, keys_here, preferred_element_type=jnp.float32
            )
            * score_scale
        )
        allowed = (segment[:, :, None] == key_segment[:, None, :]) & (
            positions[None, :, None] >= key_positions[None, None, :]
        )
        allowed = allowed[:, None, None]
        return (jnp.where(allowed, scores, NEGATIVE), allowed, keys_here, values_here)

    stat_shape = (row_count, KV_HEADS, GROUP, length)

    def stats_step(number, carried):
        peak_score, running_sum = carried
        scores, allowed, unused_keys, unused_values = block_scores(number, all_keys, all_values)
        new_peak = jnp.maximum(peak_score, jnp.max(scores, axis=-1))
        fresh = jnp.sum(jnp.where(allowed, jnp.exp(scores - new_peak[..., None]), 0.0), axis=-1)
        return (new_peak, running_sum * jnp.exp(peak_score - new_peak) + fresh)

    peak_score, running_sum = lax.fori_loop(
        0,
        block_count,
        stats_step,
        (jnp.full(stat_shape, NEGATIVE, jnp.float32), jnp.zeros(stat_shape, jnp.float32)),
    )
    log_total = peak_score + jnp.log(running_sum)

    def probabilities(scores, allowed):
        return jnp.where(allowed, jnp.exp(scores - log_total[..., None]), 0.0)

    out_shape = (row_count, length, KV_HEADS, GROUP, HEAD_DIM)

    def output_step(number, carried):
        rounded, exact_sum = carried
        scores, allowed, keys_here, values_here = block_scores(number, all_keys, all_values)
        weights = probabilities(scores, allowed)
        rounded = rounded + jnp.einsum(
            "rkgts,rskh->rtkgh",
            weights.astype(jnp.bfloat16),
            values_here,
            preferred_element_type=jnp.float32,
        )
        exact_sum = exact_sum + jnp.einsum(
            "rkgts,rskh->rtkgh", weights, values_here.astype(jnp.float32), precision=HIGHEST
        )
        return (rounded, exact_sum)

    rounded, exact_sum = lax.fori_loop(
        0,
        block_count,
        output_step,
        (jnp.zeros(out_shape, jnp.float32), jnp.zeros(out_shape, jnp.float32)),
    )
    attended_low = rounded.reshape(row_count, length, HEADS * HEAD_DIM).astype(jnp.bfloat16)
    result = hidden + dense(attended_low, output_matrix)

    def attend_backward(gradient):
        gradient_low = gradient.astype(jnp.bfloat16)
        grad_output = weight_grad(attended_low, gradient_low)
        grad_attended = (
            back_dense(gradient_low, output_matrix).astype(jnp.bfloat16).reshape(out_shape)
        )
        row_delta = jnp.einsum(
            "rtkgh,rtkgh->rkgt", grad_attended.astype(jnp.float32), exact_sum, precision=HIGHEST
        )
        key_source, value_source = (all_keys, all_values)

        def grad_step(number, carried):
            grad_query, grad_keys, grad_values = carried
            scores, allowed, keys_here, values_here = block_scores(number, key_source, value_source)
            weights = probabilities(scores, allowed)
            grad_weights = jnp.einsum(
                "rtkgh,rskh->rkgts", grad_attended, values_here, preferred_element_type=jnp.float32
            )
            grad_scores = (weights * (grad_weights - row_delta[..., None])).astype(jnp.bfloat16)
            grad_query = (
                grad_query
                + jnp.einsum(
                    "rkgts,rskh->rtkgh", grad_scores, keys_here, preferred_element_type=jnp.float32
                )
                * score_scale
            )
            key_part = (
                jnp.einsum(
                    "rkgts,rtkgh->rskh", grad_scores, query_low, preferred_element_type=jnp.float32
                )
                * score_scale
            )
            value_part = jnp.einsum(
                "rkgts,rtkgh->rskh",
                weights.astype(jnp.bfloat16),
                grad_attended,
                preferred_element_type=jnp.float32,
            )
            grad_keys = lax.dynamic_update_slice_in_dim(grad_keys, key_part, number * key_block, 1)
            grad_values = lax.dynamic_update_slice_in_dim(
                grad_values, value_part, number * key_block, 1
            )
            return (grad_query, grad_keys, grad_values)

        key_shape = (row_count, total_length, KV_HEADS, HEAD_DIM)
        grad_query, grad_keys, grad_values = lax.fori_loop(
            0,
            block_count,
            grad_step,
            (
                jnp.zeros(out_shape, jnp.float32),
                jnp.zeros(key_shape, jnp.float32),
                jnp.zeros(key_shape, jnp.float32),
            ),
        )
        local_keys, local_values = (
            lax.psum_scatter(
                grad_keys.astype(jnp.bfloat16), "seq", scatter_dimension=1, tiled=True
            ).astype(jnp.float32),
            lax.psum_scatter(
                grad_values.astype(jnp.bfloat16), "seq", scatter_dimension=1, tiled=True
            ).astype(jnp.float32),
        )
        grad_queries, grad_query_norm = query_back(
            grad_query.reshape(row_count, length, HEADS, HEAD_DIM)
        )
        grad_keys_raw, grad_key_norm = key_back(local_keys)
        query_grad_low = grad_queries.reshape(row_count, length, HEADS * HEAD_DIM).astype(
            jnp.bfloat16
        )
        key_grad_low = grad_keys_raw.reshape(row_count, length, KV_HEADS * HEAD_DIM).astype(
            jnp.bfloat16
        )
        value_grad_low = local_values.reshape(row_count, length, KV_HEADS * HEAD_DIM).astype(
            jnp.bfloat16
        )
        grad_normed = (
            back_dense(query_grad_low, query_matrix)
            + back_dense(key_grad_low, key_matrix)
            + back_dense(value_grad_low, value_matrix)
        )
        grad_hidden, grad_gain = norm_back(grad_normed)
        return (
            gradient + grad_hidden,
            (
                grad_gain,
                weight_grad(
                    normed_low,
                    jnp.concatenate([query_grad_low, key_grad_low, value_grad_low], axis=-1),
                ),
                grad_query_norm,
                grad_key_norm,
                grad_output,
            ),
        )

    return (result, attend_backward)


def reduce_entries(pairs):
    entries = []
    x_first = g_first = chunk = 0
    for x_count, g_count in pairs:
        entries.append((x_first, x_count, g_first, g_count, chunk))
        x_first += x_count
        g_first += g_count
        chunk += x_count * g_count
    return entries, x_first, g_first, chunk


def locate(entries, q):
    x_block, g_block = jnp.int32(0), jnp.int32(0)
    for x_first, x_count, g_first, g_count, chunk in entries:
        here = q - chunk
        inside = here >= 0
        x_block = jnp.where(inside, x_first + lax.rem(jnp.maximum(here, 0), x_count), x_block)
        g_block = jnp.where(inside, g_first + jnp.maximum(here, 0) // x_count, g_block)
    return x_block, g_block


def seq_steps(bits):
    upper = list(range(1, bits))
    middle = (len(upper) + 1) // 2
    kinds = []
    for order in (upper, upper[middle:] + upper[:middle]):
        held = sorted(upper, reverse=True)
        steps = []
        for bit in order:
            place = held.index(bit)
            steps.append((bit, 2**place, 2 ** (len(held) - 1 - place)))
            held.remove(bit)
        kinds.append(steps)
    return kinds


def exchange_scratch(row_count, shards, block_rows, x_blocks, g_blocks, tokens):
    bits = shards.bit_length() - 1
    block = (block_rows, COLS)
    comm = []
    for steps in seq_steps(bits):
        for _, above, below in steps:
            comm.append(pltpu.VMEM((2, above, 2, below) + block, jnp.bfloat16))
            comm.append(pltpu.VMEM((SLOTS, above, below) + block, jnp.bfloat16))
    z_steps = row_count - 1
    return [
        pltpu.VMEM((shards // 2, 2, x_blocks, block_rows, tokens), jnp.bfloat16),
        pltpu.VMEM((tokens, g_blocks * COLS), jnp.bfloat16),
        pltpu.VMEM((2, 2, shards // 2) + block, jnp.bfloat16),
        pltpu.VMEM((2, SLOTS, shards // 2) + block, jnp.bfloat16),
        *comm,
        *[pltpu.VMEM((2, ZSLOTS) + block, jnp.bfloat16) for _ in range(5)],
        pltpu.SemaphoreType.DMA((2, bits, SLOTS)),
        pltpu.SemaphoreType.DMA((2, bits, SLOTS)),
        pltpu.SemaphoreType.DMA((2, z_steps, ZSLOTS)),
        pltpu.SemaphoreType.DMA((2, z_steps, ZSLOTS)),
        pltpu.SemaphoreType.DMA((2, ZSLOTS)),
    ]


class Exchange:
    def __init__(self, entries, row_count, shards, outs, scratch, locals_at=(), local=None):
        self.entries, self.outs = entries, outs
        self.locals_at, self.local = locals_at, local
        self.bits = bits = shards.bit_length() - 1
        self.kinds = seq_steps(bits)
        (self.x_all, self.g_all, self.send_zero, self.recv_zero, *rest) = scratch
        self.held, self.received = [[], []], [[], []]
        for kind in range(2):
            for _ in self.kinds[kind]:
                self.held[kind].append(rest.pop(0))
                self.received[kind].append(rest.pop(0))
        self.z_own, self.z_in, self.z_part, self.z_cross, self.z_total = rest[:5]
        self.seq_send, self.seq_recv, self.z_send, self.z_recv, self.out_sem = rest[5:]
        self.row, self.seq = lax.axis_index("row"), lax.axis_index("seq")
        self.row_count, self.shards = row_count, shards
        self.value = [lax.rem(self.seq // (1 << bit), 2) for bit in range(bits)]
        self.partner = [self.seq + (1 << bit) * (1 - 2 * self.value[bit]) for bit in range(bits)]
        last = entries[-1]
        self.pairs = (last[4] + last[1] * last[3]) // 2 + len(locals_at)
        half = row_count // 2
        self.depth = half - 1
        lower = self.row < half
        self.level = jnp.where(lower, self.row, row_count - 1 - self.row)
        self.toward = jnp.where(lower, self.row + 1, self.row - 1)
        self.away = jnp.where(lower, self.row - 1, self.row + 1)

    def meet(self):
        barrier = pltpu.get_barrier_semaphore()
        others = [(self.row, partner) for partner in self.partner]
        for step in (1, self.row_count - 1):
            others.append((lax.rem(self.row + step, self.row_count), self.seq))
        for step in (1, self.shards - 1):
            others.append((self.row, lax.rem(self.seq + step, self.shards)))
        for other in others:
            pl.semaphore_signal(barrier, inc=1, device_id=other, device_id_type=MESH)
        pl.semaphore_wait(barrier, len(others))

    def is_local(self, index):
        found = index < 0
        for at in self.locals_at:
            found = jnp.logical_or(found, index == at)
        return found

    def chunk(self, kind, index):
        before = sum([jnp.where(index > at, 1, 0) for at in self.locals_at], 0)
        return 2 * (index - before) + kind

    def product(self, kind, index, side):
        x_block, g_block = locate(self.entries, self.chunk(kind, index))
        left = self.x_all[:, side, x_block]
        columns = pl.ds(pl.multiple_of(g_block * COLS, COLS), COLS)
        return jnp.dot(
            left.reshape(left.shape[0] * left.shape[1], left.shape[2]),
            self.g_all[:, columns],
            preferred_element_type=jnp.float32,
        )

    def seq_copy(self, kind, step, slot):
        if step == 0:
            bit = 0
            source = self.send_zero.at[kind, lax.rem(slot, 2)]
            target = self.recv_zero.at[kind, slot]
        else:
            bit = self.kinds[kind][step - 1][0]
            source = self.held[kind][step - 1].at[lax.rem(slot, 2), :, 1 - self.value[bit]]
            target = self.received[kind][step - 1].at[slot]
        return pltpu.make_async_remote_copy(
            src_ref=source,
            dst_ref=target,
            send_sem=self.seq_send.at[kind, step, slot],
            recv_sem=self.seq_recv.at[kind, step, slot],
            device_id=(self.row, self.partner[bit]),
            device_id_type=MESH,
        )

    def seq_sum(self, kind, step, slot):
        bit = self.kinds[kind][step - 2][0]
        mine = self.held[kind][step - 2][lax.rem(slot, 2), :, self.value[bit]].astype(jnp.float32)
        return mine + self.received[kind][step - 2][slot].astype(jnp.float32)

    def z_copy(self, kind, step, slot):
        if step < self.depth:
            source = self.z_own if step == 0 else self.z_part
            target, where = self.z_in, self.toward
        elif step == self.depth:
            source = self.z_own if self.depth == 0 else self.z_part
            target, where = self.z_cross, self.toward
        else:
            source, target, where = self.z_total, self.z_total, self.away
        return pltpu.make_async_remote_copy(
            src_ref=source.at[kind, slot],
            dst_ref=target.at[kind, slot],
            send_sem=self.z_send.at[kind, step, slot],
            recv_sem=self.z_recv.at[kind, step, slot],
            device_id=(where, self.seq),
            device_id_type=MESH,
        )

    def start_out(self, kind, slot, index):
        q = self.chunk(kind, index)
        rows = self.z_total.shape[2]
        for out, (_, x_count, _, g_count, chunk) in zip(self.outs, self.entries):
            here = q - chunk

            @pl.when(jnp.logical_and(here >= 0, here < x_count * g_count))
            def _():
                row_at = pl.multiple_of(lax.rem(here, x_count) * rows, rows)
                column_at = pl.multiple_of(here // x_count * COLS, COLS)
                pltpu.make_async_copy(
                    self.z_total.at[kind, slot],
                    out.at[pl.ds(row_at, rows), pl.ds(column_at, COLS)],
                    self.out_sem.at[kind, slot],
                ).start()

    def first(self, kind, index):
        slot = lax.rem(index, SLOTS)
        target = self.send_zero

        def put():
            target[kind, lax.rem(slot, 2)] = (
                self.product(kind, index, 1 - self.value[0])
                .astype(jnp.bfloat16)
                .reshape(target.shape[2:])
            )

        if self.local is None:
            put()
        else:
            pl.when(jnp.logical_not(self.is_local(index)))(put)

            @pl.when(self.is_local(index))
            def _():
                target[kind, lax.rem(slot, 2)] = self.local.part(kind, index, 1 - self.value[0])

        self.seq_copy(kind, 0, slot).start()

    def second(self, kind, index):
        slot = lax.rem(index, SLOTS)
        self.seq_copy(kind, 0, slot).wait()
        target = self.held[kind][0]

        def put():
            mine = self.product(kind, index, self.value[0])
            total = mine + self.recv_zero[kind, slot].astype(jnp.float32).reshape(mine.shape)
            target[lax.rem(slot, 2)] = total.astype(jnp.bfloat16).reshape(target.shape[1:])

        if self.local is None:
            put()
        else:
            pl.when(jnp.logical_not(self.is_local(index)))(put)

            @pl.when(self.is_local(index))
            def _():
                mine = self.local.part(kind, index, self.value[0]).astype(jnp.float32)
                total = mine + self.recv_zero[kind, slot].astype(jnp.float32)
                target[lax.rem(slot, 2)] = total.astype(jnp.bfloat16).reshape(target.shape[1:])

        self.seq_copy(kind, 1, slot).start()

    def middle(self, step):
        def run(kind, index):
            slot = lax.rem(index, SLOTS)
            self.seq_copy(kind, step - 1, slot).wait()
            total = self.seq_sum(kind, step, slot)
            target = self.held[kind][step - 1]
            target[lax.rem(slot, 2)] = total.astype(jnp.bfloat16).reshape(target.shape[1:])
            self.seq_copy(kind, step, slot).start()

        return run

    def last(self, kind, index):
        slot, z_slot = lax.rem(index, SLOTS), lax.rem(index, ZSLOTS)
        self.seq_copy(kind, self.bits - 1, slot).wait()
        total = self.seq_sum(kind, self.bits, slot).reshape(self.z_own.shape[2:])

        def put():
            self.z_own[kind, z_slot] = total.astype(jnp.bfloat16)

            @pl.when(self.level == 0)
            def _():
                self.z_copy(kind, 0, z_slot).start()

        if self.local is None:
            put()
        else:
            pl.when(jnp.logical_not(self.is_local(index)))(put)

            @pl.when(self.is_local(index))
            def _():
                self.local.take(kind, index, total)

    def z_stage(self, step):
        level, depth = self.level, self.depth

        def run(kind, index):
            slot = lax.rem(index, ZSLOTS)
            if step <= depth:

                @pl.when(level == step)
                def _():
                    self.z_copy(kind, step - 1, slot).wait_recv()
                    self.z_part[kind, slot] = (
                        self.z_own[kind, slot].astype(jnp.float32)
                        + self.z_in[kind, slot].astype(jnp.float32)
                    ).astype(jnp.bfloat16)
                    self.z_copy(kind, step, slot).start()

                @pl.when(level == step - 1)
                def _():
                    self.z_copy(kind, step - 1, slot).wait_send()

            elif step == depth + 1:

                @pl.when(level == depth)
                def _():
                    self.z_copy(kind, depth, slot).wait()
                    own = self.z_own if depth == 0 else self.z_part
                    self.z_total[kind, slot] = (
                        own[kind, slot].astype(jnp.float32)
                        + self.z_cross[kind, slot].astype(jnp.float32)
                    ).astype(jnp.bfloat16)
                    if depth > 0:
                        self.z_copy(kind, step, slot).start()
                    self.start_out(kind, slot, index)

            else:
                receiver = 2 * depth + 1 - step

                @pl.when(level == receiver)
                def _():
                    self.z_copy(kind, step - 1, slot).wait_recv()
                    if receiver > 0:
                        self.z_copy(kind, step, slot).start()
                    self.start_out(kind, slot, index)

                @pl.when(level == receiver + 1)
                def _():
                    self.z_copy(kind, step - 1, slot).wait_send()

        return run

    def finish(self, kind, index):
        slot = lax.rem(index, ZSLOTS)
        rows = self.z_total.shape[2]
        pltpu.make_async_copy(
            self.z_total.at[kind, slot],
            self.outs[0].at[pl.ds(0, rows), pl.ds(0, COLS)],
            self.out_sem.at[kind, slot],
        ).wait()

    def run(self, task):
        stages = [(self.first, False), (self.second, False)]
        stages += [(self.middle(step), False) for step in range(2, self.bits)]
        stages += [(self.last, False)]
        stages += [(self.z_stage(step), True) for step in range(1, 2 * self.depth + 2)]
        stages += [(self.finish, True)]

        def iteration(i, carried):
            for at, (stage, summed_only) in enumerate(stages):
                index = i - at
                here = jnp.logical_and(index >= 0, index < self.pairs)
                if summed_only and self.locals_at:
                    here = jnp.logical_and(here, jnp.logical_not(self.is_local(index)))

                @pl.when(here)
                def _():
                    for kind in range(2):
                        stage(kind, index)

            if task is not None:
                task(i)
            return carried

        lax.fori_loop(0, self.pairs + len(stages) - 1, iteration, 0)


def reduce_kernel(entries, row_count, shards, *refs):
    count = len(entries)
    xs, gs, outs = refs[:count], refs[count : 2 * count], refs[2 * count : 3 * count]
    load_x, load_g, *scratch = refs[3 * count :]
    exchange = Exchange(entries, row_count, shards, outs, scratch)
    copies = []
    for at, (x_first, x_count, g_first, g_count, _) in enumerate(entries):
        x_part = exchange.x_all.at[:, :, pl.ds(x_first, x_count)]
        g_part = exchange.g_all.at[:, pl.ds(g_first * COLS, g_count * COLS)]
        copies.append(pltpu.make_async_copy(xs[at], x_part, load_x.at[at]))
        copies.append(pltpu.make_async_copy(gs[at], g_part, load_g.at[at]))
    for copy in copies:
        copy.start()
    exchange.meet()
    for copy in copies:
        copy.wait()
    exchange.run(None)


def reduce_gradients(pairs, row_count, shards, collective_id):
    block_rows, tokens = pairs[0][0].shape[3:]
    entries, x_blocks, g_blocks, chunks = reduce_entries(
        [(x.shape[2], g.shape[1] // COLS) for x, g in pairs]
    )
    return pl.pallas_call(
        functools.partial(reduce_kernel, entries, row_count, shards),
        out_shape=[
            jax.ShapeDtypeStruct((x_count * block_rows, g_count * COLS), jnp.bfloat16)
            for _, x_count, _, g_count, _ in entries
        ],
        in_specs=[pl.BlockSpec(memory_space=pl.ANY)] * (2 * len(pairs)),
        out_specs=[pl.BlockSpec(memory_space=pl.ANY)] * len(pairs),
        scratch_shapes=[
            pltpu.SemaphoreType.DMA((len(pairs),)),
            pltpu.SemaphoreType.DMA((len(pairs),)),
            *exchange_scratch(row_count, shards, block_rows, x_blocks, g_blocks, tokens),
        ],
        compiler_params=pltpu.CompilerParams(
            collective_id=collective_id, has_side_effects=True, vmem_limit_bytes=52 * 2**20
        ),
        cost_estimate=pl.CostEstimate(
            flops=2 * chunks * shards * block_rows * COLS * tokens,
            bytes_accessed=2 * chunks * block_rows * COLS,
            transcendentals=0,
        ),
    )(*[x for x, _ in pairs], *[g for _, g in pairs])


def body(
    tokens,
    lengths,
    mixer_gain,
    mixer_input,
    mixer_kernel,
    mixer_output,
    first_gain,
    first_gate,
    first_up,
    first_down,
    attend_gain,
    query_weight,
    key_weight,
    value_weight,
    query_gain,
    key_gain,
    attend_output,
    second_gain,
    second_gate,
    second_up,
    second_down,
    cotangent,
):
    length = tokens.shape[1]
    positions = lax.axis_index("seq") * length + jnp.arange(length, dtype=jnp.int32)
    segment, seg_start = segment_info(lengths, positions)
    offsets = positions[None, :] - seg_start
    hidden = tokens.astype(jnp.float32)
    hidden, mixer_back = mixer_block(
        hidden, mixer_gain, mixer_input, mixer_kernel, mixer_output, seg_start, positions
    )
    hidden, first_back = feed_block(hidden, first_gain, first_gate, first_up, first_down)
    hidden, attend_back = attend_block(
        hidden,
        lengths,
        attend_gain,
        query_weight,
        key_weight,
        value_weight,
        query_gain,
        key_gain,
        attend_output,
        segment,
        positions,
        offsets,
    )
    hidden, second_back = feed_block(hidden, second_gain, second_gate, second_up, second_down)
    gradient = cotangent.astype(jnp.float32)
    gradient, second_grads = second_back(gradient)
    gradient, attend_grads = attend_back(gradient)
    gradient, first_grads = first_back(gradient)
    gradient, mixer_grads = mixer_back(gradient)
    second_gain_sum, second_wide, second_down_pair = second_grads
    attend_gain_sum, attend_wide, query_gain_sum, key_gain_sum, attend_output_pair = attend_grads
    first_gain_sum, first_wide, first_down_pair = first_grads
    mixer_gain_sum, mixer_input_pair, mixer_kernel_sum, mixer_output_pair = mixer_grads
    row_count, shards = lax.axis_size("row"), lax.axis_size("seq")
    block_rows = math.gcd(tokens.shape[2] // shards, first_down.shape[0] // shards)

    def operands(pair):
        inputs, gradient_low = pair
        token_count = inputs.shape[0] * inputs.shape[1]
        inputs = inputs.reshape(token_count, -1).T
        blocks = inputs.shape[0] // shards // block_rows
        return (
            inputs.reshape(shards // 2, 2, blocks, block_rows, token_count),
            gradient_low.reshape(token_count, -1),
        )

    wide_vectors = jnp.concatenate(
        [
            mixer_kernel_sum,
            jnp.stack([mixer_gain_sum, first_gain_sum, attend_gain_sum, second_gain_sum]),
        ]
    )
    vector_count = wide_vectors.shape[0]
    vectors = jnp.concatenate(
        [
            part.reshape(-1, shards, part.shape[-1] // shards)
            .transpose(1, 0, 2)
            .reshape(shards, -1)
            for part in (wide_vectors, jnp.stack([query_gain_sum, key_gain_sum]))
        ],
        axis=1,
    )
    vector_rows = -(-vectors.shape[1] // COLS)
    token_count = tokens.shape[0] * tokens.shape[1]
    vectors = jnp.pad(vectors, ((0, 0), (0, vector_rows * COLS - vectors.shape[1])))
    vectors = vectors.reshape(shards * vector_rows, COLS).astype(jnp.bfloat16)
    vectors = jnp.pad(vectors, ((0, token_count - shards * vector_rows), (0, 0)))
    shard_at = lax.broadcasted_iota(jnp.int32, (shards, 2 * block_rows, token_count), 0)
    row_at = lax.broadcasted_iota(jnp.int32, (shards, 2 * block_rows, token_count), 1)
    token_at = lax.broadcasted_iota(jnp.int32, (shards, 2 * block_rows, token_count), 2)
    picks = (row_at < vector_rows) & (token_at == shard_at * vector_rows + row_at)
    picks = picks.astype(jnp.bfloat16).reshape(shards // 2, 2, 2, block_rows, token_count)
    (
        grad_second_down,
        second_both,
        grad_attend_output,
        attend_three,
        grad_first_down,
        first_both,
        grad_mixer_output,
        grad_mixer_input,
        vector_sums,
    ) = reduce_gradients(
        [
            operands(second_down_pair),
            operands(second_wide),
            operands(attend_output_pair),
            operands(attend_wide),
            operands(first_down_pair),
            operands(first_wide),
            operands(mixer_output_pair),
            operands(mixer_input_pair),
            (picks, vectors),
        ],
        row_count,
        shards,
        0,
    )

    def single(value):
        return value.astype(jnp.float32)

    hidden_columns = first_gate.shape[1]
    query_columns, key_columns = query_weight.shape[1], key_weight.shape[1]
    vector_sums = single(vector_sums[:vector_rows]).reshape(-1)
    width = tokens.shape[2] // shards
    wide_sums = vector_sums[: vector_count * width].reshape(vector_count, width)
    head_width = HEAD_DIM // shards
    head_sums = vector_sums[vector_count * width :][: 2 * head_width].reshape(2, head_width)
    return (
        hidden.astype(jnp.bfloat16),
        gradient.astype(jnp.bfloat16),
        wide_sums[3],
        single(grad_mixer_input),
        wide_sums[:3],
        single(grad_mixer_output),
        wide_sums[4],
        single(first_both[:, :hidden_columns]),
        single(first_both[:, hidden_columns:]),
        single(grad_first_down),
        wide_sums[5],
        single(attend_three[:, :query_columns]),
        single(attend_three[:, query_columns : query_columns + key_columns]),
        single(attend_three[:, query_columns + key_columns :]),
        head_sums[0],
        head_sums[1],
        single(grad_attend_output),
        wide_sums[6],
        single(second_both[:, :hidden_columns]),
        single(second_both[:, hidden_columns:]),
        single(grad_second_down),
    )


def dot_nt(left, right):
    return lax.dot_general(
        left, right, (((1,), (1,)), ((), ())), preferred_element_type=jnp.float32
    )


def dot_tn(left, right):
    return lax.dot_general(
        left, right, (((0,), (0,)), ((), ())), preferred_element_type=jnp.float32
    )


def lanes_below(shape, bound, period):
    return lax.rem(lax.broadcasted_iota(jnp.int32, shape, len(shape) - 1), period) < bound


def two_heads(pair, low):
    pair = pair.astype(jnp.float32)
    turned = pltpu.roll(pair, HEAD_DIM, 1)
    first = lanes_below(pair.shape, HEAD_DIM, 2 * HEAD_DIM)
    if low:
        parts = [jnp.where(first, pair, 0.0), jnp.where(first, turned, 0.0)]
    else:
        parts = [jnp.where(first, 0.0, turned), jnp.where(first, 0.0, pair)]
    return jnp.concatenate(parts, axis=0).astype(jnp.bfloat16)


def segment_start(lengths, which, place):
    end, start = jnp.int32(0), jnp.zeros(place.shape, jnp.int32)
    for number in range(lengths.shape[1]):
        end = end + lengths[which, number]
        start = jnp.where(place >= end, end, start)
    return start


def both_halves(value):
    value = jnp.broadcast_to(value, (8,) + value.shape[1:])
    return (value + pltpu.roll(value, HEAD_DIM, 1))[0:1]


def head_tools(lane):
    head_of = lax.broadcasted_iota(jnp.int32, (lane, lane), 0) // HEAD_DIM
    ones = head_of == lax.broadcasted_iota(jnp.int32, (lane, lane), 1) // HEAD_DIM
    ones = ones.astype(jnp.float32).astype(jnp.bfloat16)

    def head_mean(value):
        total = jnp.dot(value.astype(jnp.bfloat16), ones, preferred_element_type=jnp.float32)
        return total * (1.0 / HEAD_DIM)

    def turn(value):
        half = HEAD_DIM // 2
        first = lanes_below(value.shape, half, HEAD_DIM)
        return jnp.where(first, pltpu.roll(value, lane - half, 1), pltpu.roll(value, half, 1))

    return head_mean, turn


def forward_kernel(names, out_names, scratch_names, shards, *refs):
    at = types.SimpleNamespace(**dict(zip(names + out_names + scratch_names, refs)))
    row, seq = lax.axis_index("row"), lax.axis_index("seq")
    tokens, width = at.low_one.shape
    rows, total_length = at.both.shape[:2]
    length = tokens // rows
    lane = 2 * HEAD_DIM
    blocks = width // COLS
    hidden_blocks = at.first_gate.shape[1] // COLS
    bits = [lax.rem(seq // (1 << bit), 2) for bit in range(3)]
    partner = [seq + (1 << bit) * (1 - 2 * bits[bit]) for bit in range(3)]
    head_mean, turn = head_tools(lane)

    ahead = at.tiles_a.shape[0]

    def tile_copies(step, slot):
        name, j = step
        b, c = at.tiles_b.at[slot], at.tiles_c.at[slot]

        def columns(block):
            return pl.ds(block * COLS if isinstance(block, int) else pl.multiple_of(block * COLS, COLS), COLS)

        if name == MIXER_INPUT:
            first, second = ((0, 4), (1, 5), (2, 3))[j]
            moves = [
                (at.mixer_input.at[:, columns(first)], b),
                (at.mixer_input.at[:, columns(second)], c),
            ]
        elif name == KEYS:
            moves = [(at.key_weight, b), (at.value_weight, c)]
        elif name == FIRST:
            moves = [
                (at.first_gate.at[:, columns(j)], b),
                (at.first_up.at[:, columns(j)], c),
                (at.first_down.at[columns(j)], at.tiles_a.at[slot]),
            ]
        else:
            matrix = {
                MIXER_OUTPUT: at.mixer_output,
                QUERIES: at.query_weight,
                ATTEND_OUTPUT: at.attend_output,
            }[name]
            moves = [(matrix.at[:, columns(0)], b), (matrix.at[:, columns(1)], c)]
        return [
            pltpu.make_async_copy(source, target, at.tile_sem.at[slot, place])
            for place, (source, target) in enumerate(moves)
        ]

    steps = [(MIXER_INPUT, 0), (MIXER_INPUT, 1), (MIXER_INPUT, 2), (MIXER_OUTPUT, 0)]
    first_at = len(steps)
    steps += [(FIRST, j) for j in range(hidden_blocks)]
    steps += [(KEYS, 0), (QUERIES, 0), (ATTEND_OUTPUT, 0)]

    def begin(number):
        for copy in tile_copies(steps[number], number % ahead):
            copy.wait()
        later = number + ahead - 1
        if later < len(steps):
            for copy in tile_copies(steps[later], later % ahead):
                copy.start()
        return number % ahead

    saves = []

    def save(source, target):
        copy = pltpu.make_async_copy(source, target, at.save_sem.at[len(saves)])
        copy.start()
        saves.append(copy)

    def normed(hidden, number, target):
        for first in range(0, tokens, 64):
            span = pl.ds(first, 64)
            value = hidden[span]
            inverse = lax.rsqrt(jnp.mean(value * value, axis=-1, keepdims=True) + EPS)
            value = value * inverse * at.vectors[number : number + 1, :]
            target[span] = value.astype(jnp.bfloat16)

    def times(left, tile):
        return jnp.dot(left[...], tile, preferred_element_type=jnp.float32)

    token_load = pltpu.make_async_copy(at.tokens, at.attended, at.load_sem.at[0])
    token_load.start()
    for number in range(ahead - 1):
        for copy in tile_copies(steps[number], number):
            copy.start()
    at.halo_in[...] = jnp.zeros_like(at.halo_in)
    barrier = pltpu.get_barrier_semaphore()
    others = partner + [lax.rem(seq + step, shards) for step in (1, shards - 1)]
    for other in others:
        pl.semaphore_signal(barrier, inc=1, device_id=(row, other), device_id_type=MESH)
    at.vectors[...] = jnp.zeros_like(at.vectors)
    gains = [at.second_gain, at.attend_gain, at.first_gain, at.mixer_gain]
    for number, gain in enumerate(gains):
        at.vectors[number : number + 1, :] = gain[...].astype(jnp.float32).reshape(1, width)
    at.vectors[4:7, :] = at.mixer_kernel[...].astype(jnp.float32)
    for number, gain in enumerate((at.query_gain, at.key_gain)):
        at.vectors[7 + number : 8 + number, 0:HEAD_DIM] = (
            gain[...].astype(jnp.float32).reshape(1, HEAD_DIM)
        )
    half = HEAD_DIM // 2
    lane_at = lax.broadcasted_iota(jnp.int32, (length, lane), 1)
    power = lax.rem(lane_at, half).astype(jnp.float32) * (-2.0 * math.log(THETA) / HEAD_DIM)
    inverse = jnp.exp(power)
    side = jnp.where(lanes_below((length, lane), half, HEAD_DIM), -1.0, 1.0)
    place = lax.broadcasted_iota(jnp.int32, (length, lane), 0) + seq * length
    for which in range(rows):
        start = segment_start(at.lengths, which, place)
        angle = (place - start).astype(jnp.float32) * inverse
        span = pl.ds(which * length, length)
        at.seg_start[span] = start
        at.cosine[span] = jnp.cos(angle)
        at.sine[span] = jnp.sin(angle) * side
    save(at.vectors, at.vectors_out)
    save(at.cosine, at.cosine_out)
    save(at.sine, at.sine_out)
    token_load.wait()
    at.hidden_a[...] = at.attended[...].astype(jnp.float32)
    save(at.hidden_a, at.hidden_zero)
    normed(at.hidden_a, 3, at.low_one)
    pl.semaphore_wait(barrier, len(others))

    for number, (first, second) in enumerate(((0, 4), (1, 5))):
        slot = begin(number)
        entry = times(at.low_one, at.tiles_b[slot])
        carrier = times(at.low_one, at.tiles_c[slot])
        columns = pl.ds(number * COLS, COLS)
        product = (entry * carrier).astype(jnp.bfloat16)
        at.mixed_low[pl.ds(3 * tokens, tokens), columns] = product
        product = product.astype(jnp.float32)
        at.gates_low[pl.ds(0, tokens), columns] = entry.astype(jnp.bfloat16)
        at.gates_low[pl.ds(2 * tokens, tokens), columns] = carrier.astype(jnp.bfloat16)
        for which in range(rows):
            last = product[(which + 1) * length - 8 : (which + 1) * length]
            at.halo_out[which, :, columns] = last
    halo = pltpu.make_async_remote_copy(
        src_ref=at.halo_out,
        dst_ref=at.halo_in,
        send_sem=at.halo_sem.at[0],
        recv_sem=at.halo_sem.at[1],
        device_id=(row, jnp.minimum(seq + 1, shards - 1)),
        device_id_type=MESH,
    )

    @pl.when(seq < shards - 1)
    def _():
        halo.start()

    slot = begin(2)
    for block, tile in enumerate((at.tiles_b, at.tiles_c)):
        at.work[:, pl.ds(block * COLS, COLS)] = times(at.low_one, tile[slot])

    @pl.when(seq > 0)
    def _():
        halo.wait_recv()

    @pl.when(seq < shards - 1)
    def _():
        halo.wait_send()

    position = lax.rem(lax.broadcasted_iota(jnp.int32, (tokens, lane), 0), length) + seq * length
    keep_one = position - 1 >= at.seg_start[...]
    keep_two = position - 2 >= at.seg_start[...]
    edge = lax.broadcasted_iota(jnp.int32, (8, lane), 0)
    for part_at in range(0, width, lane):
        columns = pl.ds(part_at, lane)
        current = at.mixed_low[pl.ds(3 * tokens, tokens), columns].astype(jnp.float32)
        shifted = []
        for steps_back, keep in ((1, keep_one), (2, keep_two)):
            back = pltpu.roll(current, steps_back, 0)
            pieces = []
            for which in range(rows):
                before = pltpu.roll(at.halo_in[which, :, columns], steps_back, 0)
                start = which * length
                pieces.append(jnp.where(edge < steps_back, before, back[start : start + 8]))
                pieces.append(back[start + 8 : start + length])
            back = jnp.concatenate(pieces, axis=0)
            shifted.append(jnp.where(keep, back, 0.0))
        one, two = shifted
        convolved = at.vectors[6:7, columns] * current + at.vectors[5:6, columns] * one
        convolved += at.vectors[4:5, columns] * two
        exit_gate = at.work[:, columns]
        at.mixed_low[pl.ds(0, tokens), columns] = convolved.astype(jnp.bfloat16)
        at.mixed_low[pl.ds(tokens, tokens), columns] = two.astype(jnp.bfloat16)
        at.mixed_low[pl.ds(2 * tokens, tokens), columns] = one.astype(jnp.bfloat16)
        at.gates_low[pl.ds(tokens, tokens), columns] = exit_gate.astype(jnp.bfloat16)
        at.low_two[:, columns] = (exit_gate * convolved).astype(jnp.bfloat16)
    save(at.mixed_low, at.mixer_saved)
    save(at.gates_low, at.projected)

    def add_output(number, left, before, after):
        slot = begin(number)
        for block, tile in enumerate((at.tiles_b, at.tiles_c)):
            columns = pl.ds(block * COLS, COLS)
            after[:, columns] = before[:, columns] + times(left, tile[slot])

    add_output(3, at.low_two, at.hidden_a, at.hidden_b)
    save(at.hidden_b, at.hidden_one)
    normed(at.hidden_b, 2, at.low_three)
    at.hidden_c[...] = at.hidden_b[...]

    def feed_tile(j, carried):
        slot = lax.rem(first_at + j, ahead)
        for copy in tile_copies((FIRST, j), slot):
            copy.wait()
        later = j + ahead - 1
        later_slot = lax.rem(first_at + later, ahead)

        @pl.when(later < hidden_blocks)
        def _():
            for copy in tile_copies((FIRST, later), later_slot):
                copy.start()

        for past, step in enumerate(steps[first_at + hidden_blocks :][: ahead - 1]):

            @pl.when(later == hidden_blocks + past)
            def _():
                for copy in tile_copies(step, later_slot):
                    copy.start()

        gate_value = times(at.low_three, at.tiles_b[slot])
        up_value = times(at.low_three, at.tiles_c[slot])
        columns = pl.ds(pl.multiple_of(j * COLS, COLS), COLS)
        at.gate_low[:, columns] = gate_value.astype(jnp.bfloat16)
        at.up_low[:, columns] = up_value.astype(jnp.bfloat16)
        active = gate_value / (1.0 + jnp.exp(-gate_value)) * up_value
        active = active.astype(jnp.bfloat16)
        at.active_low[:, columns] = active
        at.hidden_c[...] += jnp.dot(
            active, at.tiles_a[slot], preferred_element_type=jnp.float32
        )
        return carried

    lax.fori_loop(0, hidden_blocks, feed_tile, 0)
    save(at.hidden_c, at.hidden_two)
    save(at.gate_low, at.gate_one)
    save(at.up_low, at.up_one)
    normed(at.hidden_c, 1, at.low_four)

    def head_path(raw, gain):
        value = raw * lax.rsqrt(head_mean(raw * raw) + EPS) * gain
        return value * at.cosine[...] + turn(value) * at.sine[...]

    keys_at = first_at + hidden_blocks
    slot = begin(keys_at)
    at.work[:, pl.ds(0, width // 2)] = times(at.low_four, at.tiles_b[slot])
    at.work[:, pl.ds(width // 2, width // 2)] = times(at.low_four, at.tiles_c[slot])
    at.keys_low[...] = at.work[:, pl.ds(0, width // 2)].astype(jnp.bfloat16)
    save(at.keys_low, at.keys_raw)
    first = lanes_below((tokens, lane), HEAD_DIM, lane)
    own = pl.ds(pl.multiple_of(seq * length, length), length)
    for pair in range(width // lane // 2):
        keys = head_path(at.work[:, pl.ds(pair * lane, lane)], both_halves(at.vectors[8:9, pl.ds(0, lane)]))
        values = at.work[:, pl.ds(width // 2 + pair * lane, lane)]
        even = jnp.where(first, keys, pltpu.roll(values, HEAD_DIM, 1)).astype(jnp.bfloat16)
        odd = jnp.where(first, pltpu.roll(keys, HEAD_DIM, 1), values).astype(jnp.bfloat16)
        for which, value in enumerate((even, odd)):
            columns = pl.ds((2 * pair + which) * lane, lane)
            at.both[:, own, columns] = value.reshape(rows, length, lane)

    def piece(owner, which=None):
        span = pl.ds(pl.multiple_of(owner * length, length), length)
        return at.both.at[:, span] if which is None else at.both.at[which, span]

    def send(number, part, bit):
        return pltpu.make_async_remote_copy(
            src_ref=part,
            dst_ref=part,
            send_sem=at.gather_send.at[number],
            recv_sem=at.gather_recv.at[number],
            device_id=(row, partner[bit]),
            device_id_type=MESH,
        )

    def flip(owner, bit):
        value = lax.rem(owner // (1 << bit), 2)
        return owner + (1 << bit) * (1 - 2 * value)

    across, along = partner[1], partner[2]
    corner = flip(across, 2)
    near_zero, far_one = send(0, piece(seq, 0), 1), send(1, piece(seq, 1), 2)
    near_one, far_zero = send(2, piece(seq, 1), 1), send(3, piece(seq, 0), 2)
    twin = send(4, piece(seq), 0)
    for copy in (near_zero, far_one, near_one, far_zero, twin):
        copy.start()

    slot = begin(keys_at + 1)
    for block, tile in enumerate((at.tiles_b, at.tiles_c)):
        at.work[:, pl.ds(block * COLS, COLS)] = times(at.low_four, tile[slot])
    at.queries_low[...] = at.work[...].astype(jnp.bfloat16)
    save(at.queries_low, at.queries_raw)
    for head in range(width // lane):
        columns = pl.ds(head * lane, lane)
        query = head_path(at.work[:, columns], both_halves(at.vectors[7:8, pl.ds(0, lane)])).astype(jnp.bfloat16)
        query = query * jnp.bfloat16(HEAD_DIM**-0.5)
        at.scaled[:, columns] = query
        for which in range(rows):
            at.paired[which * (width // lane) + head] = two_heads(
                query[which * length : (which + 1) * length], True
            )
    save(at.scaled, at.queries_out)

    def transposed(low, target):
        for first in range(0, tokens, lane):
            span = pl.ds(first, lane)
            value = low[span].astype(jnp.float32).T.astype(jnp.bfloat16)
            target[:, :, :, :, span] = value.reshape(target.shape[:-1] + (lane,))

    transposed(at.low_one, at.turned_one)
    save(at.turned_one, at.mixer_in_x)
    near_zero.wait()
    far_one.wait()
    near_forward = send(5, piece(across, 0), 2)
    far_forward = send(6, piece(along, 1), 1)
    near_forward.start()
    far_forward.start()
    transposed(at.low_two, at.turned_two)
    save(at.turned_two, at.gated_x)

    at.sums[...] = jnp.zeros_like(at.sums)
    pairs_of = width // lane
    together = 4
    chip = seq // 2

    def attend(other):
        @pl.when(other <= chip)
        def _():
            span = pl.ds(pl.multiple_of(other * 2 * length, 2 * length), 2 * length)
            shape = (length, 2 * length)
            key_at = lax.broadcasted_iota(jnp.int32, shape, 1) + other * 2 * length
            query_at = lax.broadcasted_iota(jnp.int32, shape, 0) + seq * length
            first = lanes_below((2 * length, lane), HEAD_DIM, lane)
            for which in range(rows):
                start = at.seg_start[pl.ds(which * length, length)]
                start = jnp.concatenate([start, start], axis=1)
                allowed = jnp.logical_and(key_at >= start, key_at <= query_at)
                allowed = jnp.concatenate([allowed, allowed], axis=0)

                def some(group, carried):
                    heads = [group * together + head for head in range(together)]
                    boths = [
                        at.both[which, span, pl.ds(pl.multiple_of(head * lane, lane), lane)]
                        for head in heads
                    ]
                    places = [which * pairs_of + head for head in heads]
                    scores = [
                        dot_nt(at.paired[place], both) for place, both in zip(places, boths)
                    ]
                    for place, score, both in zip(places, scores, boths):
                        weights = jnp.where(allowed, jnp.exp(score), 0.0).astype(jnp.bfloat16)
                        right = jnp.where(first, 1.0, both.astype(jnp.float32))
                        at.sums[place] += jnp.dot(
                            weights, right.astype(jnp.bfloat16), preferred_element_type=jnp.float32
                        )
                    return carried

                lax.fori_loop(0, pairs_of // together, some, 0)

    twin.wait()
    attend(chip)
    near_one.wait()
    near_share = send(7, piece(across), 0)
    near_share.start()
    far_zero.wait()
    far_share = send(8, piece(along), 0)
    far_share.start()
    transposed(at.low_three, at.turned_three)
    save(at.turned_three, at.first_in_x)
    near_share.wait()
    attend(across // 2)
    transposed(at.low_four, at.turned_four)
    save(at.turned_four, at.attend_in_x)
    far_share.wait()
    attend(along // 2)

    block_rows = at.turned_active.shape[3]
    x_count = at.turned_active.shape[2]
    for j in range(hidden_blocks):
        for first in range(0, tokens, lane):
            span = pl.ds(first, lane)
            value = at.active_low[span, pl.ds(j * COLS, COLS)].astype(jnp.float32).T
            value = value.astype(jnp.bfloat16)
            for block in range(COLS // block_rows):
                place = j * (COLS // block_rows) + block
                shard = place // x_count
                at.turned_active[shard // 2, shard % 2, place % x_count, :, span] = value[
                    block * block_rows : (block + 1) * block_rows
                ]
    save(at.turned_active, at.active_x)
    near_forward.wait()
    far_forward.wait()
    corner_share = send(9, piece(corner), 0)
    corner_share.start()
    corner_share.wait()
    save(at.both, at.keys_values)
    attend(corner // 2)

    first = lanes_below((length, lane), HEAD_DIM, lane)
    for which in range(rows):
        span = pl.ds(which * length, length)
        for head in range(pairs_of):
            value = at.sums[which * pairs_of + head]
            value = value * (1.0 / pltpu.roll(value, HEAD_DIM, 1))
            value = jnp.where(first, pltpu.roll(value[:length], HEAD_DIM, 1), value[length:])
            at.attended[span, pl.ds(head * lane, lane)] = value.astype(jnp.bfloat16)
    add_output(keys_at + 2, at.attended, at.hidden_c, at.hidden_d)
    save(at.hidden_d, at.hidden_three)
    transposed(at.attended, at.turned_five)
    save(at.turned_five, at.attended_x)
    for copy in saves:
        copy.wait()


def forward(arrays, resident, rows, shards, collective_id):
    tokens, width = arrays["tokens"].shape
    hidden_columns = arrays["first_gate"].shape[1]
    length = tokens // rows
    total_length = length * shards
    block_rows = math.gcd(width // shards, hidden_columns // shards)
    low, full = jnp.bfloat16, jnp.float32

    def x_shape(columns):
        return (shards // 2, 2, columns // shards // block_rows, block_rows, tokens)

    outs = dict(
        hidden_zero=((tokens, width), full),
        hidden_one=((tokens, width), full),
        hidden_two=((tokens, width), full),
        hidden_three=((tokens, width), full),
        gate_one=((tokens, hidden_columns), low),
        up_one=((tokens, hidden_columns), low),
        queries_out=((tokens, width), low),
        queries_raw=((tokens, width), low),
        keys_raw=((tokens, width // 2), low),
        keys_values=((rows, total_length, width), low),
        mixer_saved=((4 * tokens, width), low),
        projected=((3 * tokens, width), low),
        mixer_in_x=(x_shape(width), low),
        gated_x=(x_shape(width), low),
        first_in_x=(x_shape(width), low),
        attend_in_x=(x_shape(width), low),
        attended_x=(x_shape(width), low),
        active_x=(x_shape(hidden_columns), low),
        vectors_out=((16, width), full),
        cosine_out=((tokens, 2 * HEAD_DIM), full),
        sine_out=((tokens, 2 * HEAD_DIM), full),
    )
    pairs = rows * width // (2 * HEAD_DIM)
    dma = pltpu.SemaphoreType.DMA
    scratch = dict(
        tiles_a=pltpu.VMEM((4, COLS, width), low),
        tiles_b=pltpu.VMEM((4, width, COLS), low),
        tiles_c=pltpu.VMEM((4, width, COLS), low),
        hidden_a=pltpu.VMEM((tokens, width), full),
        hidden_b=pltpu.VMEM((tokens, width), full),
        hidden_c=pltpu.VMEM((tokens, width), full),
        hidden_d=pltpu.VMEM((tokens, width), full),
        low_one=pltpu.VMEM((tokens, width), low),
        low_two=pltpu.VMEM((tokens, width), low),
        low_three=pltpu.VMEM((tokens, width), low),
        low_four=pltpu.VMEM((tokens, width), low),
        attended=pltpu.VMEM((tokens, width), low),
        work=pltpu.VMEM((tokens, width), full),
        mixed_low=pltpu.VMEM((4 * tokens, width), low),
        gates_low=pltpu.VMEM((3 * tokens, width), low),
        gate_low=pltpu.VMEM((tokens, hidden_columns), low),
        up_low=pltpu.VMEM((tokens, hidden_columns), low),
        active_low=pltpu.VMEM((tokens, hidden_columns), low),
        keys_low=pltpu.VMEM((tokens, width // 2), low),
        queries_low=pltpu.VMEM((tokens, width), low),
        scaled=pltpu.VMEM((tokens, width), low),
        both=pltpu.VMEM((rows, total_length, width), low),
        paired=pltpu.VMEM((pairs, 2 * length, 2 * HEAD_DIM), low),
        sums=pltpu.VMEM((pairs, 2 * length, 2 * HEAD_DIM), full),
        turned_one=pltpu.VMEM(x_shape(width), low),
        turned_two=pltpu.VMEM(x_shape(width), low),
        turned_three=pltpu.VMEM(x_shape(width), low),
        turned_four=pltpu.VMEM(x_shape(width), low),
        turned_five=pltpu.VMEM(x_shape(width), low),
        turned_active=pltpu.VMEM(x_shape(hidden_columns), low),
        vectors=pltpu.VMEM((16, width), full),
        cosine=pltpu.VMEM((tokens, 2 * HEAD_DIM), full),
        sine=pltpu.VMEM((tokens, 2 * HEAD_DIM), full),
        seg_start=pltpu.VMEM((tokens, 2 * HEAD_DIM), jnp.int32),
        halo_out=pltpu.VMEM((rows, 8, width), full),
        halo_in=pltpu.VMEM((rows, 8, width), full),
        tile_sem=dma((4, 3)),
        load_sem=dma((1,)),
        save_sem=dma((len(outs),)),
        halo_sem=dma((2,)),
        gather_send=dma((10,)),
        gather_recv=dma((10,)),
    )
    spaces = dict.fromkeys(resident, pltpu.VMEM)
    spaces["lengths"] = pltpu.SMEM
    any_space = pl.BlockSpec(memory_space=pl.ANY)
    weights = sum(value.size for value in arrays.values())
    results = pl.pallas_call(
        functools.partial(forward_kernel, list(arrays), list(outs), list(scratch), shards),
        out_shape=[jax.ShapeDtypeStruct(shape, kind) for shape, kind in outs.values()],
        in_specs=[pl.BlockSpec(memory_space=spaces.get(name, pl.ANY)) for name in arrays],
        out_specs=[any_space] * len(outs),
        scratch_shapes=list(scratch.values()),
        compiler_params=pltpu.CompilerParams(
            collective_id=collective_id, has_side_effects=True, vmem_limit_bytes=60 * 2**20
        ),
        cost_estimate=pl.CostEstimate(
            flops=2 * weights * tokens, bytes_accessed=2 * weights, transcendentals=0
        ),
    )(*arrays.values())
    return dict(zip(outs, results))


SECOND, ATTEND_OUTPUT, ATTENTION, QUERIES, KEYS, FIRST, MIXER_OUTPUT, HALO, MIXER_INPUT, CLOSE = range(10)
BACKWARD_STARTS = {
    SECOND: 0,
    ATTEND_OUTPUT: 8,
    ATTENTION: 10,
    QUERIES: 26,
    KEYS: 31,
    FIRST: 32,
    MIXER_OUTPUT: 41,
    HALO: 43,
    MIXER_INPUT: 44,
    CLOSE: 47,
}
LOCAL_PAIRS = (18, 19, 26, 27)


def backward_kernel(names, entries, row_count, shards, *refs):
    at = types.SimpleNamespace(**dict(zip(names, refs)))
    outs = refs[len(names) : len(names) + len(entries)]
    token_out, mixed_out = refs[len(names) + len(entries) : len(names) + len(entries) + 2]
    scratch = refs[len(names) + len(entries) + 2 :]
    (
        tiles_a,
        tiles_b,
        tiles_c,
        saved,
        keys_values,
        key_grads,
        key_sums,
        queries,
        attended_grad,
        wide,
        queries_raw,
        keys_raw,
        gradient,
        normed_grad,
        hidden,
        halo_out,
        halo_in,
        small,
        tile_sem,
        load_sem,
        halo_sem,
        *scratch,
    ) = scratch
    local = types.SimpleNamespace()
    exchange = Exchange(entries, row_count, shards, outs, scratch, LOCAL_PAIRS, local)
    x_all, g_all = exchange.x_all, exchange.g_all
    seq, row = exchange.seq, exchange.row
    tokens, width = gradient.shape
    rows = keys_values.shape[0]
    length = tokens // rows
    hidden_blocks = at.first_gate.shape[1] // COLS
    blocks = width // COLS
    g_at = [entry[2] * COLS for entry in entries]
    second_wide, second_down, output_at, heads_at, first_down, first_wide = g_at[:6]
    mixer_out_at, mixer_in_at, small_at = g_at[6:]
    starts = BACKWARD_STARTS

    def local_place(kind, index):
        first, second, third, fourth = LOCAL_PAIRS
        row_at = jnp.where(index >= third, 1, 0)
        quad = jnp.where(jnp.logical_or(index == second, index == fourth), 1, 0)
        return row_at, pl.ds(pl.multiple_of(quad * COLS, COLS), COLS)

    def part(kind, index, side):
        row_at, columns = local_place(kind, index)
        return key_grads[row_at, :, side, kind, :, columns]

    def take(kind, index, total):
        row_at, columns = local_place(kind, index)
        key_sums[row_at, kind, :, columns] = total.astype(jnp.bfloat16)

    local.part, local.take = part, take

    def tile_copies(name, j, slot):
        columns = pl.ds(pl.multiple_of(j * COLS, COLS), COLS)
        a, b, c = tiles_a.at[slot], tiles_b.at[slot], tiles_c.at[slot]
        if name == SECOND:
            moves = [
                (at.second_gate.at[:, columns], b),
                (at.second_up.at[:, columns], c),
                (at.second_down.at[columns], a),
            ]
        elif name == FIRST:
            moves = [
                (at.first_down.at[columns], a),
                (at.first_gate.at[:, columns], b),
                (at.first_up.at[:, columns], c),
                (at.gate_one.at[:, columns], saved.at[slot, 0]),
                (at.up_one.at[:, columns], saved.at[slot, 1]),
            ]
        elif name == ATTEND_OUTPUT:
            moves = [(at.attend_output.at[columns], a)]
        elif name == MIXER_OUTPUT:
            moves = [(at.mixer_output.at[columns], a)]
        elif name == QUERIES:
            moves = [
                (at.query_weight.at[:, pl.ds(0, COLS)], b),
                (at.query_weight.at[:, pl.ds(COLS, COLS)], c),
            ]
        elif name == KEYS:
            moves = [(at.key_weight, b), (at.value_weight, c)]
        else:
            even = pl.multiple_of(2 * j * COLS, COLS)
            odd = pl.multiple_of((2 * j + 1) * COLS, COLS)
            moves = [
                (at.mixer_input.at[:, pl.ds(even, COLS)], b),
                (at.mixer_input.at[:, pl.ds(odd, COLS)], c),
            ]
        return [
            pltpu.make_async_copy(source, target, tile_sem.at[slot, place])
            for place, (source, target) in enumerate(moves)
        ]

    steps = [
        (SECOND, hidden_blocks),
        (ATTEND_OUTPUT, blocks),
        (QUERIES, 1),
        (KEYS, 1),
        (FIRST, hidden_blocks),
        (MIXER_OUTPUT, blocks),
        (MIXER_INPUT, 3 * blocks // 2),
    ]
    first_step, total = {}, 0
    for name, number in steps:
        first_step[name] = total
        total += number
    order = [name for name, _ in steps]
    numbers = dict(steps)

    def tile_step(name, j):
        slot = (first_step[name] + j) % 2 if isinstance(j, int) else lax.rem(first_step[name] + j, 2)
        for copy in tile_copies(name, j, slot):
            copy.wait()

        @pl.when(j + 1 < numbers[name])
        def _():
            for copy in tile_copies(name, j + 1, 1 - slot):
                copy.start()

        if name != order[-1]:
            following = order[order.index(name) + 1]

            @pl.when(j + 1 == numbers[name])
            def _():
                for copy in tile_copies(following, 0, 1 - slot):
                    copy.start()

        return slot

    def load(place, source, target):
        return pltpu.make_async_copy(source, target, load_sem.at[place])

    count = len(entries)
    x_loads = [
        load(number, at.xs[number - 2], x_all.at[:, :, pl.ds(x_first, x_count)])
        for number, (x_first, x_count, _, _, _) in enumerate(entries)
        if 2 <= number < count - 1
    ]
    cotangent_load = load(count, at.cotangent, g_all.at[:, pl.ds(second_down, width)])
    middle_loads = [
        load(count + 1, at.queries_out, queries),
        load(count + 2, at.keys_values, keys_values),
        load(count + 5, at.keys_raw, keys_raw),
    ]
    raw_load = load(count + 4, at.queries_raw, queries_raw)
    staged = queries_raw
    late_loads = [
        load(count + 6, at.mixer_saved, keys_values.at[0]),
        load(count + 7, at.projected, keys_values.at[1, pl.ds(0, 3 * tokens)]),
    ]
    hidden_loads = [
        load(count + 8, source, hidden)
        for source in (at.hidden_three, at.hidden_two, at.hidden_one, at.hidden_zero)
    ]
    out_copy = load(count + 9, staged, token_out)
    mixed_copy = load(count + 9, staged, mixed_out)

    hidden_loads[0].start()
    cotangent_load.start()
    for copy in tile_copies(SECOND, 0, 0):
        copy.start()
    for copy in middle_loads + x_loads:
        copy.start()
    normed_grad[...] = jnp.zeros_like(normed_grad)
    small[...] = jnp.zeros_like(small)
    g_all[:, pl.ds(small_at, COLS)] = jnp.zeros((tokens, COLS), jnp.bfloat16)
    wide[...] = jnp.zeros_like(wide)
    hidden_loads[0].wait()
    normed = attended_grad
    x_two = entries[0][0]
    for first in range(0, tokens, 128):
        span = pl.ds(first, 128)
        value = hidden[span]
        inverse = lax.rsqrt(jnp.mean(value * value, axis=-1, keepdims=True) + EPS)
        value = value * inverse * at.vectors[0:1, :]
        normed[span] = value.astype(jnp.bfloat16)
        turned = value.T.astype(jnp.bfloat16)
        shape = x_all.shape[:2] + (2,) + x_all.shape[3:4] + (128,)
        x_all[:, :, x_two : x_two + 2, :, pl.ds(first, 128)] = turned.reshape(shape)
    cotangent_load.wait()
    gradient[...] = g_all[:, pl.ds(second_down, width)].astype(jnp.float32)

    def low_gradient(place):
        g_all[:, pl.ds(place, width)] = gradient[...].astype(jnp.bfloat16)

    def norm_back(number):
        if number > 0:
            hidden_loads[number].wait()
        gain = at.vectors[number : number + 1, :]
        sums = jnp.zeros((1, width), jnp.float32)
        piece = 64
        for first in range(0, tokens, piece):
            span = pl.ds(first, piece)
            value, upper = hidden[span], normed_grad[span]
            inverse = lax.rsqrt(jnp.mean(value * value, axis=-1, keepdims=True) + EPS)
            value = value * inverse
            sums = sums + jnp.sum(upper * value, axis=0, keepdims=True)
            upper = upper * gain
            shift = jnp.mean(upper * value, axis=-1, keepdims=True)
            gradient[span] = gradient[span] + inverse * (upper - value * shift)
        for block in range(blocks):
            place = blocks * number + block
            small[place : place + 1, :] = sums[:, block * COLS : (block + 1) * COLS]
        normed_grad[...] = jnp.zeros_like(normed_grad)
        if number + 1 < len(hidden_loads):
            hidden_loads[number + 1].start()

    def feed_tile(name, j, gradient_at, wide_at):
        slot = tile_step(name, j)
        low = g_all[:, pl.ds(gradient_at, width)]
        active_grad = dot_nt(low, tiles_a[slot])
        if name == SECOND:
            gate_value = jnp.dot(normed[...], tiles_b[slot], preferred_element_type=jnp.float32)
            up_value = jnp.dot(normed[...], tiles_c[slot], preferred_element_type=jnp.float32)
        else:
            gate_value = saved[slot, 0].astype(jnp.float32)
            up_value = saved[slot, 1].astype(jnp.float32)
        share = 1.0 / (1.0 + jnp.exp(-gate_value))
        if name == SECOND:
            active = gate_value * share * up_value
            wide[...] += jnp.dot(
                active.astype(jnp.bfloat16), tiles_a[slot], preferred_element_type=jnp.float32
            )
            turned = active.T.astype(jnp.bfloat16)
            x_down, x_count = entries[1][:2]
            block_rows = x_all.shape[3]
            for block in range(COLS // block_rows):
                place = j * (COLS // block_rows) + block
                shard = place // x_count
                part = turned[block * block_rows : (block + 1) * block_rows]
                x_all[shard // 2, lax.rem(shard, 2), x_down + lax.rem(place, x_count)] = part
        up_grad = (active_grad * gate_value * share).astype(jnp.bfloat16)
        gate_grad = active_grad * up_value * share * (1.0 + gate_value * (1.0 - share))
        gate_grad = gate_grad.astype(jnp.bfloat16)
        gate_place = pl.multiple_of(wide_at + j * COLS, COLS)
        up_place = pl.multiple_of(wide_at + (hidden_blocks + j) * COLS, COLS)
        g_all[:, pl.ds(gate_place, COLS)] = gate_grad
        g_all[:, pl.ds(up_place, COLS)] = up_grad
        normed_grad[...] += dot_nt(gate_grad, tiles_b[slot]) + dot_nt(up_grad, tiles_c[slot])

    def output_tile(name, j, gradient_at, target):
        slot = tile_step(name, j)
        low = g_all[:, pl.ds(gradient_at, width)]
        value = dot_nt(low, tiles_a[slot])
        target[:, j * COLS : (j + 1) * COLS] = value.astype(target.dtype)

    def attention_head(row_at, head):
        span = pl.ds(pl.multiple_of(row_at * length, length), length)
        columns = pl.ds(pl.multiple_of(head * 2 * HEAD_DIM, 2 * HEAD_DIM), 2 * HEAD_DIM)
        query = two_heads(queries[span, columns], True)
        upper = two_heads(attended_grad[span, columns], False)
        both = keys_values[row_at, :, columns]
        key_at = lax.broadcasted_iota(jnp.int32, (both.shape[0], length), 0)
        query_at = lax.broadcasted_iota(jnp.int32, (both.shape[0], length), 1) + seq * length
        start = segment_start(at.lengths, row_at, query_at[0:8])[0:1]
        allowed = jnp.logical_and(key_at >= start, key_at <= query_at)
        weights = jnp.exp(dot_nt(both, query))
        weights = jnp.where(jnp.concatenate([allowed, allowed], axis=1), weights, 0.0)
        weights = weights * (1.0 / jnp.sum(weights, axis=0, keepdims=True))
        weight_grad_value = dot_nt(both, upper)
        delta = jnp.sum(weights * weight_grad_value, axis=0, keepdims=True)
        score_grad = (weights * (weight_grad_value - delta)).astype(jnp.bfloat16)
        both_grad = jnp.dot(score_grad, query, preferred_element_type=jnp.float32)
        both_grad += jnp.dot(
            weights.astype(jnp.bfloat16), upper, preferred_element_type=jnp.float32
        )
        shape = key_grads.shape[1:5] + (2 * HEAD_DIM,)
        key_grads[row_at, :, :, :, :, columns] = both_grad.astype(jnp.bfloat16).reshape(shape)
        query_grad = dot_tn(score_grad, both) * HEAD_DIM ** (-0.5)
        first = lanes_below((length, 2 * HEAD_DIM), HEAD_DIM, 2 * HEAD_DIM)
        wide[span, columns] = jnp.where(
            first, query_grad[:length], pltpu.roll(query_grad[length:], HEAD_DIM, 1)
        )

    lane = 2 * HEAD_DIM
    head_mean, turn = head_tools(lane)

    def head_back(value, raw, gain):
        value = value * at.cosine[...] - turn(value) * at.sine[...]
        raw = raw.astype(jnp.float32)
        inverse = lax.rsqrt(head_mean(raw * raw) + EPS)
        raw = raw * inverse
        sums = jnp.sum(value * raw, axis=0, keepdims=True)
        value = value * gain
        return inverse * (value - raw * head_mean(value * raw)), sums

    head_row = 7 * blocks

    def query_heads():
        sums = jnp.zeros((1, lane), jnp.float32)
        for part_at in range(0, width, lane):
            columns = pl.ds(part_at, lane)
            value, more = head_back(wide[:, columns], queries_raw[:, columns], both_halves(at.vectors[7:8, pl.ds(0, lane)]))
            g_all[:, pl.ds(heads_at + part_at, lane)] = value.astype(jnp.bfloat16)
            sums = sums + more
        small[head_row : head_row + 1, 0:lane] = both_halves(sums)

    def key_heads():
        sums = jnp.zeros((1, lane), jnp.float32)
        first = lanes_below((tokens, lane), HEAD_DIM, lane)
        for pair in range(width // lane // 2):
            even, odd = [
                key_sums[:, :, :, pl.ds((2 * pair + which) * lane, lane)]
                .astype(jnp.float32)
                .reshape(tokens, lane)
                for which in range(2)
            ]
            key_value = jnp.where(first, even, pltpu.roll(odd, HEAD_DIM, 1))
            value_value = jnp.where(first, pltpu.roll(even, HEAD_DIM, 1), odd)
            columns = pl.ds(pair * lane, lane)
            value, more = head_back(key_value, keys_raw[:, columns], both_halves(at.vectors[8:9, pl.ds(0, lane)]))
            place = heads_at + width + pair * lane
            g_all[:, pl.ds(place, lane)] = value.astype(jnp.bfloat16)
            place += width // 2
            g_all[:, pl.ds(place, lane)] = value_value.astype(jnp.bfloat16)
            sums = sums + more
        small[head_row : head_row + 1, lane : 2 * lane] = both_halves(sums)

    def project_back(name, j, even_at, odd_at):
        slot = tile_step(name, j)
        normed_grad[...] += dot_nt(g_all[:, pl.ds(even_at, COLS)], tiles_b[slot]) + dot_nt(
            g_all[:, pl.ds(odd_at, COLS)], tiles_c[slot]
        )

    def halo_copy():
        return pltpu.make_async_remote_copy(
            src_ref=halo_out,
            dst_ref=halo_in,
            send_sem=halo_sem.at[0],
            recv_sem=halo_sem.at[1],
            device_id=(row, jnp.maximum(seq - 1, 0)),
            device_id_type=MESH,
        )

    def saved_part(number, columns):
        return keys_values[0, pl.ds(number * tokens, tokens), columns].astype(jnp.float32)

    def projected_part(number, columns):
        return keys_values[1, pl.ds(number * tokens, tokens), columns].astype(jnp.float32)

    def convolution_back():
        within = lax.rem(lax.broadcasted_iota(jnp.int32, (tokens, lane), 0), length)
        position = within + seq * length
        start = [
            segment_start(at.lengths, which, position[which * length : (which + 1) * length])
            for which in range(rows)
        ]
        start = jnp.concatenate(start, axis=0)
        keep_one = position - 1 >= start
        keep_two = position - 2 >= start
        edge = lax.broadcasted_iota(jnp.int32, (8, lane), 0)
        for part_at in range(0, width, lane):
            columns = pl.ds(part_at, lane)
            gated_grad = wide[:, columns]
            exit_grad = gated_grad * saved_part(0, columns)
            place = mixer_in_at + width + part_at
            g_all[:, pl.ds(place, lane)] = exit_grad.astype(jnp.bfloat16)
            conv_grad = gated_grad * projected_part(1, columns)
            block, inside = part_at // COLS, part_at % COLS
            for tap in range(3):
                sums = jnp.sum(conv_grad * saved_part(1 + tap, columns), axis=0, keepdims=True)
                place = blocks * (4 + tap) + block
                small[place : place + 1, inside : inside + lane] = sums
            two = jnp.where(keep_two, at.vectors[4:5, columns] * conv_grad, 0.0)
            one = jnp.where(keep_one, at.vectors[5:6, columns] * conv_grad, 0.0)
            here = at.vectors[6:7, columns] * conv_grad
            here += jnp.where(within < length - 1, pltpu.roll(one, tokens - 1, 0), 0.0)
            here += jnp.where(within < length - 2, pltpu.roll(two, tokens - 2, 0), 0.0)
            normed_grad[:, columns] = here
            for which in range(rows):
                span = slice(which * length, which * length + 8)
                sent = two[span] + jnp.where(edge == 1, pltpu.roll(one[span], 1, 0), 0.0)
                halo_out[which, :, columns] = jnp.where(edge < 2, sent, 0.0)

        @pl.when(seq > 0)
        def _():
            halo_copy().start()

    def product_back():
        @pl.when(seq < shards - 1)
        def _():
            halo_copy().wait_recv()
            for which in range(rows):
                span = pl.ds((which + 1) * length - 8, 8)
                normed_grad[span] = normed_grad[span] + pltpu.roll(halo_in[which], 6, 0)

        @pl.when(seq > 0)
        def _():
            halo_copy().wait_send()

        for part_at in range(0, width, lane):
            columns = pl.ds(part_at, lane)
            product_grad = normed_grad[:, columns]
            entry_grad = product_grad * projected_part(2, columns)
            carrier_grad = product_grad * projected_part(0, columns)
            g_all[:, pl.ds(mixer_in_at + part_at, lane)] = entry_grad.astype(jnp.bfloat16)
            place = mixer_in_at + 2 * width + part_at
            g_all[:, pl.ds(place, lane)] = carrier_grad.astype(jnp.bfloat16)
        normed_grad[...] = jnp.zeros_like(normed_grad)

    def task(i):
        def when(name, run, after=0, number=1):
            j = i - (starts[name] + after)

            @pl.when(jnp.logical_and(j >= 0, j < number))
            def _():
                run(j)

        when(
            SECOND,
            lambda j: feed_tile(SECOND, j + 1, second_down, second_wide),
            0,
            hidden_blocks - 1,
        )

        def waits(j):
            for copy in middle_loads + x_loads:
                copy.wait()

        when(ATTEND_OUTPUT, waits)

        def to_attended(j):
            staged[...] = (hidden[...] + wide[...]).astype(jnp.bfloat16)
            mixed_copy.start()
            norm_back(0)
            low_gradient(output_at)
            output_tile(ATTEND_OUTPUT, 0, output_at, attended_grad)

        when(ATTEND_OUTPUT, to_attended)
        when(ATTEND_OUTPUT, lambda j: output_tile(ATTEND_OUTPUT, 1, output_at, attended_grad), 1)

        def staged_free(j):
            mixed_copy.wait()
            raw_load.start()

        when(ATTENTION, staged_free)

        def attention(j):
            attention_head(j // KV_HEADS, lax.rem(j, KV_HEADS))

        when(ATTENTION, attention, 0, rows * KV_HEADS)

        def to_queries(j):
            raw_load.wait()
            for copy in late_loads:
                copy.start()
            query_heads()

        when(QUERIES, to_queries)
        def pick_rows(j):
            block_rows = x_all.shape[3]
            shape = (shards * 2 * block_rows, tokens)
            place = lax.broadcasted_iota(jnp.int32, shape, 0)
            vector, shard = lax.rem(place, 2 * block_rows), place // (2 * block_rows)
            wanted = blocks * vector + jnp.where(vector < 7, shard * blocks // shards, 0)
            found = lax.broadcasted_iota(jnp.int32, shape, 1) == wanted
            found = jnp.logical_and(found, vector < 8).astype(jnp.float32).astype(jnp.bfloat16)
            x_first = entries[-1][0]
            target = x_all.shape[:2] + (2, block_rows, tokens)
            x_all[:, :, x_first : x_first + 2] = found.reshape(target)

        when(QUERIES, pick_rows, 2)
        when(QUERIES, lambda j: project_back(QUERIES, 0, heads_at, heads_at + COLS), 1)

        def to_keys(j):
            key_heads()
            project_back(KEYS, 0, heads_at + width, heads_at + width + COLS)
            norm_back(1)
            low_gradient(first_down)

        when(KEYS, to_keys)
        when(FIRST, lambda j: feed_tile(FIRST, j, first_down, first_wide), 0, hidden_blocks)

        def to_gated(j):
            norm_back(2)
            low_gradient(mixer_out_at)
            output_tile(MIXER_OUTPUT, 0, mixer_out_at, wide)
            for copy in late_loads:
                copy.wait()

        when(MIXER_OUTPUT, to_gated)

        def to_convolved(j):
            output_tile(MIXER_OUTPUT, 1, mixer_out_at, wide)
            convolution_back()

        when(MIXER_OUTPUT, to_convolved, 1)
        when(HALO, lambda j: product_back())

        def mixer_tile(j):
            even = pl.multiple_of(mixer_in_at + 2 * j * COLS, COLS)
            project_back(MIXER_INPUT, j, even, pl.multiple_of(even + COLS, COLS))

        when(MIXER_INPUT, mixer_tile, 0, numbers[MIXER_INPUT])

        def close(j):
            norm_back(3)
            staged[...] = gradient[...].astype(jnp.bfloat16)
            out_copy.start()
            g_all[pl.ds(0, small.shape[0]), pl.ds(small_at, COLS)] = small[...].astype(jnp.bfloat16)

        when(CLOSE, close)
        when(CLOSE, lambda j: out_copy.wait(), 1)

    exchange.meet()
    feed_tile(SECOND, 0, second_down, second_wide)
    exchange.run(task)


def backward(groups, arrays, resident, row_count, shards, collective_id):
    xs = [x for x, _ in groups if not isinstance(x, int)]
    block_rows, tokens = xs[0].shape[3:]
    width = arrays["cotangent"].shape[1]
    entries, x_blocks, g_blocks, chunks = reduce_entries(
        [(x if isinstance(x, int) else x.shape[2], columns // COLS) for x, columns in groups]
    )
    names = ["xs_%d" % number for number in range(len(xs))] + list(arrays)
    values = list(xs) + list(arrays.values())
    rows, total_length = arrays["keys_values"].shape[:2]
    any_space = pl.BlockSpec(memory_space=pl.ANY)
    spaces = dict.fromkeys(resident, pltpu.VMEM)
    spaces["lengths"] = pltpu.SMEM
    key_blocks = total_length // shards // block_rows

    def kernel(*refs):
        xs_refs, others = refs[: len(xs)], refs[len(xs) : len(values)]
        named = [("xs", xs_refs)] + list(zip(arrays, others))
        backward_kernel(
            [name for name, _ in named],
            entries,
            row_count,
            shards,
            *[ref for _, ref in named],
            *refs[len(values) :],
        )

    low, full = jnp.bfloat16, jnp.float32
    return pl.pallas_call(
        kernel,
        out_shape=[
            jax.ShapeDtypeStruct((x_count * block_rows, g_count * COLS), low)
            for _, x_count, _, g_count, _ in entries
        ]
        + [jax.ShapeDtypeStruct((tokens, width), low)] * 2,
        in_specs=[pl.BlockSpec(memory_space=spaces.get(name, pl.ANY)) for name in names],
        out_specs=[any_space] * (len(entries) + 2),
        scratch_shapes=[
            pltpu.VMEM((2, COLS, width), low),
            pltpu.VMEM((2, width, COLS), low),
            pltpu.VMEM((2, width, COLS), low),
            pltpu.VMEM((2, 2, tokens, COLS), low),
            pltpu.VMEM((rows, total_length, width), low),
            pltpu.VMEM((rows, shards // 2, 2, key_blocks, block_rows, width), low),
            pltpu.VMEM((rows, key_blocks, block_rows, width), low),
            pltpu.VMEM((tokens, width), low),
            pltpu.VMEM((tokens, width), low),
            pltpu.VMEM((tokens, width), full),
            pltpu.VMEM((tokens, width), low),
            pltpu.VMEM((tokens, width // 2), low),
            pltpu.VMEM((tokens, width), full),
            pltpu.VMEM((tokens, width), full),
            pltpu.VMEM((tokens, width), full),
            pltpu.VMEM((rows, 8, width), full),
            pltpu.VMEM((rows, 8, width), full),
            pltpu.VMEM((16, COLS), full),
            pltpu.SemaphoreType.DMA((2, 5)),
            pltpu.SemaphoreType.DMA((len(entries) + 10,)),
            pltpu.SemaphoreType.DMA((2,)),
            *exchange_scratch(row_count, shards, block_rows, x_blocks, g_blocks, tokens),
        ],
        compiler_params=pltpu.CompilerParams(
            collective_id=collective_id, has_side_effects=True, vmem_limit_bytes=63 * 2**20
        ),
        cost_estimate=pl.CostEstimate(
            flops=4 * chunks * shards * block_rows * COLS * tokens,
            bytes_accessed=2 * chunks * shards * block_rows * COLS,
            transcendentals=0,
        ),
    )(*values)


def fused_body(
    tokens,
    lengths,
    mixer_gain,
    mixer_input,
    mixer_kernel,
    mixer_output,
    first_gain,
    first_gate,
    first_up,
    first_down,
    attend_gain,
    query_weight,
    key_weight,
    value_weight,
    query_gain,
    key_gain,
    attend_output,
    second_gain,
    second_gate,
    second_up,
    second_down,
    cotangent,
):
    full, low = jnp.float32, jnp.bfloat16
    rows, length, width = tokens.shape
    token_count = rows * length
    lane = 2 * HEAD_DIM
    row_count, shards = lax.axis_size("row"), lax.axis_size("seq")
    seq = lax.axis_index("seq")
    tables = dict(
        lengths=lengths,
        mixer_kernel=mixer_kernel,
        mixer_gain=mixer_gain,
        first_gain=first_gain,
        attend_gain=attend_gain,
        second_gain=second_gain,
        query_gain=query_gain,
        key_gain=key_gain,
    )
    arrays = dict(
        tokens=tokens.reshape(token_count, width),
        mixer_input=mixer_input,
        mixer_output=mixer_output,
        first_gate=first_gate,
        first_up=first_up,
        first_down=first_down,
        query_weight=query_weight,
        key_weight=key_weight,
        value_weight=value_weight,
        attend_output=attend_output,
        **tables,
    )
    saved = types.SimpleNamespace(**forward(arrays, tuple(tables), rows, shards, 2))
    block_rows = saved.attended_x.shape[3]
    weights = dict(
        second_down=second_down,
        second_gate=second_gate,
        second_up=second_up,
        attend_output=attend_output,
        query_weight=query_weight,
        key_weight=key_weight,
        value_weight=value_weight,
        first_down=first_down,
        first_gate=first_gate,
        first_up=first_up,
        mixer_output=mixer_output,
        mixer_input=mixer_input,
    )
    tables = dict(vectors=saved.vectors_out, cosine=saved.cosine_out, sine=saved.sine_out)
    arrays = dict(
        lengths=lengths,
        cotangent=cotangent.reshape(token_count, width),
        gate_one=saved.gate_one,
        up_one=saved.up_one,
        hidden_three=saved.hidden_three,
        hidden_two=saved.hidden_two,
        hidden_one=saved.hidden_one,
        hidden_zero=saved.hidden_zero,
        queries_out=saved.queries_out,
        keys_values=saved.keys_values,
        queries_raw=saved.queries_raw,
        keys_raw=saved.keys_raw,
        mixer_saved=saved.mixer_saved,
        projected=saved.projected,
        **tables,
        **weights,
    )
    hidden_columns = first_gate.shape[1]
    head_columns = width + 2 * key_weight.shape[1]
    groups = [
        (width // shards // block_rows, 2 * hidden_columns),
        (hidden_columns // shards // block_rows, width),
        (saved.attended_x, width),
        (saved.attend_in_x, head_columns),
        (saved.active_x, width),
        (saved.first_in_x, 2 * hidden_columns),
        (saved.gated_x, width),
        (saved.mixer_in_x, 3 * width),
        (2, COLS),
    ]
    (
        second_both,
        grad_second_down,
        grad_attend_output,
        attend_three,
        grad_first_down,
        first_both,
        grad_mixer_output,
        grad_mixer_input,
        sums,
        token_grad,
        mixed,
    ) = backward(groups, arrays, tuple(tables), row_count, shards, 1)

    def single(value):
        return value.astype(full)

    share = width // shards
    vectors = single(
        lax.dynamic_slice(sums, (0, lax.rem(seq, COLS // share) * share), (7, share))
    )
    head_share = HEAD_DIM // shards
    heads = [
        single(lax.dynamic_slice(sums, (7, which * lane + seq * head_share), (1, head_share)))[0]
        for which in range(2)
    ]
    key_columns = key_weight.shape[1]
    return (
        mixed.reshape(tokens.shape),
        token_grad.reshape(tokens.shape),
        vectors[3],
        single(grad_mixer_input),
        vectors[4:7],
        single(grad_mixer_output),
        vectors[2],
        single(first_both[:, :hidden_columns]),
        single(first_both[:, hidden_columns:]),
        single(grad_first_down),
        vectors[1],
        single(attend_three[:, :width]),
        single(attend_three[:, width : width + key_columns]),
        single(attend_three[:, width + key_columns :]),
        heads[0],
        heads[1],
        single(grad_attend_output),
        vectors[0],
        single(second_both[:, :hidden_columns]),
        single(second_both[:, hidden_columns:]),
        single(grad_second_down),
    )


def fused_or_general(*args):
    tokens = args[0]
    rows, length, width = tokens.shape
    row_count, shards = lax.axis_size("row"), lax.axis_size("seq")
    key_bytes = 2 * rows * length * shards * width
    if key_bytes <= 4 * 2**20 and shards == 8 and 4 * rows == shards and row_count == 4:
        return fused_body(*args)
    return body(*args)


def solution(mesh):
    in_specs = (
        P("row", "seq", None),
        P("row", None),
        P(),
        P(),
        P(),
        P(),
        P(),
        P(),
        P(),
        P(),
        P(),
        P(),
        P(),
        P(),
        P(),
        P(),
        P(),
        P(),
        P(),
        P(),
        P(),
        P("row", "seq", None),
    )
    out_specs = (
        P("row", "seq", None),
        P("row", "seq", None),
        P("seq"),
        P("seq", None),
        P(None, "seq"),
        P("seq", None),
        P("seq"),
        P("seq", None),
        P("seq", None),
        P("seq", None),
        P("seq"),
        P("seq", None),
        P("seq", None),
        P("seq", None),
        P("seq"),
        P("seq"),
        P("seq", None),
        P("seq"),
        P("seq", None),
        P("seq", None),
        P("seq", None),
    )
    return jax.shard_map(fused_or_general, mesh=mesh, in_specs=in_specs, out_specs=out_specs, check_vma=False)
```

```python
import functools
import math
import types

import jax
import jax.numpy as jnp
from jax import lax
from jax.experimental import pallas as pl
from jax.experimental.pallas import tpu as pltpu
from jax.sharding import PartitionSpec as P

HEADS = 16
KV_HEADS = 8
HEAD_DIM = 64
GROUP = 2


EPS = 1e-05
THETA = 1000000.0
NEGATIVE = -1e30
HIGHEST = lax.Precision.HIGHEST
MESH = pl.DeviceIdType.MESH
COLS = 512
SLOTS = 4
ZSLOTS = 6


def passed_along(value, axis, steps):
    count = lax.axis_size(axis)
    initial, last = (max(0, -steps), min(count, count - steps))
    return lax.ppermute(value, axis, [(source, source + steps) for source in range(initial, last)])


def segment_info(lengths, positions):
    boundary = jnp.cumsum(lengths, axis=-1)
    passed = boundary[:, None, :] <= positions[None, :, None]
    segment = jnp.sum(passed.astype(jnp.int32), axis=-1)
    seg_start = jnp.max(jnp.where(passed, boundary[:, None, :], 0), axis=-1)
    return (segment, seg_start)


def norm_rows(values, norm_gain):
    return values * lax.rsqrt(jnp.mean(values * values, axis=-1, keepdims=True) + EPS) * norm_gain


def rotate(values, offsets):
    half_dim = values.shape[-1] // 2
    inverse = THETA ** (-2.0 * jnp.arange(half_dim, dtype=jnp.float32) / values.shape[-1])
    angles = offsets.astype(jnp.float32)[:, :, None, None] * inverse
    cosine = jnp.cos(angles)
    sine_table = jnp.sin(angles)
    leading = values[..., :half_dim]
    trailing = values[..., half_dim:]
    return jnp.concatenate(
        [leading * cosine - trailing * sine_table, trailing * cosine + leading * sine_table],
        axis=-1,
    )


def swiglu(gate_value, upward):
    return gate_value / (1.0 + jnp.exp(-gate_value)) * upward


def dense(inputs, matrix):
    return jnp.einsum("rtd,df->rtf", inputs, matrix, preferred_element_type=jnp.float32)


def weight_grad(inputs, gradient):
    return (inputs, gradient)


def back_dense(gradient, matrix):
    return jnp.einsum("rtf,df->rtd", gradient, matrix, preferred_element_type=jnp.float32)


def mixer_block(hidden, norm_gain, input_matrix, kernel, output_matrix, seg_start, positions):
    feature_columns = hidden.shape[-1]
    length = hidden.shape[1]
    normed, norm_back = jax.vjp(norm_rows, hidden, norm_gain.astype(jnp.float32))
    normed_low = normed.astype(jnp.bfloat16)
    projected_rows = dense(normed_low, input_matrix)
    input_gate_value = projected_rows[..., :feature_columns]
    exit_gate = projected_rows[..., feature_columns : 2 * feature_columns]
    carry_value = projected_rows[..., 2 * feature_columns :]
    gated_product_reduced = (input_gate_value * carry_value).astype(jnp.bfloat16)
    previous = passed_along(gated_product_reduced[:, length - 2 :, :], "seq", 1)
    extended = jnp.concatenate([previous, gated_product_reduced], axis=1).astype(jnp.float32)
    keep_one = (positions[None, :] - 1 >= seg_start).astype(jnp.float32)[..., None]
    keep_two = (positions[None, :] - 2 >= seg_start).astype(jnp.float32)[..., None]
    kernel_taps = kernel.astype(jnp.float32)
    two_back = extended[:, :length]
    one_back = extended[:, 1 : length + 1]
    current = extended[:, 2:]
    convolved = (
        kernel_taps[2] * current
        + kernel_taps[1] * keep_one * one_back
        + kernel_taps[0] * keep_two * two_back
    )
    gated_low = (exit_gate * convolved).astype(jnp.bfloat16)
    result = hidden + dense(gated_low, output_matrix)

    def mixer_backward(gradient):
        gradient_low = gradient.astype(jnp.bfloat16)
        grad_output = weight_grad(gated_low, gradient_low)
        grad_gated = back_dense(gradient_low, output_matrix)
        output_gate_gradient = grad_gated * convolved
        grad_conv = grad_gated * exit_gate
        grad_kernel = jnp.stack(
            [
                jnp.sum(grad_conv * keep_two * two_back, axis=(0, 1)),
                jnp.sum(grad_conv * keep_one * one_back, axis=(0, 1)),
                jnp.sum(grad_conv * current, axis=(0, 1)),
            ]
        )
        grad_extended = jnp.pad(kernel_taps[0] * keep_two * grad_conv, ((0, 0), (0, 2), (0, 0)))
        grad_extended = grad_extended + jnp.pad(
            kernel_taps[1] * keep_one * grad_conv, ((0, 0), (1, 1), (0, 0))
        )
        grad_extended = grad_extended + jnp.pad(
            kernel_taps[2] * grad_conv, ((0, 0), (2, 0), (0, 0))
        )
        returned = passed_along(grad_extended[:, :2, :], "seq", -1)
        gated_product_gradient = grad_extended[:, 2:] + jnp.pad(
            returned, ((0, 0), (length - 2, 0), (0, 0))
        )
        grad_projected = jnp.concatenate(
            [
                gated_product_gradient * carry_value,
                output_gate_gradient,
                gated_product_gradient * input_gate_value,
            ],
            axis=-1,
        ).astype(jnp.bfloat16)
        grad_input = weight_grad(normed_low, grad_projected)
        grad_normed = back_dense(grad_projected, input_matrix)
        grad_hidden, grad_gain = norm_back(grad_normed)
        return (gradient + grad_hidden, (grad_gain, grad_input, grad_kernel, grad_output))

    return (result, mixer_backward)


def feed_block(hidden, norm_gain, gate_matrix, up_matrix, down_matrix):
    normed, norm_back = jax.vjp(norm_rows, hidden, norm_gain.astype(jnp.float32))
    normed_low = normed.astype(jnp.bfloat16)
    gate_value = dense(normed_low, gate_matrix)
    upward = dense(normed_low, up_matrix)
    active, active_back = jax.vjp(swiglu, gate_value, upward)
    active_low = active.astype(jnp.bfloat16)
    result = hidden + dense(active_low, down_matrix)

    def feed_backward(gradient):
        gradient_low = gradient.astype(jnp.bfloat16)
        grad_down = weight_grad(active_low, gradient_low)
        grad_gate, grad_upward = active_back(back_dense(gradient_low, down_matrix))
        gate_low = grad_gate.astype(jnp.bfloat16)
        upward_low = grad_upward.astype(jnp.bfloat16)
        grad_normed = back_dense(gate_low, gate_matrix) + back_dense(upward_low, up_matrix)
        grad_hidden, grad_gain = norm_back(grad_normed)
        return (
            gradient + grad_hidden,
            (
                grad_gain,
                weight_grad(normed_low, jnp.concatenate([gate_low, upward_low], axis=-1)),
                grad_down,
            ),
        )

    return (result, feed_backward)


def attend_block(
    hidden,
    lengths,
    norm_gain,
    query_matrix,
    key_matrix,
    value_matrix,
    query_norm,
    key_norm,
    output_matrix,
    segment,
    positions,
    offsets,
):
    row_count, length, feature_columns = hidden.shape
    score_scale = HEAD_DIM ** (-0.5)
    normed, norm_back = jax.vjp(norm_rows, hidden, norm_gain.astype(jnp.float32))
    normed_low = normed.astype(jnp.bfloat16)

    def head_path(projected_rows, head_gain):
        return rotate(norm_rows(projected_rows, head_gain), offsets)

    queries = dense(normed_low, query_matrix).reshape(row_count, length, HEADS, HEAD_DIM)
    keys_raw = dense(normed_low, key_matrix).reshape(row_count, length, KV_HEADS, HEAD_DIM)
    values_raw = dense(normed_low, value_matrix)
    query_rot, query_back = jax.vjp(head_path, queries, query_norm.astype(jnp.float32))
    key_rot, key_back = jax.vjp(head_path, keys_raw, key_norm.astype(jnp.float32))
    query_low = query_rot.astype(jnp.bfloat16).reshape(row_count, length, KV_HEADS, GROUP, HEAD_DIM)
    key_low = key_rot.astype(jnp.bfloat16)
    value_low = values_raw.astype(jnp.bfloat16).reshape(row_count, length, KV_HEADS, HEAD_DIM)
    all_keys, all_values = (
        lax.all_gather(key_low, "seq", axis=1, tiled=True),
        lax.all_gather(value_low, "seq", axis=1, tiled=True),
    )
    total_length = all_keys.shape[1]
    key_block = min(512, total_length)
    block_count = (positions[length - 1] + key_block) // key_block

    def block_scores(number, key_source, value_source):
        first_key = number * key_block
        keys_here = lax.dynamic_slice_in_dim(key_source, first_key, key_block, 1)
        values_here = lax.dynamic_slice_in_dim(value_source, first_key, key_block, 1)
        key_positions = first_key + jnp.arange(key_block, dtype=jnp.int32)
        key_segment, unused = segment_info(lengths, key_positions)
        scores = (
            jnp.einsum(
                "rtkgh,rskh->rkgts", query_low, keys_here, preferred_element_type=jnp.float32
            )
            * score_scale
        )
        allowed = (segment[:, :, None] == key_segment[:, None, :]) & (
            positions[None, :, None] >= key_positions[None, None, :]
        )
        allowed = allowed[:, None, None]
        return (jnp.where(allowed, scores, NEGATIVE), allowed, keys_here, values_here)

    stat_shape = (row_count, KV_HEADS, GROUP, length)

    def stats_step(number, carried):
        peak_score, running_sum = carried
        scores, allowed, unused_keys, unused_values = block_scores(number, all_keys, all_values)
        new_peak = jnp.maximum(peak_score, jnp.max(scores, axis=-1))
        fresh = jnp.sum(jnp.where(allowed, jnp.exp(scores - new_peak[..., None]), 0.0), axis=-1)
        return (new_peak, running_sum * jnp.exp(peak_score - new_peak) + fresh)

    peak_score, running_sum = lax.fori_loop(
        0,
        block_count,
        stats_step,
        (jnp.full(stat_shape, NEGATIVE, jnp.float32), jnp.zeros(stat_shape, jnp.float32)),
    )
    log_total = peak_score + jnp.log(running_sum)

    def probabilities(scores, allowed):
        return jnp.where(allowed, jnp.exp(scores - log_total[..., None]), 0.0)

    out_shape = (row_count, length, KV_HEADS, GROUP, HEAD_DIM)

    def output_step(number, carried):
        rounded, exact_sum = carried
        scores, allowed, keys_here, values_here = block_scores(number, all_keys, all_values)
        weights = probabilities(scores, allowed)
        rounded = rounded + jnp.einsum(
            "rkgts,rskh->rtkgh",
            weights.astype(jnp.bfloat16),
            values_here,
            preferred_element_type=jnp.float32,
        )
        exact_sum = exact_sum + jnp.einsum(
            "rkgts,rskh->rtkgh", weights, values_here.astype(jnp.float32), precision=HIGHEST
        )
        return (rounded, exact_sum)

    rounded, exact_sum = lax.fori_loop(
        0,
        block_count,
        output_step,
        (jnp.zeros(out_shape, jnp.float32), jnp.zeros(out_shape, jnp.float32)),
    )
    attended_low = rounded.reshape(row_count, length, HEADS * HEAD_DIM).astype(jnp.bfloat16)
    result = hidden + dense(attended_low, output_matrix)

    def attend_backward(gradient):
        gradient_low = gradient.astype(jnp.bfloat16)
        grad_output = weight_grad(attended_low, gradient_low)
        grad_attended = (
            back_dense(gradient_low, output_matrix).astype(jnp.bfloat16).reshape(out_shape)
        )
        row_delta = jnp.einsum(
            "rtkgh,rtkgh->rkgt", grad_attended.astype(jnp.float32), exact_sum, precision=HIGHEST
        )
        key_source, value_source = (all_keys, all_values)

        def grad_step(number, carried):
            grad_query, grad_keys, grad_values = carried
            scores, allowed, keys_here, values_here = block_scores(number, key_source, value_source)
            weights = probabilities(scores, allowed)
            grad_weights = jnp.einsum(
                "rtkgh,rskh->rkgts", grad_attended, values_here, preferred_element_type=jnp.float32
            )
            grad_scores = (weights * (grad_weights - row_delta[..., None])).astype(jnp.bfloat16)
            grad_query = (
                grad_query
                + jnp.einsum(
                    "rkgts,rskh->rtkgh", grad_scores, keys_here, preferred_element_type=jnp.float32
                )
                * score_scale
            )
            key_part = (
                jnp.einsum(
                    "rkgts,rtkgh->rskh", grad_scores, query_low, preferred_element_type=jnp.float32
                )
                * score_scale
            )
            value_part = jnp.einsum(
                "rkgts,rtkgh->rskh",
                weights.astype(jnp.bfloat16),
                grad_attended,
                preferred_element_type=jnp.float32,
            )
            grad_keys = lax.dynamic_update_slice_in_dim(grad_keys, key_part, number * key_block, 1)
            grad_values = lax.dynamic_update_slice_in_dim(
                grad_values, value_part, number * key_block, 1
            )
            return (grad_query, grad_keys, grad_values)

        key_shape = (row_count, total_length, KV_HEADS, HEAD_DIM)
        grad_query, grad_keys, grad_values = lax.fori_loop(
            0,
            block_count,
            grad_step,
            (
                jnp.zeros(out_shape, jnp.float32),
                jnp.zeros(key_shape, jnp.float32),
                jnp.zeros(key_shape, jnp.float32),
            ),
        )
        local_keys, local_values = (
            lax.psum_scatter(
                grad_keys.astype(jnp.bfloat16), "seq", scatter_dimension=1, tiled=True
            ).astype(jnp.float32),
            lax.psum_scatter(
                grad_values.astype(jnp.bfloat16), "seq", scatter_dimension=1, tiled=True
            ).astype(jnp.float32),
        )
        grad_queries, grad_query_norm = query_back(
            grad_query.reshape(row_count, length, HEADS, HEAD_DIM)
        )
        grad_keys_raw, grad_key_norm = key_back(local_keys)
        query_grad_low = grad_queries.reshape(row_count, length, HEADS * HEAD_DIM).astype(
            jnp.bfloat16
        )
        key_grad_low = grad_keys_raw.reshape(row_count, length, KV_HEADS * HEAD_DIM).astype(
            jnp.bfloat16
        )
        value_grad_low = local_values.reshape(row_count, length, KV_HEADS * HEAD_DIM).astype(
            jnp.bfloat16
        )
        grad_normed = (
            back_dense(query_grad_low, query_matrix)
            + back_dense(key_grad_low, key_matrix)
            + back_dense(value_grad_low, value_matrix)
        )
        grad_hidden, grad_gain = norm_back(grad_normed)
        return (
            gradient + grad_hidden,
            (
                grad_gain,
                weight_grad(
                    normed_low,
                    jnp.concatenate([query_grad_low, key_grad_low, value_grad_low], axis=-1),
                ),
                grad_query_norm,
                grad_key_norm,
                grad_output,
            ),
        )

    return (result, attend_backward)


def reduce_entries(pairs):
    entries = []
    x_first = g_first = chunk = 0
    for x_count, g_count in pairs:
        entries.append((x_first, x_count, g_first, g_count, chunk))
        x_first += x_count
        g_first += g_count
        chunk += x_count * g_count
    return entries, x_first, g_first, chunk


def locate(entries, q):
    x_block, g_block = jnp.int32(0), jnp.int32(0)
    for x_first, x_count, g_first, g_count, chunk in entries:
        here = q - chunk
        inside = here >= 0
        x_block = jnp.where(inside, x_first + lax.rem(jnp.maximum(here, 0), x_count), x_block)
        g_block = jnp.where(inside, g_first + jnp.maximum(here, 0) // x_count, g_block)
    return x_block, g_block


def seq_steps(bits):
    upper = list(range(1, bits))
    middle = (len(upper) + 1) // 2
    kinds = []
    for order in (upper, upper[middle:] + upper[:middle]):
        held = sorted(upper, reverse=True)
        steps = []
        for bit in order:
            place = held.index(bit)
            steps.append((bit, 2**place, 2 ** (len(held) - 1 - place)))
            held.remove(bit)
        kinds.append(steps)
    return kinds


def exchange_scratch(row_count, shards, block_rows, x_blocks, g_blocks, tokens):
    bits = shards.bit_length() - 1
    block = (block_rows, COLS)
    comm = []
    for steps in seq_steps(bits):
        for _, above, below in steps:
            comm.append(pltpu.VMEM((2, above, 2, below) + block, jnp.bfloat16))
            comm.append(pltpu.VMEM((SLOTS, above, below) + block, jnp.bfloat16))
    z_steps = row_count - 1
    return [
        pltpu.VMEM((shards // 2, 2, x_blocks, block_rows, tokens), jnp.bfloat16),
        pltpu.VMEM((tokens, g_blocks * COLS), jnp.bfloat16),
        pltpu.VMEM((2, 2, shards // 2) + block, jnp.bfloat16),
        pltpu.VMEM((2, SLOTS, shards // 2) + block, jnp.bfloat16),
        *comm,
        *[pltpu.VMEM((2, ZSLOTS) + block, jnp.bfloat16) for _ in range(5)],
        pltpu.SemaphoreType.DMA((2, bits, SLOTS)),
        pltpu.SemaphoreType.DMA((2, bits, SLOTS)),
        pltpu.SemaphoreType.DMA((2, z_steps, ZSLOTS)),
        pltpu.SemaphoreType.DMA((2, z_steps, ZSLOTS)),
        pltpu.SemaphoreType.DMA((2, ZSLOTS)),
    ]


class Exchange:
    def __init__(self, entries, row_count, shards, outs, scratch, locals_at=(), local=None):
        self.last_rows = None
        self.entries, self.outs = entries, outs
        self.locals_at, self.local = locals_at, local
        self.bits = bits = shards.bit_length() - 1
        self.kinds = seq_steps(bits)
        (self.x_all, self.g_all, self.send_zero, self.recv_zero, *rest) = scratch
        self.held, self.received = [[], []], [[], []]
        for kind in range(2):
            for _ in self.kinds[kind]:
                self.held[kind].append(rest.pop(0))
                self.received[kind].append(rest.pop(0))
        self.z_own, self.z_in, self.z_part, self.z_cross, self.z_total = rest[:5]
        self.seq_send, self.seq_recv, self.z_send, self.z_recv, self.out_sem = rest[5:]
        self.row, self.seq = lax.axis_index("row"), lax.axis_index("seq")
        self.row_count, self.shards = row_count, shards
        self.value = [lax.rem(self.seq // (1 << bit), 2) for bit in range(bits)]
        self.partner = [self.seq + (1 << bit) * (1 - 2 * self.value[bit]) for bit in range(bits)]
        last = entries[-1]
        self.pairs = (last[4] + last[1] * last[3]) // 2 + len(locals_at)
        half = row_count // 2
        self.depth = half - 1
        lower = self.row < half
        self.level = jnp.where(lower, self.row, row_count - 1 - self.row)
        self.toward = jnp.where(lower, self.row + 1, self.row - 1)
        self.away = jnp.where(lower, self.row - 1, self.row + 1)

    def meet(self):
        barrier = pltpu.get_barrier_semaphore()
        others = [(self.row, partner) for partner in self.partner]
        for step in (1, self.row_count - 1):
            others.append((lax.rem(self.row + step, self.row_count), self.seq))
        for step in (1, self.shards - 1):
            others.append((self.row, lax.rem(self.seq + step, self.shards)))
        for other in others:
            pl.semaphore_signal(barrier, inc=1, device_id=other, device_id_type=MESH)
        pl.semaphore_wait(barrier, len(others))

    def is_local(self, index):
        found = index < 0
        for at in self.locals_at:
            found = jnp.logical_or(found, index == at)
        return found

    def chunk(self, kind, index):
        before = sum([jnp.where(index > at, 1, 0) for at in self.locals_at], 0)
        return 2 * (index - before) + kind

    def product(self, kind, index, side):
        x_block, g_block = locate(self.entries, self.chunk(kind, index))
        left = self.x_all[:, side, x_block]
        columns = pl.ds(pl.multiple_of(g_block * COLS, COLS), COLS)
        return jnp.dot(
            left.reshape(left.shape[0] * left.shape[1], left.shape[2]),
            self.g_all[:, columns],
            preferred_element_type=jnp.float32,
        )

    def sized(self, kind, index, act):
        if self.last_rows is None or kind == 1:
            act(None)
        else:
            pl.when(index < self.pairs - 1)(lambda: act(None))
            pl.when(index == self.pairs - 1)(lambda: act(self.last_rows))

    def seq_start(self, kind, step, slot, index):
        self.sized(kind, index, lambda rows: self.seq_copy(kind, step, slot, rows).start())

    def seq_wait(self, kind, step, slot, index):
        self.sized(kind, index, lambda rows: self.seq_copy(kind, step, slot, rows).wait())

    def z_start(self, kind, step, slot, index):
        self.sized(kind, index, lambda rows: self.z_copy(kind, step, slot, rows).start())

    def z_wait(self, kind, step, slot, index):
        self.sized(kind, index, lambda rows: self.z_copy(kind, step, slot, rows).wait())

    def z_wait_recv(self, kind, step, slot, index):
        self.sized(kind, index, lambda rows: self.z_copy(kind, step, slot, rows).wait_recv())

    def z_wait_send(self, kind, step, slot, index):
        self.sized(kind, index, lambda rows: self.z_copy(kind, step, slot, rows).wait_send())

    def seq_copy(self, kind, step, slot, rows):
        some = pl.ds(0, self.z_own.shape[2] if rows is None else rows)
        if step == 0:
            bit = 0
            source = self.send_zero.at[kind, lax.rem(slot, 2), :, some]
            target = self.recv_zero.at[kind, slot, :, some]
        else:
            bit = self.kinds[kind][step - 1][0]
            away = 1 - self.value[bit]
            source = self.held[kind][step - 1].at[lax.rem(slot, 2), :, away, :, some]
            target = self.received[kind][step - 1].at[slot, :, :, some]
        return pltpu.make_async_remote_copy(
            src_ref=source,
            dst_ref=target,
            send_sem=self.seq_send.at[kind, step, slot],
            recv_sem=self.seq_recv.at[kind, step, slot],
            device_id=(self.row, self.partner[bit]),
            device_id_type=MESH,
        )

    def seq_sum(self, kind, step, slot):
        bit = self.kinds[kind][step - 2][0]
        mine = self.held[kind][step - 2][lax.rem(slot, 2), :, self.value[bit]].astype(jnp.float32)
        return mine + self.received[kind][step - 2][slot].astype(jnp.float32)

    def z_copy(self, kind, step, slot, rows):
        some = pl.ds(0, self.z_own.shape[2] if rows is None else rows)
        if step < self.depth:
            source = self.z_own if step == 0 else self.z_part
            target, where = self.z_in, self.toward
        elif step == self.depth:
            source = self.z_own if self.depth == 0 else self.z_part
            target, where = self.z_cross, self.toward
        else:
            source, target, where = self.z_total, self.z_total, self.away
        return pltpu.make_async_remote_copy(
            src_ref=source.at[kind, slot, some],
            dst_ref=target.at[kind, slot, some],
            send_sem=self.z_send.at[kind, step, slot],
            recv_sem=self.z_recv.at[kind, step, slot],
            device_id=(where, self.seq),
            device_id_type=MESH,
        )

    def start_out(self, kind, slot, index):
        q = self.chunk(kind, index)
        rows = self.z_total.shape[2]
        for out, (_, x_count, _, g_count, chunk) in zip(self.outs, self.entries):
            here = q - chunk

            @pl.when(jnp.logical_and(here >= 0, here < x_count * g_count))
            def _():
                row_at = pl.multiple_of(lax.rem(here, x_count) * rows, rows)
                column_at = pl.multiple_of(here // x_count * COLS, COLS)
                pltpu.make_async_copy(
                    self.z_total.at[kind, slot],
                    out.at[pl.ds(row_at, rows), pl.ds(column_at, COLS)],
                    self.out_sem.at[kind, slot],
                ).start()

    def first(self, kind, index):
        slot = lax.rem(index, SLOTS)
        target = self.send_zero

        def put():
            target[kind, lax.rem(slot, 2)] = (
                self.product(kind, index, 1 - self.value[0])
                .astype(jnp.bfloat16)
                .reshape(target.shape[2:])
            )

        if self.local is None:
            put()
        else:
            pl.when(jnp.logical_not(self.is_local(index)))(put)

            @pl.when(self.is_local(index))
            def _():
                target[kind, lax.rem(slot, 2)] = self.local.part(kind, index, 1 - self.value[0])

        self.seq_start(kind, 0, slot, index)

    def second(self, kind, index):
        slot = lax.rem(index, SLOTS)
        self.seq_wait(kind, 0, slot, index)
        target = self.held[kind][0]

        def put():
            mine = self.product(kind, index, self.value[0])
            total = mine + self.recv_zero[kind, slot].astype(jnp.float32).reshape(mine.shape)
            target[lax.rem(slot, 2)] = total.astype(jnp.bfloat16).reshape(target.shape[1:])

        if self.local is None:
            put()
        else:
            pl.when(jnp.logical_not(self.is_local(index)))(put)

            @pl.when(self.is_local(index))
            def _():
                mine = self.local.part(kind, index, self.value[0]).astype(jnp.float32)
                total = mine + self.recv_zero[kind, slot].astype(jnp.float32)
                target[lax.rem(slot, 2)] = total.astype(jnp.bfloat16).reshape(target.shape[1:])

        self.seq_start(kind, 1, slot, index)

    def middle(self, step):
        def run(kind, index):
            slot = lax.rem(index, SLOTS)
            self.seq_wait(kind, step - 1, slot, index)
            total = self.seq_sum(kind, step, slot)
            target = self.held[kind][step - 1]
            target[lax.rem(slot, 2)] = total.astype(jnp.bfloat16).reshape(target.shape[1:])
            self.seq_start(kind, step, slot, index)

        return run

    def last(self, kind, index):
        slot, z_slot = lax.rem(index, SLOTS), lax.rem(index, ZSLOTS)
        self.seq_wait(kind, self.bits - 1, slot, index)
        total = self.seq_sum(kind, self.bits, slot).reshape(self.z_own.shape[2:])

        def put():
            self.z_own[kind, z_slot] = total.astype(jnp.bfloat16)

            @pl.when(self.level == 0)
            def _():
                self.z_start(kind, 0, z_slot, index)

        if self.local is None:
            put()
        else:
            pl.when(jnp.logical_not(self.is_local(index)))(put)

            @pl.when(self.is_local(index))
            def _():
                self.local.take(kind, index, total)

    def z_stage(self, step):
        level, depth = self.level, self.depth

        def run(kind, index):
            slot = lax.rem(index, ZSLOTS)
            if step <= depth:

                @pl.when(level == step)
                def _():
                    self.z_wait_recv(kind, step - 1, slot, index)
                    self.z_part[kind, slot] = (
                        self.z_own[kind, slot].astype(jnp.float32)
                        + self.z_in[kind, slot].astype(jnp.float32)
                    ).astype(jnp.bfloat16)
                    self.z_start(kind, step, slot, index)

                @pl.when(level == step - 1)
                def _():
                    self.z_wait_send(kind, step - 1, slot, index)

            elif step == depth + 1:

                @pl.when(level == depth)
                def _():
                    self.z_wait(kind, depth, slot, index)
                    own = self.z_own if depth == 0 else self.z_part
                    self.z_total[kind, slot] = (
                        own[kind, slot].astype(jnp.float32)
                        + self.z_cross[kind, slot].astype(jnp.float32)
                    ).astype(jnp.bfloat16)
                    if depth > 0:
                        self.z_start(kind, step, slot, index)
                    self.start_out(kind, slot, index)

            else:
                receiver = 2 * depth + 1 - step

                @pl.when(level == receiver)
                def _():
                    self.z_wait_recv(kind, step - 1, slot, index)
                    if receiver > 0:
                        self.z_start(kind, step, slot, index)
                    self.start_out(kind, slot, index)

                @pl.when(level == receiver + 1)
                def _():
                    self.z_wait_send(kind, step - 1, slot, index)

        return run

    def finish(self, kind, index):
        slot = lax.rem(index, ZSLOTS)
        rows = self.z_total.shape[2]
        pltpu.make_async_copy(
            self.z_total.at[kind, slot],
            self.outs[0].at[pl.ds(0, rows), pl.ds(0, COLS)],
            self.out_sem.at[kind, slot],
        ).wait()

    def run(self, task):
        stages = [(self.first, False), (self.second, False)]
        stages += [(self.middle(step), False) for step in range(2, self.bits)]
        stages += [(self.last, False)]
        stages += [(self.z_stage(step), True) for step in range(1, 2 * self.depth + 2)]
        stages += [(self.finish, True)]

        def iteration(i, carried):
            for at, (stage, summed_only) in enumerate(stages):
                index = i - at
                here = jnp.logical_and(index >= 0, index < self.pairs)
                if summed_only and self.locals_at:
                    here = jnp.logical_and(here, jnp.logical_not(self.is_local(index)))

                @pl.when(here)
                def _():
                    stage(0, index)
                    if self.last_rows is None:
                        stage(1, index)

                if self.last_rows is not None:

                    @pl.when(jnp.logical_and(here, index < self.pairs - 1))
                    def _():
                        stage(1, index)

            if task is not None:
                task(i)
            return carried

        lax.fori_loop(0, self.pairs + len(stages) - 1, iteration, 0)


def reduce_kernel(entries, row_count, shards, *refs):
    count = len(entries)
    xs, gs, outs = refs[:count], refs[count : 2 * count], refs[2 * count : 3 * count]
    load_x, load_g, *scratch = refs[3 * count :]
    exchange = Exchange(entries, row_count, shards, outs, scratch)
    copies = []
    for at, (x_first, x_count, g_first, g_count, _) in enumerate(entries):
        x_part = exchange.x_all.at[:, :, pl.ds(x_first, x_count)]
        g_part = exchange.g_all.at[:, pl.ds(g_first * COLS, g_count * COLS)]
        copies.append(pltpu.make_async_copy(xs[at], x_part, load_x.at[at]))
        copies.append(pltpu.make_async_copy(gs[at], g_part, load_g.at[at]))
    for copy in copies:
        copy.start()
    exchange.meet()
    for copy in copies:
        copy.wait()
    exchange.run(None)


def reduce_gradients(pairs, row_count, shards, collective_id):
    block_rows, tokens = pairs[0][0].shape[3:]
    entries, x_blocks, g_blocks, chunks = reduce_entries(
        [(x.shape[2], g.shape[1] // COLS) for x, g in pairs]
    )
    return pl.pallas_call(
        functools.partial(reduce_kernel, entries, row_count, shards),
        out_shape=[
            jax.ShapeDtypeStruct((x_count * block_rows, g_count * COLS), jnp.bfloat16)
            for _, x_count, _, g_count, _ in entries
        ],
        in_specs=[pl.BlockSpec(memory_space=pl.ANY)] * (2 * len(pairs)),
        out_specs=[pl.BlockSpec(memory_space=pl.ANY)] * len(pairs),
        scratch_shapes=[
            pltpu.SemaphoreType.DMA((len(pairs),)),
            pltpu.SemaphoreType.DMA((len(pairs),)),
            *exchange_scratch(row_count, shards, block_rows, x_blocks, g_blocks, tokens),
        ],
        compiler_params=pltpu.CompilerParams(
            collective_id=collective_id, has_side_effects=True, vmem_limit_bytes=52 * 2**20
        ),
        cost_estimate=pl.CostEstimate(
            flops=2 * chunks * shards * block_rows * COLS * tokens,
            bytes_accessed=2 * chunks * block_rows * COLS,
            transcendentals=0,
        ),
    )(*[x for x, _ in pairs], *[g for _, g in pairs])


def body(
    tokens,
    lengths,
    mixer_gain,
    mixer_input,
    mixer_kernel,
    mixer_output,
    first_gain,
    first_gate,
    first_up,
    first_down,
    attend_gain,
    query_weight,
    key_weight,
    value_weight,
    query_gain,
    key_gain,
    attend_output,
    second_gain,
    second_gate,
    second_up,
    second_down,
    cotangent,
):
    length = tokens.shape[1]
    positions = lax.axis_index("seq") * length + jnp.arange(length, dtype=jnp.int32)
    segment, seg_start = segment_info(lengths, positions)
    offsets = positions[None, :] - seg_start
    hidden = tokens.astype(jnp.float32)
    hidden, mixer_back = mixer_block(
        hidden, mixer_gain, mixer_input, mixer_kernel, mixer_output, seg_start, positions
    )
    hidden, first_back = feed_block(hidden, first_gain, first_gate, first_up, first_down)
    hidden, attend_back = attend_block(
        hidden,
        lengths,
        attend_gain,
        query_weight,
        key_weight,
        value_weight,
        query_gain,
        key_gain,
        attend_output,
        segment,
        positions,
        offsets,
    )
    hidden, second_back = feed_block(hidden, second_gain, second_gate, second_up, second_down)
    gradient = cotangent.astype(jnp.float32)
    gradient, second_grads = second_back(gradient)
    gradient, attend_grads = attend_back(gradient)
    gradient, first_grads = first_back(gradient)
    gradient, mixer_grads = mixer_back(gradient)
    second_gain_sum, second_wide, second_down_pair = second_grads
    attend_gain_sum, attend_wide, query_gain_sum, key_gain_sum, attend_output_pair = attend_grads
    first_gain_sum, first_wide, first_down_pair = first_grads
    mixer_gain_sum, mixer_input_pair, mixer_kernel_sum, mixer_output_pair = mixer_grads
    row_count, shards = lax.axis_size("row"), lax.axis_size("seq")
    block_rows = math.gcd(tokens.shape[2] // shards, first_down.shape[0] // shards)

    def operands(pair):
        inputs, gradient_low = pair
        token_count = inputs.shape[0] * inputs.shape[1]
        inputs = inputs.reshape(token_count, -1).T
        blocks = inputs.shape[0] // shards // block_rows
        return (
            inputs.reshape(shards // 2, 2, blocks, block_rows, token_count),
            gradient_low.reshape(token_count, -1),
        )

    wide_vectors = jnp.concatenate(
        [
            mixer_kernel_sum,
            jnp.stack([mixer_gain_sum, first_gain_sum, attend_gain_sum, second_gain_sum]),
        ]
    )
    vector_count = wide_vectors.shape[0]
    vectors = jnp.concatenate(
        [
            part.reshape(-1, shards, part.shape[-1] // shards)
            .transpose(1, 0, 2)
            .reshape(shards, -1)
            for part in (wide_vectors, jnp.stack([query_gain_sum, key_gain_sum]))
        ],
        axis=1,
    )
    vector_rows = -(-vectors.shape[1] // COLS)
    token_count = tokens.shape[0] * tokens.shape[1]
    vectors = jnp.pad(vectors, ((0, 0), (0, vector_rows * COLS - vectors.shape[1])))
    vectors = vectors.reshape(shards * vector_rows, COLS).astype(jnp.bfloat16)
    vectors = jnp.pad(vectors, ((0, token_count - shards * vector_rows), (0, 0)))
    shard_at = lax.broadcasted_iota(jnp.int32, (shards, 2 * block_rows, token_count), 0)
    row_at = lax.broadcasted_iota(jnp.int32, (shards, 2 * block_rows, token_count), 1)
    token_at = lax.broadcasted_iota(jnp.int32, (shards, 2 * block_rows, token_count), 2)
    picks = (row_at < vector_rows) & (token_at == shard_at * vector_rows + row_at)
    picks = picks.astype(jnp.bfloat16).reshape(shards // 2, 2, 2, block_rows, token_count)
    (
        grad_second_down,
        second_both,
        grad_attend_output,
        attend_three,
        grad_first_down,
        first_both,
        grad_mixer_output,
        grad_mixer_input,
        vector_sums,
    ) = reduce_gradients(
        [
            operands(second_down_pair),
            operands(second_wide),
            operands(attend_output_pair),
            operands(attend_wide),
            operands(first_down_pair),
            operands(first_wide),
            operands(mixer_output_pair),
            operands(mixer_input_pair),
            (picks, vectors),
        ],
        row_count,
        shards,
        0,
    )

    def single(value):
        return value.astype(jnp.float32)

    hidden_columns = first_gate.shape[1]
    query_columns, key_columns = query_weight.shape[1], key_weight.shape[1]
    vector_sums = single(vector_sums[:vector_rows]).reshape(-1)
    width = tokens.shape[2] // shards
    wide_sums = vector_sums[: vector_count * width].reshape(vector_count, width)
    head_width = HEAD_DIM // shards
    head_sums = vector_sums[vector_count * width :][: 2 * head_width].reshape(2, head_width)
    return (
        hidden.astype(jnp.bfloat16),
        gradient.astype(jnp.bfloat16),
        wide_sums[3],
        single(grad_mixer_input),
        wide_sums[:3],
        single(grad_mixer_output),
        wide_sums[4],
        single(first_both[:, :hidden_columns]),
        single(first_both[:, hidden_columns:]),
        single(grad_first_down),
        wide_sums[5],
        single(attend_three[:, :query_columns]),
        single(attend_three[:, query_columns : query_columns + key_columns]),
        single(attend_three[:, query_columns + key_columns :]),
        head_sums[0],
        head_sums[1],
        single(grad_attend_output),
        wide_sums[6],
        single(second_both[:, :hidden_columns]),
        single(second_both[:, hidden_columns:]),
        single(grad_second_down),
    )


def finish_kernel(cuts, count, shards, *refs):
    passed, sums_in, refs = refs[:2], refs[2], refs[3:]
    ins, outs = refs[:count], refs[count : count + len(cuts)]
    refs = refs[count + len(cuts) :]
    passed_out, vectors, taps_out, heads, refs = refs[:2], refs[2:6], refs[6], refs[7:9], refs[9:]
    lows, fulls = refs[:count], refs[count : count + len(cuts)]
    held, sums, load_sem, save_sem, pass_sem = refs[count + len(cuts) :]
    moves = [
        pltpu.make_async_copy(source, held.at[number], pass_sem.at[number])
        for number, source in enumerate(passed)
    ]
    moves.append(pltpu.make_async_copy(sums_in, sums, pass_sem.at[2]))
    loads = [
        pltpu.make_async_copy(ins[number], lows[number], load_sem.at[number])
        for number in range(count)
    ]
    for load in loads + moves:
        load.start()
    saves, waited = [], set()
    for number, (source, first, columns) in enumerate(cuts):
        if source not in waited:
            loads[source].wait()
            waited.add(source)
        low, full = lows[source], fulls[number]
        rows = low.shape[0]
        piece = 64 if rows % 64 == 0 else rows

        def convert(at, carried):
            span = pl.ds(pl.multiple_of(at * 16, 16), 16)
            full[span] = low[span, pl.ds(first, columns)].astype(jnp.float32)
            return carried

        for start in range(0, rows, piece):
            lax.fori_loop(start // 16, (start + piece) // 16, convert, 0)
            span = pl.ds(start, piece)
            save = pltpu.make_async_copy(
                full.at[span], outs[number].at[span], save_sem.at[len(saves)]
            )
            save.start()
            saves.append(save)
    for move in moves:
        move.wait()
    for number, target in enumerate(passed_out):
        save = pltpu.make_async_copy(held.at[number], target, pass_sem.at[number])
        save.start()
        saves.append(save)
    seq = lax.axis_index("seq")
    share = vectors[0].shape[0]
    value = sums[pl.ds(0, 16)].astype(jnp.float32)
    chosen = jnp.zeros((16, share), jnp.float32)
    for place in range(COLS // share):
        here = lax.rem(seq, COLS // share) == place
        chosen = jnp.where(here, value[:, place * share : (place + 1) * share], chosen)
    for number, vector in enumerate(vectors):
        vector[...] = chosen[number : number + 1].reshape(share)
    taps_out[...] = chosen[4:7]
    lane = 2 * HEAD_DIM
    for number, head in enumerate(heads):
        line = value[0:8, number * lane : (number + 1) * lane]
        part = head.shape[0]
        chosen = jnp.zeros((1, part), jnp.float32)
        for place in range(shards):
            chosen = jnp.where(seq == place, line[7:8, place * part : (place + 1) * part], chosen)
        head[...] = chosen.reshape(part)
    for save in saves:
        save.wait()


def to_full(passed, sums, lows, cuts, shards):
    any_space = pl.BlockSpec(memory_space=pl.ANY)
    shapes = [(lows[source].shape[0], columns) for source, _, columns in cuts]
    pieces = sum(rows // 64 if rows % 64 == 0 else 1 for rows, _ in shapes)
    size = sum(low.size for low in lows)
    width = passed[0].shape[1]
    small = [(width // shards,)] * 4 + [(3, width // shards)] + [(HEAD_DIM // shards,)] * 2
    results = pl.pallas_call(
        functools.partial(finish_kernel, cuts, len(lows), shards),
        out_shape=[jax.ShapeDtypeStruct(shape, jnp.float32) for shape in shapes]
        + [jax.ShapeDtypeStruct(value.shape, value.dtype) for value in passed]
        + [jax.ShapeDtypeStruct(shape, jnp.float32) for shape in small],
        in_specs=[any_space] * (3 + len(lows)),
        out_specs=[any_space] * (len(cuts) + 2)
        + [pl.BlockSpec(memory_space=pltpu.VMEM)] * len(small),
        scratch_shapes=[
            *[pltpu.VMEM(low.shape, low.dtype) for low in lows],
            *[pltpu.VMEM(shape, jnp.float32) for shape in shapes],
            pltpu.VMEM((2,) + passed[0].shape, passed[0].dtype),
            pltpu.VMEM(sums.shape, sums.dtype),
            pltpu.SemaphoreType.DMA((len(lows),)),
            pltpu.SemaphoreType.DMA((pieces,)),
            pltpu.SemaphoreType.DMA((3,)),
        ],
        compiler_params=pltpu.CompilerParams(vmem_limit_bytes=62 * 2**20),
        cost_estimate=pl.CostEstimate(flops=size, bytes_accessed=6 * size, transcendentals=0),
    )(*passed, sums, *lows)
    cut_count = len(cuts)
    return results[:cut_count], results[cut_count : cut_count + 2], results[cut_count + 2 :]


def dot_nt(left, right):
    return lax.dot_general(
        left, right, (((1,), (1,)), ((), ())), preferred_element_type=jnp.float32
    )


def dot_tn(left, right):
    return lax.dot_general(
        left, right, (((0,), (0,)), ((), ())), preferred_element_type=jnp.float32
    )


def lanes_below(shape, bound, period):
    return lax.rem(lax.broadcasted_iota(jnp.int32, shape, len(shape) - 1), period) < bound


def two_heads(pair, low):
    pair = pair.astype(jnp.float32)
    turned = pltpu.roll(pair, HEAD_DIM, 1)
    first = lanes_below(pair.shape, HEAD_DIM, 2 * HEAD_DIM)
    if low:
        parts = [jnp.where(first, pair, 0.0), jnp.where(first, turned, 0.0)]
    else:
        parts = [jnp.where(first, 0.0, turned), jnp.where(first, 0.0, pair)]
    return jnp.concatenate(parts, axis=0).astype(jnp.bfloat16)


def segment_start(lengths, which, place):
    end, start = jnp.int32(0), jnp.zeros(place.shape, jnp.int32)
    for number in range(lengths.shape[1]):
        end = end + lengths[which, number]
        start = jnp.where(place >= end, end, start)
    return start


def both_halves(value):
    value = jnp.broadcast_to(value, (8,) + value.shape[1:])
    return (value + pltpu.roll(value, HEAD_DIM, 1))[0:1]


def head_tools(lane):
    head_of = lax.broadcasted_iota(jnp.int32, (lane, lane), 0) // HEAD_DIM
    ones = head_of == lax.broadcasted_iota(jnp.int32, (lane, lane), 1) // HEAD_DIM
    ones = ones.astype(jnp.float32).astype(jnp.bfloat16)

    def head_mean(value):
        total = jnp.dot(value.astype(jnp.bfloat16), ones, preferred_element_type=jnp.float32)
        return total * (1.0 / HEAD_DIM)

    def turn(value):
        half = HEAD_DIM // 2
        first = lanes_below(value.shape, half, HEAD_DIM)
        return jnp.where(first, pltpu.roll(value, lane - half, 1), pltpu.roll(value, half, 1))

    return head_mean, turn


def forward_kernel(names, out_names, scratch_names, shards, *refs):
    at = types.SimpleNamespace(**dict(zip(names + out_names + scratch_names, refs)))
    row, seq = lax.axis_index("row"), lax.axis_index("seq")
    tokens, width = at.low_one.shape
    rows, total_length = at.both.shape[:2]
    length = tokens // rows
    lane = 2 * HEAD_DIM
    blocks = width // COLS
    hidden_blocks = at.first_gate.shape[1] // COLS
    bits = [lax.rem(seq // (1 << bit), 2) for bit in range(3)]
    partner = [seq + (1 << bit) * (1 - 2 * bits[bit]) for bit in range(3)]
    head_mean, turn = head_tools(lane)

    ahead = at.tiles_a.shape[0]

    def tile_copies(step, slot):
        name, j = step
        b, c = at.tiles_b.at[slot], at.tiles_c.at[slot]

        def columns(block):
            return pl.ds(block * COLS if isinstance(block, int) else pl.multiple_of(block * COLS, COLS), COLS)

        if name == MIXER_INPUT:
            first, second = ((0, 4), (1, 5), (2, 3))[j]
            moves = [
                (at.mixer_input.at[:, columns(first)], b),
                (at.mixer_input.at[:, columns(second)], c),
            ]
        elif name == KEYS:
            moves = [(at.key_weight, b), (at.value_weight, c)]
        elif name == FIRST:
            moves = [
                (at.first_gate.at[:, columns(j)], b),
                (at.first_up.at[:, columns(j)], c),
                (at.first_down.at[columns(j)], at.tiles_a.at[slot]),
            ]
        else:
            matrix = {
                MIXER_OUTPUT: at.mixer_output,
                QUERIES: at.query_weight,
                ATTEND_OUTPUT: at.attend_output,
            }[name]
            moves = [(matrix.at[:, columns(0)], b), (matrix.at[:, columns(1)], c)]
        return [
            pltpu.make_async_copy(source, target, at.tile_sem.at[slot, place])
            for place, (source, target) in enumerate(moves)
        ]

    steps = [(MIXER_INPUT, 0), (MIXER_INPUT, 1), (MIXER_INPUT, 2), (MIXER_OUTPUT, 0)]
    first_at = len(steps)
    steps += [(FIRST, j) for j in range(hidden_blocks)]
    steps += [(KEYS, 0), (QUERIES, 0), (ATTEND_OUTPUT, 0)]

    def begin(number):
        for copy in tile_copies(steps[number], number % ahead):
            copy.wait()
        later = number + ahead - 1
        if later < len(steps):
            for copy in tile_copies(steps[later], later % ahead):
                copy.start()
        return number % ahead

    saves = []

    streaming = [True]

    def save(source, target):
        copy = pltpu.make_async_copy(source, target, at.save_sem.at[len(saves)])
        if not streaming[0]:
            copy.start()
        saves.append(copy)

    def normed(hidden, number, target):
        for first in range(0, tokens, 64):
            span = pl.ds(first, 64)
            value = hidden[span]
            inverse = lax.rsqrt(jnp.mean(value * value, axis=-1, keepdims=True) + EPS)
            value = value * inverse * at.vectors[number : number + 1, :]
            target[span] = value.astype(jnp.bfloat16)

    def times(left, tile):
        return jnp.dot(left[...], tile, preferred_element_type=jnp.float32)

    token_load = pltpu.make_async_copy(at.tokens, at.attended, at.load_sem.at[0])
    token_load.start()
    for number in range(ahead - 1):
        for copy in tile_copies(steps[number], number):
            copy.start()
    at.halo_in[...] = jnp.zeros_like(at.halo_in)
    barrier = pltpu.get_barrier_semaphore()
    others = partner + [lax.rem(seq + step, shards) for step in (1, shards - 1)]
    for other in others:
        pl.semaphore_signal(barrier, inc=1, device_id=(row, other), device_id_type=MESH)
    at.vectors[...] = jnp.zeros_like(at.vectors)
    gains = [at.second_gain, at.attend_gain, at.first_gain, at.mixer_gain]
    for number, gain in enumerate(gains):
        at.vectors[number : number + 1, :] = gain[...].astype(jnp.float32).reshape(1, width)
    at.vectors[4:7, :] = at.mixer_kernel[...].astype(jnp.float32)
    for number, gain in enumerate((at.query_gain, at.key_gain)):
        at.vectors[7 + number : 8 + number, 0:HEAD_DIM] = (
            gain[...].astype(jnp.float32).reshape(1, HEAD_DIM)
        )
    half = HEAD_DIM // 2
    lane_at = lax.broadcasted_iota(jnp.int32, (length, lane), 1)
    power = lax.rem(lane_at, half).astype(jnp.float32) * (-2.0 * math.log(THETA) / HEAD_DIM)
    inverse = jnp.exp(power)
    side = jnp.where(lanes_below((length, lane), half, HEAD_DIM), -1.0, 1.0)
    place = lax.broadcasted_iota(jnp.int32, (length, lane), 0) + seq * length
    for which in range(rows):
        start = segment_start(at.lengths, which, place)
        angle = (place - start).astype(jnp.float32) * inverse
        span = pl.ds(which * length, length)
        at.seg_start[span] = start
        at.cosine[span] = jnp.cos(angle)
        at.sine[span] = jnp.sin(angle) * side
    save(at.vectors, at.vectors_out)
    save(at.cosine, at.cosine_out)
    save(at.sine, at.sine_out)
    token_load.wait()
    at.hidden_a[...] = at.attended[...].astype(jnp.float32)
    save(at.hidden_a, at.hidden_zero)
    normed(at.hidden_a, 3, at.low_one)
    pl.semaphore_wait(barrier, len(others))

    for number, (first, second) in enumerate(((0, 4), (1, 5))):
        slot = begin(number)
        entry = times(at.low_one, at.tiles_b[slot])
        carrier = times(at.low_one, at.tiles_c[slot])
        columns = pl.ds(number * COLS, COLS)
        product = (entry * carrier).astype(jnp.bfloat16)
        at.mixed_low[pl.ds(3 * tokens, tokens), columns] = product
        product = product.astype(jnp.float32)
        at.gates_low[pl.ds(0, tokens), columns] = entry.astype(jnp.bfloat16)
        at.gates_low[pl.ds(2 * tokens, tokens), columns] = carrier.astype(jnp.bfloat16)
        for which in range(rows):
            last = product[(which + 1) * length - 8 : (which + 1) * length]
            at.halo_out[which, :, columns] = last
    halo = pltpu.make_async_remote_copy(
        src_ref=at.halo_out,
        dst_ref=at.halo_in,
        send_sem=at.halo_sem.at[0],
        recv_sem=at.halo_sem.at[1],
        device_id=(row, jnp.minimum(seq + 1, shards - 1)),
        device_id_type=MESH,
    )

    @pl.when(seq < shards - 1)
    def _():
        halo.start()

    slot = begin(2)
    for block, tile in enumerate((at.tiles_b, at.tiles_c)):
        at.work[:, pl.ds(block * COLS, COLS)] = times(at.low_one, tile[slot])

    @pl.when(seq > 0)
    def _():
        halo.wait_recv()

    @pl.when(seq < shards - 1)
    def _():
        halo.wait_send()

    position = lax.rem(lax.broadcasted_iota(jnp.int32, (tokens, lane), 0), length) + seq * length
    keep_one = position - 1 >= at.seg_start[...]
    keep_two = position - 2 >= at.seg_start[...]
    edge = lax.broadcasted_iota(jnp.int32, (8, lane), 0)
    for part_at in range(0, width, lane):
        columns = pl.ds(part_at, lane)
        current = at.mixed_low[pl.ds(3 * tokens, tokens), columns].astype(jnp.float32)
        shifted = []
        for steps_back, keep in ((1, keep_one), (2, keep_two)):
            back = pltpu.roll(current, steps_back, 0)
            pieces = []
            for which in range(rows):
                before = pltpu.roll(at.halo_in[which, :, columns], steps_back, 0)
                start = which * length
                pieces.append(jnp.where(edge < steps_back, before, back[start : start + 8]))
                pieces.append(back[start + 8 : start + length])
            back = jnp.concatenate(pieces, axis=0)
            shifted.append(jnp.where(keep, back, 0.0))
        one, two = shifted
        convolved = at.vectors[6:7, columns] * current + at.vectors[5:6, columns] * one
        convolved += at.vectors[4:5, columns] * two
        exit_gate = at.work[:, columns]
        at.mixed_low[pl.ds(0, tokens), columns] = convolved.astype(jnp.bfloat16)
        at.mixed_low[pl.ds(tokens, tokens), columns] = two.astype(jnp.bfloat16)
        at.mixed_low[pl.ds(2 * tokens, tokens), columns] = one.astype(jnp.bfloat16)
        at.gates_low[pl.ds(tokens, tokens), columns] = exit_gate.astype(jnp.bfloat16)
        at.low_two[:, columns] = (exit_gate * convolved).astype(jnp.bfloat16)
    save(at.mixed_low, at.mixer_saved)
    save(at.gates_low, at.projected)

    def add_output(number, left, before, after):
        slot = begin(number)
        for block, tile in enumerate((at.tiles_b, at.tiles_c)):
            columns = pl.ds(block * COLS, COLS)
            after[:, columns] = before[:, columns] + times(left, tile[slot])

    add_output(3, at.low_two, at.hidden_a, at.hidden_b)
    save(at.hidden_b, at.hidden_one)
    normed(at.hidden_b, 2, at.low_three)
    at.hidden_c[...] = at.hidden_b[...]

    def feed_tile(j, carried):
        slot = lax.rem(first_at + j, ahead)
        for copy in tile_copies((FIRST, j), slot):
            copy.wait()
        later = j + ahead - 1
        later_slot = lax.rem(first_at + later, ahead)

        @pl.when(later < hidden_blocks)
        def _():
            for copy in tile_copies((FIRST, later), later_slot):
                copy.start()

        for past, step in enumerate(steps[first_at + hidden_blocks :][: ahead - 1]):

            @pl.when(later == hidden_blocks + past)
            def _():
                for copy in tile_copies(step, later_slot):
                    copy.start()

        gate_value = times(at.low_three, at.tiles_b[slot])
        up_value = times(at.low_three, at.tiles_c[slot])
        columns = pl.ds(pl.multiple_of(j * COLS, COLS), COLS)
        at.gate_low[:, columns] = gate_value.astype(jnp.bfloat16)
        at.up_low[:, columns] = up_value.astype(jnp.bfloat16)
        active = gate_value / (1.0 + jnp.exp(-gate_value)) * up_value
        active = active.astype(jnp.bfloat16)
        at.active_low[:, columns] = active
        at.hidden_c[...] += jnp.dot(
            active, at.tiles_a[slot], preferred_element_type=jnp.float32
        )
        return carried

    lax.fori_loop(0, hidden_blocks, feed_tile, 0)
    save(at.hidden_c, at.hidden_two)
    save(at.gate_low, at.gate_one)
    save(at.up_low, at.up_one)
    normed(at.hidden_c, 1, at.low_four)

    def head_path(raw, gain):
        value = raw * lax.rsqrt(head_mean(raw * raw) + EPS) * gain
        return value * at.cosine[...] + turn(value) * at.sine[...]

    keys_at = first_at + hidden_blocks
    slot = begin(keys_at)
    at.work[:, pl.ds(0, width // 2)] = times(at.low_four, at.tiles_b[slot])
    at.work[:, pl.ds(width // 2, width // 2)] = times(at.low_four, at.tiles_c[slot])
    at.keys_low[...] = at.work[:, pl.ds(0, width // 2)].astype(jnp.bfloat16)
    save(at.keys_low, at.keys_raw)
    first = lanes_below((tokens, lane), HEAD_DIM, lane)
    own = pl.ds(pl.multiple_of(seq * length, length), length)
    for pair in range(width // lane // 2):
        keys = head_path(at.work[:, pl.ds(pair * lane, lane)], both_halves(at.vectors[8:9, pl.ds(0, lane)]))
        values = at.work[:, pl.ds(width // 2 + pair * lane, lane)]
        even = jnp.where(first, keys, pltpu.roll(values, HEAD_DIM, 1)).astype(jnp.bfloat16)
        odd = jnp.where(first, pltpu.roll(keys, HEAD_DIM, 1), values).astype(jnp.bfloat16)
        for which, value in enumerate((even, odd)):
            columns = pl.ds((2 * pair + which) * lane, lane)
            at.both[:, own, columns] = value.reshape(rows, length, lane)

    def piece(owner, which=None):
        span = pl.ds(pl.multiple_of(owner * length, length), length)
        return at.both.at[:, span] if which is None else at.both.at[which, span]

    def send(number, part, bit):
        return pltpu.make_async_remote_copy(
            src_ref=part,
            dst_ref=part,
            send_sem=at.gather_send.at[number],
            recv_sem=at.gather_recv.at[number],
            device_id=(row, partner[bit]),
            device_id_type=MESH,
        )

    def flip(owner, bit):
        value = lax.rem(owner // (1 << bit), 2)
        return owner + (1 << bit) * (1 - 2 * value)

    across, along = partner[1], partner[2]
    corner = flip(across, 2)
    near_zero, far_one = send(0, piece(seq, 0), 1), send(1, piece(seq, 1), 2)
    near_one, far_zero = send(2, piece(seq, 1), 1), send(3, piece(seq, 0), 2)
    twin = send(4, piece(seq), 0)
    for copy in (near_zero, far_one, near_one, far_zero, twin):
        copy.start()
    streaming[0] = False
    for copy in saves:
        copy.start()

    slot = begin(keys_at + 1)
    for block, tile in enumerate((at.tiles_b, at.tiles_c)):
        at.work[:, pl.ds(block * COLS, COLS)] = times(at.low_four, tile[slot])
    at.queries_low[...] = at.work[...].astype(jnp.bfloat16)
    save(at.queries_low, at.queries_raw)
    for head in range(width // lane):
        columns = pl.ds(head * lane, lane)
        query = head_path(at.work[:, columns], both_halves(at.vectors[7:8, pl.ds(0, lane)])).astype(jnp.bfloat16)
        query = query * jnp.bfloat16(HEAD_DIM**-0.5)
        at.scaled[:, columns] = query
        for which in range(rows):
            at.paired[which * (width // lane) + head] = two_heads(
                query[which * length : (which + 1) * length], True
            )
    save(at.scaled, at.queries_out)

    def transposed(low, target):
        for first in range(0, tokens, lane):
            span = pl.ds(first, lane)
            value = low[span].astype(jnp.float32).T.astype(jnp.bfloat16)
            target[:, :, :, :, span] = value.reshape(target.shape[:-1] + (lane,))

    transposed(at.low_one, at.turned_one)
    save(at.turned_one, at.mixer_in_x)
    near_zero.wait()
    far_one.wait()
    near_forward = send(5, piece(across, 0), 2)
    far_forward = send(6, piece(along, 1), 1)
    near_forward.start()
    far_forward.start()
    transposed(at.low_two, at.turned_two)
    save(at.turned_two, at.gated_x)

    at.sums[...] = jnp.zeros_like(at.sums)
    pairs_of = width // lane
    together = 4
    chip = seq // 2

    def attend(other):
        @pl.when(other <= chip)
        def _():
            span = pl.ds(pl.multiple_of(other * 2 * length, 2 * length), 2 * length)
            shape = (length, 2 * length)
            key_at = lax.broadcasted_iota(jnp.int32, shape, 1) + other * 2 * length
            query_at = lax.broadcasted_iota(jnp.int32, shape, 0) + seq * length
            first = lanes_below((2 * length, lane), HEAD_DIM, lane)
            for which in range(rows):
                start = at.seg_start[pl.ds(which * length, length)]
                start = jnp.concatenate([start, start], axis=1)
                allowed = jnp.logical_and(key_at >= start, key_at <= query_at)
                allowed = jnp.concatenate([allowed, allowed], axis=0)

                def some(group, carried):
                    heads = [group * together + head for head in range(together)]
                    boths = [
                        at.both[which, span, pl.ds(pl.multiple_of(head * lane, lane), lane)]
                        for head in heads
                    ]
                    places = [which * pairs_of + head for head in heads]
                    scores = [
                        dot_nt(at.paired[place], both) for place, both in zip(places, boths)
                    ]
                    for place, score, both in zip(places, scores, boths):
                        weights = jnp.where(allowed, jnp.exp(score), 0.0).astype(jnp.bfloat16)
                        right = jnp.where(first, 1.0, both.astype(jnp.float32))
                        at.sums[place] += jnp.dot(
                            weights, right.astype(jnp.bfloat16), preferred_element_type=jnp.float32
                        )
                    return carried

                lax.fori_loop(0, pairs_of // together, some, 0)

    twin.wait()
    attend(chip)
    near_one.wait()
    near_share = send(7, piece(across), 0)
    near_share.start()
    far_zero.wait()
    far_share = send(8, piece(along), 0)
    far_share.start()
    transposed(at.low_three, at.turned_three)
    save(at.turned_three, at.first_in_x)
    near_share.wait()
    attend(across // 2)
    transposed(at.low_four, at.turned_four)
    save(at.turned_four, at.attend_in_x)
    far_share.wait()
    attend(along // 2)

    block_rows = at.turned_active.shape[3]
    x_count = at.turned_active.shape[2]
    for j in range(hidden_blocks):
        for first in range(0, tokens, lane):
            span = pl.ds(first, lane)
            value = at.active_low[span, pl.ds(j * COLS, COLS)].astype(jnp.float32).T
            value = value.astype(jnp.bfloat16)
            for block in range(COLS // block_rows):
                place = j * (COLS // block_rows) + block
                shard = place // x_count
                at.turned_active[shard // 2, shard % 2, place % x_count, :, span] = value[
                    block * block_rows : (block + 1) * block_rows
                ]
    save(at.turned_active, at.active_x)
    near_forward.wait()
    far_forward.wait()
    corner_share = send(9, piece(corner), 0)
    corner_share.start()
    corner_share.wait()
    save(at.both, at.keys_values)
    attend(corner // 2)

    first = lanes_below((length, lane), HEAD_DIM, lane)
    for which in range(rows):
        span = pl.ds(which * length, length)
        for head in range(pairs_of):
            value = at.sums[which * pairs_of + head]
            value = value * (1.0 / pltpu.roll(value, HEAD_DIM, 1))
            value = jnp.where(first, pltpu.roll(value[:length], HEAD_DIM, 1), value[length:])
            at.attended[span, pl.ds(head * lane, lane)] = value.astype(jnp.bfloat16)
    add_output(keys_at + 2, at.attended, at.hidden_c, at.hidden_d)
    save(at.hidden_d, at.hidden_three)
    transposed(at.attended, at.turned_five)
    save(at.turned_five, at.attended_x)
    for copy in saves:
        copy.wait()


def forward(arrays, resident, rows, shards, collective_id):
    tokens, width = arrays["tokens"].shape
    hidden_columns = arrays["first_gate"].shape[1]
    length = tokens // rows
    total_length = length * shards
    block_rows = math.gcd(width // shards, hidden_columns // shards)
    low, full = jnp.bfloat16, jnp.float32

    def x_shape(columns):
        return (shards // 2, 2, columns // shards // block_rows, block_rows, tokens)

    outs = dict(
        hidden_zero=((tokens, width), full),
        hidden_one=((tokens, width), full),
        hidden_two=((tokens, width), full),
        hidden_three=((tokens, width), full),
        gate_one=((tokens, hidden_columns), low),
        up_one=((tokens, hidden_columns), low),
        queries_out=((tokens, width), low),
        queries_raw=((tokens, width), low),
        keys_raw=((tokens, width // 2), low),
        keys_values=((rows, total_length, width), low),
        mixer_saved=((4 * tokens, width), low),
        projected=((3 * tokens, width), low),
        mixer_in_x=(x_shape(width), low),
        gated_x=(x_shape(width), low),
        first_in_x=(x_shape(width), low),
        attend_in_x=(x_shape(width), low),
        attended_x=(x_shape(width), low),
        active_x=(x_shape(hidden_columns), low),
        vectors_out=((16, width), full),
        cosine_out=((tokens, 2 * HEAD_DIM), full),
        sine_out=((tokens, 2 * HEAD_DIM), full),
    )
    pairs = rows * width // (2 * HEAD_DIM)
    dma = pltpu.SemaphoreType.DMA
    scratch = dict(
        tiles_a=pltpu.VMEM((4, COLS, width), low),
        tiles_b=pltpu.VMEM((4, width, COLS), low),
        tiles_c=pltpu.VMEM((4, width, COLS), low),
        hidden_a=pltpu.VMEM((tokens, width), full),
        hidden_b=pltpu.VMEM((tokens, width), full),
        hidden_c=pltpu.VMEM((tokens, width), full),
        hidden_d=pltpu.VMEM((tokens, width), full),
        low_one=pltpu.VMEM((tokens, width), low),
        low_two=pltpu.VMEM((tokens, width), low),
        low_three=pltpu.VMEM((tokens, width), low),
        low_four=pltpu.VMEM((tokens, width), low),
        attended=pltpu.VMEM((tokens, width), low),
        work=pltpu.VMEM((tokens, width), full),
        mixed_low=pltpu.VMEM((4 * tokens, width), low),
        gates_low=pltpu.VMEM((3 * tokens, width), low),
        gate_low=pltpu.VMEM((tokens, hidden_columns), low),
        up_low=pltpu.VMEM((tokens, hidden_columns), low),
        active_low=pltpu.VMEM((tokens, hidden_columns), low),
        keys_low=pltpu.VMEM((tokens, width // 2), low),
        queries_low=pltpu.VMEM((tokens, width), low),
        scaled=pltpu.VMEM((tokens, width), low),
        both=pltpu.VMEM((rows, total_length, width), low),
        paired=pltpu.VMEM((pairs, 2 * length, 2 * HEAD_DIM), low),
        sums=pltpu.VMEM((pairs, 2 * length, 2 * HEAD_DIM), full),
        turned_one=pltpu.VMEM(x_shape(width), low),
        turned_two=pltpu.VMEM(x_shape(width), low),
        turned_three=pltpu.VMEM(x_shape(width), low),
        turned_four=pltpu.VMEM(x_shape(width), low),
        turned_five=pltpu.VMEM(x_shape(width), low),
        turned_active=pltpu.VMEM(x_shape(hidden_columns), low),
        vectors=pltpu.VMEM((16, width), full),
        cosine=pltpu.VMEM((tokens, 2 * HEAD_DIM), full),
        sine=pltpu.VMEM((tokens, 2 * HEAD_DIM), full),
        seg_start=pltpu.VMEM((tokens, 2 * HEAD_DIM), jnp.int32),
        halo_out=pltpu.VMEM((rows, 8, width), full),
        halo_in=pltpu.VMEM((rows, 8, width), full),
        tile_sem=dma((4, 3)),
        load_sem=dma((1,)),
        save_sem=dma((len(outs),)),
        halo_sem=dma((2,)),
        gather_send=dma((10,)),
        gather_recv=dma((10,)),
    )
    spaces = dict.fromkeys(resident, pltpu.VMEM)
    spaces["lengths"] = pltpu.SMEM
    any_space = pl.BlockSpec(memory_space=pl.ANY)
    weights = sum(value.size for value in arrays.values())
    results = pl.pallas_call(
        functools.partial(forward_kernel, list(arrays), list(outs), list(scratch), shards),
        out_shape=[jax.ShapeDtypeStruct(shape, kind) for shape, kind in outs.values()],
        in_specs=[pl.BlockSpec(memory_space=spaces.get(name, pl.ANY)) for name in arrays],
        out_specs=[any_space] * len(outs),
        scratch_shapes=list(scratch.values()),
        compiler_params=pltpu.CompilerParams(
            collective_id=collective_id, has_side_effects=True, vmem_limit_bytes=60 * 2**20
        ),
        cost_estimate=pl.CostEstimate(
            flops=2 * weights * tokens, bytes_accessed=2 * weights, transcendentals=0
        ),
    )(*arrays.values())
    return dict(zip(outs, results))


SECOND, ATTEND_OUTPUT, ATTENTION, QUERIES, KEYS, FIRST, MIXER_OUTPUT, HALO, MIXER_INPUT, CLOSE = range(10)
BACKWARD_STARTS = {
    SECOND: 0,
    ATTEND_OUTPUT: 8,
    ATTENTION: 10,
    QUERIES: 26,
    KEYS: 31,
    FIRST: 32,
    MIXER_OUTPUT: 41,
    HALO: 43,
    MIXER_INPUT: 44,
    CLOSE: 47,
}
LOCAL_PAIRS = (18, 19, 26, 27)


def backward_kernel(names, entries, row_count, shards, *refs):
    at = types.SimpleNamespace(**dict(zip(names, refs)))
    outs = refs[len(names) : len(names) + len(entries)]
    token_out, mixed_out = refs[len(names) + len(entries) : len(names) + len(entries) + 2]
    scratch = refs[len(names) + len(entries) + 2 :]
    (
        tiles_a,
        tiles_b,
        tiles_c,
        saved,
        keys_values,
        key_grads,
        key_sums,
        queries,
        attended_grad,
        wide,
        queries_raw,
        keys_raw,
        gradient,
        normed_grad,
        hidden,
        halo_out,
        halo_in,
        small,
        tile_sem,
        load_sem,
        halo_sem,
        *scratch,
    ) = scratch
    local = types.SimpleNamespace()
    exchange = Exchange(entries, row_count, shards, outs, scratch, LOCAL_PAIRS, local)
    exchange.last_rows = 16
    x_all, g_all = exchange.x_all, exchange.g_all
    seq, row = exchange.seq, exchange.row
    tokens, width = gradient.shape
    rows = keys_values.shape[0]
    length = tokens // rows
    hidden_blocks = at.first_gate.shape[1] // COLS
    blocks = width // COLS
    g_at = [entry[2] * COLS for entry in entries]
    second_wide, second_down, output_at, heads_at, first_down, first_wide = g_at[:6]
    mixer_out_at, mixer_in_at, small_at = g_at[6:]
    starts = BACKWARD_STARTS

    def local_place(kind, index):
        first, second, third, fourth = LOCAL_PAIRS
        row_at = jnp.where(index >= third, 1, 0)
        quad = jnp.where(jnp.logical_or(index == second, index == fourth), 1, 0)
        return row_at, pl.ds(pl.multiple_of(quad * COLS, COLS), COLS)

    def part(kind, index, side):
        row_at, columns = local_place(kind, index)
        return key_grads[row_at, :, side, kind, :, columns]

    def take(kind, index, total):
        row_at, columns = local_place(kind, index)
        key_sums[row_at, kind, :, columns] = total.astype(jnp.bfloat16)

    local.part, local.take = part, take

    def tile_copies(name, j, slot):
        columns = pl.ds(pl.multiple_of(j * COLS, COLS), COLS)
        a, b, c = tiles_a.at[slot], tiles_b.at[slot], tiles_c.at[slot]
        if name == SECOND:
            moves = [
                (at.second_gate.at[:, columns], b),
                (at.second_up.at[:, columns], c),
                (at.second_down.at[columns], a),
            ]
        elif name == FIRST:
            moves = [
                (at.first_down.at[columns], a),
                (at.first_gate.at[:, columns], b),
                (at.first_up.at[:, columns], c),
                (at.gate_one.at[:, columns], saved.at[slot, 0]),
                (at.up_one.at[:, columns], saved.at[slot, 1]),
            ]
        elif name == ATTEND_OUTPUT:
            moves = [(at.attend_output.at[columns], a)]
        elif name == MIXER_OUTPUT:
            moves = [(at.mixer_output.at[columns], a)]
        elif name == QUERIES:
            moves = [
                (at.query_weight.at[:, pl.ds(0, COLS)], b),
                (at.query_weight.at[:, pl.ds(COLS, COLS)], c),
            ]
        elif name == KEYS:
            moves = [(at.key_weight, b), (at.value_weight, c)]
        else:
            even = pl.multiple_of(2 * j * COLS, COLS)
            odd = pl.multiple_of((2 * j + 1) * COLS, COLS)
            moves = [
                (at.mixer_input.at[:, pl.ds(even, COLS)], b),
                (at.mixer_input.at[:, pl.ds(odd, COLS)], c),
            ]
        return [
            pltpu.make_async_copy(source, target, tile_sem.at[slot, place])
            for place, (source, target) in enumerate(moves)
        ]

    steps = [
        (SECOND, hidden_blocks),
        (ATTEND_OUTPUT, blocks),
        (QUERIES, 1),
        (KEYS, 1),
        (FIRST, hidden_blocks),
        (MIXER_OUTPUT, blocks),
        (MIXER_INPUT, 3 * blocks // 2),
    ]
    first_step, total = {}, 0
    for name, number in steps:
        first_step[name] = total
        total += number
    order = [name for name, _ in steps]
    numbers = dict(steps)

    def tile_step(name, j):
        slot = (first_step[name] + j) % 2 if isinstance(j, int) else lax.rem(first_step[name] + j, 2)
        for copy in tile_copies(name, j, slot):
            copy.wait()

        @pl.when(j + 1 < numbers[name])
        def _():
            for copy in tile_copies(name, j + 1, 1 - slot):
                copy.start()

        if name != order[-1]:
            following = order[order.index(name) + 1]

            @pl.when(j + 1 == numbers[name])
            def _():
                for copy in tile_copies(following, 0, 1 - slot):
                    copy.start()

        return slot

    def load(place, source, target):
        return pltpu.make_async_copy(source, target, load_sem.at[place])

    count = len(entries)
    x_loads = [
        load(number, at.xs[number - 2], x_all.at[:, :, pl.ds(x_first, x_count)])
        for number, (x_first, x_count, _, _, _) in enumerate(entries)
        if 2 <= number < count - 1
    ]
    cotangent_load = load(count, at.cotangent, g_all.at[:, pl.ds(second_down, width)])
    middle_loads = [
        load(count + 1, at.queries_out, queries),
        load(count + 2, at.keys_values, keys_values),
        load(count + 5, at.keys_raw, keys_raw),
    ]
    raw_load = load(count + 4, at.queries_raw, queries_raw)
    staged = queries_raw
    late_loads = [
        load(count + 6, at.mixer_saved, keys_values.at[0]),
        load(count + 7, at.projected, keys_values.at[1, pl.ds(0, 3 * tokens)]),
    ]
    hidden_loads = [
        load(count + 8, source, hidden)
        for source in (at.hidden_three, at.hidden_two, at.hidden_one, at.hidden_zero)
    ]
    out_copy = load(count + 9, staged, token_out)
    mixed_copy = load(count + 9, staged, mixed_out)

    hidden_loads[0].start()
    cotangent_load.start()
    for copy in tile_copies(SECOND, 0, 0):
        copy.start()
    for copy in middle_loads + x_loads:
        copy.start()
    normed_grad[...] = jnp.zeros_like(normed_grad)
    small[...] = jnp.zeros_like(small)
    g_all[:, pl.ds(small_at, COLS)] = jnp.zeros((tokens, COLS), jnp.bfloat16)
    wide[...] = jnp.zeros_like(wide)
    hidden_loads[0].wait()
    normed = attended_grad
    x_two = entries[0][0]
    for first in range(0, tokens, 128):
        span = pl.ds(first, 128)
        value = hidden[span]
        inverse = lax.rsqrt(jnp.mean(value * value, axis=-1, keepdims=True) + EPS)
        value = value * inverse * at.vectors[0:1, :]
        normed[span] = value.astype(jnp.bfloat16)
        turned = value.T.astype(jnp.bfloat16)
        shape = x_all.shape[:2] + (2,) + x_all.shape[3:4] + (128,)
        x_all[:, :, x_two : x_two + 2, :, pl.ds(first, 128)] = turned.reshape(shape)
    cotangent_load.wait()
    gradient[...] = g_all[:, pl.ds(second_down, width)].astype(jnp.float32)

    def low_gradient(place):
        g_all[:, pl.ds(place, width)] = gradient[...].astype(jnp.bfloat16)

    def norm_back(number):
        if number > 0:
            hidden_loads[number].wait()
        gain = at.vectors[number : number + 1, :]
        sums = jnp.zeros((1, width), jnp.float32)
        piece = 64
        for first in range(0, tokens, piece):
            span = pl.ds(first, piece)
            value, upper = hidden[span], normed_grad[span]
            inverse = lax.rsqrt(jnp.mean(value * value, axis=-1, keepdims=True) + EPS)
            value = value * inverse
            sums = sums + jnp.sum(upper * value, axis=0, keepdims=True)
            upper = upper * gain
            shift = jnp.mean(upper * value, axis=-1, keepdims=True)
            gradient[span] = gradient[span] + inverse * (upper - value * shift)
        for block in range(blocks):
            place = blocks * number + block
            small[place : place + 1, :] = sums[:, block * COLS : (block + 1) * COLS]
        normed_grad[...] = jnp.zeros_like(normed_grad)
        if number + 1 < len(hidden_loads):
            hidden_loads[number + 1].start()

    def feed_tile(name, j, gradient_at, wide_at):
        slot = tile_step(name, j)
        low = g_all[:, pl.ds(gradient_at, width)]
        active_grad = dot_nt(low, tiles_a[slot])
        if name == SECOND:
            gate_value = jnp.dot(normed[...], tiles_b[slot], preferred_element_type=jnp.float32)
            up_value = jnp.dot(normed[...], tiles_c[slot], preferred_element_type=jnp.float32)
        else:
            gate_value = saved[slot, 0].astype(jnp.float32)
            up_value = saved[slot, 1].astype(jnp.float32)
        share = 1.0 / (1.0 + jnp.exp(-gate_value))
        if name == SECOND:
            active = gate_value * share * up_value
            wide[...] += jnp.dot(
                active.astype(jnp.bfloat16), tiles_a[slot], preferred_element_type=jnp.float32
            )
            turned = active.T.astype(jnp.bfloat16)
            x_down, x_count = entries[1][:2]
            block_rows = x_all.shape[3]
            for block in range(COLS // block_rows):
                place = j * (COLS // block_rows) + block
                shard = place // x_count
                part = turned[block * block_rows : (block + 1) * block_rows]
                x_all[shard // 2, lax.rem(shard, 2), x_down + lax.rem(place, x_count)] = part
        up_grad = (active_grad * gate_value * share).astype(jnp.bfloat16)
        gate_grad = active_grad * up_value * share * (1.0 + gate_value * (1.0 - share))
        gate_grad = gate_grad.astype(jnp.bfloat16)
        gate_place = pl.multiple_of(wide_at + j * COLS, COLS)
        up_place = pl.multiple_of(wide_at + (hidden_blocks + j) * COLS, COLS)
        g_all[:, pl.ds(gate_place, COLS)] = gate_grad
        g_all[:, pl.ds(up_place, COLS)] = up_grad
        normed_grad[...] += dot_nt(gate_grad, tiles_b[slot]) + dot_nt(up_grad, tiles_c[slot])

    def output_tile(name, j, gradient_at, target):
        slot = tile_step(name, j)
        low = g_all[:, pl.ds(gradient_at, width)]
        value = dot_nt(low, tiles_a[slot])
        target[:, j * COLS : (j + 1) * COLS] = value.astype(target.dtype)

    def attention_head(row_at, head):
        span = pl.ds(pl.multiple_of(row_at * length, length), length)
        columns = pl.ds(pl.multiple_of(head * 2 * HEAD_DIM, 2 * HEAD_DIM), 2 * HEAD_DIM)
        query = two_heads(queries[span, columns], True)
        upper = two_heads(attended_grad[span, columns], False)
        both = keys_values[row_at, :, columns]
        key_at = lax.broadcasted_iota(jnp.int32, (both.shape[0], length), 0)
        query_at = lax.broadcasted_iota(jnp.int32, (both.shape[0], length), 1) + seq * length
        start = segment_start(at.lengths, row_at, query_at[0:8])[0:1]
        allowed = jnp.logical_and(key_at >= start, key_at <= query_at)
        weights = jnp.exp(dot_nt(both, query))
        weights = jnp.where(jnp.concatenate([allowed, allowed], axis=1), weights, 0.0)
        weights = weights * (1.0 / jnp.sum(weights, axis=0, keepdims=True))
        weight_grad_value = dot_nt(both, upper)
        delta = jnp.sum(weights * weight_grad_value, axis=0, keepdims=True)
        score_grad = (weights * (weight_grad_value - delta)).astype(jnp.bfloat16)
        both_grad = jnp.dot(score_grad, query, preferred_element_type=jnp.float32)
        both_grad += jnp.dot(
            weights.astype(jnp.bfloat16), upper, preferred_element_type=jnp.float32
        )
        shape = key_grads.shape[1:5] + (2 * HEAD_DIM,)
        key_grads[row_at, :, :, :, :, columns] = both_grad.astype(jnp.bfloat16).reshape(shape)
        query_grad = dot_tn(score_grad, both) * HEAD_DIM ** (-0.5)
        first = lanes_below((length, 2 * HEAD_DIM), HEAD_DIM, 2 * HEAD_DIM)
        wide[span, columns] = jnp.where(
            first, query_grad[:length], pltpu.roll(query_grad[length:], HEAD_DIM, 1)
        )

    lane = 2 * HEAD_DIM
    head_mean, turn = head_tools(lane)

    def head_back(value, raw, gain):
        value = value * at.cosine[...] - turn(value) * at.sine[...]
        raw = raw.astype(jnp.float32)
        inverse = lax.rsqrt(head_mean(raw * raw) + EPS)
        raw = raw * inverse
        sums = jnp.sum(value * raw, axis=0, keepdims=True)
        value = value * gain
        return inverse * (value - raw * head_mean(value * raw)), sums

    head_row = 7 * blocks

    def query_heads():
        sums = jnp.zeros((1, lane), jnp.float32)
        for part_at in range(0, width, lane):
            columns = pl.ds(part_at, lane)
            value, more = head_back(wide[:, columns], queries_raw[:, columns], both_halves(at.vectors[7:8, pl.ds(0, lane)]))
            g_all[:, pl.ds(heads_at + part_at, lane)] = value.astype(jnp.bfloat16)
            sums = sums + more
        small[head_row : head_row + 1, 0:lane] = both_halves(sums)

    def key_heads():
        sums = jnp.zeros((1, lane), jnp.float32)
        first = lanes_below((tokens, lane), HEAD_DIM, lane)
        for pair in range(width // lane // 2):
            even, odd = [
                key_sums[:, :, :, pl.ds((2 * pair + which) * lane, lane)]
                .astype(jnp.float32)
                .reshape(tokens, lane)
                for which in range(2)
            ]
            key_value = jnp.where(first, even, pltpu.roll(odd, HEAD_DIM, 1))
            value_value = jnp.where(first, pltpu.roll(even, HEAD_DIM, 1), odd)
            columns = pl.ds(pair * lane, lane)
            value, more = head_back(key_value, keys_raw[:, columns], both_halves(at.vectors[8:9, pl.ds(0, lane)]))
            place = heads_at + width + pair * lane
            g_all[:, pl.ds(place, lane)] = value.astype(jnp.bfloat16)
            place += width // 2
            g_all[:, pl.ds(place, lane)] = value_value.astype(jnp.bfloat16)
            sums = sums + more
        small[head_row : head_row + 1, lane : 2 * lane] = both_halves(sums)

    def project_back(name, j, even_at, odd_at):
        slot = tile_step(name, j)
        normed_grad[...] += dot_nt(g_all[:, pl.ds(even_at, COLS)], tiles_b[slot]) + dot_nt(
            g_all[:, pl.ds(odd_at, COLS)], tiles_c[slot]
        )

    def halo_copy():
        return pltpu.make_async_remote_copy(
            src_ref=halo_out,
            dst_ref=halo_in,
            send_sem=halo_sem.at[0],
            recv_sem=halo_sem.at[1],
            device_id=(row, jnp.maximum(seq - 1, 0)),
            device_id_type=MESH,
        )

    def saved_part(number, columns):
        return keys_values[0, pl.ds(number * tokens, tokens), columns].astype(jnp.float32)

    def projected_part(number, columns):
        return keys_values[1, pl.ds(number * tokens, tokens), columns].astype(jnp.float32)

    def convolution_back():
        within = lax.rem(lax.broadcasted_iota(jnp.int32, (tokens, lane), 0), length)
        position = within + seq * length
        start = [
            segment_start(at.lengths, which, position[which * length : (which + 1) * length])
            for which in range(rows)
        ]
        start = jnp.concatenate(start, axis=0)
        keep_one = position - 1 >= start
        keep_two = position - 2 >= start
        edge = lax.broadcasted_iota(jnp.int32, (8, lane), 0)
        for part_at in range(0, width, lane):
            columns = pl.ds(part_at, lane)
            gated_grad = wide[:, columns]
            exit_grad = gated_grad * saved_part(0, columns)
            place = mixer_in_at + width + part_at
            g_all[:, pl.ds(place, lane)] = exit_grad.astype(jnp.bfloat16)
            conv_grad = gated_grad * projected_part(1, columns)
            block, inside = part_at // COLS, part_at % COLS
            for tap in range(3):
                sums = jnp.sum(conv_grad * saved_part(1 + tap, columns), axis=0, keepdims=True)
                place = blocks * (4 + tap) + block
                small[place : place + 1, inside : inside + lane] = sums
            two = jnp.where(keep_two, at.vectors[4:5, columns] * conv_grad, 0.0)
            one = jnp.where(keep_one, at.vectors[5:6, columns] * conv_grad, 0.0)
            here = at.vectors[6:7, columns] * conv_grad
            here += jnp.where(within < length - 1, pltpu.roll(one, tokens - 1, 0), 0.0)
            here += jnp.where(within < length - 2, pltpu.roll(two, tokens - 2, 0), 0.0)
            normed_grad[:, columns] = here
            for which in range(rows):
                span = slice(which * length, which * length + 8)
                sent = two[span] + jnp.where(edge == 1, pltpu.roll(one[span], 1, 0), 0.0)
                halo_out[which, :, columns] = jnp.where(edge < 2, sent, 0.0)

        @pl.when(seq > 0)
        def _():
            halo_copy().start()

    def product_back():
        @pl.when(seq < shards - 1)
        def _():
            halo_copy().wait_recv()
            for which in range(rows):
                span = pl.ds((which + 1) * length - 8, 8)
                normed_grad[span] = normed_grad[span] + pltpu.roll(halo_in[which], 6, 0)

        @pl.when(seq > 0)
        def _():
            halo_copy().wait_send()

        for part_at in range(0, width, lane):
            columns = pl.ds(part_at, lane)
            product_grad = normed_grad[:, columns]
            entry_grad = product_grad * projected_part(2, columns)
            carrier_grad = product_grad * projected_part(0, columns)
            g_all[:, pl.ds(mixer_in_at + part_at, lane)] = entry_grad.astype(jnp.bfloat16)
            place = mixer_in_at + 2 * width + part_at
            g_all[:, pl.ds(place, lane)] = carrier_grad.astype(jnp.bfloat16)
        normed_grad[...] = jnp.zeros_like(normed_grad)

    def task(i):
        def when(name, run, after=0, number=1):
            j = i - (starts[name] + after)

            @pl.when(jnp.logical_and(j >= 0, j < number))
            def _():
                run(j)

        when(
            SECOND,
            lambda j: feed_tile(SECOND, j + 1, second_down, second_wide),
            0,
            hidden_blocks - 1,
        )

        def waits(j):
            for copy in middle_loads + x_loads:
                copy.wait()

        when(ATTEND_OUTPUT, waits)

        def to_attended(j):
            staged[...] = (hidden[...] + wide[...]).astype(jnp.bfloat16)
            mixed_copy.start()
            norm_back(0)
            low_gradient(output_at)
            output_tile(ATTEND_OUTPUT, 0, output_at, attended_grad)

        when(ATTEND_OUTPUT, to_attended)
        when(ATTEND_OUTPUT, lambda j: output_tile(ATTEND_OUTPUT, 1, output_at, attended_grad), 1)

        def staged_free(j):
            mixed_copy.wait()
            raw_load.start()

        when(ATTENTION, staged_free)

        def attention(j):
            attention_head(j // KV_HEADS, lax.rem(j, KV_HEADS))

        when(ATTENTION, attention, 0, rows * KV_HEADS)

        def to_queries(j):
            raw_load.wait()
            for copy in late_loads:
                copy.start()
            query_heads()

        when(QUERIES, to_queries)
        def pick_rows(j):
            block_rows = x_all.shape[3]
            shape = (shards * 2 * block_rows, tokens)
            place = lax.broadcasted_iota(jnp.int32, shape, 0)
            vector, shard = lax.rem(place, 2 * block_rows), place // (2 * block_rows)
            wanted = blocks * vector + jnp.where(vector < 7, shard * blocks // shards, 0)
            found = lax.broadcasted_iota(jnp.int32, shape, 1) == wanted
            found = jnp.logical_and(found, vector < 8).astype(jnp.float32).astype(jnp.bfloat16)
            x_first = entries[-1][0]
            target = x_all.shape[:2] + (2, block_rows, tokens)
            x_all[:, :, x_first : x_first + 2] = found.reshape(target)

        when(QUERIES, pick_rows, 2)
        when(QUERIES, lambda j: project_back(QUERIES, 0, heads_at, heads_at + COLS), 1)

        def to_keys(j):
            key_heads()
            project_back(KEYS, 0, heads_at + width, heads_at + width + COLS)
            norm_back(1)
            low_gradient(first_down)

        when(KEYS, to_keys)
        when(FIRST, lambda j: feed_tile(FIRST, j, first_down, first_wide), 0, hidden_blocks)

        def to_gated(j):
            norm_back(2)
            low_gradient(mixer_out_at)
            output_tile(MIXER_OUTPUT, 0, mixer_out_at, wide)
            for copy in late_loads:
                copy.wait()

        when(MIXER_OUTPUT, to_gated)

        def to_convolved(j):
            output_tile(MIXER_OUTPUT, 1, mixer_out_at, wide)
            convolution_back()

        when(MIXER_OUTPUT, to_convolved, 1)
        when(HALO, lambda j: product_back())

        def mixer_tile(j):
            even = pl.multiple_of(mixer_in_at + 2 * j * COLS, COLS)
            project_back(MIXER_INPUT, j, even, pl.multiple_of(even + COLS, COLS))

        when(MIXER_INPUT, mixer_tile, 0, numbers[MIXER_INPUT])

        def close(j):
            norm_back(3)
            staged[...] = gradient[...].astype(jnp.bfloat16)
            out_copy.start()
            g_all[pl.ds(0, small.shape[0]), pl.ds(small_at, COLS)] = small[...].astype(jnp.bfloat16)

        when(CLOSE, close)
        when(CLOSE, lambda j: out_copy.wait(), 1)

    exchange.meet()
    feed_tile(SECOND, 0, second_down, second_wide)
    exchange.run(task)


def backward(groups, arrays, resident, row_count, shards, collective_id):
    xs = [x for x, _ in groups if not isinstance(x, int)]
    block_rows, tokens = xs[0].shape[3:]
    width = arrays["cotangent"].shape[1]
    entries, x_blocks, g_blocks, chunks = reduce_entries(
        [(x if isinstance(x, int) else x.shape[2], columns // COLS) for x, columns in groups]
    )
    names = ["xs_%d" % number for number in range(len(xs))] + list(arrays)
    values = list(xs) + list(arrays.values())
    rows, total_length = arrays["keys_values"].shape[:2]
    any_space = pl.BlockSpec(memory_space=pl.ANY)
    spaces = dict.fromkeys(resident, pltpu.VMEM)
    spaces["lengths"] = pltpu.SMEM
    key_blocks = total_length // shards // block_rows

    def kernel(*refs):
        xs_refs, others = refs[: len(xs)], refs[len(xs) : len(values)]
        named = [("xs", xs_refs)] + list(zip(arrays, others))
        backward_kernel(
            [name for name, _ in named],
            entries,
            row_count,
            shards,
            *[ref for _, ref in named],
            *refs[len(values) :],
        )

    low, full = jnp.bfloat16, jnp.float32
    return pl.pallas_call(
        kernel,
        out_shape=[
            jax.ShapeDtypeStruct((x_count * block_rows, g_count * COLS), low)
            for _, x_count, _, g_count, _ in entries
        ]
        + [jax.ShapeDtypeStruct((tokens, width), low)] * 2,
        in_specs=[pl.BlockSpec(memory_space=spaces.get(name, pl.ANY)) for name in names],
        out_specs=[any_space] * (len(entries) + 2),
        scratch_shapes=[
            pltpu.VMEM((2, COLS, width), low),
            pltpu.VMEM((2, width, COLS), low),
            pltpu.VMEM((2, width, COLS), low),
            pltpu.VMEM((2, 2, tokens, COLS), low),
            pltpu.VMEM((rows, total_length, width), low),
            pltpu.VMEM((rows, shards // 2, 2, key_blocks, block_rows, width), low),
            pltpu.VMEM((rows, key_blocks, block_rows, width), low),
            pltpu.VMEM((tokens, width), low),
            pltpu.VMEM((tokens, width), low),
            pltpu.VMEM((tokens, width), full),
            pltpu.VMEM((tokens, width), low),
            pltpu.VMEM((tokens, width // 2), low),
            pltpu.VMEM((tokens, width), full),
            pltpu.VMEM((tokens, width), full),
            pltpu.VMEM((tokens, width), full),
            pltpu.VMEM((rows, 8, width), full),
            pltpu.VMEM((rows, 8, width), full),
            pltpu.VMEM((16, COLS), full),
            pltpu.SemaphoreType.DMA((2, 5)),
            pltpu.SemaphoreType.DMA((len(entries) + 10,)),
            pltpu.SemaphoreType.DMA((2,)),
            *exchange_scratch(row_count, shards, block_rows, x_blocks, g_blocks, tokens),
        ],
        compiler_params=pltpu.CompilerParams(
            collective_id=collective_id, has_side_effects=True, vmem_limit_bytes=63 * 2**20
        ),
        cost_estimate=pl.CostEstimate(
            flops=4 * chunks * shards * block_rows * COLS * tokens,
            bytes_accessed=2 * chunks * shards * block_rows * COLS,
            transcendentals=0,
        ),
    )(*values)


def fused_body(
    tokens,
    lengths,
    mixer_gain,
    mixer_input,
    mixer_kernel,
    mixer_output,
    first_gain,
    first_gate,
    first_up,
    first_down,
    attend_gain,
    query_weight,
    key_weight,
    value_weight,
    query_gain,
    key_gain,
    attend_output,
    second_gain,
    second_gate,
    second_up,
    second_down,
    cotangent,
):
    full, low = jnp.float32, jnp.bfloat16
    rows, length, width = tokens.shape
    token_count = rows * length
    lane = 2 * HEAD_DIM
    row_count, shards = lax.axis_size("row"), lax.axis_size("seq")
    seq = lax.axis_index("seq")
    tables = dict(
        lengths=lengths,
        mixer_kernel=mixer_kernel,
        mixer_gain=mixer_gain,
        first_gain=first_gain,
        attend_gain=attend_gain,
        second_gain=second_gain,
        query_gain=query_gain,
        key_gain=key_gain,
    )
    arrays = dict(
        tokens=tokens.reshape(token_count, width),
        mixer_input=mixer_input,
        mixer_output=mixer_output,
        first_gate=first_gate,
        first_up=first_up,
        first_down=first_down,
        query_weight=query_weight,
        key_weight=key_weight,
        value_weight=value_weight,
        attend_output=attend_output,
        **tables,
    )
    saved = types.SimpleNamespace(**forward(arrays, tuple(tables), rows, shards, 2))
    block_rows = saved.attended_x.shape[3]
    weights = dict(
        second_down=second_down,
        second_gate=second_gate,
        second_up=second_up,
        attend_output=attend_output,
        query_weight=query_weight,
        key_weight=key_weight,
        value_weight=value_weight,
        first_down=first_down,
        first_gate=first_gate,
        first_up=first_up,
        mixer_output=mixer_output,
        mixer_input=mixer_input,
    )
    tables = dict(vectors=saved.vectors_out, cosine=saved.cosine_out, sine=saved.sine_out)
    arrays = dict(
        lengths=lengths,
        cotangent=cotangent.reshape(token_count, width),
        gate_one=saved.gate_one,
        up_one=saved.up_one,
        hidden_three=saved.hidden_three,
        hidden_two=saved.hidden_two,
        hidden_one=saved.hidden_one,
        hidden_zero=saved.hidden_zero,
        queries_out=saved.queries_out,
        keys_values=saved.keys_values,
        queries_raw=saved.queries_raw,
        keys_raw=saved.keys_raw,
        mixer_saved=saved.mixer_saved,
        projected=saved.projected,
        **tables,
        **weights,
    )
    hidden_columns = first_gate.shape[1]
    head_columns = width + 2 * key_weight.shape[1]
    groups = [
        (width // shards // block_rows, 2 * hidden_columns),
        (hidden_columns // shards // block_rows, width),
        (saved.attended_x, width),
        (saved.attend_in_x, head_columns),
        (saved.active_x, width),
        (saved.first_in_x, 2 * hidden_columns),
        (saved.gated_x, width),
        (saved.mixer_in_x, 3 * width),
        (2, COLS),
    ]
    (
        second_both,
        grad_second_down,
        grad_attend_output,
        attend_three,
        grad_first_down,
        first_both,
        grad_mixer_output,
        grad_mixer_input,
        sums,
        token_grad,
        mixed,
    ) = backward(groups, arrays, tuple(tables), row_count, shards, 1)

    key_columns = key_weight.shape[1]
    lows = [second_both, first_both, grad_second_down, grad_first_down]
    lows += [attend_three, grad_attend_output, grad_mixer_output, grad_mixer_input]
    fulls, (mixed, token_grad), small = to_full(
        (mixed, token_grad),
        sums,
        lows,
        (
            (0, 0, hidden_columns),
            (0, hidden_columns, hidden_columns),
            (1, 0, hidden_columns),
            (1, hidden_columns, hidden_columns),
            (2, 0, width),
            (3, 0, width),
            (4, 0, width),
            (4, width, key_columns),
            (4, width + key_columns, key_columns),
            (5, 0, width),
            (6, 0, width),
            (7, 0, 3 * width),
        ),
        shards,
    )
    (
        second_gate_full,
        second_up_full,
        first_gate_full,
        first_up_full,
        second_down_full,
        first_down_full,
        query_full,
        key_full,
        value_full,
        attend_output_full,
        mixer_output_full,
        mixer_input_full,
    ) = fulls
    return (
        mixed.reshape(tokens.shape),
        token_grad.reshape(tokens.shape),
        small[3],
        mixer_input_full,
        small[4],
        mixer_output_full,
        small[2],
        first_gate_full,
        first_up_full,
        first_down_full,
        small[1],
        query_full,
        key_full,
        value_full,
        small[5],
        small[6],
        attend_output_full,
        small[0],
        second_gate_full,
        second_up_full,
        second_down_full,
    )


def fused_or_general(*args):
    tokens = args[0]
    rows, length, width = tokens.shape
    row_count, shards = lax.axis_size("row"), lax.axis_size("seq")
    key_bytes = 2 * rows * length * shards * width
    if key_bytes <= 4 * 2**20 and shards == 8 and 4 * rows == shards and row_count == 4:
        return fused_body(*args)
    return body(*args)


def solution(mesh):
    in_specs = (
        P("row", "seq", None),
        P("row", None),
        P(),
        P(),
        P(),
        P(),
        P(),
        P(),
        P(),
        P(),
        P(),
        P(),
        P(),
        P(),
        P(),
        P(),
        P(),
        P(),
        P(),
        P(),
        P(),
        P("row", "seq", None),
    )
    out_specs = (
        P("row", "seq", None),
        P("row", "seq", None),
        P("seq"),
        P("seq", None),
        P(None, "seq"),
        P("seq", None),
        P("seq"),
        P("seq", None),
        P("seq", None),
        P("seq", None),
        P("seq"),
        P("seq", None),
        P("seq", None),
        P("seq", None),
        P("seq"),
        P("seq"),
        P("seq", None),
        P("seq"),
        P("seq", None),
        P("seq", None),
        P("seq", None),
    )
    return jax.shard_map(fused_or_general, mesh=mesh, in_specs=in_specs, out_specs=out_specs, check_vma=False)
```

```python
import functools
import math
import types

import jax
import jax.numpy as jnp
from jax import lax
from jax.experimental import pallas as pl
from jax.experimental.pallas import tpu as pltpu
from jax.sharding import PartitionSpec as P

HEADS = 16
KV_HEADS = 8
HEAD_DIM = 64
GROUP = 2


EPS = 1e-05
THETA = 1000000.0
NEGATIVE = -1e30
HIGHEST = lax.Precision.HIGHEST
MESH = pl.DeviceIdType.MESH
COLS = 512
SLOTS = 4
ZSLOTS = 6


def passed_along(value, axis, steps):
    count = lax.axis_size(axis)
    initial, last = (max(0, -steps), min(count, count - steps))
    return lax.ppermute(value, axis, [(source, source + steps) for source in range(initial, last)])


def segment_info(lengths, positions):
    boundary = jnp.cumsum(lengths, axis=-1)
    passed = boundary[:, None, :] <= positions[None, :, None]
    segment = jnp.sum(passed.astype(jnp.int32), axis=-1)
    seg_start = jnp.max(jnp.where(passed, boundary[:, None, :], 0), axis=-1)
    return (segment, seg_start)


def norm_rows(values, norm_gain):
    return values * lax.rsqrt(jnp.mean(values * values, axis=-1, keepdims=True) + EPS) * norm_gain


def rotate(values, offsets):
    half_dim = values.shape[-1] // 2
    inverse = THETA ** (-2.0 * jnp.arange(half_dim, dtype=jnp.float32) / values.shape[-1])
    angles = offsets.astype(jnp.float32)[:, :, None, None] * inverse
    cosine = jnp.cos(angles)
    sine_table = jnp.sin(angles)
    leading = values[..., :half_dim]
    trailing = values[..., half_dim:]
    return jnp.concatenate(
        [leading * cosine - trailing * sine_table, trailing * cosine + leading * sine_table],
        axis=-1,
    )


def swiglu(gate_value, upward):
    return gate_value / (1.0 + jnp.exp(-gate_value)) * upward


def dense(inputs, matrix):
    return jnp.einsum("rtd,df->rtf", inputs, matrix, preferred_element_type=jnp.float32)


def weight_grad(inputs, gradient):
    return (inputs, gradient)


def back_dense(gradient, matrix):
    return jnp.einsum("rtf,df->rtd", gradient, matrix, preferred_element_type=jnp.float32)


def mixer_block(hidden, norm_gain, input_matrix, kernel, output_matrix, seg_start, positions):
    feature_columns = hidden.shape[-1]
    length = hidden.shape[1]
    normed, norm_back = jax.vjp(norm_rows, hidden, norm_gain.astype(jnp.float32))
    normed_low = normed.astype(jnp.bfloat16)
    projected_rows = dense(normed_low, input_matrix)
    input_gate_value = projected_rows[..., :feature_columns]
    exit_gate = projected_rows[..., feature_columns : 2 * feature_columns]
    carry_value = projected_rows[..., 2 * feature_columns :]
    gated_product_reduced = (input_gate_value * carry_value).astype(jnp.bfloat16)
    previous = passed_along(gated_product_reduced[:, length - 2 :, :], "seq", 1)
    extended = jnp.concatenate([previous, gated_product_reduced], axis=1).astype(jnp.float32)
    keep_one = (positions[None, :] - 1 >= seg_start).astype(jnp.float32)[..., None]
    keep_two = (positions[None, :] - 2 >= seg_start).astype(jnp.float32)[..., None]
    kernel_taps = kernel.astype(jnp.float32)
    two_back = extended[:, :length]
    one_back = extended[:, 1 : length + 1]
    current = extended[:, 2:]
    convolved = (
        kernel_taps[2] * current
        + kernel_taps[1] * keep_one * one_back
        + kernel_taps[0] * keep_two * two_back
    )
    gated_low = (exit_gate * convolved).astype(jnp.bfloat16)
    result = hidden + dense(gated_low, output_matrix)

    def mixer_backward(gradient):
        gradient_low = gradient.astype(jnp.bfloat16)
        grad_output = weight_grad(gated_low, gradient_low)
        grad_gated = back_dense(gradient_low, output_matrix)
        output_gate_gradient = grad_gated * convolved
        grad_conv = grad_gated * exit_gate
        grad_kernel = jnp.stack(
            [
                jnp.sum(grad_conv * keep_two * two_back, axis=(0, 1)),
                jnp.sum(grad_conv * keep_one * one_back, axis=(0, 1)),
                jnp.sum(grad_conv * current, axis=(0, 1)),
            ]
        )
        grad_extended = jnp.pad(kernel_taps[0] * keep_two * grad_conv, ((0, 0), (0, 2), (0, 0)))
        grad_extended = grad_extended + jnp.pad(
            kernel_taps[1] * keep_one * grad_conv, ((0, 0), (1, 1), (0, 0))
        )
        grad_extended = grad_extended + jnp.pad(
            kernel_taps[2] * grad_conv, ((0, 0), (2, 0), (0, 0))
        )
        returned = passed_along(grad_extended[:, :2, :], "seq", -1)
        gated_product_gradient = grad_extended[:, 2:] + jnp.pad(
            returned, ((0, 0), (length - 2, 0), (0, 0))
        )
        grad_projected = jnp.concatenate(
            [
                gated_product_gradient * carry_value,
                output_gate_gradient,
                gated_product_gradient * input_gate_value,
            ],
            axis=-1,
        ).astype(jnp.bfloat16)
        grad_input = weight_grad(normed_low, grad_projected)
        grad_normed = back_dense(grad_projected, input_matrix)
        grad_hidden, grad_gain = norm_back(grad_normed)
        return (gradient + grad_hidden, (grad_gain, grad_input, grad_kernel, grad_output))

    return (result, mixer_backward)


def feed_block(hidden, norm_gain, gate_matrix, up_matrix, down_matrix):
    normed, norm_back = jax.vjp(norm_rows, hidden, norm_gain.astype(jnp.float32))
    normed_low = normed.astype(jnp.bfloat16)
    gate_value = dense(normed_low, gate_matrix)
    upward = dense(normed_low, up_matrix)
    active, active_back = jax.vjp(swiglu, gate_value, upward)
    active_low = active.astype(jnp.bfloat16)
    result = hidden + dense(active_low, down_matrix)

    def feed_backward(gradient):
        gradient_low = gradient.astype(jnp.bfloat16)
        grad_down = weight_grad(active_low, gradient_low)
        grad_gate, grad_upward = active_back(back_dense(gradient_low, down_matrix))
        gate_low = grad_gate.astype(jnp.bfloat16)
        upward_low = grad_upward.astype(jnp.bfloat16)
        grad_normed = back_dense(gate_low, gate_matrix) + back_dense(upward_low, up_matrix)
        grad_hidden, grad_gain = norm_back(grad_normed)
        return (
            gradient + grad_hidden,
            (
                grad_gain,
                weight_grad(normed_low, jnp.concatenate([gate_low, upward_low], axis=-1)),
                grad_down,
            ),
        )

    return (result, feed_backward)


def attend_block(
    hidden,
    lengths,
    norm_gain,
    query_matrix,
    key_matrix,
    value_matrix,
    query_norm,
    key_norm,
    output_matrix,
    segment,
    positions,
    offsets,
):
    row_count, length, feature_columns = hidden.shape
    score_scale = HEAD_DIM ** (-0.5)
    normed, norm_back = jax.vjp(norm_rows, hidden, norm_gain.astype(jnp.float32))
    normed_low = normed.astype(jnp.bfloat16)

    def head_path(projected_rows, head_gain):
        return rotate(norm_rows(projected_rows, head_gain), offsets)

    queries = dense(normed_low, query_matrix).reshape(row_count, length, HEADS, HEAD_DIM)
    keys_raw = dense(normed_low, key_matrix).reshape(row_count, length, KV_HEADS, HEAD_DIM)
    values_raw = dense(normed_low, value_matrix)
    query_rot, query_back = jax.vjp(head_path, queries, query_norm.astype(jnp.float32))
    key_rot, key_back = jax.vjp(head_path, keys_raw, key_norm.astype(jnp.float32))
    query_low = query_rot.astype(jnp.bfloat16).reshape(row_count, length, KV_HEADS, GROUP, HEAD_DIM)
    key_low = key_rot.astype(jnp.bfloat16)
    value_low = values_raw.astype(jnp.bfloat16).reshape(row_count, length, KV_HEADS, HEAD_DIM)
    all_keys, all_values = (
        lax.all_gather(key_low, "seq", axis=1, tiled=True),
        lax.all_gather(value_low, "seq", axis=1, tiled=True),
    )
    total_length = all_keys.shape[1]
    key_block = min(512, total_length)
    block_count = (positions[length - 1] + key_block) // key_block

    def block_scores(number, key_source, value_source):
        first_key = number * key_block
        keys_here = lax.dynamic_slice_in_dim(key_source, first_key, key_block, 1)
        values_here = lax.dynamic_slice_in_dim(value_source, first_key, key_block, 1)
        key_positions = first_key + jnp.arange(key_block, dtype=jnp.int32)
        key_segment, unused = segment_info(lengths, key_positions)
        scores = (
            jnp.einsum(
                "rtkgh,rskh->rkgts", query_low, keys_here, preferred_element_type=jnp.float32
            )
            * score_scale
        )
        allowed = (segment[:, :, None] == key_segment[:, None, :]) & (
            positions[None, :, None] >= key_positions[None, None, :]
        )
        allowed = allowed[:, None, None]
        return (jnp.where(allowed, scores, NEGATIVE), allowed, keys_here, values_here)

    stat_shape = (row_count, KV_HEADS, GROUP, length)

    def stats_step(number, carried):
        peak_score, running_sum = carried
        scores, allowed, unused_keys, unused_values = block_scores(number, all_keys, all_values)
        new_peak = jnp.maximum(peak_score, jnp.max(scores, axis=-1))
        fresh = jnp.sum(jnp.where(allowed, jnp.exp(scores - new_peak[..., None]), 0.0), axis=-1)
        return (new_peak, running_sum * jnp.exp(peak_score - new_peak) + fresh)

    peak_score, running_sum = lax.fori_loop(
        0,
        block_count,
        stats_step,
        (jnp.full(stat_shape, NEGATIVE, jnp.float32), jnp.zeros(stat_shape, jnp.float32)),
    )
    log_total = peak_score + jnp.log(running_sum)

    def probabilities(scores, allowed):
        return jnp.where(allowed, jnp.exp(scores - log_total[..., None]), 0.0)

    out_shape = (row_count, length, KV_HEADS, GROUP, HEAD_DIM)

    def output_step(number, carried):
        rounded, exact_sum = carried
        scores, allowed, keys_here, values_here = block_scores(number, all_keys, all_values)
        weights = probabilities(scores, allowed)
        rounded = rounded + jnp.einsum(
            "rkgts,rskh->rtkgh",
            weights.astype(jnp.bfloat16),
            values_here,
            preferred_element_type=jnp.float32,
        )
        exact_sum = exact_sum + jnp.einsum(
            "rkgts,rskh->rtkgh", weights, values_here.astype(jnp.float32), precision=HIGHEST
        )
        return (rounded, exact_sum)

    rounded, exact_sum = lax.fori_loop(
        0,
        block_count,
        output_step,
        (jnp.zeros(out_shape, jnp.float32), jnp.zeros(out_shape, jnp.float32)),
    )
    attended_low = rounded.reshape(row_count, length, HEADS * HEAD_DIM).astype(jnp.bfloat16)
    result = hidden + dense(attended_low, output_matrix)

    def attend_backward(gradient):
        gradient_low = gradient.astype(jnp.bfloat16)
        grad_output = weight_grad(attended_low, gradient_low)
        grad_attended = (
            back_dense(gradient_low, output_matrix).astype(jnp.bfloat16).reshape(out_shape)
        )
        row_delta = jnp.einsum(
            "rtkgh,rtkgh->rkgt", grad_attended.astype(jnp.float32), exact_sum, precision=HIGHEST
        )
        key_source, value_source = (all_keys, all_values)

        def grad_step(number, carried):
            grad_query, grad_keys, grad_values = carried
            scores, allowed, keys_here, values_here = block_scores(number, key_source, value_source)
            weights = probabilities(scores, allowed)
            grad_weights = jnp.einsum(
                "rtkgh,rskh->rkgts", grad_attended, values_here, preferred_element_type=jnp.float32
            )
            grad_scores = (weights * (grad_weights - row_delta[..., None])).astype(jnp.bfloat16)
            grad_query = (
                grad_query
                + jnp.einsum(
                    "rkgts,rskh->rtkgh", grad_scores, keys_here, preferred_element_type=jnp.float32
                )
                * score_scale
            )
            key_part = (
                jnp.einsum(
                    "rkgts,rtkgh->rskh", grad_scores, query_low, preferred_element_type=jnp.float32
                )
                * score_scale
            )
            value_part = jnp.einsum(
                "rkgts,rtkgh->rskh",
                weights.astype(jnp.bfloat16),
                grad_attended,
                preferred_element_type=jnp.float32,
            )
            grad_keys = lax.dynamic_update_slice_in_dim(grad_keys, key_part, number * key_block, 1)
            grad_values = lax.dynamic_update_slice_in_dim(
                grad_values, value_part, number * key_block, 1
            )
            return (grad_query, grad_keys, grad_values)

        key_shape = (row_count, total_length, KV_HEADS, HEAD_DIM)
        grad_query, grad_keys, grad_values = lax.fori_loop(
            0,
            block_count,
            grad_step,
            (
                jnp.zeros(out_shape, jnp.float32),
                jnp.zeros(key_shape, jnp.float32),
                jnp.zeros(key_shape, jnp.float32),
            ),
        )
        local_keys, local_values = (
            lax.psum_scatter(
                grad_keys.astype(jnp.bfloat16), "seq", scatter_dimension=1, tiled=True
            ).astype(jnp.float32),
            lax.psum_scatter(
                grad_values.astype(jnp.bfloat16), "seq", scatter_dimension=1, tiled=True
            ).astype(jnp.float32),
        )
        grad_queries, grad_query_norm = query_back(
            grad_query.reshape(row_count, length, HEADS, HEAD_DIM)
        )
        grad_keys_raw, grad_key_norm = key_back(local_keys)
        query_grad_low = grad_queries.reshape(row_count, length, HEADS * HEAD_DIM).astype(
            jnp.bfloat16
        )
        key_grad_low = grad_keys_raw.reshape(row_count, length, KV_HEADS * HEAD_DIM).astype(
            jnp.bfloat16
        )
        value_grad_low = local_values.reshape(row_count, length, KV_HEADS * HEAD_DIM).astype(
            jnp.bfloat16
        )
        grad_normed = (
            back_dense(query_grad_low, query_matrix)
            + back_dense(key_grad_low, key_matrix)
            + back_dense(value_grad_low, value_matrix)
        )
        grad_hidden, grad_gain = norm_back(grad_normed)
        return (
            gradient + grad_hidden,
            (
                grad_gain,
                weight_grad(
                    normed_low,
                    jnp.concatenate([query_grad_low, key_grad_low, value_grad_low], axis=-1),
                ),
                grad_query_norm,
                grad_key_norm,
                grad_output,
            ),
        )

    return (result, attend_backward)


def reduce_entries(pairs):
    entries = []
    x_first = g_first = chunk = 0
    for x_count, g_count in pairs:
        entries.append((x_first, x_count, g_first, g_count, chunk))
        x_first += x_count
        g_first += g_count
        chunk += x_count * g_count
    return entries, x_first, g_first, chunk


def locate(entries, q):
    x_block, g_block = jnp.int32(0), jnp.int32(0)
    for x_first, x_count, g_first, g_count, chunk in entries:
        here = q - chunk
        inside = here >= 0
        x_block = jnp.where(inside, x_first + lax.rem(jnp.maximum(here, 0), x_count), x_block)
        g_block = jnp.where(inside, g_first + jnp.maximum(here, 0) // x_count, g_block)
    return x_block, g_block


def seq_steps(bits):
    upper = list(range(1, bits))
    middle = (len(upper) + 1) // 2
    kinds = []
    for order in (upper, upper[middle:] + upper[:middle]):
        held = sorted(upper, reverse=True)
        steps = []
        for bit in order:
            place = held.index(bit)
            steps.append((bit, 2**place, 2 ** (len(held) - 1 - place)))
            held.remove(bit)
        kinds.append(steps)
    return kinds


def exchange_scratch(row_count, shards, block_rows, x_blocks, g_blocks, tokens):
    bits = shards.bit_length() - 1
    block = (block_rows, COLS)
    comm = []
    for steps in seq_steps(bits):
        for _, above, below in steps:
            comm.append(pltpu.VMEM((2, above, 2, below) + block, jnp.bfloat16))
            comm.append(pltpu.VMEM((SLOTS, above, below) + block, jnp.bfloat16))
    z_steps = row_count - 1
    own_slots = 3 if row_count <= 4 else ZSLOTS
    return [
        pltpu.VMEM((shards // 2, 2, x_blocks, block_rows, tokens), jnp.bfloat16),
        pltpu.VMEM((tokens, g_blocks * COLS), jnp.bfloat16),
        pltpu.VMEM((2, 2, shards // 2) + block, jnp.bfloat16),
        pltpu.VMEM((2, SLOTS, shards // 2) + block, jnp.bfloat16),
        *comm,
        *[
            pltpu.VMEM((2, count) + block, jnp.bfloat16)
            for count in (own_slots, ZSLOTS, own_slots, ZSLOTS, ZSLOTS)
        ],
        pltpu.SemaphoreType.DMA((2, bits, SLOTS)),
        pltpu.SemaphoreType.DMA((2, bits, SLOTS)),
        pltpu.SemaphoreType.DMA((2, z_steps, ZSLOTS)),
        pltpu.SemaphoreType.DMA((2, z_steps, ZSLOTS)),
        pltpu.SemaphoreType.DMA((2, ZSLOTS)),
    ]


class Exchange:
    def __init__(self, entries, row_count, shards, outs, scratch, locals_at=(), local=None):
        self.last_rows, self.fold = None, None
        self.entries, self.outs = entries, outs
        self.locals_at, self.local = locals_at, local
        self.bits = bits = shards.bit_length() - 1
        self.kinds = seq_steps(bits)
        (self.x_all, self.g_all, self.send_zero, self.recv_zero, *rest) = scratch
        self.held, self.received = [[], []], [[], []]
        for kind in range(2):
            for _ in self.kinds[kind]:
                self.held[kind].append(rest.pop(0))
                self.received[kind].append(rest.pop(0))
        self.z_own, self.z_in, self.z_part, self.z_cross, self.z_total = rest[:5]
        self.seq_send, self.seq_recv, self.z_send, self.z_recv, self.out_sem = rest[5:]
        self.row, self.seq = lax.axis_index("row"), lax.axis_index("seq")
        self.row_count, self.shards = row_count, shards
        self.value = [lax.rem(self.seq // (1 << bit), 2) for bit in range(bits)]
        self.partner = [self.seq + (1 << bit) * (1 - 2 * self.value[bit]) for bit in range(bits)]
        last = entries[-1]
        self.pairs = (last[4] + last[1] * last[3]) // 2 + len(locals_at)
        half = row_count // 2
        self.depth = half - 1
        lower = self.row < half
        self.level = jnp.where(lower, self.row, row_count - 1 - self.row)
        self.toward = jnp.where(lower, self.row + 1, self.row - 1)
        self.away = jnp.where(lower, self.row - 1, self.row + 1)

    def meet(self):
        barrier = pltpu.get_barrier_semaphore()
        others = [(self.row, partner) for partner in self.partner]
        for step in (1, self.row_count - 1):
            others.append((lax.rem(self.row + step, self.row_count), self.seq))
        for step in (1, self.shards - 1):
            others.append((self.row, lax.rem(self.seq + step, self.shards)))
        if self.fold is not None:
            others.append((self.fold.far, self.seq))
        for other in others:
            pl.semaphore_signal(barrier, inc=1, device_id=other, device_id_type=MESH)
        pl.semaphore_wait(barrier, len(others))

    def is_local(self, index):
        found = index < 0
        for at in self.locals_at:
            found = jnp.logical_or(found, index == at)
        return found

    def chunk(self, kind, index):
        before = sum([jnp.where(index > at, 1, 0) for at in self.locals_at], 0)
        return 2 * (index - before) + kind

    def product(self, kind, index, side):
        x_block, g_block = locate(self.entries, self.chunk(kind, index))
        left = self.x_all[:, side, x_block]
        columns = pl.ds(pl.multiple_of(g_block * COLS, COLS), COLS)
        return jnp.dot(
            left.reshape(left.shape[0] * left.shape[1], left.shape[2]),
            self.g_all[:, columns],
            preferred_element_type=jnp.float32,
        )

    def sized(self, kind, index, act):
        if self.last_rows is None or kind == 1:
            act(None)
        else:
            pl.when(index < self.pairs - 1)(lambda: act(None))
            pl.when(index == self.pairs - 1)(lambda: act(self.last_rows))

    def own_slot(self, slot):
        return lax.rem(slot, self.z_own.shape[1])

    def seq_start(self, kind, step, slot, index):
        self.sized(kind, index, lambda rows: self.seq_copy(kind, step, slot, rows).start())

    def seq_wait(self, kind, step, slot, index):
        self.sized(kind, index, lambda rows: self.seq_copy(kind, step, slot, rows).wait())

    def z_start(self, kind, step, slot, index):
        self.sized(kind, index, lambda rows: self.z_copy(kind, step, slot, rows).start())

    def z_wait(self, kind, step, slot, index):
        self.sized(kind, index, lambda rows: self.z_copy(kind, step, slot, rows).wait())

    def z_wait_recv(self, kind, step, slot, index):
        self.sized(kind, index, lambda rows: self.z_copy(kind, step, slot, rows).wait_recv())

    def z_wait_send(self, kind, step, slot, index):
        self.sized(kind, index, lambda rows: self.z_copy(kind, step, slot, rows).wait_send())

    def seq_copy(self, kind, step, slot, rows):
        some = pl.ds(0, self.z_own.shape[2] if rows is None else rows)
        if step == 0:
            bit = 0
            source = self.send_zero.at[kind, lax.rem(slot, 2), :, some]
            target = self.recv_zero.at[kind, slot, :, some]
        else:
            bit = self.kinds[kind][step - 1][0]
            away = 1 - self.value[bit]
            source = self.held[kind][step - 1].at[lax.rem(slot, 2), :, away, :, some]
            target = self.received[kind][step - 1].at[slot, :, :, some]
        return pltpu.make_async_remote_copy(
            src_ref=source,
            dst_ref=target,
            send_sem=self.seq_send.at[kind, step, slot],
            recv_sem=self.seq_recv.at[kind, step, slot],
            device_id=(self.row, self.partner[bit]),
            device_id_type=MESH,
        )

    def seq_sum(self, kind, step, slot):
        bit = self.kinds[kind][step - 2][0]
        mine = self.held[kind][step - 2][lax.rem(slot, 2), :, self.value[bit]].astype(jnp.float32)
        return mine + self.received[kind][step - 2][slot].astype(jnp.float32)

    def z_copy(self, kind, step, slot, rows):
        some = pl.ds(0, self.z_own.shape[2] if rows is None else rows)
        if step < self.depth:
            source = self.z_own if step == 0 else self.z_part
            target, where = self.z_in, self.toward
        elif step == self.depth:
            source = self.z_own if self.depth == 0 else self.z_part
            target, where = self.z_cross, self.toward
        else:
            source, target, where = self.z_total, self.z_total, self.away
        return pltpu.make_async_remote_copy(
            src_ref=source.at[kind, slot if source is self.z_total else self.own_slot(slot), some],
            dst_ref=target.at[kind, slot, some],
            send_sem=self.z_send.at[kind, step, slot],
            recv_sem=self.z_recv.at[kind, step, slot],
            device_id=(where, self.seq),
            device_id_type=MESH,
        )

    def start_out(self, kind, slot, index):
        q = self.chunk(kind, index)
        rows = self.z_total.shape[2]
        for out, (_, x_count, _, g_count, chunk) in zip(self.outs, self.entries):
            here = q - chunk

            @pl.when(jnp.logical_and(here >= 0, here < x_count * g_count))
            def _():
                row_at = pl.multiple_of(lax.rem(here, x_count) * rows, rows)
                column_at = pl.multiple_of(here // x_count * COLS, COLS)
                pltpu.make_async_copy(
                    self.z_total.at[kind, slot],
                    out.at[pl.ds(row_at, rows), pl.ds(column_at, COLS)],
                    self.out_sem.at[kind, slot],
                ).start()

    def first(self, kind, index):
        slot = lax.rem(index, SLOTS)
        target = self.send_zero

        def put():
            target[kind, lax.rem(slot, 2)] = (
                self.product(kind, index, 1 - self.value[0])
                .astype(jnp.bfloat16)
                .reshape(target.shape[2:])
            )

        if self.local is None:
            put()
        else:
            pl.when(jnp.logical_not(self.is_local(index)))(put)

            @pl.when(self.is_local(index))
            def _():
                target[kind, lax.rem(slot, 2)] = self.local.part(kind, index, 1 - self.value[0])

        self.seq_start(kind, 0, slot, index)

    def second(self, kind, index):
        slot = lax.rem(index, SLOTS)
        self.seq_wait(kind, 0, slot, index)
        target = self.held[kind][0]

        def put():
            mine = self.product(kind, index, self.value[0])
            total = mine + self.recv_zero[kind, slot].astype(jnp.float32).reshape(mine.shape)
            target[lax.rem(slot, 2)] = total.astype(jnp.bfloat16).reshape(target.shape[1:])

        if self.local is None:
            put()
        else:
            pl.when(jnp.logical_not(self.is_local(index)))(put)

            @pl.when(self.is_local(index))
            def _():
                mine = self.local.part(kind, index, self.value[0]).astype(jnp.float32)
                total = mine + self.recv_zero[kind, slot].astype(jnp.float32)
                target[lax.rem(slot, 2)] = total.astype(jnp.bfloat16).reshape(target.shape[1:])

        self.seq_start(kind, 1, slot, index)

    def middle(self, step):
        def run(kind, index):
            slot = lax.rem(index, SLOTS)
            self.seq_wait(kind, step - 1, slot, index)
            total = self.seq_sum(kind, step, slot)
            target = self.held[kind][step - 1]
            target[lax.rem(slot, 2)] = total.astype(jnp.bfloat16).reshape(target.shape[1:])
            self.seq_start(kind, step, slot, index)

        return run

    def last(self, kind, index):
        slot, z_slot = lax.rem(index, SLOTS), lax.rem(index, ZSLOTS)
        self.seq_wait(kind, self.bits - 1, slot, index)
        total = self.seq_sum(kind, self.bits, slot).reshape(self.z_own.shape[2:])

        def put():
            self.z_own[kind, self.own_slot(z_slot)] = total.astype(jnp.bfloat16)

            @pl.when(self.level == 0)
            def _():
                self.z_start(kind, 0, z_slot, index)

        if self.local is None:
            put()
        else:
            pl.when(jnp.logical_not(self.is_local(index)))(put)

            @pl.when(self.is_local(index))
            def _():
                self.local.take(kind, index, total)

    def z_stage(self, step):
        level, depth = self.level, self.depth

        def run(kind, index):
            slot = lax.rem(index, ZSLOTS)
            if step <= depth:

                @pl.when(level == step)
                def _():
                    self.z_wait_recv(kind, step - 1, slot, index)
                    self.z_part[kind, self.own_slot(slot)] = (
                        self.z_own[kind, self.own_slot(slot)].astype(jnp.float32)
                        + self.z_in[kind, slot].astype(jnp.float32)
                    ).astype(jnp.bfloat16)
                    self.z_start(kind, step, slot, index)

                @pl.when(level == step - 1)
                def _():
                    self.z_wait_send(kind, step - 1, slot, index)

            elif step == depth + 1:

                @pl.when(level == depth)
                def _():
                    self.z_wait(kind, depth, slot, index)
                    own = self.z_own if depth == 0 else self.z_part
                    self.z_total[kind, slot] = (
                        own[kind, self.own_slot(slot)].astype(jnp.float32)
                        + self.z_cross[kind, slot].astype(jnp.float32)
                    ).astype(jnp.bfloat16)
                    if depth > 0:
                        self.z_start(kind, step, slot, index)
                    self.start_out(kind, slot, index)

            else:
                receiver = 2 * depth + 1 - step

                @pl.when(level == receiver)
                def _():
                    self.z_wait_recv(kind, step - 1, slot, index)
                    if receiver > 0:
                        self.z_start(kind, step, slot, index)
                    self.start_out(kind, slot, index)

                @pl.when(level == receiver + 1)
                def _():
                    self.z_wait_send(kind, step - 1, slot, index)

        return run

    def finish(self, kind, index):
        slot = lax.rem(index, ZSLOTS)
        rows = self.z_total.shape[2]
        pltpu.make_async_copy(
            self.z_total.at[kind, slot],
            self.outs[0].at[pl.ds(0, rows), pl.ds(0, COLS)],
            self.out_sem.at[kind, slot],
        ).wait()

    def run(self, task):
        stages = [(self.first, False), (self.second, False)]
        stages += [(self.middle(step), False) for step in range(2, self.bits)]
        stages += [(self.last, False)]
        stages += [(self.z_stage(step), True) for step in range(1, 2 * self.depth + 2)]
        stages += [(self.finish, True)]

        def iteration(i, carried):
            for at, (stage, summed_only) in enumerate(stages):
                index = i - at
                here = jnp.logical_and(index >= 0, index < self.pairs)
                if summed_only and self.locals_at:
                    here = jnp.logical_and(here, jnp.logical_not(self.is_local(index)))

                @pl.when(here)
                def _():
                    stage(0, index)
                    if self.last_rows is None:
                        stage(1, index)

                if self.last_rows is not None:

                    @pl.when(jnp.logical_and(here, index < self.pairs - 1))
                    def _():
                        stage(1, index)

            if self.fold is not None:
                self.fold.advance(i)
            if task is not None:
                task(i)
            return carried

        total = self.pairs + len(stages) - 1
        if self.fold is not None:
            total = max(total, self.fold.end)
        lax.fori_loop(0, total, iteration, 0)


FOLD_START, FOLD_PERIOD = 8, 3


def fold_scratch(shards, block_rows):
    half = (block_rows // 2, COLS)
    low = jnp.bfloat16
    orders = []
    for steps in seq_steps(shards.bit_length() - 1):
        for _, above, below in steps:
            orders.append(pltpu.VMEM((above, 2, below) + half, low))
            orders.append(pltpu.VMEM((2, above, below) + half, low))
    return [
        pltpu.VMEM((shards // 2, block_rows, COLS), low),
        pltpu.VMEM((2, shards // 2, block_rows, COLS), low),
        pltpu.VMEM((shards // 2, 2) + half, low),
        pltpu.VMEM((2, shards // 2) + half, low),
        *orders,
        pltpu.VMEM(half, low),
        pltpu.VMEM((3,) + half, low),
        pltpu.VMEM((3, 2) + half, low),
        pltpu.SemaphoreType.DMA((6, 3)),
        pltpu.SemaphoreType.DMA((6, 3)),
        pltpu.SemaphoreType.DMA((2, 3)),
    ]


class Fold:
    def __init__(self, exchange, entry, out, scratch):
        self.exchange, self.entry, self.out = exchange, entry, out
        (self.send, self.received, self.halves, self.half_in, *rest) = scratch
        self.held, self.held_in = [[], []], [[], []]
        for order in range(2):
            for _ in exchange.kinds[order]:
                self.held[order].append(rest.pop(0))
                self.held_in[order].append(rest.pop(0))
        self.own, self.cross, self.total, self.send_sem, self.recv_sem, self.out_sem = rest
        row = exchange.row
        self.bit = lax.rem(row, 2)
        self.near, self.far = row + 1 - 2 * self.bit, lax.rem(row + 2, 4)
        self.count = entry[1] * entry[3]
        self.stages = [
            (0, self.first),
            (1, self.second),
            (3, self.third),
            (4, self.fourth),
            (5, self.fifth),
            (7, self.sixth),
            (9, self.seventh),
            (10, self.finish),
        ]
        self.end = FOLD_START + FOLD_PERIOD * (self.count - 1) + 11

    def advance(self, i):
        for offset, run in self.stages:
            since = i - (FOLD_START + offset)
            number = jnp.maximum(since, 0) // FOLD_PERIOD
            here = jnp.logical_and(since >= 0, lax.rem(jnp.maximum(since, 0), FOLD_PERIOD) == 0)
            here = jnp.logical_and(here, number < self.count)

            @pl.when(here)
            def _():
                run(number)

    def copy(self, step, number, order=0):
        exchange = self.exchange
        row, seq, two, three = exchange.row, exchange.seq, lax.rem(number, 2), lax.rem(number, 3)
        if step == 0:
            source, target = self.send, self.received.at[two]
            device = (row, exchange.partner[0])
        elif step == 1:
            source, target = self.halves.at[:, 1 - self.bit], self.half_in.at[two]
            device = (self.near, seq)
        elif step < 4:
            bit = exchange.kinds[order][step - 2][0]
            source = self.held[order][step - 2].at[:, 1 - exchange.value[bit]]
            target = self.held_in[order][step - 2].at[lax.rem(number // 2, 2)]
            device = (row, exchange.partner[bit])
        elif step == 4:
            source, target = self.own, self.cross.at[three]
            device = (self.far, seq)
        else:
            source = target = self.total.at[three, self.bit]
            device = (self.near, seq)
        return pltpu.make_async_remote_copy(
            src_ref=source,
            dst_ref=target,
            send_sem=self.send_sem.at[step, three],
            recv_sem=self.recv_sem.at[step, three],
            device_id=device,
            device_id_type=MESH,
        )

    def product(self, number, side):
        x_first, x_count, g_first = self.entry[:3]
        left = self.exchange.x_all[:, side, x_first + lax.rem(number, x_count)]
        columns = pl.ds(pl.multiple_of((g_first + number // x_count) * COLS, COLS), COLS)
        return jnp.dot(
            left.reshape(left.shape[0] * left.shape[1], left.shape[2]),
            self.exchange.g_all[:, columns],
            preferred_element_type=jnp.float32,
        )

    def first(self, number):
        value = self.product(number, 1 - self.exchange.value[0]).astype(jnp.bfloat16)
        self.send[...] = value.reshape(self.send.shape)
        self.copy(0, number).start()

    def second(self, number):
        self.copy(0, number).wait()
        mine = self.product(number, self.exchange.value[0])
        other = self.received[lax.rem(number, 2)].astype(jnp.float32)
        total = mine + other.reshape(mine.shape)
        self.halves[...] = total.astype(jnp.bfloat16).reshape(self.halves.shape)
        self.copy(1, number).start()

    def by_order(self, number, run):
        for order in range(2):
            pl.when(lax.rem(number, 2) == order)(functools.partial(run, order))

    def third(self, number):
        self.copy(1, number).wait()
        total = self.halves[:, self.bit].astype(jnp.float32)
        total = total + self.half_in[lax.rem(number, 2)].astype(jnp.float32)
        total = total.astype(jnp.bfloat16)

        def go(order):
            target = self.held[order][0]
            target[...] = total.reshape(target.shape)
            self.copy(2, number, order).start()

        self.by_order(number, go)

    def summed(self, number, order, step):
        bit = self.exchange.kinds[order][step][0]
        mine = self.held[order][step][:, self.exchange.value[bit]].astype(jnp.float32)
        other = self.held_in[order][step][lax.rem(number // 2, 2)].astype(jnp.float32)
        return (mine + other).astype(jnp.bfloat16)

    def fourth(self, number):
        def go(order):
            self.copy(2, number, order).wait()
            target = self.held[order][1]
            target[...] = self.summed(number, order, 0).reshape(target.shape)
            self.copy(3, number, order).start()

        self.by_order(number, go)

    def fifth(self, number):
        def go(order):
            self.copy(3, number, order).wait()
            self.own[...] = self.summed(number, order, 1).reshape(self.own.shape)

        self.by_order(number, go)
        self.copy(4, number).start()

    def sixth(self, number):
        self.copy(4, number).wait()
        three = lax.rem(number, 3)
        total = self.own[...].astype(jnp.float32) + self.cross[three].astype(jnp.float32)
        self.total[three, self.bit] = total.astype(jnp.bfloat16)
        self.copy(5, number).start()

    def out_copies(self, number):
        x_count, rows = self.entry[1], self.own.shape[0]
        three = lax.rem(number, 3)
        columns = pl.ds(pl.multiple_of(number // x_count * COLS, COLS), COLS)
        copies = []
        for half in range(2):
            at = pl.multiple_of((2 * lax.rem(number, x_count) + half) * rows, rows)
            copies.append(
                pltpu.make_async_copy(
                    self.total.at[three, half],
                    self.out.at[pl.ds(at, rows), columns],
                    self.out_sem.at[half, three],
                )
            )
        return copies

    def seventh(self, number):
        self.copy(5, number).wait()
        for copy in self.out_copies(number):
            copy.start()

    def finish(self, number):
        for copy in self.out_copies(number):
            copy.wait()


def reduce_kernel(entries, row_count, shards, *refs):
    count = len(entries)
    xs, gs, outs = refs[:count], refs[count : 2 * count], refs[2 * count : 3 * count]
    load_x, load_g, *scratch = refs[3 * count :]
    exchange = Exchange(entries, row_count, shards, outs, scratch)
    copies = []
    for at, (x_first, x_count, g_first, g_count, _) in enumerate(entries):
        x_part = exchange.x_all.at[:, :, pl.ds(x_first, x_count)]
        g_part = exchange.g_all.at[:, pl.ds(g_first * COLS, g_count * COLS)]
        copies.append(pltpu.make_async_copy(xs[at], x_part, load_x.at[at]))
        copies.append(pltpu.make_async_copy(gs[at], g_part, load_g.at[at]))
    for copy in copies:
        copy.start()
    exchange.meet()
    for copy in copies:
        copy.wait()
    exchange.run(None)


def reduce_gradients(pairs, row_count, shards, collective_id):
    block_rows, tokens = pairs[0][0].shape[3:]
    entries, x_blocks, g_blocks, chunks = reduce_entries(
        [(x.shape[2], g.shape[1] // COLS) for x, g in pairs]
    )
    return pl.pallas_call(
        functools.partial(reduce_kernel, entries, row_count, shards),
        out_shape=[
            jax.ShapeDtypeStruct((x_count * block_rows, g_count * COLS), jnp.bfloat16)
            for _, x_count, _, g_count, _ in entries
        ],
        in_specs=[pl.BlockSpec(memory_space=pl.ANY)] * (2 * len(pairs)),
        out_specs=[pl.BlockSpec(memory_space=pl.ANY)] * len(pairs),
        scratch_shapes=[
            pltpu.SemaphoreType.DMA((len(pairs),)),
            pltpu.SemaphoreType.DMA((len(pairs),)),
            *exchange_scratch(row_count, shards, block_rows, x_blocks, g_blocks, tokens),
        ],
        compiler_params=pltpu.CompilerParams(
            collective_id=collective_id, has_side_effects=True, vmem_limit_bytes=52 * 2**20
        ),
        cost_estimate=pl.CostEstimate(
            flops=2 * chunks * shards * block_rows * COLS * tokens,
            bytes_accessed=2 * chunks * block_rows * COLS,
            transcendentals=0,
        ),
    )(*[x for x, _ in pairs], *[g for _, g in pairs])


def body(
    tokens,
    lengths,
    mixer_gain,
    mixer_input,
    mixer_kernel,
    mixer_output,
    first_gain,
    first_gate,
    first_up,
    first_down,
    attend_gain,
    query_weight,
    key_weight,
    value_weight,
    query_gain,
    key_gain,
    attend_output,
    second_gain,
    second_gate,
    second_up,
    second_down,
    cotangent,
):
    length = tokens.shape[1]
    positions = lax.axis_index("seq") * length + jnp.arange(length, dtype=jnp.int32)
    segment, seg_start = segment_info(lengths, positions)
    offsets = positions[None, :] - seg_start
    hidden = tokens.astype(jnp.float32)
    hidden, mixer_back = mixer_block(
        hidden, mixer_gain, mixer_input, mixer_kernel, mixer_output, seg_start, positions
    )
    hidden, first_back = feed_block(hidden, first_gain, first_gate, first_up, first_down)
    hidden, attend_back = attend_block(
        hidden,
        lengths,
        attend_gain,
        query_weight,
        key_weight,
        value_weight,
        query_gain,
        key_gain,
        attend_output,
        segment,
        positions,
        offsets,
    )
    hidden, second_back = feed_block(hidden, second_gain, second_gate, second_up, second_down)
    gradient = cotangent.astype(jnp.float32)
    gradient, second_grads = second_back(gradient)
    gradient, attend_grads = attend_back(gradient)
    gradient, first_grads = first_back(gradient)
    gradient, mixer_grads = mixer_back(gradient)
    second_gain_sum, second_wide, second_down_pair = second_grads
    attend_gain_sum, attend_wide, query_gain_sum, key_gain_sum, attend_output_pair = attend_grads
    first_gain_sum, first_wide, first_down_pair = first_grads
    mixer_gain_sum, mixer_input_pair, mixer_kernel_sum, mixer_output_pair = mixer_grads
    row_count, shards = lax.axis_size("row"), lax.axis_size("seq")
    block_rows = math.gcd(tokens.shape[2] // shards, first_down.shape[0] // shards)

    def operands(pair):
        inputs, gradient_low = pair
        token_count = inputs.shape[0] * inputs.shape[1]
        inputs = inputs.reshape(token_count, -1).T
        blocks = inputs.shape[0] // shards // block_rows
        return (
            inputs.reshape(shards // 2, 2, blocks, block_rows, token_count),
            gradient_low.reshape(token_count, -1),
        )

    wide_vectors = jnp.concatenate(
        [
            mixer_kernel_sum,
            jnp.stack([mixer_gain_sum, first_gain_sum, attend_gain_sum, second_gain_sum]),
        ]
    )
    vector_count = wide_vectors.shape[0]
    vectors = jnp.concatenate(
        [
            part.reshape(-1, shards, part.shape[-1] // shards)
            .transpose(1, 0, 2)
            .reshape(shards, -1)
            for part in (wide_vectors, jnp.stack([query_gain_sum, key_gain_sum]))
        ],
        axis=1,
    )
    vector_rows = -(-vectors.shape[1] // COLS)
    token_count = tokens.shape[0] * tokens.shape[1]
    vectors = jnp.pad(vectors, ((0, 0), (0, vector_rows * COLS - vectors.shape[1])))
    vectors = vectors.reshape(shards * vector_rows, COLS).astype(jnp.bfloat16)
    vectors = jnp.pad(vectors, ((0, token_count - shards * vector_rows), (0, 0)))
    shard_at = lax.broadcasted_iota(jnp.int32, (shards, 2 * block_rows, token_count), 0)
    row_at = lax.broadcasted_iota(jnp.int32, (shards, 2 * block_rows, token_count), 1)
    token_at = lax.broadcasted_iota(jnp.int32, (shards, 2 * block_rows, token_count), 2)
    picks = (row_at < vector_rows) & (token_at == shard_at * vector_rows + row_at)
    picks = picks.astype(jnp.bfloat16).reshape(shards // 2, 2, 2, block_rows, token_count)
    (
        grad_second_down,
        second_both,
        grad_attend_output,
        attend_three,
        grad_first_down,
        first_both,
        grad_mixer_output,
        grad_mixer_input,
        vector_sums,
    ) = reduce_gradients(
        [
            operands(second_down_pair),
            operands(second_wide),
            operands(attend_output_pair),
            operands(attend_wide),
            operands(first_down_pair),
            operands(first_wide),
            operands(mixer_output_pair),
            operands(mixer_input_pair),
            (picks, vectors),
        ],
        row_count,
        shards,
        0,
    )

    def single(value):
        return value.astype(jnp.float32)

    hidden_columns = first_gate.shape[1]
    query_columns, key_columns = query_weight.shape[1], key_weight.shape[1]
    vector_sums = single(vector_sums[:vector_rows]).reshape(-1)
    width = tokens.shape[2] // shards
    wide_sums = vector_sums[: vector_count * width].reshape(vector_count, width)
    head_width = HEAD_DIM // shards
    head_sums = vector_sums[vector_count * width :][: 2 * head_width].reshape(2, head_width)
    return (
        hidden.astype(jnp.bfloat16),
        gradient.astype(jnp.bfloat16),
        wide_sums[3],
        single(grad_mixer_input),
        wide_sums[:3],
        single(grad_mixer_output),
        wide_sums[4],
        single(first_both[:, :hidden_columns]),
        single(first_both[:, hidden_columns:]),
        single(grad_first_down),
        wide_sums[5],
        single(attend_three[:, :query_columns]),
        single(attend_three[:, query_columns : query_columns + key_columns]),
        single(attend_three[:, query_columns + key_columns :]),
        head_sums[0],
        head_sums[1],
        single(grad_attend_output),
        wide_sums[6],
        single(second_both[:, :hidden_columns]),
        single(second_both[:, hidden_columns:]),
        single(grad_second_down),
    )


def finish_kernel(cuts, count, shards, *refs):
    passed, sums_in, refs = refs[:2], refs[2], refs[3:]
    ins, outs = refs[:count], refs[count : count + len(cuts)]
    refs = refs[count + len(cuts) :]
    passed_out, vectors, taps_out, heads, refs = refs[:2], refs[2:6], refs[6], refs[7:9], refs[9:]
    lows, fulls = refs[:count], refs[count : count + len(cuts)]
    held, sums, load_sem, save_sem, pass_sem = refs[count + len(cuts) :]
    moves = [
        pltpu.make_async_copy(source, held.at[number], pass_sem.at[number])
        for number, source in enumerate(passed)
    ]
    moves.append(pltpu.make_async_copy(sums_in, sums, pass_sem.at[2]))
    loads = [
        pltpu.make_async_copy(ins[number], lows[number], load_sem.at[number])
        for number in range(count)
    ]
    for load in loads + moves:
        load.start()
    saves, waited = [], set()
    for number, (source, first, columns) in enumerate(cuts):
        if source not in waited:
            loads[source].wait()
            waited.add(source)
        low, full = lows[source], fulls[number]
        rows = low.shape[0]
        piece = 64 if rows % 64 == 0 else rows

        def convert(at, carried):
            span = pl.ds(pl.multiple_of(at * 16, 16), 16)
            full[span] = low[span, pl.ds(first, columns)].astype(jnp.float32)
            return carried

        for start in range(0, rows, piece):
            lax.fori_loop(start // 16, (start + piece) // 16, convert, 0)
            span = pl.ds(start, piece)
            save = pltpu.make_async_copy(
                full.at[span], outs[number].at[span], save_sem.at[len(saves)]
            )
            save.start()
            saves.append(save)
    for move in moves:
        move.wait()
    for number, target in enumerate(passed_out):
        save = pltpu.make_async_copy(held.at[number], target, pass_sem.at[number])
        save.start()
        saves.append(save)
    seq = lax.axis_index("seq")
    share = vectors[0].shape[0]
    value = sums[pl.ds(0, 16)].astype(jnp.float32)
    chosen = jnp.zeros((16, share), jnp.float32)
    for place in range(COLS // share):
        here = lax.rem(seq, COLS // share) == place
        chosen = jnp.where(here, value[:, place * share : (place + 1) * share], chosen)
    for number, vector in enumerate(vectors):
        vector[...] = chosen[number : number + 1].reshape(share)
    taps_out[...] = chosen[4:7]
    lane = 2 * HEAD_DIM
    for number, head in enumerate(heads):
        line = value[0:8, number * lane : (number + 1) * lane]
        part = head.shape[0]
        chosen = jnp.zeros((1, part), jnp.float32)
        for place in range(shards):
            chosen = jnp.where(seq == place, line[7:8, place * part : (place + 1) * part], chosen)
        head[...] = chosen.reshape(part)
    for save in saves:
        save.wait()


def to_full(passed, sums, lows, cuts, shards):
    any_space = pl.BlockSpec(memory_space=pl.ANY)
    shapes = [(lows[source].shape[0], columns) for source, _, columns in cuts]
    pieces = sum(rows // 64 if rows % 64 == 0 else 1 for rows, _ in shapes)
    size = sum(low.size for low in lows)
    width = passed[0].shape[1]
    small = [(width // shards,)] * 4 + [(3, width // shards)] + [(HEAD_DIM // shards,)] * 2
    results = pl.pallas_call(
        functools.partial(finish_kernel, cuts, len(lows), shards),
        out_shape=[jax.ShapeDtypeStruct(shape, jnp.float32) for shape in shapes]
        + [jax.ShapeDtypeStruct(value.shape, value.dtype) for value in passed]
        + [jax.ShapeDtypeStruct(shape, jnp.float32) for shape in small],
        in_specs=[any_space] * (3 + len(lows)),
        out_specs=[any_space] * (len(cuts) + 2)
        + [pl.BlockSpec(memory_space=pltpu.VMEM)] * len(small),
        scratch_shapes=[
            *[pltpu.VMEM(low.shape, low.dtype) for low in lows],
            *[pltpu.VMEM(shape, jnp.float32) for shape in shapes],
            pltpu.VMEM((2,) + passed[0].shape, passed[0].dtype),
            pltpu.VMEM(sums.shape, sums.dtype),
            pltpu.SemaphoreType.DMA((len(lows),)),
            pltpu.SemaphoreType.DMA((pieces,)),
            pltpu.SemaphoreType.DMA((3,)),
        ],
        compiler_params=pltpu.CompilerParams(vmem_limit_bytes=62 * 2**20),
        cost_estimate=pl.CostEstimate(flops=size, bytes_accessed=6 * size, transcendentals=0),
    )(*passed, sums, *lows)
    cut_count = len(cuts)
    return results[:cut_count], results[cut_count : cut_count + 2], results[cut_count + 2 :]


def dot_nt(left, right):
    return lax.dot_general(
        left, right, (((1,), (1,)), ((), ())), preferred_element_type=jnp.float32
    )


def dot_tn(left, right):
    return lax.dot_general(
        left, right, (((0,), (0,)), ((), ())), preferred_element_type=jnp.float32
    )


def lanes_below(shape, bound, period):
    return lax.rem(lax.broadcasted_iota(jnp.int32, shape, len(shape) - 1), period) < bound


def two_heads(pair, low):
    pair = pair.astype(jnp.float32)
    turned = pltpu.roll(pair, HEAD_DIM, 1)
    first = lanes_below(pair.shape, HEAD_DIM, 2 * HEAD_DIM)
    if low:
        parts = [jnp.where(first, pair, 0.0), jnp.where(first, turned, 0.0)]
    else:
        parts = [jnp.where(first, 0.0, turned), jnp.where(first, 0.0, pair)]
    return jnp.concatenate(parts, axis=0).astype(jnp.bfloat16)


def segment_start(lengths, which, place):
    end, start = jnp.int32(0), jnp.zeros(place.shape, jnp.int32)
    for number in range(lengths.shape[1]):
        end = end + lengths[which, number]
        start = jnp.where(place >= end, end, start)
    return start


def both_halves(value):
    value = jnp.broadcast_to(value, (8,) + value.shape[1:])
    return (value + pltpu.roll(value, HEAD_DIM, 1))[0:1]


def head_tools(lane):
    head_of = lax.broadcasted_iota(jnp.int32, (lane, lane), 0) // HEAD_DIM
    ones = head_of == lax.broadcasted_iota(jnp.int32, (lane, lane), 1) // HEAD_DIM
    ones = ones.astype(jnp.float32).astype(jnp.bfloat16)

    def head_mean(value):
        total = jnp.dot(value.astype(jnp.bfloat16), ones, preferred_element_type=jnp.float32)
        return total * (1.0 / HEAD_DIM)

    def turn(value):
        half = HEAD_DIM // 2
        first = lanes_below(value.shape, half, HEAD_DIM)
        return jnp.where(first, pltpu.roll(value, lane - half, 1), pltpu.roll(value, half, 1))

    return head_mean, turn


def forward_kernel(names, out_names, scratch_names, shards, *refs):
    at = types.SimpleNamespace(**dict(zip(names + out_names + scratch_names, refs)))
    row, seq = lax.axis_index("row"), lax.axis_index("seq")
    tokens, width = at.low_one.shape
    rows, total_length = at.both.shape[:2]
    length = tokens // rows
    lane = 2 * HEAD_DIM
    blocks = width // COLS
    hidden_blocks = at.first_gate.shape[1] // COLS
    bits = [lax.rem(seq // (1 << bit), 2) for bit in range(3)]
    partner = [seq + (1 << bit) * (1 - 2 * bits[bit]) for bit in range(3)]
    head_mean, turn = head_tools(lane)

    ahead = at.tiles_a.shape[0]

    def tile_copies(step, slot):
        name, j = step
        b, c = at.tiles_b.at[slot], at.tiles_c.at[slot]

        def columns(block):
            return pl.ds(block * COLS if isinstance(block, int) else pl.multiple_of(block * COLS, COLS), COLS)

        if name == MIXER_INPUT:
            first, second = ((0, 4), (1, 5), (2, 3))[j]
            moves = [
                (at.mixer_input.at[:, columns(first)], b),
                (at.mixer_input.at[:, columns(second)], c),
            ]
        elif name == KEYS:
            moves = [(at.key_weight, b), (at.value_weight, c)]
        elif name == FIRST:
            moves = [
                (at.first_gate.at[:, columns(j)], b),
                (at.first_up.at[:, columns(j)], c),
                (at.first_down.at[columns(j)], at.tiles_a.at[slot]),
            ]
        else:
            matrix = {
                MIXER_OUTPUT: at.mixer_output,
                QUERIES: at.query_weight,
                ATTEND_OUTPUT: at.attend_output,
            }[name]
            moves = [(matrix.at[:, columns(0)], b), (matrix.at[:, columns(1)], c)]
        return [
            pltpu.make_async_copy(source, target, at.tile_sem.at[slot, place])
            for place, (source, target) in enumerate(moves)
        ]

    steps = [(MIXER_INPUT, 0), (MIXER_INPUT, 1), (MIXER_INPUT, 2), (MIXER_OUTPUT, 0)]
    first_at = len(steps)
    steps += [(FIRST, j) for j in range(hidden_blocks)]
    steps += [(KEYS, 0), (QUERIES, 0), (ATTEND_OUTPUT, 0)]

    def begin(number):
        for copy in tile_copies(steps[number], number % ahead):
            copy.wait()
        later = number + ahead - 1
        if later < len(steps):
            for copy in tile_copies(steps[later], later % ahead):
                copy.start()
        return number % ahead

    saves = []

    streaming = [True]

    def save(source, target):
        copy = pltpu.make_async_copy(source, target, at.save_sem.at[len(saves)])
        if not streaming[0]:
            copy.start()
        saves.append(copy)

    def normed(hidden, number, target):
        for first in range(0, tokens, 64):
            span = pl.ds(first, 64)
            value = hidden[span]
            inverse = lax.rsqrt(jnp.mean(value * value, axis=-1, keepdims=True) + EPS)
            value = value * inverse * at.vectors[number : number + 1, :]
            target[span] = value.astype(jnp.bfloat16)

    def times(left, tile):
        return jnp.dot(left[...], tile, preferred_element_type=jnp.float32)

    token_load = pltpu.make_async_copy(at.tokens, at.attended, at.load_sem.at[0])
    token_load.start()
    for number in range(ahead - 1):
        for copy in tile_copies(steps[number], number):
            copy.start()
    at.halo_in[...] = jnp.zeros_like(at.halo_in)
    barrier = pltpu.get_barrier_semaphore()
    others = partner + [lax.rem(seq + step, shards) for step in (1, shards - 1)]
    for other in others:
        pl.semaphore_signal(barrier, inc=1, device_id=(row, other), device_id_type=MESH)
    at.vectors[...] = jnp.zeros_like(at.vectors)
    gains = [at.second_gain, at.attend_gain, at.first_gain, at.mixer_gain]
    for number, gain in enumerate(gains):
        at.vectors[number : number + 1, :] = gain[...].astype(jnp.float32).reshape(1, width)
    at.vectors[4:7, :] = at.mixer_kernel[...].astype(jnp.float32)
    for number, gain in enumerate((at.query_gain, at.key_gain)):
        at.vectors[7 + number : 8 + number, 0:HEAD_DIM] = (
            gain[...].astype(jnp.float32).reshape(1, HEAD_DIM)
        )
    half = HEAD_DIM // 2
    lane_at = lax.broadcasted_iota(jnp.int32, (length, lane), 1)
    power = lax.rem(lane_at, half).astype(jnp.float32) * (-2.0 * math.log(THETA) / HEAD_DIM)
    inverse = jnp.exp(power)
    side = jnp.where(lanes_below((length, lane), half, HEAD_DIM), -1.0, 1.0)
    place = lax.broadcasted_iota(jnp.int32, (length, lane), 0) + seq * length
    for which in range(rows):
        start = segment_start(at.lengths, which, place)
        angle = (place - start).astype(jnp.float32) * inverse
        span = pl.ds(which * length, length)
        at.seg_start[span] = start
        at.cosine[span] = jnp.cos(angle)
        at.sine[span] = jnp.sin(angle) * side
    save(at.vectors, at.vectors_out)
    save(at.cosine, at.cosine_out)
    save(at.sine, at.sine_out)
    token_load.wait()
    at.hidden_a[...] = at.attended[...].astype(jnp.float32)
    save(at.hidden_a, at.hidden_zero)
    normed(at.hidden_a, 3, at.low_one)
    pl.semaphore_wait(barrier, len(others))

    for number, (first, second) in enumerate(((0, 4), (1, 5))):
        slot = begin(number)
        entry = times(at.low_one, at.tiles_b[slot])
        carrier = times(at.low_one, at.tiles_c[slot])
        columns = pl.ds(number * COLS, COLS)
        product = (entry * carrier).astype(jnp.bfloat16)
        at.mixed_low[pl.ds(3 * tokens, tokens), columns] = product
        product = product.astype(jnp.float32)
        at.gates_low[pl.ds(0, tokens), columns] = entry.astype(jnp.bfloat16)
        at.gates_low[pl.ds(2 * tokens, tokens), columns] = carrier.astype(jnp.bfloat16)
        for which in range(rows):
            last = product[(which + 1) * length - 8 : (which + 1) * length]
            at.halo_out[which, :, columns] = last
    halo = pltpu.make_async_remote_copy(
        src_ref=at.halo_out,
        dst_ref=at.halo_in,
        send_sem=at.halo_sem.at[0],
        recv_sem=at.halo_sem.at[1],
        device_id=(row, jnp.minimum(seq + 1, shards - 1)),
        device_id_type=MESH,
    )

    @pl.when(seq < shards - 1)
    def _():
        halo.start()

    slot = begin(2)
    for block, tile in enumerate((at.tiles_b, at.tiles_c)):
        at.work[:, pl.ds(block * COLS, COLS)] = times(at.low_one, tile[slot])

    @pl.when(seq > 0)
    def _():
        halo.wait_recv()

    @pl.when(seq < shards - 1)
    def _():
        halo.wait_send()

    position = lax.rem(lax.broadcasted_iota(jnp.int32, (tokens, lane), 0), length) + seq * length
    keep_one = position - 1 >= at.seg_start[...]
    keep_two = position - 2 >= at.seg_start[...]
    edge = lax.broadcasted_iota(jnp.int32, (8, lane), 0)
    for part_at in range(0, width, lane):
        columns = pl.ds(part_at, lane)
        current = at.mixed_low[pl.ds(3 * tokens, tokens), columns].astype(jnp.float32)
        shifted = []
        for steps_back, keep in ((1, keep_one), (2, keep_two)):
            back = pltpu.roll(current, steps_back, 0)
            pieces = []
            for which in range(rows):
                before = pltpu.roll(at.halo_in[which, :, columns], steps_back, 0)
                start = which * length
                pieces.append(jnp.where(edge < steps_back, before, back[start : start + 8]))
                pieces.append(back[start + 8 : start + length])
            back = jnp.concatenate(pieces, axis=0)
            shifted.append(jnp.where(keep, back, 0.0))
        one, two = shifted
        convolved = at.vectors[6:7, columns] * current + at.vectors[5:6, columns] * one
        convolved += at.vectors[4:5, columns] * two
        exit_gate = at.work[:, columns]
        at.mixed_low[pl.ds(0, tokens), columns] = convolved.astype(jnp.bfloat16)
        at.mixed_low[pl.ds(tokens, tokens), columns] = two.astype(jnp.bfloat16)
        at.mixed_low[pl.ds(2 * tokens, tokens), columns] = one.astype(jnp.bfloat16)
        at.gates_low[pl.ds(tokens, tokens), columns] = exit_gate.astype(jnp.bfloat16)
        at.low_two[:, columns] = (exit_gate * convolved).astype(jnp.bfloat16)
    save(at.mixed_low, at.mixer_saved)
    save(at.gates_low, at.projected)

    def add_output(number, left, before, after):
        slot = begin(number)
        for block, tile in enumerate((at.tiles_b, at.tiles_c)):
            columns = pl.ds(block * COLS, COLS)
            after[:, columns] = before[:, columns] + times(left, tile[slot])

    add_output(3, at.low_two, at.hidden_a, at.hidden_b)
    save(at.hidden_b, at.hidden_one)
    normed(at.hidden_b, 2, at.low_three)
    at.hidden_c[...] = at.hidden_b[...]

    def feed_tile(j, carried):
        slot = lax.rem(first_at + j, ahead)
        for copy in tile_copies((FIRST, j), slot):
            copy.wait()
        later = j + ahead - 1
        later_slot = lax.rem(first_at + later, ahead)

        @pl.when(later < hidden_blocks)
        def _():
            for copy in tile_copies((FIRST, later), later_slot):
                copy.start()

        for past, step in enumerate(steps[first_at + hidden_blocks :][: ahead - 1]):

            @pl.when(later == hidden_blocks + past)
            def _():
                for copy in tile_copies(step, later_slot):
                    copy.start()

        gate_value = times(at.low_three, at.tiles_b[slot])
        up_value = times(at.low_three, at.tiles_c[slot])
        columns = pl.ds(pl.multiple_of(j * COLS, COLS), COLS)
        at.gate_low[:, columns] = gate_value.astype(jnp.bfloat16)
        at.up_low[:, columns] = up_value.astype(jnp.bfloat16)
        active = gate_value / (1.0 + jnp.exp(-gate_value)) * up_value
        active = active.astype(jnp.bfloat16)
        at.active_low[:, columns] = active
        at.hidden_c[...] += jnp.dot(
            active, at.tiles_a[slot], preferred_element_type=jnp.float32
        )
        return carried

    lax.fori_loop(0, hidden_blocks, feed_tile, 0)
    save(at.hidden_c, at.hidden_two)
    save(at.gate_low, at.gate_one)
    save(at.up_low, at.up_one)
    normed(at.hidden_c, 1, at.low_four)

    def head_path(raw, gain):
        value = raw * lax.rsqrt(head_mean(raw * raw) + EPS) * gain
        return value * at.cosine[...] + turn(value) * at.sine[...]

    keys_at = first_at + hidden_blocks
    slot = begin(keys_at)
    at.work[:, pl.ds(0, width // 2)] = times(at.low_four, at.tiles_b[slot])
    at.work[:, pl.ds(width // 2, width // 2)] = times(at.low_four, at.tiles_c[slot])
    at.keys_low[...] = at.work[:, pl.ds(0, width // 2)].astype(jnp.bfloat16)
    save(at.keys_low, at.keys_raw)
    first = lanes_below((tokens, lane), HEAD_DIM, lane)
    own = pl.ds(pl.multiple_of(seq * length, length), length)
    for pair in range(width // lane // 2):
        keys = head_path(at.work[:, pl.ds(pair * lane, lane)], both_halves(at.vectors[8:9, pl.ds(0, lane)]))
        values = at.work[:, pl.ds(width // 2 + pair * lane, lane)]
        even = jnp.where(first, keys, pltpu.roll(values, HEAD_DIM, 1)).astype(jnp.bfloat16)
        odd = jnp.where(first, pltpu.roll(keys, HEAD_DIM, 1), values).astype(jnp.bfloat16)
        for which, value in enumerate((even, odd)):
            columns = pl.ds((2 * pair + which) * lane, lane)
            at.both[:, own, columns] = value.reshape(rows, length, lane)

    def piece(owner, which=None):
        span = pl.ds(pl.multiple_of(owner * length, length), length)
        return at.both.at[:, span] if which is None else at.both.at[which, span]

    def send(number, part, bit):
        return pltpu.make_async_remote_copy(
            src_ref=part,
            dst_ref=part,
            send_sem=at.gather_send.at[number],
            recv_sem=at.gather_recv.at[number],
            device_id=(row, partner[bit]),
            device_id_type=MESH,
        )

    def flip(owner, bit):
        value = lax.rem(owner // (1 << bit), 2)
        return owner + (1 << bit) * (1 - 2 * value)

    across, along = partner[1], partner[2]
    corner = flip(across, 2)
    near_zero, far_one = send(0, piece(seq, 0), 1), send(1, piece(seq, 1), 2)
    near_one, far_zero = send(2, piece(seq, 1), 1), send(3, piece(seq, 0), 2)
    twin = send(4, piece(seq), 0)
    for copy in (near_zero, far_one, near_one, far_zero, twin):
        copy.start()
    streaming[0] = False
    for copy in saves:
        copy.start()

    slot = begin(keys_at + 1)
    for block, tile in enumerate((at.tiles_b, at.tiles_c)):
        at.work[:, pl.ds(block * COLS, COLS)] = times(at.low_four, tile[slot])
    at.queries_low[...] = at.work[...].astype(jnp.bfloat16)
    save(at.queries_low, at.queries_raw)
    for head in range(width // lane):
        columns = pl.ds(head * lane, lane)
        query = head_path(at.work[:, columns], both_halves(at.vectors[7:8, pl.ds(0, lane)])).astype(jnp.bfloat16)
        query = query * jnp.bfloat16(HEAD_DIM**-0.5)
        at.scaled[:, columns] = query
        for which in range(rows):
            at.paired[which * (width // lane) + head] = two_heads(
                query[which * length : (which + 1) * length], True
            )
    save(at.scaled, at.queries_out)

    def transposed(low, target):
        for first in range(0, tokens, lane):
            span = pl.ds(first, lane)
            value = low[span].astype(jnp.float32).T.astype(jnp.bfloat16)
            target[:, :, :, :, span] = value.reshape(target.shape[:-1] + (lane,))

    transposed(at.low_one, at.turned_one)
    save(at.turned_one, at.mixer_in_x)
    near_zero.wait()
    far_one.wait()
    near_forward = send(5, piece(across, 0), 2)
    far_forward = send(6, piece(along, 1), 1)
    near_forward.start()
    far_forward.start()
    transposed(at.low_two, at.turned_two)
    save(at.turned_two, at.gated_x)

    at.sums[...] = jnp.zeros_like(at.sums)
    pairs_of = width // lane
    together = 4
    chip = seq // 2

    def attend(other):
        @pl.when(other <= chip)
        def _():
            span = pl.ds(pl.multiple_of(other * 2 * length, 2 * length), 2 * length)
            shape = (length, 2 * length)
            key_at = lax.broadcasted_iota(jnp.int32, shape, 1) + other * 2 * length
            query_at = lax.broadcasted_iota(jnp.int32, shape, 0) + seq * length
            first = lanes_below((2 * length, lane), HEAD_DIM, lane)
            for which in range(rows):
                start = at.seg_start[pl.ds(which * length, length)]
                start = jnp.concatenate([start, start], axis=1)
                allowed = jnp.logical_and(key_at >= start, key_at <= query_at)
                allowed = jnp.concatenate([allowed, allowed], axis=0)

                def some(group, carried):
                    heads = [group * together + head for head in range(together)]
                    boths = [
                        at.both[which, span, pl.ds(pl.multiple_of(head * lane, lane), lane)]
                        for head in heads
                    ]
                    places = [which * pairs_of + head for head in heads]
                    scores = [
                        dot_nt(at.paired[place], both) for place, both in zip(places, boths)
                    ]
                    for place, score, both in zip(places, scores, boths):
                        weights = jnp.where(allowed, jnp.exp(score), 0.0).astype(jnp.bfloat16)
                        right = jnp.where(first, 1.0, both.astype(jnp.float32))
                        at.sums[place] += jnp.dot(
                            weights, right.astype(jnp.bfloat16), preferred_element_type=jnp.float32
                        )
                    return carried

                lax.fori_loop(0, pairs_of // together, some, 0)

    twin.wait()
    attend(chip)
    near_one.wait()
    near_share = send(7, piece(across), 0)
    near_share.start()
    far_zero.wait()
    far_share = send(8, piece(along), 0)
    far_share.start()
    transposed(at.low_three, at.turned_three)
    save(at.turned_three, at.first_in_x)
    near_share.wait()
    attend(across // 2)
    transposed(at.low_four, at.turned_four)
    save(at.turned_four, at.attend_in_x)
    far_share.wait()
    attend(along // 2)

    block_rows = at.turned_active.shape[3]
    x_count = at.turned_active.shape[2]
    for j in range(hidden_blocks):
        for first in range(0, tokens, lane):
            span = pl.ds(first, lane)
            value = at.active_low[span, pl.ds(j * COLS, COLS)].astype(jnp.float32).T
            value = value.astype(jnp.bfloat16)
            for block in range(COLS // block_rows):
                place = j * (COLS // block_rows) + block
                shard = place // x_count
                at.turned_active[shard // 2, shard % 2, place % x_count, :, span] = value[
                    block * block_rows : (block + 1) * block_rows
                ]
    save(at.turned_active, at.active_x)
    near_forward.wait()
    far_forward.wait()
    corner_share = send(9, piece(corner), 0)
    corner_share.start()
    corner_share.wait()
    save(at.both, at.keys_values)
    attend(corner // 2)

    first = lanes_below((length, lane), HEAD_DIM, lane)
    for which in range(rows):
        span = pl.ds(which * length, length)
        for head in range(pairs_of):
            value = at.sums[which * pairs_of + head]
            value = value * (1.0 / pltpu.roll(value, HEAD_DIM, 1))
            value = jnp.where(first, pltpu.roll(value[:length], HEAD_DIM, 1), value[length:])
            at.attended[span, pl.ds(head * lane, lane)] = value.astype(jnp.bfloat16)
    add_output(keys_at + 2, at.attended, at.hidden_c, at.hidden_d)
    save(at.hidden_d, at.hidden_three)
    transposed(at.attended, at.turned_five)
    save(at.turned_five, at.attended_x)
    for copy in saves:
        copy.wait()


def forward(arrays, resident, rows, shards, collective_id):
    tokens, width = arrays["tokens"].shape
    hidden_columns = arrays["first_gate"].shape[1]
    length = tokens // rows
    total_length = length * shards
    block_rows = math.gcd(width // shards, hidden_columns // shards)
    low, full = jnp.bfloat16, jnp.float32

    def x_shape(columns):
        return (shards // 2, 2, columns // shards // block_rows, block_rows, tokens)

    outs = dict(
        hidden_zero=((tokens, width), full),
        hidden_one=((tokens, width), full),
        hidden_two=((tokens, width), full),
        hidden_three=((tokens, width), full),
        gate_one=((tokens, hidden_columns), low),
        up_one=((tokens, hidden_columns), low),
        queries_out=((tokens, width), low),
        queries_raw=((tokens, width), low),
        keys_raw=((tokens, width // 2), low),
        keys_values=((rows, total_length, width), low),
        mixer_saved=((4 * tokens, width), low),
        projected=((3 * tokens, width), low),
        mixer_in_x=(x_shape(width), low),
        gated_x=(x_shape(width), low),
        first_in_x=(x_shape(width), low),
        attend_in_x=(x_shape(width), low),
        attended_x=(x_shape(width), low),
        active_x=(x_shape(hidden_columns), low),
        vectors_out=((16, width), full),
        cosine_out=((tokens, 2 * HEAD_DIM), full),
        sine_out=((tokens, 2 * HEAD_DIM), full),
    )
    pairs = rows * width // (2 * HEAD_DIM)
    dma = pltpu.SemaphoreType.DMA
    scratch = dict(
        tiles_a=pltpu.VMEM((4, COLS, width), low),
        tiles_b=pltpu.VMEM((4, width, COLS), low),
        tiles_c=pltpu.VMEM((4, width, COLS), low),
        hidden_a=pltpu.VMEM((tokens, width), full),
        hidden_b=pltpu.VMEM((tokens, width), full),
        hidden_c=pltpu.VMEM((tokens, width), full),
        hidden_d=pltpu.VMEM((tokens, width), full),
        low_one=pltpu.VMEM((tokens, width), low),
        low_two=pltpu.VMEM((tokens, width), low),
        low_three=pltpu.VMEM((tokens, width), low),
        low_four=pltpu.VMEM((tokens, width), low),
        attended=pltpu.VMEM((tokens, width), low),
        work=pltpu.VMEM((tokens, width), full),
        mixed_low=pltpu.VMEM((4 * tokens, width), low),
        gates_low=pltpu.VMEM((3 * tokens, width), low),
        gate_low=pltpu.VMEM((tokens, hidden_columns), low),
        up_low=pltpu.VMEM((tokens, hidden_columns), low),
        active_low=pltpu.VMEM((tokens, hidden_columns), low),
        keys_low=pltpu.VMEM((tokens, width // 2), low),
        queries_low=pltpu.VMEM((tokens, width), low),
        scaled=pltpu.VMEM((tokens, width), low),
        both=pltpu.VMEM((rows, total_length, width), low),
        paired=pltpu.VMEM((pairs, 2 * length, 2 * HEAD_DIM), low),
        sums=pltpu.VMEM((pairs, 2 * length, 2 * HEAD_DIM), full),
        turned_one=pltpu.VMEM(x_shape(width), low),
        turned_two=pltpu.VMEM(x_shape(width), low),
        turned_three=pltpu.VMEM(x_shape(width), low),
        turned_four=pltpu.VMEM(x_shape(width), low),
        turned_five=pltpu.VMEM(x_shape(width), low),
        turned_active=pltpu.VMEM(x_shape(hidden_columns), low),
        vectors=pltpu.VMEM((16, width), full),
        cosine=pltpu.VMEM((tokens, 2 * HEAD_DIM), full),
        sine=pltpu.VMEM((tokens, 2 * HEAD_DIM), full),
        seg_start=pltpu.VMEM((tokens, 2 * HEAD_DIM), jnp.int32),
        halo_out=pltpu.VMEM((rows, 8, width), full),
        halo_in=pltpu.VMEM((rows, 8, width), full),
        tile_sem=dma((4, 3)),
        load_sem=dma((1,)),
        save_sem=dma((len(outs),)),
        halo_sem=dma((2,)),
        gather_send=dma((10,)),
        gather_recv=dma((10,)),
    )
    spaces = dict.fromkeys(resident, pltpu.VMEM)
    spaces["lengths"] = pltpu.SMEM
    any_space = pl.BlockSpec(memory_space=pl.ANY)
    weights = sum(value.size for value in arrays.values())
    results = pl.pallas_call(
        functools.partial(forward_kernel, list(arrays), list(outs), list(scratch), shards),
        out_shape=[jax.ShapeDtypeStruct(shape, kind) for shape, kind in outs.values()],
        in_specs=[pl.BlockSpec(memory_space=spaces.get(name, pl.ANY)) for name in arrays],
        out_specs=[any_space] * len(outs),
        scratch_shapes=list(scratch.values()),
        compiler_params=pltpu.CompilerParams(
            collective_id=collective_id, has_side_effects=True, vmem_limit_bytes=60 * 2**20
        ),
        cost_estimate=pl.CostEstimate(
            flops=2 * weights * tokens, bytes_accessed=2 * weights, transcendentals=0
        ),
    )(*arrays.values())
    return dict(zip(outs, results))


SECOND, ATTEND_OUTPUT, ATTENTION, QUERIES, KEYS, FIRST, MIXER_OUTPUT, HALO, MIXER_INPUT, CLOSE = range(10)
BACKWARD_STARTS = {
    SECOND: 0,
    ATTEND_OUTPUT: 8,
    ATTENTION: 10,
    QUERIES: 18,
    KEYS: 23,
    FIRST: 24,
    MIXER_OUTPUT: 33,
    HALO: 35,
    MIXER_INPUT: 36,
    CLOSE: 39,
}
FOLDED = 1
LOCAL_PAIRS = (14, 15, 18, 19)


def backward_kernel(names, entries, row_count, shards, *refs):
    at = types.SimpleNamespace(**dict(zip(names, refs)))
    outs = refs[len(names) : len(names) + len(entries)]
    token_out, mixed_out = refs[len(names) + len(entries) : len(names) + len(entries) + 2]
    scratch = refs[len(names) + len(entries) + 2 :]
    (
        tiles_a,
        tiles_b,
        tiles_c,
        saved,
        keys_values,
        key_grads,
        key_sums,
        queries,
        attended_grad,
        wide,
        queries_raw,
        keys_raw,
        gradient,
        normed_grad,
        hidden,
        halo_out,
        halo_in,
        small,
        tile_sem,
        load_sem,
        halo_sem,
        *scratch,
    ) = scratch
    local = types.SimpleNamespace()
    plain, chunk = [], 0
    for number, entry in enumerate(entries):
        if number != FOLDED:
            plain.append(entry[:4] + (chunk,))
            chunk += entry[1] * entry[3]
    plain_outs = [out for number, out in enumerate(outs) if number != FOLDED]
    fold_count = len(fold_scratch(shards, 2))
    fold_refs, scratch = scratch[:fold_count], scratch[fold_count:]
    exchange = Exchange(plain, row_count, shards, plain_outs, scratch, LOCAL_PAIRS, local)
    exchange.last_rows = 16
    exchange.fold = Fold(exchange, entries[FOLDED], outs[FOLDED], fold_refs)
    x_all, g_all = exchange.x_all, exchange.g_all
    seq, row = exchange.seq, exchange.row
    tokens, width = gradient.shape
    rows = keys_values.shape[0]
    length = tokens // rows
    hidden_blocks = at.first_gate.shape[1] // COLS
    blocks = width // COLS
    g_at = [entry[2] * COLS for entry in entries]
    second_wide, second_down, output_at, heads_at, first_down, first_wide = g_at[:6]
    mixer_out_at, mixer_in_at, small_at = g_at[6:]
    starts = BACKWARD_STARTS

    def local_place(kind, index):
        first, second, third, fourth = LOCAL_PAIRS
        row_at = jnp.where(index >= third, 1, 0)
        quad = jnp.where(jnp.logical_or(index == second, index == fourth), 1, 0)
        return row_at, pl.ds(pl.multiple_of(quad * COLS, COLS), COLS)

    def part(kind, index, side):
        row_at, columns = local_place(kind, index)
        return key_grads[row_at, :, side, kind, :, columns]

    def take(kind, index, total):
        row_at, columns = local_place(kind, index)
        key_sums[row_at, kind, :, columns] = total.astype(jnp.bfloat16)

    local.part, local.take = part, take

    def tile_copies(name, j, slot):
        columns = pl.ds(pl.multiple_of(j * COLS, COLS), COLS)
        a, b, c = tiles_a.at[slot], tiles_b.at[slot], tiles_c.at[slot]
        if name == SECOND:
            moves = [
                (at.second_gate.at[:, columns], b),
                (at.second_up.at[:, columns], c),
                (at.second_down.at[columns], a),
            ]
        elif name == FIRST:
            moves = [
                (at.first_down.at[columns], a),
                (at.first_gate.at[:, columns], b),
                (at.first_up.at[:, columns], c),
                (at.gate_one.at[:, columns], saved.at[slot, 0]),
                (at.up_one.at[:, columns], saved.at[slot, 1]),
            ]
        elif name == ATTEND_OUTPUT:
            moves = [(at.attend_output.at[columns], a)]
        elif name == MIXER_OUTPUT:
            moves = [(at.mixer_output.at[columns], a)]
        elif name == QUERIES:
            moves = [
                (at.query_weight.at[:, pl.ds(0, COLS)], b),
                (at.query_weight.at[:, pl.ds(COLS, COLS)], c),
            ]
        elif name == KEYS:
            moves = [(at.key_weight, b), (at.value_weight, c)]
        else:
            even = pl.multiple_of(2 * j * COLS, COLS)
            odd = pl.multiple_of((2 * j + 1) * COLS, COLS)
            moves = [
                (at.mixer_input.at[:, pl.ds(even, COLS)], b),
                (at.mixer_input.at[:, pl.ds(odd, COLS)], c),
            ]
        return [
            pltpu.make_async_copy(source, target, tile_sem.at[slot, place])
            for place, (source, target) in enumerate(moves)
        ]

    steps = [
        (SECOND, hidden_blocks),
        (ATTEND_OUTPUT, blocks),
        (QUERIES, 1),
        (KEYS, 1),
        (FIRST, hidden_blocks),
        (MIXER_OUTPUT, blocks),
        (MIXER_INPUT, 3 * blocks // 2),
    ]
    first_step, total = {}, 0
    for name, number in steps:
        first_step[name] = total
        total += number
    order = [name for name, _ in steps]
    numbers = dict(steps)

    def tile_step(name, j):
        slot = (first_step[name] + j) % 2 if isinstance(j, int) else lax.rem(first_step[name] + j, 2)
        for copy in tile_copies(name, j, slot):
            copy.wait()

        @pl.when(j + 1 < numbers[name])
        def _():
            for copy in tile_copies(name, j + 1, 1 - slot):
                copy.start()

        if name != order[-1]:
            following = order[order.index(name) + 1]

            @pl.when(j + 1 == numbers[name])
            def _():
                for copy in tile_copies(following, 0, 1 - slot):
                    copy.start()

        return slot

    def load(place, source, target):
        return pltpu.make_async_copy(source, target, load_sem.at[place])

    count = len(entries)
    x_loads = [
        load(number, at.xs[number - 2], x_all.at[:, :, pl.ds(x_first, x_count)])
        for number, (x_first, x_count, _, _, _) in enumerate(entries)
        if 2 <= number < count - 1
    ]
    cotangent_load = load(count, at.cotangent, g_all.at[:, pl.ds(second_down, width)])
    middle_loads = [
        load(count + 1, at.queries_out, queries),
        load(count + 2, at.keys_values, keys_values),
        load(count + 5, at.keys_raw, keys_raw),
    ]
    raw_load = load(count + 4, at.queries_raw, queries_raw)
    staged = queries_raw
    late_loads = [
        load(count + 6, at.mixer_saved, keys_values.at[0]),
        load(count + 7, at.projected, keys_values.at[1, pl.ds(0, 3 * tokens)]),
    ]
    hidden_loads = [
        load(count + 8, source, hidden)
        for source in (at.hidden_three, at.hidden_two, at.hidden_one, at.hidden_zero)
    ]
    out_copy = load(count + 9, staged, token_out)
    mixed_copy = load(count + 9, staged, mixed_out)

    hidden_loads[0].start()
    cotangent_load.start()
    for copy in tile_copies(SECOND, 0, 0):
        copy.start()
    for copy in middle_loads + x_loads:
        copy.start()
    normed_grad[...] = jnp.zeros_like(normed_grad)
    small[...] = jnp.zeros_like(small)
    g_all[:, pl.ds(small_at, COLS)] = jnp.zeros((tokens, COLS), jnp.bfloat16)
    wide[...] = jnp.zeros_like(wide)
    hidden_loads[0].wait()
    normed = attended_grad
    x_two = entries[0][0]
    for first in range(0, tokens, 128):
        span = pl.ds(first, 128)
        value = hidden[span]
        inverse = lax.rsqrt(jnp.mean(value * value, axis=-1, keepdims=True) + EPS)
        value = value * inverse * at.vectors[0:1, :]
        normed[span] = value.astype(jnp.bfloat16)
        turned = value.T.astype(jnp.bfloat16)
        shape = x_all.shape[:2] + (2,) + x_all.shape[3:4] + (128,)
        x_all[:, :, x_two : x_two + 2, :, pl.ds(first, 128)] = turned.reshape(shape)
    cotangent_load.wait()
    gradient[...] = g_all[:, pl.ds(second_down, width)].astype(jnp.float32)

    def low_gradient(place):
        g_all[:, pl.ds(place, width)] = gradient[...].astype(jnp.bfloat16)

    def norm_back(number):
        if number > 0:
            hidden_loads[number].wait()
        gain = at.vectors[number : number + 1, :]
        sums = jnp.zeros((1, width), jnp.float32)
        piece = 64
        for first in range(0, tokens, piece):
            span = pl.ds(first, piece)
            value, upper = hidden[span], normed_grad[span]
            inverse = lax.rsqrt(jnp.mean(value * value, axis=-1, keepdims=True) + EPS)
            value = value * inverse
            sums = sums + jnp.sum(upper * value, axis=0, keepdims=True)
            upper = upper * gain
            shift = jnp.mean(upper * value, axis=-1, keepdims=True)
            gradient[span] = gradient[span] + inverse * (upper - value * shift)
        for block in range(blocks):
            place = blocks * number + block
            small[place : place + 1, :] = sums[:, block * COLS : (block + 1) * COLS]
        normed_grad[...] = jnp.zeros_like(normed_grad)
        if number + 1 < len(hidden_loads):
            hidden_loads[number + 1].start()

    def feed_tile(name, j, gradient_at, wide_at):
        slot = tile_step(name, j)
        low = g_all[:, pl.ds(gradient_at, width)]
        active_grad = dot_nt(low, tiles_a[slot])
        if name == SECOND:
            gate_value = jnp.dot(normed[...], tiles_b[slot], preferred_element_type=jnp.float32)
            up_value = jnp.dot(normed[...], tiles_c[slot], preferred_element_type=jnp.float32)
        else:
            gate_value = saved[slot, 0].astype(jnp.float32)
            up_value = saved[slot, 1].astype(jnp.float32)
        share = 1.0 / (1.0 + jnp.exp(-gate_value))
        if name == SECOND:
            active = gate_value * share * up_value
            wide[...] += jnp.dot(
                active.astype(jnp.bfloat16), tiles_a[slot], preferred_element_type=jnp.float32
            )
            turned = active.T.astype(jnp.bfloat16)
            x_down, x_count = entries[1][:2]
            block_rows = x_all.shape[3]
            for block in range(COLS // block_rows):
                place = j * (COLS // block_rows) + block
                shard = place // x_count
                part = turned[block * block_rows : (block + 1) * block_rows]
                x_all[shard // 2, lax.rem(shard, 2), x_down + lax.rem(place, x_count)] = part
        up_grad = (active_grad * gate_value * share).astype(jnp.bfloat16)
        gate_grad = active_grad * up_value * share * (1.0 + gate_value * (1.0 - share))
        gate_grad = gate_grad.astype(jnp.bfloat16)
        gate_place = pl.multiple_of(wide_at + j * COLS, COLS)
        up_place = pl.multiple_of(wide_at + (hidden_blocks + j) * COLS, COLS)
        g_all[:, pl.ds(gate_place, COLS)] = gate_grad
        g_all[:, pl.ds(up_place, COLS)] = up_grad
        normed_grad[...] += dot_nt(gate_grad, tiles_b[slot]) + dot_nt(up_grad, tiles_c[slot])

    def output_tile(name, j, gradient_at, target):
        slot = tile_step(name, j)
        low = g_all[:, pl.ds(gradient_at, width)]
        value = dot_nt(low, tiles_a[slot])
        target[:, j * COLS : (j + 1) * COLS] = value.astype(target.dtype)

    def attention_head(row_at, head):
        span = pl.ds(pl.multiple_of(row_at * length, length), length)
        columns = pl.ds(pl.multiple_of(head * 2 * HEAD_DIM, 2 * HEAD_DIM), 2 * HEAD_DIM)
        query = two_heads(queries[span, columns], True)
        upper = two_heads(attended_grad[span, columns], False)
        both = keys_values[row_at, :, columns]
        key_at = lax.broadcasted_iota(jnp.int32, (both.shape[0], length), 0)
        query_at = lax.broadcasted_iota(jnp.int32, (both.shape[0], length), 1) + seq * length
        start = segment_start(at.lengths, row_at, query_at[0:8])[0:1]
        allowed = jnp.logical_and(key_at >= start, key_at <= query_at)
        weights = jnp.exp(dot_nt(both, query))
        weights = jnp.where(jnp.concatenate([allowed, allowed], axis=1), weights, 0.0)
        weights = weights * (1.0 / jnp.sum(weights, axis=0, keepdims=True))
        weight_grad_value = dot_nt(both, upper)
        delta = jnp.sum(weights * weight_grad_value, axis=0, keepdims=True)
        score_grad = (weights * (weight_grad_value - delta)).astype(jnp.bfloat16)
        both_grad = jnp.dot(score_grad, query, preferred_element_type=jnp.float32)
        both_grad += jnp.dot(
            weights.astype(jnp.bfloat16), upper, preferred_element_type=jnp.float32
        )
        shape = key_grads.shape[1:5] + (2 * HEAD_DIM,)
        key_grads[row_at, :, :, :, :, columns] = both_grad.astype(jnp.bfloat16).reshape(shape)
        query_grad = dot_tn(score_grad, both) * HEAD_DIM ** (-0.5)
        first = lanes_below((length, 2 * HEAD_DIM), HEAD_DIM, 2 * HEAD_DIM)
        wide[span, columns] = jnp.where(
            first, query_grad[:length], pltpu.roll(query_grad[length:], HEAD_DIM, 1)
        )

    lane = 2 * HEAD_DIM
    head_mean, turn = head_tools(lane)

    def head_back(value, raw, gain):
        value = value * at.cosine[...] - turn(value) * at.sine[...]
        raw = raw.astype(jnp.float32)
        inverse = lax.rsqrt(head_mean(raw * raw) + EPS)
        raw = raw * inverse
        sums = jnp.sum(value * raw, axis=0, keepdims=True)
        value = value * gain
        return inverse * (value - raw * head_mean(value * raw)), sums

    head_row = 7 * blocks

    def query_heads():
        sums = jnp.zeros((1, lane), jnp.float32)
        for part_at in range(0, width, lane):
            columns = pl.ds(part_at, lane)
            value, more = head_back(wide[:, columns], queries_raw[:, columns], both_halves(at.vectors[7:8, pl.ds(0, lane)]))
            g_all[:, pl.ds(heads_at + part_at, lane)] = value.astype(jnp.bfloat16)
            sums = sums + more
        small[head_row : head_row + 1, 0:lane] = both_halves(sums)

    def key_heads():
        sums = jnp.zeros((1, lane), jnp.float32)
        first = lanes_below((tokens, lane), HEAD_DIM, lane)
        for pair in range(width // lane // 2):
            even, odd = [
                key_sums[:, :, :, pl.ds((2 * pair + which) * lane, lane)]
                .astype(jnp.float32)
                .reshape(tokens, lane)
                for which in range(2)
            ]
            key_value = jnp.where(first, even, pltpu.roll(odd, HEAD_DIM, 1))
            value_value = jnp.where(first, pltpu.roll(even, HEAD_DIM, 1), odd)
            columns = pl.ds(pair * lane, lane)
            value, more = head_back(key_value, keys_raw[:, columns], both_halves(at.vectors[8:9, pl.ds(0, lane)]))
            place = heads_at + width + pair * lane
            g_all[:, pl.ds(place, lane)] = value.astype(jnp.bfloat16)
            place += width // 2
            g_all[:, pl.ds(place, lane)] = value_value.astype(jnp.bfloat16)
            sums = sums + more
        small[head_row : head_row + 1, lane : 2 * lane] = both_halves(sums)

    def project_back(name, j, even_at, odd_at):
        slot = tile_step(name, j)
        normed_grad[...] += dot_nt(g_all[:, pl.ds(even_at, COLS)], tiles_b[slot]) + dot_nt(
            g_all[:, pl.ds(odd_at, COLS)], tiles_c[slot]
        )

    def halo_copy():
        return pltpu.make_async_remote_copy(
            src_ref=halo_out,
            dst_ref=halo_in,
            send_sem=halo_sem.at[0],
            recv_sem=halo_sem.at[1],
            device_id=(row, jnp.maximum(seq - 1, 0)),
            device_id_type=MESH,
        )

    def saved_part(number, columns):
        return keys_values[0, pl.ds(number * tokens, tokens), columns].astype(jnp.float32)

    def projected_part(number, columns):
        return keys_values[1, pl.ds(number * tokens, tokens), columns].astype(jnp.float32)

    def convolution_back():
        within = lax.rem(lax.broadcasted_iota(jnp.int32, (tokens, lane), 0), length)
        position = within + seq * length
        start = [
            segment_start(at.lengths, which, position[which * length : (which + 1) * length])
            for which in range(rows)
        ]
        start = jnp.concatenate(start, axis=0)
        keep_one = position - 1 >= start
        keep_two = position - 2 >= start
        edge = lax.broadcasted_iota(jnp.int32, (8, lane), 0)
        for part_at in range(0, width, lane):
            columns = pl.ds(part_at, lane)
            gated_grad = wide[:, columns]
            exit_grad = gated_grad * saved_part(0, columns)
            place = mixer_in_at + width + part_at
            g_all[:, pl.ds(place, lane)] = exit_grad.astype(jnp.bfloat16)
            conv_grad = gated_grad * projected_part(1, columns)
            block, inside = part_at // COLS, part_at % COLS
            for tap in range(3):
                sums = jnp.sum(conv_grad * saved_part(1 + tap, columns), axis=0, keepdims=True)
                place = blocks * (4 + tap) + block
                small[place : place + 1, inside : inside + lane] = sums
            two = jnp.where(keep_two, at.vectors[4:5, columns] * conv_grad, 0.0)
            one = jnp.where(keep_one, at.vectors[5:6, columns] * conv_grad, 0.0)
            here = at.vectors[6:7, columns] * conv_grad
            here += jnp.where(within < length - 1, pltpu.roll(one, tokens - 1, 0), 0.0)
            here += jnp.where(within < length - 2, pltpu.roll(two, tokens - 2, 0), 0.0)
            normed_grad[:, columns] = here
            for which in range(rows):
                span = slice(which * length, which * length + 8)
                sent = two[span] + jnp.where(edge == 1, pltpu.roll(one[span], 1, 0), 0.0)
                halo_out[which, :, columns] = jnp.where(edge < 2, sent, 0.0)

        @pl.when(seq > 0)
        def _():
            halo_copy().start()

    def product_back():
        @pl.when(seq < shards - 1)
        def _():
            halo_copy().wait_recv()
            for which in range(rows):
                span = pl.ds((which + 1) * length - 8, 8)
                normed_grad[span] = normed_grad[span] + pltpu.roll(halo_in[which], 6, 0)

        @pl.when(seq > 0)
        def _():
            halo_copy().wait_send()

        for part_at in range(0, width, lane):
            columns = pl.ds(part_at, lane)
            product_grad = normed_grad[:, columns]
            entry_grad = product_grad * projected_part(2, columns)
            carrier_grad = product_grad * projected_part(0, columns)
            g_all[:, pl.ds(mixer_in_at + part_at, lane)] = entry_grad.astype(jnp.bfloat16)
            place = mixer_in_at + 2 * width + part_at
            g_all[:, pl.ds(place, lane)] = carrier_grad.astype(jnp.bfloat16)
        normed_grad[...] = jnp.zeros_like(normed_grad)

    def task(i):
        def when(name, run, after=0, number=1):
            j = i - (starts[name] + after)

            @pl.when(jnp.logical_and(j >= 0, j < number))
            def _():
                run(j)

        when(
            SECOND,
            lambda j: feed_tile(SECOND, j + 1, second_down, second_wide),
            0,
            hidden_blocks - 1,
        )

        def waits(j):
            for copy in middle_loads + x_loads:
                copy.wait()

        when(ATTEND_OUTPUT, waits)

        def to_attended(j):
            staged[...] = (hidden[...] + wide[...]).astype(jnp.bfloat16)
            mixed_copy.start()
            norm_back(0)
            low_gradient(output_at)
            output_tile(ATTEND_OUTPUT, 0, output_at, attended_grad)

        when(ATTEND_OUTPUT, to_attended)
        when(ATTEND_OUTPUT, lambda j: output_tile(ATTEND_OUTPUT, 1, output_at, attended_grad), 1)

        def staged_free(j):
            mixed_copy.wait()
            raw_load.start()

        when(ATTENTION, staged_free)

        def attention(j):
            pairs = KV_HEADS // 2
            for which in range(2):
                attention_head(j // pairs, 2 * lax.rem(j, pairs) + which)

        when(ATTENTION, attention, 0, rows * KV_HEADS // 2)

        def to_queries(j):
            raw_load.wait()
            for copy in late_loads:
                copy.start()
            query_heads()

        when(QUERIES, to_queries)
        def pick_rows(j):
            block_rows = x_all.shape[3]
            shape = (shards * 2 * block_rows, tokens)
            place = lax.broadcasted_iota(jnp.int32, shape, 0)
            vector, shard = lax.rem(place, 2 * block_rows), place // (2 * block_rows)
            wanted = blocks * vector + jnp.where(vector < 7, shard * blocks // shards, 0)
            found = lax.broadcasted_iota(jnp.int32, shape, 1) == wanted
            found = jnp.logical_and(found, vector < 8).astype(jnp.float32).astype(jnp.bfloat16)
            x_first = entries[-1][0]
            target = x_all.shape[:2] + (2, block_rows, tokens)
            x_all[:, :, x_first : x_first + 2] = found.reshape(target)

        when(QUERIES, pick_rows, 2)
        when(QUERIES, lambda j: project_back(QUERIES, 0, heads_at, heads_at + COLS), 1)

        def to_keys(j):
            key_heads()
            project_back(KEYS, 0, heads_at + width, heads_at + width + COLS)
            norm_back(1)
            low_gradient(first_down)

        when(KEYS, to_keys)
        when(FIRST, lambda j: feed_tile(FIRST, j, first_down, first_wide), 0, hidden_blocks)

        def to_gated(j):
            norm_back(2)
            low_gradient(mixer_out_at)
            output_tile(MIXER_OUTPUT, 0, mixer_out_at, wide)
            for copy in late_loads:
                copy.wait()

        when(MIXER_OUTPUT, to_gated)

        def to_convolved(j):
            output_tile(MIXER_OUTPUT, 1, mixer_out_at, wide)
            convolution_back()

        when(MIXER_OUTPUT, to_convolved, 1)
        when(HALO, lambda j: product_back())

        def mixer_tile(j):
            even = pl.multiple_of(mixer_in_at + 2 * j * COLS, COLS)
            project_back(MIXER_INPUT, j, even, pl.multiple_of(even + COLS, COLS))

        when(MIXER_INPUT, mixer_tile, 0, numbers[MIXER_INPUT])

        def close(j):
            norm_back(3)
            staged[...] = gradient[...].astype(jnp.bfloat16)
            out_copy.start()
            g_all[pl.ds(0, small.shape[0]), pl.ds(small_at, COLS)] = small[...].astype(jnp.bfloat16)

        when(CLOSE, close)
        when(CLOSE, lambda j: out_copy.wait(), 1)

    exchange.meet()
    feed_tile(SECOND, 0, second_down, second_wide)
    exchange.run(task)


def backward(groups, arrays, resident, row_count, shards, collective_id):
    xs = [x for x, _ in groups if not isinstance(x, int)]
    block_rows, tokens = xs[0].shape[3:]
    width = arrays["cotangent"].shape[1]
    entries, x_blocks, g_blocks, chunks = reduce_entries(
        [(x if isinstance(x, int) else x.shape[2], columns // COLS) for x, columns in groups]
    )
    names = ["xs_%d" % number for number in range(len(xs))] + list(arrays)
    values = list(xs) + list(arrays.values())
    rows, total_length = arrays["keys_values"].shape[:2]
    any_space = pl.BlockSpec(memory_space=pl.ANY)
    spaces = dict.fromkeys(resident, pltpu.VMEM)
    spaces["lengths"] = pltpu.SMEM
    key_blocks = total_length // shards // block_rows

    def kernel(*refs):
        xs_refs, others = refs[: len(xs)], refs[len(xs) : len(values)]
        named = [("xs", xs_refs)] + list(zip(arrays, others))
        backward_kernel(
            [name for name, _ in named],
            entries,
            row_count,
            shards,
            *[ref for _, ref in named],
            *refs[len(values) :],
        )

    low, full = jnp.bfloat16, jnp.float32
    return pl.pallas_call(
        kernel,
        out_shape=[
            jax.ShapeDtypeStruct((x_count * block_rows, g_count * COLS), low)
            for _, x_count, _, g_count, _ in entries
        ]
        + [jax.ShapeDtypeStruct((tokens, width), low)] * 2,
        in_specs=[pl.BlockSpec(memory_space=spaces.get(name, pl.ANY)) for name in names],
        out_specs=[any_space] * (len(entries) + 2),
        scratch_shapes=[
            pltpu.VMEM((2, COLS, width), low),
            pltpu.VMEM((2, width, COLS), low),
            pltpu.VMEM((2, width, COLS), low),
            pltpu.VMEM((2, 2, tokens, COLS), low),
            pltpu.VMEM((rows, total_length, width), low),
            pltpu.VMEM((rows, shards // 2, 2, key_blocks, block_rows, width), low),
            pltpu.VMEM((rows, key_blocks, block_rows, width), low),
            pltpu.VMEM((tokens, width), low),
            pltpu.VMEM((tokens, width), low),
            pltpu.VMEM((tokens, width), full),
            pltpu.VMEM((tokens, width), low),
            pltpu.VMEM((tokens, width // 2), low),
            pltpu.VMEM((tokens, width), full),
            pltpu.VMEM((tokens, width), full),
            pltpu.VMEM((tokens, width), full),
            pltpu.VMEM((rows, 8, width), full),
            pltpu.VMEM((rows, 8, width), full),
            pltpu.VMEM((16, COLS), full),
            pltpu.SemaphoreType.DMA((2, 5)),
            pltpu.SemaphoreType.DMA((len(entries) + 10,)),
            pltpu.SemaphoreType.DMA((2,)),
            *fold_scratch(shards, block_rows),
            *exchange_scratch(row_count, shards, block_rows, x_blocks, g_blocks, tokens),
        ],
        compiler_params=pltpu.CompilerParams(
            collective_id=collective_id, has_side_effects=True, vmem_limit_bytes=63 * 2**20
        ),
        cost_estimate=pl.CostEstimate(
            flops=4 * chunks * shards * block_rows * COLS * tokens,
            bytes_accessed=2 * chunks * shards * block_rows * COLS,
            transcendentals=0,
        ),
    )(*values)


def fused_body(
    tokens,
    lengths,
    mixer_gain,
    mixer_input,
    mixer_kernel,
    mixer_output,
    first_gain,
    first_gate,
    first_up,
    first_down,
    attend_gain,
    query_weight,
    key_weight,
    value_weight,
    query_gain,
    key_gain,
    attend_output,
    second_gain,
    second_gate,
    second_up,
    second_down,
    cotangent,
):
    full, low = jnp.float32, jnp.bfloat16
    rows, length, width = tokens.shape
    token_count = rows * length
    lane = 2 * HEAD_DIM
    row_count, shards = lax.axis_size("row"), lax.axis_size("seq")
    seq = lax.axis_index("seq")
    tables = dict(
        lengths=lengths,
        mixer_kernel=mixer_kernel,
        mixer_gain=mixer_gain,
        first_gain=first_gain,
        attend_gain=attend_gain,
        second_gain=second_gain,
        query_gain=query_gain,
        key_gain=key_gain,
    )
    arrays = dict(
        tokens=tokens.reshape(token_count, width),
        mixer_input=mixer_input,
        mixer_output=mixer_output,
        first_gate=first_gate,
        first_up=first_up,
        first_down=first_down,
        query_weight=query_weight,
        key_weight=key_weight,
        value_weight=value_weight,
        attend_output=attend_output,
        **tables,
    )
    saved = types.SimpleNamespace(**forward(arrays, tuple(tables), rows, shards, 2))
    block_rows = saved.attended_x.shape[3]
    weights = dict(
        second_down=second_down,
        second_gate=second_gate,
        second_up=second_up,
        attend_output=attend_output,
        query_weight=query_weight,
        key_weight=key_weight,
        value_weight=value_weight,
        first_down=first_down,
        first_gate=first_gate,
        first_up=first_up,
        mixer_output=mixer_output,
        mixer_input=mixer_input,
    )
    tables = dict(vectors=saved.vectors_out, cosine=saved.cosine_out, sine=saved.sine_out)
    arrays = dict(
        lengths=lengths,
        cotangent=cotangent.reshape(token_count, width),
        gate_one=saved.gate_one,
        up_one=saved.up_one,
        hidden_three=saved.hidden_three,
        hidden_two=saved.hidden_two,
        hidden_one=saved.hidden_one,
        hidden_zero=saved.hidden_zero,
        queries_out=saved.queries_out,
        keys_values=saved.keys_values,
        queries_raw=saved.queries_raw,
        keys_raw=saved.keys_raw,
        mixer_saved=saved.mixer_saved,
        projected=saved.projected,
        **tables,
        **weights,
    )
    hidden_columns = first_gate.shape[1]
    head_columns = width + 2 * key_weight.shape[1]
    groups = [
        (width // shards // block_rows, 2 * hidden_columns),
        (hidden_columns // shards // block_rows, width),
        (saved.attended_x, width),
        (saved.attend_in_x, head_columns),
        (saved.active_x, width),
        (saved.first_in_x, 2 * hidden_columns),
        (saved.gated_x, width),
        (saved.mixer_in_x, 3 * width),
        (2, COLS),
    ]
    (
        second_both,
        grad_second_down,
        grad_attend_output,
        attend_three,
        grad_first_down,
        first_both,
        grad_mixer_output,
        grad_mixer_input,
        sums,
        token_grad,
        mixed,
    ) = backward(groups, arrays, tuple(tables), row_count, shards, 1)

    key_columns = key_weight.shape[1]
    lows = [second_both, first_both, grad_second_down, grad_first_down]
    lows += [attend_three, grad_attend_output, grad_mixer_output, grad_mixer_input]
    fulls, (mixed, token_grad), small = to_full(
        (mixed, token_grad),
        sums,
        lows,
        (
            (0, 0, hidden_columns),
            (0, hidden_columns, hidden_columns),
            (1, 0, hidden_columns),
            (1, hidden_columns, hidden_columns),
            (2, 0, width),
            (3, 0, width),
            (4, 0, width),
            (4, width, key_columns),
            (4, width + key_columns, key_columns),
            (5, 0, width),
            (6, 0, width),
            (7, 0, 3 * width),
        ),
        shards,
    )
    (
        second_gate_full,
        second_up_full,
        first_gate_full,
        first_up_full,
        second_down_full,
        first_down_full,
        query_full,
        key_full,
        value_full,
        attend_output_full,
        mixer_output_full,
        mixer_input_full,
    ) = fulls
    return (
        mixed.reshape(tokens.shape),
        token_grad.reshape(tokens.shape),
        small[3],
        mixer_input_full,
        small[4],
        mixer_output_full,
        small[2],
        first_gate_full,
        first_up_full,
        first_down_full,
        small[1],
        query_full,
        key_full,
        value_full,
        small[5],
        small[6],
        attend_output_full,
        small[0],
        second_gate_full,
        second_up_full,
        second_down_full,
    )


def fused_or_general(*args):
    tokens = args[0]
    rows, length, width = tokens.shape
    row_count, shards = lax.axis_size("row"), lax.axis_size("seq")
    key_bytes = 2 * rows * length * shards * width
    if key_bytes <= 4 * 2**20 and shards == 8 and 4 * rows == shards and row_count == 4:
        return fused_body(*args)
    return body(*args)


def solution(mesh):
    in_specs = (
        P("row", "seq", None),
        P("row", None),
        P(),
        P(),
        P(),
        P(),
        P(),
        P(),
        P(),
        P(),
        P(),
        P(),
        P(),
        P(),
        P(),
        P(),
        P(),
        P(),
        P(),
        P(),
        P(),
        P("row", "seq", None),
    )
    out_specs = (
        P("row", "seq", None),
        P("row", "seq", None),
        P("seq"),
        P("seq", None),
        P(None, "seq"),
        P("seq", None),
        P("seq"),
        P("seq", None),
        P("seq", None),
        P("seq", None),
        P("seq"),
        P("seq", None),
        P("seq", None),
        P("seq", None),
        P("seq"),
        P("seq"),
        P("seq", None),
        P("seq"),
        P("seq", None),
        P("seq", None),
        P("seq", None),
    )
    return jax.shard_map(fused_or_general, mesh=mesh, in_specs=in_specs, out_specs=out_specs, check_vma=False)
```

```python
import functools
import math
import types

import jax
import jax.numpy as jnp
from jax import lax
from jax.experimental import pallas as pl
from jax.experimental.pallas import tpu as pltpu
from jax.sharding import PartitionSpec as P

HEADS = 16
KV_HEADS = 8
HEAD_DIM = 64
GROUP = 2


EPS = 1e-05
THETA = 1000000.0
NEGATIVE = -1e30
HIGHEST = lax.Precision.HIGHEST
MESH = pl.DeviceIdType.MESH
COLS = 512
SLOTS = 4
ZSLOTS = 6


def passed_along(value, axis, steps):
    count = lax.axis_size(axis)
    initial, last = (max(0, -steps), min(count, count - steps))
    return lax.ppermute(value, axis, [(source, source + steps) for source in range(initial, last)])


def segment_info(lengths, positions):
    boundary = jnp.cumsum(lengths, axis=-1)
    passed = boundary[:, None, :] <= positions[None, :, None]
    segment = jnp.sum(passed.astype(jnp.int32), axis=-1)
    seg_start = jnp.max(jnp.where(passed, boundary[:, None, :], 0), axis=-1)
    return (segment, seg_start)


def norm_rows(values, norm_gain):
    return values * lax.rsqrt(jnp.mean(values * values, axis=-1, keepdims=True) + EPS) * norm_gain


def rotate(values, offsets):
    half_dim = values.shape[-1] // 2
    inverse = THETA ** (-2.0 * jnp.arange(half_dim, dtype=jnp.float32) / values.shape[-1])
    angles = offsets.astype(jnp.float32)[:, :, None, None] * inverse
    cosine = jnp.cos(angles)
    sine_table = jnp.sin(angles)
    leading = values[..., :half_dim]
    trailing = values[..., half_dim:]
    return jnp.concatenate(
        [leading * cosine - trailing * sine_table, trailing * cosine + leading * sine_table],
        axis=-1,
    )


def swiglu(gate_value, upward):
    return gate_value / (1.0 + jnp.exp(-gate_value)) * upward


def dense(inputs, matrix):
    return jnp.einsum("rtd,df->rtf", inputs, matrix, preferred_element_type=jnp.float32)


def weight_grad(inputs, gradient):
    return (inputs, gradient)


def back_dense(gradient, matrix):
    return jnp.einsum("rtf,df->rtd", gradient, matrix, preferred_element_type=jnp.float32)


def mixer_block(hidden, norm_gain, input_matrix, kernel, output_matrix, seg_start, positions):
    feature_columns = hidden.shape[-1]
    length = hidden.shape[1]
    normed, norm_back = jax.vjp(norm_rows, hidden, norm_gain.astype(jnp.float32))
    normed_low = normed.astype(jnp.bfloat16)
    projected_rows = dense(normed_low, input_matrix)
    input_gate_value = projected_rows[..., :feature_columns]
    exit_gate = projected_rows[..., feature_columns : 2 * feature_columns]
    carry_value = projected_rows[..., 2 * feature_columns :]
    gated_product_reduced = (input_gate_value * carry_value).astype(jnp.bfloat16)
    previous = passed_along(gated_product_reduced[:, length - 2 :, :], "seq", 1)
    extended = jnp.concatenate([previous, gated_product_reduced], axis=1).astype(jnp.float32)
    keep_one = (positions[None, :] - 1 >= seg_start).astype(jnp.float32)[..., None]
    keep_two = (positions[None, :] - 2 >= seg_start).astype(jnp.float32)[..., None]
    kernel_taps = kernel.astype(jnp.float32)
    two_back = extended[:, :length]
    one_back = extended[:, 1 : length + 1]
    current = extended[:, 2:]
    convolved = (
        kernel_taps[2] * current
        + kernel_taps[1] * keep_one * one_back
        + kernel_taps[0] * keep_two * two_back
    )
    gated_low = (exit_gate * convolved).astype(jnp.bfloat16)
    result = hidden + dense(gated_low, output_matrix)

    def mixer_backward(gradient):
        gradient_low = gradient.astype(jnp.bfloat16)
        grad_output = weight_grad(gated_low, gradient_low)
        grad_gated = back_dense(gradient_low, output_matrix)
        output_gate_gradient = grad_gated * convolved
        grad_conv = grad_gated * exit_gate
        grad_kernel = jnp.stack(
            [
                jnp.sum(grad_conv * keep_two * two_back, axis=(0, 1)),
                jnp.sum(grad_conv * keep_one * one_back, axis=(0, 1)),
                jnp.sum(grad_conv * current, axis=(0, 1)),
            ]
        )
        grad_extended = jnp.pad(kernel_taps[0] * keep_two * grad_conv, ((0, 0), (0, 2), (0, 0)))
        grad_extended = grad_extended + jnp.pad(
            kernel_taps[1] * keep_one * grad_conv, ((0, 0), (1, 1), (0, 0))
        )
        grad_extended = grad_extended + jnp.pad(
            kernel_taps[2] * grad_conv, ((0, 0), (2, 0), (0, 0))
        )
        returned = passed_along(grad_extended[:, :2, :], "seq", -1)
        gated_product_gradient = grad_extended[:, 2:] + jnp.pad(
            returned, ((0, 0), (length - 2, 0), (0, 0))
        )
        grad_projected = jnp.concatenate(
            [
                gated_product_gradient * carry_value,
                output_gate_gradient,
                gated_product_gradient * input_gate_value,
            ],
            axis=-1,
        ).astype(jnp.bfloat16)
        grad_input = weight_grad(normed_low, grad_projected)
        grad_normed = back_dense(grad_projected, input_matrix)
        grad_hidden, grad_gain = norm_back(grad_normed)
        return (gradient + grad_hidden, (grad_gain, grad_input, grad_kernel, grad_output))

    return (result, mixer_backward)


def feed_block(hidden, norm_gain, gate_matrix, up_matrix, down_matrix):
    normed, norm_back = jax.vjp(norm_rows, hidden, norm_gain.astype(jnp.float32))
    normed_low = normed.astype(jnp.bfloat16)
    gate_value = dense(normed_low, gate_matrix)
    upward = dense(normed_low, up_matrix)
    active, active_back = jax.vjp(swiglu, gate_value, upward)
    active_low = active.astype(jnp.bfloat16)
    result = hidden + dense(active_low, down_matrix)

    def feed_backward(gradient):
        gradient_low = gradient.astype(jnp.bfloat16)
        grad_down = weight_grad(active_low, gradient_low)
        grad_gate, grad_upward = active_back(back_dense(gradient_low, down_matrix))
        gate_low = grad_gate.astype(jnp.bfloat16)
        upward_low = grad_upward.astype(jnp.bfloat16)
        grad_normed = back_dense(gate_low, gate_matrix) + back_dense(upward_low, up_matrix)
        grad_hidden, grad_gain = norm_back(grad_normed)
        return (
            gradient + grad_hidden,
            (
                grad_gain,
                weight_grad(normed_low, jnp.concatenate([gate_low, upward_low], axis=-1)),
                grad_down,
            ),
        )

    return (result, feed_backward)


def attend_block(
    hidden,
    lengths,
    norm_gain,
    query_matrix,
    key_matrix,
    value_matrix,
    query_norm,
    key_norm,
    output_matrix,
    segment,
    positions,
    offsets,
):
    row_count, length, feature_columns = hidden.shape
    score_scale = HEAD_DIM ** (-0.5)
    normed, norm_back = jax.vjp(norm_rows, hidden, norm_gain.astype(jnp.float32))
    normed_low = normed.astype(jnp.bfloat16)

    def head_path(projected_rows, head_gain):
        return rotate(norm_rows(projected_rows, head_gain), offsets)

    queries = dense(normed_low, query_matrix).reshape(row_count, length, HEADS, HEAD_DIM)
    keys_raw = dense(normed_low, key_matrix).reshape(row_count, length, KV_HEADS, HEAD_DIM)
    values_raw = dense(normed_low, value_matrix)
    query_rot, query_back = jax.vjp(head_path, queries, query_norm.astype(jnp.float32))
    key_rot, key_back = jax.vjp(head_path, keys_raw, key_norm.astype(jnp.float32))
    query_low = query_rot.astype(jnp.bfloat16).reshape(row_count, length, KV_HEADS, GROUP, HEAD_DIM)
    key_low = key_rot.astype(jnp.bfloat16)
    value_low = values_raw.astype(jnp.bfloat16).reshape(row_count, length, KV_HEADS, HEAD_DIM)
    all_keys, all_values = (
        lax.all_gather(key_low, "seq", axis=1, tiled=True),
        lax.all_gather(value_low, "seq", axis=1, tiled=True),
    )
    total_length = all_keys.shape[1]
    key_block = min(512, total_length)
    block_count = (positions[length - 1] + key_block) // key_block

    def block_scores(number, key_source, value_source):
        first_key = number * key_block
        keys_here = lax.dynamic_slice_in_dim(key_source, first_key, key_block, 1)
        values_here = lax.dynamic_slice_in_dim(value_source, first_key, key_block, 1)
        key_positions = first_key + jnp.arange(key_block, dtype=jnp.int32)
        key_segment, unused = segment_info(lengths, key_positions)
        scores = (
            jnp.einsum(
                "rtkgh,rskh->rkgts", query_low, keys_here, preferred_element_type=jnp.float32
            )
            * score_scale
        )
        allowed = (segment[:, :, None] == key_segment[:, None, :]) & (
            positions[None, :, None] >= key_positions[None, None, :]
        )
        allowed = allowed[:, None, None]
        return (jnp.where(allowed, scores, NEGATIVE), allowed, keys_here, values_here)

    stat_shape = (row_count, KV_HEADS, GROUP, length)

    def stats_step(number, carried):
        peak_score, running_sum = carried
        scores, allowed, unused_keys, unused_values = block_scores(number, all_keys, all_values)
        new_peak = jnp.maximum(peak_score, jnp.max(scores, axis=-1))
        fresh = jnp.sum(jnp.where(allowed, jnp.exp(scores - new_peak[..., None]), 0.0), axis=-1)
        return (new_peak, running_sum * jnp.exp(peak_score - new_peak) + fresh)

    peak_score, running_sum = lax.fori_loop(
        0,
        block_count,
        stats_step,
        (jnp.full(stat_shape, NEGATIVE, jnp.float32), jnp.zeros(stat_shape, jnp.float32)),
    )
    log_total = peak_score + jnp.log(running_sum)

    def probabilities(scores, allowed):
        return jnp.where(allowed, jnp.exp(scores - log_total[..., None]), 0.0)

    out_shape = (row_count, length, KV_HEADS, GROUP, HEAD_DIM)

    def output_step(number, carried):
        rounded, exact_sum = carried
        scores, allowed, keys_here, values_here = block_scores(number, all_keys, all_values)
        weights = probabilities(scores, allowed)
        rounded = rounded + jnp.einsum(
            "rkgts,rskh->rtkgh",
            weights.astype(jnp.bfloat16),
            values_here,
            preferred_element_type=jnp.float32,
        )
        exact_sum = exact_sum + jnp.einsum(
            "rkgts,rskh->rtkgh", weights, values_here.astype(jnp.float32), precision=HIGHEST
        )
        return (rounded, exact_sum)

    rounded, exact_sum = lax.fori_loop(
        0,
        block_count,
        output_step,
        (jnp.zeros(out_shape, jnp.float32), jnp.zeros(out_shape, jnp.float32)),
    )
    attended_low = rounded.reshape(row_count, length, HEADS * HEAD_DIM).astype(jnp.bfloat16)
    result = hidden + dense(attended_low, output_matrix)

    def attend_backward(gradient):
        gradient_low = gradient.astype(jnp.bfloat16)
        grad_output = weight_grad(attended_low, gradient_low)
        grad_attended = (
            back_dense(gradient_low, output_matrix).astype(jnp.bfloat16).reshape(out_shape)
        )
        row_delta = jnp.einsum(
            "rtkgh,rtkgh->rkgt", grad_attended.astype(jnp.float32), exact_sum, precision=HIGHEST
        )
        key_source, value_source = (all_keys, all_values)

        def grad_step(number, carried):
            grad_query, grad_keys, grad_values = carried
            scores, allowed, keys_here, values_here = block_scores(number, key_source, value_source)
            weights = probabilities(scores, allowed)
            grad_weights = jnp.einsum(
                "rtkgh,rskh->rkgts", grad_attended, values_here, preferred_element_type=jnp.float32
            )
            grad_scores = (weights * (grad_weights - row_delta[..., None])).astype(jnp.bfloat16)
            grad_query = (
                grad_query
                + jnp.einsum(
                    "rkgts,rskh->rtkgh", grad_scores, keys_here, preferred_element_type=jnp.float32
                )
                * score_scale
            )
            key_part = (
                jnp.einsum(
                    "rkgts,rtkgh->rskh", grad_scores, query_low, preferred_element_type=jnp.float32
                )
                * score_scale
            )
            value_part = jnp.einsum(
                "rkgts,rtkgh->rskh",
                weights.astype(jnp.bfloat16),
                grad_attended,
                preferred_element_type=jnp.float32,
            )
            grad_keys = lax.dynamic_update_slice_in_dim(grad_keys, key_part, number * key_block, 1)
            grad_values = lax.dynamic_update_slice_in_dim(
                grad_values, value_part, number * key_block, 1
            )
            return (grad_query, grad_keys, grad_values)

        key_shape = (row_count, total_length, KV_HEADS, HEAD_DIM)
        grad_query, grad_keys, grad_values = lax.fori_loop(
            0,
            block_count,
            grad_step,
            (
                jnp.zeros(out_shape, jnp.float32),
                jnp.zeros(key_shape, jnp.float32),
                jnp.zeros(key_shape, jnp.float32),
            ),
        )
        local_keys, local_values = (
            lax.psum_scatter(
                grad_keys.astype(jnp.bfloat16), "seq", scatter_dimension=1, tiled=True
            ).astype(jnp.float32),
            lax.psum_scatter(
                grad_values.astype(jnp.bfloat16), "seq", scatter_dimension=1, tiled=True
            ).astype(jnp.float32),
        )
        grad_queries, grad_query_norm = query_back(
            grad_query.reshape(row_count, length, HEADS, HEAD_DIM)
        )
        grad_keys_raw, grad_key_norm = key_back(local_keys)
        query_grad_low = grad_queries.reshape(row_count, length, HEADS * HEAD_DIM).astype(
            jnp.bfloat16
        )
        key_grad_low = grad_keys_raw.reshape(row_count, length, KV_HEADS * HEAD_DIM).astype(
            jnp.bfloat16
        )
        value_grad_low = local_values.reshape(row_count, length, KV_HEADS * HEAD_DIM).astype(
            jnp.bfloat16
        )
        grad_normed = (
            back_dense(query_grad_low, query_matrix)
            + back_dense(key_grad_low, key_matrix)
            + back_dense(value_grad_low, value_matrix)
        )
        grad_hidden, grad_gain = norm_back(grad_normed)
        return (
            gradient + grad_hidden,
            (
                grad_gain,
                weight_grad(
                    normed_low,
                    jnp.concatenate([query_grad_low, key_grad_low, value_grad_low], axis=-1),
                ),
                grad_query_norm,
                grad_key_norm,
                grad_output,
            ),
        )

    return (result, attend_backward)


def reduce_entries(pairs):
    entries = []
    x_first = g_first = chunk = 0
    for x_count, g_count in pairs:
        entries.append((x_first, x_count, g_first, g_count, chunk))
        x_first += x_count
        g_first += g_count
        chunk += x_count * g_count
    return entries, x_first, g_first, chunk


def locate(entries, q):
    x_block, g_block = jnp.int32(0), jnp.int32(0)
    for x_first, x_count, g_first, g_count, chunk in entries:
        here = q - chunk
        inside = here >= 0
        x_block = jnp.where(inside, x_first + lax.rem(jnp.maximum(here, 0), x_count), x_block)
        g_block = jnp.where(inside, g_first + jnp.maximum(here, 0) // x_count, g_block)
    return x_block, g_block


def seq_steps(bits):
    upper = list(range(1, bits))
    middle = (len(upper) + 1) // 2
    kinds = []
    for order in (upper, upper[middle:] + upper[:middle]):
        held = sorted(upper, reverse=True)
        steps = []
        for bit in order:
            place = held.index(bit)
            steps.append((bit, 2**place, 2 ** (len(held) - 1 - place)))
            held.remove(bit)
        kinds.append(steps)
    return kinds


def exchange_scratch(row_count, shards, block_rows, x_blocks, g_blocks, tokens):
    bits = shards.bit_length() - 1
    block = (block_rows, COLS)
    comm = []
    for steps in seq_steps(bits):
        for _, above, below in steps:
            comm.append(pltpu.VMEM((2, above, 2, below) + block, jnp.bfloat16))
            comm.append(pltpu.VMEM((SLOTS, above, below) + block, jnp.bfloat16))
    z_steps = row_count - 1
    own_slots = 3 if row_count <= 4 else ZSLOTS
    return [
        pltpu.VMEM((shards // 2, 2, x_blocks, block_rows, tokens), jnp.bfloat16),
        pltpu.VMEM((tokens, g_blocks * COLS), jnp.bfloat16),
        pltpu.VMEM((2, 2, shards // 2) + block, jnp.bfloat16),
        pltpu.VMEM((2, SLOTS, shards // 2) + block, jnp.bfloat16),
        *comm,
        *[
            pltpu.VMEM((2, count) + block, jnp.bfloat16)
            for count in (own_slots, ZSLOTS, own_slots, ZSLOTS, ZSLOTS)
        ],
        pltpu.SemaphoreType.DMA((2, bits, SLOTS)),
        pltpu.SemaphoreType.DMA((2, bits, SLOTS)),
        pltpu.SemaphoreType.DMA((2, z_steps, ZSLOTS)),
        pltpu.SemaphoreType.DMA((2, z_steps, ZSLOTS)),
        pltpu.SemaphoreType.DMA((2, ZSLOTS)),
    ]


class Exchange:
    def __init__(self, entries, row_count, shards, outs, scratch, locals_at=(), local=None):
        self.last_rows, self.fold = None, None
        self.entries, self.outs = entries, outs
        self.locals_at, self.local = locals_at, local
        self.bits = bits = shards.bit_length() - 1
        self.kinds = seq_steps(bits)
        (self.x_all, self.g_all, self.send_zero, self.recv_zero, *rest) = scratch
        self.held, self.received = [[], []], [[], []]
        for kind in range(2):
            for _ in self.kinds[kind]:
                self.held[kind].append(rest.pop(0))
                self.received[kind].append(rest.pop(0))
        self.z_own, self.z_in, self.z_part, self.z_cross, self.z_total = rest[:5]
        self.seq_send, self.seq_recv, self.z_send, self.z_recv, self.out_sem = rest[5:]
        self.row, self.seq = lax.axis_index("row"), lax.axis_index("seq")
        self.row_count, self.shards = row_count, shards
        self.value = [lax.rem(self.seq // (1 << bit), 2) for bit in range(bits)]
        self.partner = [self.seq + (1 << bit) * (1 - 2 * self.value[bit]) for bit in range(bits)]
        last = entries[-1]
        self.pairs = (last[4] + last[1] * last[3]) // 2 + len(locals_at)
        half = row_count // 2
        self.depth = half - 1
        lower = self.row < half
        self.level = jnp.where(lower, self.row, row_count - 1 - self.row)
        self.toward = jnp.where(lower, self.row + 1, self.row - 1)
        self.away = jnp.where(lower, self.row - 1, self.row + 1)

    def meet(self):
        barrier = pltpu.get_barrier_semaphore()
        others = [(self.row, partner) for partner in self.partner]
        for step in (1, self.row_count - 1):
            others.append((lax.rem(self.row + step, self.row_count), self.seq))
        for step in (1, self.shards - 1):
            others.append((self.row, lax.rem(self.seq + step, self.shards)))
        if self.fold is not None:
            others.append((self.fold.far, self.seq))
        for other in others:
            pl.semaphore_signal(barrier, inc=1, device_id=other, device_id_type=MESH)
        pl.semaphore_wait(barrier, len(others))

    def is_local(self, index):
        found = index < 0
        for at in self.locals_at:
            found = jnp.logical_or(found, index == at)
        return found

    def chunk(self, kind, index):
        before = sum([jnp.where(index > at, 1, 0) for at in self.locals_at], 0)
        return 2 * (index - before) + kind

    def product(self, kind, index, side):
        x_block, g_block = locate(self.entries, self.chunk(kind, index))
        left = self.x_all[:, side, x_block]
        columns = pl.ds(pl.multiple_of(g_block * COLS, COLS), COLS)
        return jnp.dot(
            left.reshape(left.shape[0] * left.shape[1], left.shape[2]),
            self.g_all[:, columns],
            preferred_element_type=jnp.float32,
        )

    def sized(self, kind, index, act):
        if self.last_rows is None or kind == 1:
            act(None)
        else:
            pl.when(index < self.pairs - 1)(lambda: act(None))
            pl.when(index == self.pairs - 1)(lambda: act(self.last_rows))

    def own_slot(self, slot):
        return lax.rem(slot, self.z_own.shape[1])

    def seq_start(self, kind, step, slot, index):
        self.sized(kind, index, lambda rows: self.seq_copy(kind, step, slot, rows).start())

    def seq_wait(self, kind, step, slot, index):
        self.sized(kind, index, lambda rows: self.seq_copy(kind, step, slot, rows).wait())

    def z_start(self, kind, step, slot, index):
        self.sized(kind, index, lambda rows: self.z_copy(kind, step, slot, rows).start())

    def z_wait(self, kind, step, slot, index):
        self.sized(kind, index, lambda rows: self.z_copy(kind, step, slot, rows).wait())

    def z_wait_recv(self, kind, step, slot, index):
        self.sized(kind, index, lambda rows: self.z_copy(kind, step, slot, rows).wait_recv())

    def z_wait_send(self, kind, step, slot, index):
        self.sized(kind, index, lambda rows: self.z_copy(kind, step, slot, rows).wait_send())

    def seq_copy(self, kind, step, slot, rows):
        some = pl.ds(0, self.z_own.shape[2] if rows is None else rows)
        if step == 0:
            bit = 0
            source = self.send_zero.at[kind, lax.rem(slot, 2), :, some]
            target = self.recv_zero.at[kind, slot, :, some]
        else:
            bit = self.kinds[kind][step - 1][0]
            away = 1 - self.value[bit]
            source = self.held[kind][step - 1].at[lax.rem(slot, 2), :, away, :, some]
            target = self.received[kind][step - 1].at[slot, :, :, some]
        return pltpu.make_async_remote_copy(
            src_ref=source,
            dst_ref=target,
            send_sem=self.seq_send.at[kind, step, slot],
            recv_sem=self.seq_recv.at[kind, step, slot],
            device_id=(self.row, self.partner[bit]),
            device_id_type=MESH,
        )

    def seq_sum(self, kind, step, slot):
        bit = self.kinds[kind][step - 2][0]
        mine = self.held[kind][step - 2][lax.rem(slot, 2), :, self.value[bit]].astype(jnp.float32)
        return mine + self.received[kind][step - 2][slot].astype(jnp.float32)

    def z_copy(self, kind, step, slot, rows):
        some = pl.ds(0, self.z_own.shape[2] if rows is None else rows)
        if step < self.depth:
            source = self.z_own if step == 0 else self.z_part
            target, where = self.z_in, self.toward
        elif step == self.depth:
            source = self.z_own if self.depth == 0 else self.z_part
            target, where = self.z_cross, self.toward
        else:
            source, target, where = self.z_total, self.z_total, self.away
        return pltpu.make_async_remote_copy(
            src_ref=source.at[kind, slot if source is self.z_total else self.own_slot(slot), some],
            dst_ref=target.at[kind, slot, some],
            send_sem=self.z_send.at[kind, step, slot],
            recv_sem=self.z_recv.at[kind, step, slot],
            device_id=(where, self.seq),
            device_id_type=MESH,
        )

    def start_out(self, kind, slot, index):
        q = self.chunk(kind, index)
        rows = self.z_total.shape[2]
        for out, (_, x_count, _, g_count, chunk) in zip(self.outs, self.entries):
            here = q - chunk

            @pl.when(jnp.logical_and(here >= 0, here < x_count * g_count))
            def _():
                row_at = pl.multiple_of(lax.rem(here, x_count) * rows, rows)
                column_at = pl.multiple_of(here // x_count * COLS, COLS)
                pltpu.make_async_copy(
                    self.z_total.at[kind, slot],
                    out.at[pl.ds(row_at, rows), pl.ds(column_at, COLS)],
                    self.out_sem.at[kind, slot],
                ).start()

    def first(self, kind, index):
        slot = lax.rem(index, SLOTS)
        target = self.send_zero

        def put():
            target[kind, lax.rem(slot, 2)] = (
                self.product(kind, index, 1 - self.value[0])
                .astype(jnp.bfloat16)
                .reshape(target.shape[2:])
            )

        if self.local is None:
            put()
        else:
            pl.when(jnp.logical_not(self.is_local(index)))(put)

            @pl.when(self.is_local(index))
            def _():
                target[kind, lax.rem(slot, 2)] = self.local.part(kind, index, 1 - self.value[0])

        self.seq_start(kind, 0, slot, index)

    def second(self, kind, index):
        slot = lax.rem(index, SLOTS)
        self.seq_wait(kind, 0, slot, index)
        target = self.held[kind][0]

        def put():
            mine = self.product(kind, index, self.value[0])
            total = mine + self.recv_zero[kind, slot].astype(jnp.float32).reshape(mine.shape)
            target[lax.rem(slot, 2)] = total.astype(jnp.bfloat16).reshape(target.shape[1:])

        if self.local is None:
            put()
        else:
            pl.when(jnp.logical_not(self.is_local(index)))(put)

            @pl.when(self.is_local(index))
            def _():
                mine = self.local.part(kind, index, self.value[0]).astype(jnp.float32)
                total = mine + self.recv_zero[kind, slot].astype(jnp.float32)
                target[lax.rem(slot, 2)] = total.astype(jnp.bfloat16).reshape(target.shape[1:])

        self.seq_start(kind, 1, slot, index)

    def middle(self, step):
        def run(kind, index):
            slot = lax.rem(index, SLOTS)
            self.seq_wait(kind, step - 1, slot, index)
            total = self.seq_sum(kind, step, slot)
            target = self.held[kind][step - 1]
            target[lax.rem(slot, 2)] = total.astype(jnp.bfloat16).reshape(target.shape[1:])
            self.seq_start(kind, step, slot, index)

        return run

    def last(self, kind, index):
        slot, z_slot = lax.rem(index, SLOTS), lax.rem(index, ZSLOTS)
        self.seq_wait(kind, self.bits - 1, slot, index)
        total = self.seq_sum(kind, self.bits, slot).reshape(self.z_own.shape[2:])

        def put():
            self.z_own[kind, self.own_slot(z_slot)] = total.astype(jnp.bfloat16)

            @pl.when(self.level == 0)
            def _():
                self.z_start(kind, 0, z_slot, index)

        if self.local is None:
            put()
        else:
            pl.when(jnp.logical_not(self.is_local(index)))(put)

            @pl.when(self.is_local(index))
            def _():
                self.local.take(kind, index, total)

    def z_stage(self, step):
        level, depth = self.level, self.depth

        def run(kind, index):
            slot = lax.rem(index, ZSLOTS)
            if step <= depth:

                @pl.when(level == step)
                def _():
                    self.z_wait_recv(kind, step - 1, slot, index)
                    self.z_part[kind, self.own_slot(slot)] = (
                        self.z_own[kind, self.own_slot(slot)].astype(jnp.float32)
                        + self.z_in[kind, slot].astype(jnp.float32)
                    ).astype(jnp.bfloat16)
                    self.z_start(kind, step, slot, index)

                @pl.when(level == step - 1)
                def _():
                    self.z_wait_send(kind, step - 1, slot, index)

            elif step == depth + 1:

                @pl.when(level == depth)
                def _():
                    self.z_wait(kind, depth, slot, index)
                    own = self.z_own if depth == 0 else self.z_part
                    self.z_total[kind, slot] = (
                        own[kind, self.own_slot(slot)].astype(jnp.float32)
                        + self.z_cross[kind, slot].astype(jnp.float32)
                    ).astype(jnp.bfloat16)
                    if depth > 0:
                        self.z_start(kind, step, slot, index)
                    self.start_out(kind, slot, index)

            else:
                receiver = 2 * depth + 1 - step

                @pl.when(level == receiver)
                def _():
                    self.z_wait_recv(kind, step - 1, slot, index)
                    if receiver > 0:
                        self.z_start(kind, step, slot, index)
                    self.start_out(kind, slot, index)

                @pl.when(level == receiver + 1)
                def _():
                    self.z_wait_send(kind, step - 1, slot, index)

        return run

    def finish(self, kind, index):
        slot = lax.rem(index, ZSLOTS)
        rows = self.z_total.shape[2]
        pltpu.make_async_copy(
            self.z_total.at[kind, slot],
            self.outs[0].at[pl.ds(0, rows), pl.ds(0, COLS)],
            self.out_sem.at[kind, slot],
        ).wait()

    def run(self, task):
        stages = [(self.first, False), (self.second, False)]
        stages += [(self.middle(step), False) for step in range(2, self.bits)]
        stages += [(self.last, False)]
        stages += [(self.z_stage(step), True) for step in range(1, 2 * self.depth + 2)]
        stages += [(self.finish, True)]

        def iteration(i, carried):
            for at, (stage, summed_only) in enumerate(stages):
                index = i - at
                here = jnp.logical_and(index >= 0, index < self.pairs)
                if summed_only and self.locals_at:
                    here = jnp.logical_and(here, jnp.logical_not(self.is_local(index)))

                @pl.when(here)
                def _():
                    stage(0, index)
                    if self.last_rows is None:
                        stage(1, index)

                if self.last_rows is not None:

                    @pl.when(jnp.logical_and(here, index < self.pairs - 1))
                    def _():
                        stage(1, index)

            if self.fold is not None:
                self.fold.advance(i)
            if task is not None:
                task(i)
            return carried

        total = self.pairs + len(stages) - 1
        if self.fold is not None:
            total = max(total, self.fold.end)
        lax.fori_loop(0, total, iteration, 0)


FOLD_START, FOLD_PERIOD = 8, 3


def fold_scratch(shards, block_rows):
    half = (block_rows // 2, COLS)
    low = jnp.bfloat16
    orders = []
    for steps in seq_steps(shards.bit_length() - 1):
        for _, above, below in steps:
            orders.append(pltpu.VMEM((above, 2, below) + half, low))
            orders.append(pltpu.VMEM((2, above, below) + half, low))
    return [
        pltpu.VMEM((shards // 2, block_rows, COLS), low),
        pltpu.VMEM((2, shards // 2, block_rows, COLS), low),
        pltpu.VMEM((shards // 2, 2) + half, low),
        pltpu.VMEM((2, shards // 2) + half, low),
        *orders,
        pltpu.VMEM(half, low),
        pltpu.VMEM((3,) + half, low),
        pltpu.VMEM((3, 2) + half, low),
        pltpu.SemaphoreType.DMA((6, 3)),
        pltpu.SemaphoreType.DMA((6, 3)),
        pltpu.SemaphoreType.DMA((2, 3)),
    ]


class Fold:
    def __init__(self, exchange, entry, out, scratch):
        self.exchange, self.entry, self.out = exchange, entry, out
        (self.send, self.received, self.halves, self.half_in, *rest) = scratch
        self.held, self.held_in = [[], []], [[], []]
        for order in range(2):
            for _ in exchange.kinds[order]:
                self.held[order].append(rest.pop(0))
                self.held_in[order].append(rest.pop(0))
        self.own, self.cross, self.total, self.send_sem, self.recv_sem, self.out_sem = rest
        row = exchange.row
        self.bit = lax.rem(row, 2)
        self.near, self.far = row + 1 - 2 * self.bit, lax.rem(row + 2, 4)
        self.count = entry[1] * entry[3]
        self.stages = [
            (0, self.first),
            (1, self.second),
            (3, self.third),
            (4, self.fourth),
            (5, self.fifth),
            (7, self.sixth),
            (9, self.seventh),
            (10, self.finish),
        ]
        self.end = FOLD_START + FOLD_PERIOD * (self.count - 1) + 11

    def advance(self, i):
        for offset, run in self.stages:
            since = i - (FOLD_START + offset)
            number = jnp.maximum(since, 0) // FOLD_PERIOD
            here = jnp.logical_and(since >= 0, lax.rem(jnp.maximum(since, 0), FOLD_PERIOD) == 0)
            here = jnp.logical_and(here, number < self.count)

            @pl.when(here)
            def _():
                run(number)

    def copy(self, step, number, order=0):
        exchange = self.exchange
        row, seq, two, three = exchange.row, exchange.seq, lax.rem(number, 2), lax.rem(number, 3)
        if step == 0:
            source, target = self.send, self.received.at[two]
            device = (row, exchange.partner[0])
        elif step == 1:
            source, target = self.halves.at[:, 1 - self.bit], self.half_in.at[two]
            device = (self.near, seq)
        elif step < 4:
            bit = exchange.kinds[order][step - 2][0]
            source = self.held[order][step - 2].at[:, 1 - exchange.value[bit]]
            target = self.held_in[order][step - 2].at[lax.rem(number // 2, 2)]
            device = (row, exchange.partner[bit])
        elif step == 4:
            source, target = self.own, self.cross.at[three]
            device = (self.far, seq)
        else:
            source = target = self.total.at[three, self.bit]
            device = (self.near, seq)
        return pltpu.make_async_remote_copy(
            src_ref=source,
            dst_ref=target,
            send_sem=self.send_sem.at[step, three],
            recv_sem=self.recv_sem.at[step, three],
            device_id=device,
            device_id_type=MESH,
        )

    def product(self, number, side):
        x_first, x_count, g_first = self.entry[:3]
        left = self.exchange.x_all[:, side, x_first + lax.rem(number, x_count)]
        columns = pl.ds(pl.multiple_of((g_first + number // x_count) * COLS, COLS), COLS)
        return jnp.dot(
            left.reshape(left.shape[0] * left.shape[1], left.shape[2]),
            self.exchange.g_all[:, columns],
            preferred_element_type=jnp.float32,
        )

    def first(self, number):
        value = self.product(number, 1 - self.exchange.value[0]).astype(jnp.bfloat16)
        self.send[...] = value.reshape(self.send.shape)
        self.copy(0, number).start()

    def second(self, number):
        self.copy(0, number).wait()
        mine = self.product(number, self.exchange.value[0])
        other = self.received[lax.rem(number, 2)].astype(jnp.float32)
        total = mine + other.reshape(mine.shape)
        self.halves[...] = total.astype(jnp.bfloat16).reshape(self.halves.shape)
        self.copy(1, number).start()

    def by_order(self, number, run):
        for order in range(2):
            pl.when(lax.rem(number, 2) == order)(functools.partial(run, order))

    def third(self, number):
        self.copy(1, number).wait()
        total = self.halves[:, self.bit].astype(jnp.float32)
        total = total + self.half_in[lax.rem(number, 2)].astype(jnp.float32)
        total = total.astype(jnp.bfloat16)

        def go(order):
            target = self.held[order][0]
            target[...] = total.reshape(target.shape)
            self.copy(2, number, order).start()

        self.by_order(number, go)

    def summed(self, number, order, step):
        bit = self.exchange.kinds[order][step][0]
        mine = self.held[order][step][:, self.exchange.value[bit]].astype(jnp.float32)
        other = self.held_in[order][step][lax.rem(number // 2, 2)].astype(jnp.float32)
        return (mine + other).astype(jnp.bfloat16)

    def fourth(self, number):
        def go(order):
            self.copy(2, number, order).wait()
            target = self.held[order][1]
            target[...] = self.summed(number, order, 0).reshape(target.shape)
            self.copy(3, number, order).start()

        self.by_order(number, go)

    def fifth(self, number):
        def go(order):
            self.copy(3, number, order).wait()
            self.own[...] = self.summed(number, order, 1).reshape(self.own.shape)

        self.by_order(number, go)
        self.copy(4, number).start()

    def sixth(self, number):
        self.copy(4, number).wait()
        three = lax.rem(number, 3)
        total = self.own[...].astype(jnp.float32) + self.cross[three].astype(jnp.float32)
        self.total[three, self.bit] = total.astype(jnp.bfloat16)
        self.copy(5, number).start()

    def out_copies(self, number):
        x_count, rows = self.entry[1], self.own.shape[0]
        three = lax.rem(number, 3)
        columns = pl.ds(pl.multiple_of(number // x_count * COLS, COLS), COLS)
        copies = []
        for half in range(2):
            at = pl.multiple_of((2 * lax.rem(number, x_count) + half) * rows, rows)
            copies.append(
                pltpu.make_async_copy(
                    self.total.at[three, half],
                    self.out.at[pl.ds(at, rows), columns],
                    self.out_sem.at[half, three],
                )
            )
        return copies

    def seventh(self, number):
        self.copy(5, number).wait()
        for copy in self.out_copies(number):
            copy.start()

    def finish(self, number):
        for copy in self.out_copies(number):
            copy.wait()


def reduce_kernel(entries, row_count, shards, *refs):
    count = len(entries)
    xs, gs, outs = refs[:count], refs[count : 2 * count], refs[2 * count : 3 * count]
    load_x, load_g, *scratch = refs[3 * count :]
    exchange = Exchange(entries, row_count, shards, outs, scratch)
    copies = []
    for at, (x_first, x_count, g_first, g_count, _) in enumerate(entries):
        x_part = exchange.x_all.at[:, :, pl.ds(x_first, x_count)]
        g_part = exchange.g_all.at[:, pl.ds(g_first * COLS, g_count * COLS)]
        copies.append(pltpu.make_async_copy(xs[at], x_part, load_x.at[at]))
        copies.append(pltpu.make_async_copy(gs[at], g_part, load_g.at[at]))
    for copy in copies:
        copy.start()
    exchange.meet()
    for copy in copies:
        copy.wait()
    exchange.run(None)


def reduce_gradients(pairs, row_count, shards, collective_id):
    block_rows, tokens = pairs[0][0].shape[3:]
    entries, x_blocks, g_blocks, chunks = reduce_entries(
        [(x.shape[2], g.shape[1] // COLS) for x, g in pairs]
    )
    return pl.pallas_call(
        functools.partial(reduce_kernel, entries, row_count, shards),
        out_shape=[
            jax.ShapeDtypeStruct((x_count * block_rows, g_count * COLS), jnp.bfloat16)
            for _, x_count, _, g_count, _ in entries
        ],
        in_specs=[pl.BlockSpec(memory_space=pl.ANY)] * (2 * len(pairs)),
        out_specs=[pl.BlockSpec(memory_space=pl.ANY)] * len(pairs),
        scratch_shapes=[
            pltpu.SemaphoreType.DMA((len(pairs),)),
            pltpu.SemaphoreType.DMA((len(pairs),)),
            *exchange_scratch(row_count, shards, block_rows, x_blocks, g_blocks, tokens),
        ],
        compiler_params=pltpu.CompilerParams(
            collective_id=collective_id, has_side_effects=True, vmem_limit_bytes=52 * 2**20
        ),
        cost_estimate=pl.CostEstimate(
            flops=2 * chunks * shards * block_rows * COLS * tokens,
            bytes_accessed=2 * chunks * block_rows * COLS,
            transcendentals=0,
        ),
    )(*[x for x, _ in pairs], *[g for _, g in pairs])


def body(
    tokens,
    lengths,
    mixer_gain,
    mixer_input,
    mixer_kernel,
    mixer_output,
    first_gain,
    first_gate,
    first_up,
    first_down,
    attend_gain,
    query_weight,
    key_weight,
    value_weight,
    query_gain,
    key_gain,
    attend_output,
    second_gain,
    second_gate,
    second_up,
    second_down,
    cotangent,
):
    length = tokens.shape[1]
    positions = lax.axis_index("seq") * length + jnp.arange(length, dtype=jnp.int32)
    segment, seg_start = segment_info(lengths, positions)
    offsets = positions[None, :] - seg_start
    hidden = tokens.astype(jnp.float32)
    hidden, mixer_back = mixer_block(
        hidden, mixer_gain, mixer_input, mixer_kernel, mixer_output, seg_start, positions
    )
    hidden, first_back = feed_block(hidden, first_gain, first_gate, first_up, first_down)
    hidden, attend_back = attend_block(
        hidden,
        lengths,
        attend_gain,
        query_weight,
        key_weight,
        value_weight,
        query_gain,
        key_gain,
        attend_output,
        segment,
        positions,
        offsets,
    )
    hidden, second_back = feed_block(hidden, second_gain, second_gate, second_up, second_down)
    gradient = cotangent.astype(jnp.float32)
    gradient, second_grads = second_back(gradient)
    gradient, attend_grads = attend_back(gradient)
    gradient, first_grads = first_back(gradient)
    gradient, mixer_grads = mixer_back(gradient)
    second_gain_sum, second_wide, second_down_pair = second_grads
    attend_gain_sum, attend_wide, query_gain_sum, key_gain_sum, attend_output_pair = attend_grads
    first_gain_sum, first_wide, first_down_pair = first_grads
    mixer_gain_sum, mixer_input_pair, mixer_kernel_sum, mixer_output_pair = mixer_grads
    row_count, shards = lax.axis_size("row"), lax.axis_size("seq")
    block_rows = math.gcd(tokens.shape[2] // shards, first_down.shape[0] // shards)

    def operands(pair):
        inputs, gradient_low = pair
        token_count = inputs.shape[0] * inputs.shape[1]
        inputs = inputs.reshape(token_count, -1).T
        blocks = inputs.shape[0] // shards // block_rows
        return (
            inputs.reshape(shards // 2, 2, blocks, block_rows, token_count),
            gradient_low.reshape(token_count, -1),
        )

    wide_vectors = jnp.concatenate(
        [
            mixer_kernel_sum,
            jnp.stack([mixer_gain_sum, first_gain_sum, attend_gain_sum, second_gain_sum]),
        ]
    )
    vector_count = wide_vectors.shape[0]
    vectors = jnp.concatenate(
        [
            part.reshape(-1, shards, part.shape[-1] // shards)
            .transpose(1, 0, 2)
            .reshape(shards, -1)
            for part in (wide_vectors, jnp.stack([query_gain_sum, key_gain_sum]))
        ],
        axis=1,
    )
    vector_rows = -(-vectors.shape[1] // COLS)
    token_count = tokens.shape[0] * tokens.shape[1]
    vectors = jnp.pad(vectors, ((0, 0), (0, vector_rows * COLS - vectors.shape[1])))
    vectors = vectors.reshape(shards * vector_rows, COLS).astype(jnp.bfloat16)
    vectors = jnp.pad(vectors, ((0, token_count - shards * vector_rows), (0, 0)))
    shard_at = lax.broadcasted_iota(jnp.int32, (shards, 2 * block_rows, token_count), 0)
    row_at = lax.broadcasted_iota(jnp.int32, (shards, 2 * block_rows, token_count), 1)
    token_at = lax.broadcasted_iota(jnp.int32, (shards, 2 * block_rows, token_count), 2)
    picks = (row_at < vector_rows) & (token_at == shard_at * vector_rows + row_at)
    picks = picks.astype(jnp.bfloat16).reshape(shards // 2, 2, 2, block_rows, token_count)
    (
        grad_second_down,
        second_both,
        grad_attend_output,
        attend_three,
        grad_first_down,
        first_both,
        grad_mixer_output,
        grad_mixer_input,
        vector_sums,
    ) = reduce_gradients(
        [
            operands(second_down_pair),
            operands(second_wide),
            operands(attend_output_pair),
            operands(attend_wide),
            operands(first_down_pair),
            operands(first_wide),
            operands(mixer_output_pair),
            operands(mixer_input_pair),
            (picks, vectors),
        ],
        row_count,
        shards,
        0,
    )

    def single(value):
        return value.astype(jnp.float32)

    hidden_columns = first_gate.shape[1]
    query_columns, key_columns = query_weight.shape[1], key_weight.shape[1]
    vector_sums = single(vector_sums[:vector_rows]).reshape(-1)
    width = tokens.shape[2] // shards
    wide_sums = vector_sums[: vector_count * width].reshape(vector_count, width)
    head_width = HEAD_DIM // shards
    head_sums = vector_sums[vector_count * width :][: 2 * head_width].reshape(2, head_width)
    return (
        hidden.astype(jnp.bfloat16),
        gradient.astype(jnp.bfloat16),
        wide_sums[3],
        single(grad_mixer_input),
        wide_sums[:3],
        single(grad_mixer_output),
        wide_sums[4],
        single(first_both[:, :hidden_columns]),
        single(first_both[:, hidden_columns:]),
        single(grad_first_down),
        wide_sums[5],
        single(attend_three[:, :query_columns]),
        single(attend_three[:, query_columns : query_columns + key_columns]),
        single(attend_three[:, query_columns + key_columns :]),
        head_sums[0],
        head_sums[1],
        single(grad_attend_output),
        wide_sums[6],
        single(second_both[:, :hidden_columns]),
        single(second_both[:, hidden_columns:]),
        single(grad_second_down),
    )


def finish_kernel(cuts, count, shards, *refs):
    passed, sums_in, refs = refs[:2], refs[2], refs[3:]
    ins, outs = refs[:count], refs[count : count + len(cuts)]
    refs = refs[count + len(cuts) :]
    passed_out, vectors, taps_out, heads, refs = refs[:2], refs[2:6], refs[6], refs[7:9], refs[9:]
    lows, fulls = refs[:count], refs[count : count + len(cuts)]
    held, sums, load_sem, save_sem, pass_sem = refs[count + len(cuts) :]
    moves = [
        pltpu.make_async_copy(source, held.at[number], pass_sem.at[number])
        for number, source in enumerate(passed)
    ]
    moves.append(pltpu.make_async_copy(sums_in, sums, pass_sem.at[2]))
    loads = [
        pltpu.make_async_copy(ins[number], lows[number], load_sem.at[number])
        for number in range(count)
    ]
    for load in loads + moves:
        load.start()
    saves, waited = [], set()
    for number, (source, first, columns) in enumerate(cuts):
        if source not in waited:
            loads[source].wait()
            waited.add(source)
        low, full = lows[source], fulls[number]
        rows = low.shape[0]
        piece = 64 if rows % 64 == 0 else rows

        def convert(at, carried):
            span = pl.ds(pl.multiple_of(at * 16, 16), 16)
            full[span] = low[span, pl.ds(first, columns)].astype(jnp.float32)
            return carried

        for start in range(0, rows, piece):
            lax.fori_loop(start // 16, (start + piece) // 16, convert, 0)
            span = pl.ds(start, piece)
            save = pltpu.make_async_copy(
                full.at[span], outs[number].at[span], save_sem.at[len(saves)]
            )
            save.start()
            saves.append(save)
    for move in moves:
        move.wait()
    for number, target in enumerate(passed_out):
        save = pltpu.make_async_copy(held.at[number], target, pass_sem.at[number])
        save.start()
        saves.append(save)
    seq = lax.axis_index("seq")
    share = vectors[0].shape[0]
    value = sums[pl.ds(0, 16)].astype(jnp.float32)
    chosen = jnp.zeros((16, share), jnp.float32)
    for place in range(COLS // share):
        here = lax.rem(seq, COLS // share) == place
        chosen = jnp.where(here, value[:, place * share : (place + 1) * share], chosen)
    for number, vector in enumerate(vectors):
        vector[...] = chosen[number : number + 1].reshape(share)
    taps_out[...] = chosen[4:7]
    lane = 2 * HEAD_DIM
    for number, head in enumerate(heads):
        line = value[0:8, number * lane : (number + 1) * lane]
        part = head.shape[0]
        chosen = jnp.zeros((1, part), jnp.float32)
        for place in range(shards):
            chosen = jnp.where(seq == place, line[7:8, place * part : (place + 1) * part], chosen)
        head[...] = chosen.reshape(part)
    for save in saves:
        save.wait()


def to_full(passed, sums, lows, cuts, shards):
    any_space = pl.BlockSpec(memory_space=pl.ANY)
    shapes = [(lows[source].shape[0], columns) for source, _, columns in cuts]
    pieces = sum(rows // 64 if rows % 64 == 0 else 1 for rows, _ in shapes)
    size = sum(low.size for low in lows)
    width = passed[0].shape[1]
    small = [(width // shards,)] * 4 + [(3, width // shards)] + [(HEAD_DIM // shards,)] * 2
    results = pl.pallas_call(
        functools.partial(finish_kernel, cuts, len(lows), shards),
        out_shape=[jax.ShapeDtypeStruct(shape, jnp.float32) for shape in shapes]
        + [jax.ShapeDtypeStruct(value.shape, value.dtype) for value in passed]
        + [jax.ShapeDtypeStruct(shape, jnp.float32) for shape in small],
        in_specs=[any_space] * (3 + len(lows)),
        out_specs=[any_space] * (len(cuts) + 2)
        + [pl.BlockSpec(memory_space=pltpu.VMEM)] * len(small),
        scratch_shapes=[
            *[pltpu.VMEM(low.shape, low.dtype) for low in lows],
            *[pltpu.VMEM(shape, jnp.float32) for shape in shapes],
            pltpu.VMEM((2,) + passed[0].shape, passed[0].dtype),
            pltpu.VMEM(sums.shape, sums.dtype),
            pltpu.SemaphoreType.DMA((len(lows),)),
            pltpu.SemaphoreType.DMA((pieces,)),
            pltpu.SemaphoreType.DMA((3,)),
        ],
        compiler_params=pltpu.CompilerParams(vmem_limit_bytes=62 * 2**20),
        cost_estimate=pl.CostEstimate(flops=size, bytes_accessed=6 * size, transcendentals=0),
    )(*passed, sums, *lows)
    cut_count = len(cuts)
    return results[:cut_count], results[cut_count : cut_count + 2], results[cut_count + 2 :]


def dot_nt(left, right):
    return lax.dot_general(
        left, right, (((1,), (1,)), ((), ())), preferred_element_type=jnp.float32
    )


def dot_tn(left, right):
    return lax.dot_general(
        left, right, (((0,), (0,)), ((), ())), preferred_element_type=jnp.float32
    )


def lanes_below(shape, bound, period):
    return lax.rem(lax.broadcasted_iota(jnp.int32, shape, len(shape) - 1), period) < bound


def two_heads(pair, low):
    pair = pair.astype(jnp.float32)
    turned = pltpu.roll(pair, HEAD_DIM, 1)
    first = lanes_below(pair.shape, HEAD_DIM, 2 * HEAD_DIM)
    if low:
        parts = [jnp.where(first, pair, 0.0), jnp.where(first, turned, 0.0)]
    else:
        parts = [jnp.where(first, 0.0, turned), jnp.where(first, 0.0, pair)]
    return jnp.concatenate(parts, axis=0).astype(jnp.bfloat16)


def single_row(lengths, total_length):
    return jnp.where(lengths[1, 0] == total_length, 1, 0)


def segment_start(lengths, which, place):
    end, start = jnp.int32(0), jnp.zeros(place.shape, jnp.int32)
    for number in range(lengths.shape[1]):
        end = end + lengths[which, number]
        start = jnp.where(place >= end, end, start)
    return start


def both_halves(value):
    value = jnp.broadcast_to(value, (8,) + value.shape[1:])
    return (value + pltpu.roll(value, HEAD_DIM, 1))[0:1]


def head_tools(lane):
    head_of = lax.broadcasted_iota(jnp.int32, (lane, lane), 0) // HEAD_DIM
    ones = head_of == lax.broadcasted_iota(jnp.int32, (lane, lane), 1) // HEAD_DIM
    ones = ones.astype(jnp.float32).astype(jnp.bfloat16)

    def head_mean(value):
        total = jnp.dot(value.astype(jnp.bfloat16), ones, preferred_element_type=jnp.float32)
        return total * (1.0 / HEAD_DIM)

    def turn(value):
        half = HEAD_DIM // 2
        first = lanes_below(value.shape, half, HEAD_DIM)
        return jnp.where(first, pltpu.roll(value, lane - half, 1), pltpu.roll(value, half, 1))

    return head_mean, turn


def forward_kernel(names, out_names, scratch_names, shards, *refs):
    at = types.SimpleNamespace(**dict(zip(names + out_names + scratch_names, refs)))
    row, seq = lax.axis_index("row"), lax.axis_index("seq")
    tokens, width = at.low_one.shape
    rows, total_length = at.both.shape[:2]
    length = tokens // rows
    lane = 2 * HEAD_DIM
    blocks = width // COLS
    hidden_blocks = at.first_gate.shape[1] // COLS
    bits = [lax.rem(seq // (1 << bit), 2) for bit in range(3)]
    partner = [seq + (1 << bit) * (1 - 2 * bits[bit]) for bit in range(3)]
    head_mean, turn = head_tools(lane)

    ahead = at.tiles_a.shape[0]

    def tile_copies(step, slot):
        name, j = step
        b, c = at.tiles_b.at[slot], at.tiles_c.at[slot]

        def columns(block):
            return pl.ds(block * COLS if isinstance(block, int) else pl.multiple_of(block * COLS, COLS), COLS)

        if name == MIXER_INPUT:
            first, second = ((0, 4), (1, 5), (2, 3))[j]
            moves = [
                (at.mixer_input.at[:, columns(first)], b),
                (at.mixer_input.at[:, columns(second)], c),
            ]
        elif name == KEYS:
            moves = [(at.key_weight, b), (at.value_weight, c)]
        elif name == FIRST:
            moves = [
                (at.first_gate.at[:, columns(j)], b),
                (at.first_up.at[:, columns(j)], c),
                (at.first_down.at[columns(j)], at.tiles_a.at[slot]),
            ]
        else:
            matrix = {
                MIXER_OUTPUT: at.mixer_output,
                QUERIES: at.query_weight,
                ATTEND_OUTPUT: at.attend_output,
            }[name]
            moves = [(matrix.at[:, columns(0)], b), (matrix.at[:, columns(1)], c)]
        return [
            pltpu.make_async_copy(source, target, at.tile_sem.at[slot, place])
            for place, (source, target) in enumerate(moves)
        ]

    steps = [(MIXER_INPUT, 0), (MIXER_INPUT, 1), (MIXER_INPUT, 2), (MIXER_OUTPUT, 0)]
    first_at = len(steps)
    steps += [(FIRST, j) for j in range(hidden_blocks)]
    steps += [(KEYS, 0), (QUERIES, 0), (ATTEND_OUTPUT, 0)]

    def begin(number):
        for copy in tile_copies(steps[number], number % ahead):
            copy.wait()
        later = number + ahead - 1
        if later < len(steps):
            for copy in tile_copies(steps[later], later % ahead):
                copy.start()
        return number % ahead

    saves = []

    streaming = [True]

    def save(source, target):
        copy = pltpu.make_async_copy(source, target, at.save_sem.at[len(saves)])
        if not streaming[0]:
            copy.start()
        saves.append(copy)

    def normed(hidden, number, target):
        for first in range(0, tokens, 64):
            span = pl.ds(first, 64)
            value = hidden[span]
            inverse = lax.rsqrt(jnp.mean(value * value, axis=-1, keepdims=True) + EPS)
            value = value * inverse * at.vectors[number : number + 1, :]
            target[span] = value.astype(jnp.bfloat16)

    def times(left, tile):
        return jnp.dot(left[...], tile, preferred_element_type=jnp.float32)

    token_load = pltpu.make_async_copy(at.tokens, at.attended, at.load_sem.at[0])
    token_load.start()
    for number in range(ahead - 1):
        for copy in tile_copies(steps[number], number):
            copy.start()
    at.halo_in[...] = jnp.zeros_like(at.halo_in)
    half_length = total_length // 2
    other_half = pl.multiple_of((1 - bits[2]) * half_length, half_length)
    at.both[1, pl.ds(other_half, half_length)] = jnp.zeros((half_length, width), jnp.bfloat16)
    barrier = pltpu.get_barrier_semaphore()
    others = partner + [lax.rem(seq + step, shards) for step in (1, shards - 1)]
    for other in others:
        pl.semaphore_signal(barrier, inc=1, device_id=(row, other), device_id_type=MESH)
    at.vectors[...] = jnp.zeros_like(at.vectors)
    gains = [at.second_gain, at.attend_gain, at.first_gain, at.mixer_gain]
    for number, gain in enumerate(gains):
        at.vectors[number : number + 1, :] = gain[...].astype(jnp.float32).reshape(1, width)
    at.vectors[4:7, :] = at.mixer_kernel[...].astype(jnp.float32)
    for number, gain in enumerate((at.query_gain, at.key_gain)):
        at.vectors[7 + number : 8 + number, 0:HEAD_DIM] = (
            gain[...].astype(jnp.float32).reshape(1, HEAD_DIM)
        )
    half = HEAD_DIM // 2
    lane_at = lax.broadcasted_iota(jnp.int32, (length, lane), 1)
    power = lax.rem(lane_at, half).astype(jnp.float32) * (-2.0 * math.log(THETA) / HEAD_DIM)
    inverse = jnp.exp(power)
    side = jnp.where(lanes_below((length, lane), half, HEAD_DIM), -1.0, 1.0)
    place = lax.broadcasted_iota(jnp.int32, (length, lane), 0) + seq * length
    for which in range(rows):
        start = segment_start(at.lengths, which, place)
        angle = (place - start).astype(jnp.float32) * inverse
        span = pl.ds(which * length, length)
        at.seg_start[span] = start
        at.cosine[span] = jnp.cos(angle)
        at.sine[span] = jnp.sin(angle) * side
    save(at.vectors, at.vectors_out)
    save(at.cosine, at.cosine_out)
    save(at.sine, at.sine_out)
    token_load.wait()
    at.hidden_a[...] = at.attended[...].astype(jnp.float32)
    save(at.hidden_a, at.hidden_zero)
    normed(at.hidden_a, 3, at.low_one)
    pl.semaphore_wait(barrier, len(others))

    for number, (first, second) in enumerate(((0, 4), (1, 5))):
        slot = begin(number)
        entry = times(at.low_one, at.tiles_b[slot])
        carrier = times(at.low_one, at.tiles_c[slot])
        columns = pl.ds(number * COLS, COLS)
        product = (entry * carrier).astype(jnp.bfloat16)
        at.mixed_low[pl.ds(3 * tokens, tokens), columns] = product
        product = product.astype(jnp.float32)
        at.gates_low[pl.ds(0, tokens), columns] = entry.astype(jnp.bfloat16)
        at.gates_low[pl.ds(2 * tokens, tokens), columns] = carrier.astype(jnp.bfloat16)
        for which in range(rows):
            last = product[(which + 1) * length - 8 : (which + 1) * length]
            at.halo_out[which, :, columns] = last
    halo = pltpu.make_async_remote_copy(
        src_ref=at.halo_out,
        dst_ref=at.halo_in,
        send_sem=at.halo_sem.at[0],
        recv_sem=at.halo_sem.at[1],
        device_id=(row, jnp.minimum(seq + 1, shards - 1)),
        device_id_type=MESH,
    )

    @pl.when(seq < shards - 1)
    def _():
        halo.start()

    slot = begin(2)
    for block, tile in enumerate((at.tiles_b, at.tiles_c)):
        at.work[:, pl.ds(block * COLS, COLS)] = times(at.low_one, tile[slot])

    @pl.when(seq > 0)
    def _():
        halo.wait_recv()

    @pl.when(seq < shards - 1)
    def _():
        halo.wait_send()

    position = lax.rem(lax.broadcasted_iota(jnp.int32, (tokens, lane), 0), length) + seq * length
    keep_one = position - 1 >= at.seg_start[...]
    keep_two = position - 2 >= at.seg_start[...]
    edge = lax.broadcasted_iota(jnp.int32, (8, lane), 0)
    for part_at in range(0, width, lane):
        columns = pl.ds(part_at, lane)
        current = at.mixed_low[pl.ds(3 * tokens, tokens), columns].astype(jnp.float32)
        shifted = []
        for steps_back, keep in ((1, keep_one), (2, keep_two)):
            back = pltpu.roll(current, steps_back, 0)
            pieces = []
            for which in range(rows):
                before = pltpu.roll(at.halo_in[which, :, columns], steps_back, 0)
                start = which * length
                pieces.append(jnp.where(edge < steps_back, before, back[start : start + 8]))
                pieces.append(back[start + 8 : start + length])
            back = jnp.concatenate(pieces, axis=0)
            shifted.append(jnp.where(keep, back, 0.0))
        one, two = shifted
        convolved = at.vectors[6:7, columns] * current + at.vectors[5:6, columns] * one
        convolved += at.vectors[4:5, columns] * two
        exit_gate = at.work[:, columns]
        at.mixed_low[pl.ds(0, tokens), columns] = convolved.astype(jnp.bfloat16)
        at.mixed_low[pl.ds(tokens, tokens), columns] = two.astype(jnp.bfloat16)
        at.mixed_low[pl.ds(2 * tokens, tokens), columns] = one.astype(jnp.bfloat16)
        at.gates_low[pl.ds(tokens, tokens), columns] = exit_gate.astype(jnp.bfloat16)
        at.low_two[:, columns] = (exit_gate * convolved).astype(jnp.bfloat16)
    save(at.mixed_low, at.mixer_saved)
    save(at.gates_low, at.projected)

    def add_output(number, left, before, after):
        slot = begin(number)
        for block, tile in enumerate((at.tiles_b, at.tiles_c)):
            columns = pl.ds(block * COLS, COLS)
            after[:, columns] = before[:, columns] + times(left, tile[slot])

    add_output(3, at.low_two, at.hidden_a, at.hidden_b)
    save(at.hidden_b, at.hidden_one)
    normed(at.hidden_b, 2, at.low_three)
    at.hidden_c[...] = at.hidden_b[...]

    def feed_tile(j, carried):
        slot = lax.rem(first_at + j, ahead)
        for copy in tile_copies((FIRST, j), slot):
            copy.wait()
        later = j + ahead - 1
        later_slot = lax.rem(first_at + later, ahead)

        @pl.when(later < hidden_blocks)
        def _():
            for copy in tile_copies((FIRST, later), later_slot):
                copy.start()

        for past, step in enumerate(steps[first_at + hidden_blocks :][: ahead - 1]):

            @pl.when(later == hidden_blocks + past)
            def _():
                for copy in tile_copies(step, later_slot):
                    copy.start()

        gate_value = times(at.low_three, at.tiles_b[slot])
        up_value = times(at.low_three, at.tiles_c[slot])
        columns = pl.ds(pl.multiple_of(j * COLS, COLS), COLS)
        at.gate_low[:, columns] = gate_value.astype(jnp.bfloat16)
        at.up_low[:, columns] = up_value.astype(jnp.bfloat16)
        active = gate_value / (1.0 + jnp.exp(-gate_value)) * up_value
        active = active.astype(jnp.bfloat16)
        at.active_low[:, columns] = active
        at.hidden_c[...] += jnp.dot(
            active, at.tiles_a[slot], preferred_element_type=jnp.float32
        )
        return carried

    lax.fori_loop(0, hidden_blocks, feed_tile, 0)
    save(at.hidden_c, at.hidden_two)
    save(at.gate_low, at.gate_one)
    save(at.up_low, at.up_one)
    normed(at.hidden_c, 1, at.low_four)

    def head_path(raw, gain):
        value = raw * lax.rsqrt(head_mean(raw * raw) + EPS) * gain
        return value * at.cosine[...] + turn(value) * at.sine[...]

    keys_at = first_at + hidden_blocks
    slot = begin(keys_at)
    at.work[:, pl.ds(0, width // 2)] = times(at.low_four, at.tiles_b[slot])
    at.work[:, pl.ds(width // 2, width // 2)] = times(at.low_four, at.tiles_c[slot])
    at.keys_low[...] = at.work[:, pl.ds(0, width // 2)].astype(jnp.bfloat16)
    save(at.keys_low, at.keys_raw)
    first = lanes_below((tokens, lane), HEAD_DIM, lane)
    own = pl.ds(pl.multiple_of(seq * length, length), length)
    for pair in range(width // lane // 2):
        keys = head_path(at.work[:, pl.ds(pair * lane, lane)], both_halves(at.vectors[8:9, pl.ds(0, lane)]))
        values = at.work[:, pl.ds(width // 2 + pair * lane, lane)]
        even = jnp.where(first, keys, pltpu.roll(values, HEAD_DIM, 1)).astype(jnp.bfloat16)
        odd = jnp.where(first, pltpu.roll(keys, HEAD_DIM, 1), values).astype(jnp.bfloat16)
        for which, value in enumerate((even, odd)):
            columns = pl.ds((2 * pair + which) * lane, lane)
            at.own_both[:, :, columns] = value.reshape(rows, length, lane)

    single = single_row(at.lengths, total_length)
    row_of = (single, 1 - single)
    for place in range(rows):
        at.both[place, own] = at.own_both[row_of[place]]

    def piece(owner, place):
        span = pl.ds(pl.multiple_of(owner * length, length), length)
        return at.both.at[place, span] if place is not None else at.both.at[:, span]

    def send(number, part, bit):
        return pltpu.make_async_remote_copy(
            src_ref=part,
            dst_ref=part,
            send_sem=at.gather_send.at[number],
            recv_sem=at.gather_recv.at[number],
            device_id=(row, partner[bit]),
            device_id_type=MESH,
        )

    across, along = partner[1], partner[2]
    corner = along + 2 * (1 - 2 * bits[1])
    near, far = send(0, piece(seq, 0), 1), send(1, piece(seq, 0), 2)
    near_short, twin = send(2, piece(seq, 1), 1), send(3, piece(seq, None), 0)
    for copy in (near, far, near_short, twin):
        copy.start()
    streaming[0] = False
    for copy in saves:
        copy.start()

    slot = begin(keys_at + 1)
    for block, tile in enumerate((at.tiles_b, at.tiles_c)):
        at.work[:, pl.ds(block * COLS, COLS)] = times(at.low_four, tile[slot])
    at.queries_low[...] = at.work[...].astype(jnp.bfloat16)
    save(at.queries_low, at.queries_raw)
    for head in range(width // lane):
        columns = pl.ds(head * lane, lane)
        query = head_path(at.work[:, columns], both_halves(at.vectors[7:8, pl.ds(0, lane)])).astype(jnp.bfloat16)
        query = query * jnp.bfloat16(HEAD_DIM**-0.5)
        at.scaled[:, columns] = query
        for which in range(rows):
            at.paired[which * (width // lane) + head] = two_heads(
                query[which * length : (which + 1) * length], True
            )
    save(at.scaled, at.queries_out)

    def transposed(low, target):
        for first in range(0, tokens, lane):
            span = pl.ds(first, lane)
            value = low[span].astype(jnp.float32).T.astype(jnp.bfloat16)
            target[:, :, :, :, span] = value.reshape(target.shape[:-1] + (lane,))

    transposed(at.low_one, at.turned_one)
    save(at.turned_one, at.mixer_in_x)
    near.wait()
    forward_copy, near_share = send(4, piece(across, 0), 2), send(5, piece(across, 0), 0)
    forward_copy.start()
    near_share.start()
    far.wait()
    far_share = send(6, piece(along, 0), 0)
    far_share.start()
    transposed(at.low_two, at.turned_two)
    save(at.turned_two, at.gated_x)

    at.sums[...] = jnp.zeros_like(at.sums)
    pairs_of = width // lane
    together = 4
    chip = seq // 2

    def attend(other, places):
        @pl.when(other <= chip)
        def _():
            span = pl.ds(pl.multiple_of(other * 2 * length, 2 * length), 2 * length)
            shape = (length, 2 * length)
            key_at = lax.broadcasted_iota(jnp.int32, shape, 1) + other * 2 * length
            query_at = lax.broadcasted_iota(jnp.int32, shape, 0) + seq * length
            first = lanes_below((2 * length, lane), HEAD_DIM, lane)
            for which in places:
                start = segment_start(at.lengths, row_of[which], query_at)
                allowed = jnp.logical_and(key_at >= start, key_at <= query_at)
                allowed = jnp.concatenate([allowed, allowed], axis=0)

                def some(group, carried):
                    heads = [group * together + head for head in range(together)]
                    boths = [
                        at.both[which, span, pl.ds(pl.multiple_of(head * lane, lane), lane)]
                        for head in heads
                    ]
                    spots = [which * pairs_of + head for head in heads]
                    scores = [
                        dot_nt(at.paired[row_of[which] * pairs_of + head], both)
                        for head, both in zip(heads, boths)
                    ]
                    for place, score, both in zip(spots, scores, boths):
                        weights = jnp.where(allowed, jnp.exp(score), 0.0).astype(jnp.bfloat16)
                        right = jnp.where(first, 1.0, both.astype(jnp.float32))
                        at.sums[place] += jnp.dot(
                            weights, right.astype(jnp.bfloat16), preferred_element_type=jnp.float32
                        )
                    return carried

                lax.fori_loop(0, pairs_of // together, some, 0)

    twin.wait()
    attend(chip, (0, 1))
    near_share.wait()
    attend(across // 2, (0,))
    far_share.wait()
    attend(along // 2, (0,))
    near_short.wait()
    short_share = send(7, piece(across, 1), 0)
    short_share.start()
    forward_copy.wait()
    corner_share = send(8, piece(corner, 0), 0)
    corner_share.start()
    transposed(at.low_three, at.turned_three)
    save(at.turned_three, at.first_in_x)
    short_share.wait()
    attend(across // 2, (1,))
    corner_share.wait()
    save(at.both, at.keys_values)
    attend(corner // 2, (0,))
    transposed(at.low_four, at.turned_four)
    save(at.turned_four, at.attend_in_x)

    block_rows = at.turned_active.shape[3]
    x_count = at.turned_active.shape[2]
    for j in range(hidden_blocks):
        for first in range(0, tokens, lane):
            span = pl.ds(first, lane)
            value = at.active_low[span, pl.ds(j * COLS, COLS)].astype(jnp.float32).T
            value = value.astype(jnp.bfloat16)
            for block in range(COLS // block_rows):
                place = j * (COLS // block_rows) + block
                shard = place // x_count
                at.turned_active[shard // 2, shard % 2, place % x_count, :, span] = value[
                    block * block_rows : (block + 1) * block_rows
                ]
    save(at.turned_active, at.active_x)
    first = lanes_below((length, lane), HEAD_DIM, lane)
    for which in range(rows):
        span = pl.ds(which * length, length)
        for head in range(pairs_of):
            place = jnp.where(single == which, 0, 1)
            value = at.sums[place * pairs_of + head]
            value = value * (1.0 / pltpu.roll(value, HEAD_DIM, 1))
            value = jnp.where(first, pltpu.roll(value[:length], HEAD_DIM, 1), value[length:])
            at.attended[span, pl.ds(head * lane, lane)] = value.astype(jnp.bfloat16)
    add_output(keys_at + 2, at.attended, at.hidden_c, at.hidden_d)
    save(at.hidden_d, at.hidden_three)
    transposed(at.attended, at.turned_five)
    save(at.turned_five, at.attended_x)
    for copy in saves:
        copy.wait()


def forward(arrays, resident, rows, shards, collective_id):
    tokens, width = arrays["tokens"].shape
    hidden_columns = arrays["first_gate"].shape[1]
    length = tokens // rows
    total_length = length * shards
    block_rows = math.gcd(width // shards, hidden_columns // shards)
    low, full = jnp.bfloat16, jnp.float32

    def x_shape(columns):
        return (shards // 2, 2, columns // shards // block_rows, block_rows, tokens)

    outs = dict(
        hidden_zero=((tokens, width), full),
        hidden_one=((tokens, width), full),
        hidden_two=((tokens, width), full),
        hidden_three=((tokens, width), full),
        gate_one=((tokens, hidden_columns), low),
        up_one=((tokens, hidden_columns), low),
        queries_out=((tokens, width), low),
        queries_raw=((tokens, width), low),
        keys_raw=((tokens, width // 2), low),
        keys_values=((rows, total_length, width), low),
        mixer_saved=((4 * tokens, width), low),
        projected=((3 * tokens, width), low),
        mixer_in_x=(x_shape(width), low),
        gated_x=(x_shape(width), low),
        first_in_x=(x_shape(width), low),
        attend_in_x=(x_shape(width), low),
        attended_x=(x_shape(width), low),
        active_x=(x_shape(hidden_columns), low),
        vectors_out=((16, width), full),
        cosine_out=((tokens, 2 * HEAD_DIM), full),
        sine_out=((tokens, 2 * HEAD_DIM), full),
    )
    pairs = rows * width // (2 * HEAD_DIM)
    dma = pltpu.SemaphoreType.DMA
    scratch = dict(
        tiles_a=pltpu.VMEM((4, COLS, width), low),
        tiles_b=pltpu.VMEM((4, width, COLS), low),
        tiles_c=pltpu.VMEM((4, width, COLS), low),
        hidden_a=pltpu.VMEM((tokens, width), full),
        hidden_b=pltpu.VMEM((tokens, width), full),
        hidden_c=pltpu.VMEM((tokens, width), full),
        hidden_d=pltpu.VMEM((tokens, width), full),
        low_one=pltpu.VMEM((tokens, width), low),
        low_two=pltpu.VMEM((tokens, width), low),
        low_three=pltpu.VMEM((tokens, width), low),
        low_four=pltpu.VMEM((tokens, width), low),
        attended=pltpu.VMEM((tokens, width), low),
        work=pltpu.VMEM((tokens, width), full),
        mixed_low=pltpu.VMEM((4 * tokens, width), low),
        gates_low=pltpu.VMEM((3 * tokens, width), low),
        gate_low=pltpu.VMEM((tokens, hidden_columns), low),
        up_low=pltpu.VMEM((tokens, hidden_columns), low),
        active_low=pltpu.VMEM((tokens, hidden_columns), low),
        keys_low=pltpu.VMEM((tokens, width // 2), low),
        queries_low=pltpu.VMEM((tokens, width), low),
        scaled=pltpu.VMEM((tokens, width), low),
        both=pltpu.VMEM((rows, total_length, width), low),
        own_both=pltpu.VMEM((rows, length, width), low),
        paired=pltpu.VMEM((pairs, 2 * length, 2 * HEAD_DIM), low),
        sums=pltpu.VMEM((pairs, 2 * length, 2 * HEAD_DIM), full),
        turned_one=pltpu.VMEM(x_shape(width), low),
        turned_two=pltpu.VMEM(x_shape(width), low),
        turned_three=pltpu.VMEM(x_shape(width), low),
        turned_four=pltpu.VMEM(x_shape(width), low),
        turned_five=pltpu.VMEM(x_shape(width), low),
        turned_active=pltpu.VMEM(x_shape(hidden_columns), low),
        vectors=pltpu.VMEM((16, width), full),
        cosine=pltpu.VMEM((tokens, 2 * HEAD_DIM), full),
        sine=pltpu.VMEM((tokens, 2 * HEAD_DIM), full),
        seg_start=pltpu.VMEM((tokens, 2 * HEAD_DIM), jnp.int32),
        halo_out=pltpu.VMEM((rows, 8, width), full),
        halo_in=pltpu.VMEM((rows, 8, width), full),
        tile_sem=dma((4, 3)),
        load_sem=dma((1,)),
        save_sem=dma((len(outs),)),
        halo_sem=dma((2,)),
        gather_send=dma((10,)),
        gather_recv=dma((10,)),
    )
    spaces = dict.fromkeys(resident, pltpu.VMEM)
    spaces["lengths"] = pltpu.SMEM
    any_space = pl.BlockSpec(memory_space=pl.ANY)
    weights = sum(value.size for value in arrays.values())
    results = pl.pallas_call(
        functools.partial(forward_kernel, list(arrays), list(outs), list(scratch), shards),
        out_shape=[jax.ShapeDtypeStruct(shape, kind) for shape, kind in outs.values()],
        in_specs=[pl.BlockSpec(memory_space=spaces.get(name, pl.ANY)) for name in arrays],
        out_specs=[any_space] * len(outs),
        scratch_shapes=list(scratch.values()),
        compiler_params=pltpu.CompilerParams(
            collective_id=collective_id, has_side_effects=True, vmem_limit_bytes=60 * 2**20
        ),
        cost_estimate=pl.CostEstimate(
            flops=2 * weights * tokens, bytes_accessed=2 * weights, transcendentals=0
        ),
    )(*arrays.values())
    return dict(zip(outs, results))


SECOND, ATTEND_OUTPUT, ATTENTION, QUERIES, KEYS, FIRST, MIXER_OUTPUT, HALO, MIXER_INPUT, CLOSE = range(10)
BACKWARD_STARTS = {
    SECOND: 0,
    ATTEND_OUTPUT: 8,
    ATTENTION: 10,
    QUERIES: 18,
    KEYS: 23,
    FIRST: 24,
    MIXER_OUTPUT: 33,
    HALO: 35,
    MIXER_INPUT: 36,
    CLOSE: 39,
}
FOLDED = 1
LOCAL_PAIRS = (14, 15, 18, 19)


def backward_kernel(names, entries, row_count, shards, *refs):
    at = types.SimpleNamespace(**dict(zip(names, refs)))
    outs = refs[len(names) : len(names) + len(entries)]
    token_out, mixed_out = refs[len(names) + len(entries) : len(names) + len(entries) + 2]
    scratch = refs[len(names) + len(entries) + 2 :]
    (
        tiles_a,
        tiles_b,
        tiles_c,
        saved,
        keys_values,
        key_grads,
        key_sums,
        queries,
        attended_grad,
        wide,
        queries_raw,
        keys_raw,
        gradient,
        normed_grad,
        hidden,
        halo_out,
        halo_in,
        small,
        tile_sem,
        load_sem,
        halo_sem,
        *scratch,
    ) = scratch
    local = types.SimpleNamespace()
    plain, chunk = [], 0
    for number, entry in enumerate(entries):
        if number != FOLDED:
            plain.append(entry[:4] + (chunk,))
            chunk += entry[1] * entry[3]
    plain_outs = [out for number, out in enumerate(outs) if number != FOLDED]
    fold_count = len(fold_scratch(shards, 2))
    fold_refs, scratch = scratch[:fold_count], scratch[fold_count:]
    exchange = Exchange(plain, row_count, shards, plain_outs, scratch, LOCAL_PAIRS, local)
    exchange.last_rows = 16
    exchange.fold = Fold(exchange, entries[FOLDED], outs[FOLDED], fold_refs)
    x_all, g_all = exchange.x_all, exchange.g_all
    seq, row = exchange.seq, exchange.row
    tokens, width = gradient.shape
    rows = keys_values.shape[0]
    length = tokens // rows
    hidden_blocks = at.first_gate.shape[1] // COLS
    blocks = width // COLS
    g_at = [entry[2] * COLS for entry in entries]
    second_wide, second_down, output_at, heads_at, first_down, first_wide = g_at[:6]
    mixer_out_at, mixer_in_at, small_at = g_at[6:]
    starts = BACKWARD_STARTS

    def local_place(kind, index):
        first, second, third, fourth = LOCAL_PAIRS
        row_at = jnp.where(index >= third, 1, 0)
        quad = jnp.where(jnp.logical_or(index == second, index == fourth), 1, 0)
        return row_at, pl.ds(pl.multiple_of(quad * COLS, COLS), COLS)

    def part(kind, index, side):
        row_at, columns = local_place(kind, index)
        return key_grads[row_at, :, side, kind, :, columns]

    def take(kind, index, total):
        row_at, columns = local_place(kind, index)
        key_sums[row_at, kind, :, columns] = total.astype(jnp.bfloat16)

    local.part, local.take = part, take

    def tile_copies(name, j, slot):
        columns = pl.ds(pl.multiple_of(j * COLS, COLS), COLS)
        a, b, c = tiles_a.at[slot], tiles_b.at[slot], tiles_c.at[slot]
        if name == SECOND:
            moves = [
                (at.second_gate.at[:, columns], b),
                (at.second_up.at[:, columns], c),
                (at.second_down.at[columns], a),
            ]
        elif name == FIRST:
            moves = [
                (at.first_down.at[columns], a),
                (at.first_gate.at[:, columns], b),
                (at.first_up.at[:, columns], c),
                (at.gate_one.at[:, columns], saved.at[slot, 0]),
                (at.up_one.at[:, columns], saved.at[slot, 1]),
            ]
        elif name == ATTEND_OUTPUT:
            moves = [(at.attend_output.at[columns], a)]
        elif name == MIXER_OUTPUT:
            moves = [(at.mixer_output.at[columns], a)]
        elif name == QUERIES:
            moves = [
                (at.query_weight.at[:, pl.ds(0, COLS)], b),
                (at.query_weight.at[:, pl.ds(COLS, COLS)], c),
            ]
        elif name == KEYS:
            moves = [(at.key_weight, b), (at.value_weight, c)]
        else:
            even = pl.multiple_of(2 * j * COLS, COLS)
            odd = pl.multiple_of((2 * j + 1) * COLS, COLS)
            moves = [
                (at.mixer_input.at[:, pl.ds(even, COLS)], b),
                (at.mixer_input.at[:, pl.ds(odd, COLS)], c),
            ]
        return [
            pltpu.make_async_copy(source, target, tile_sem.at[slot, place])
            for place, (source, target) in enumerate(moves)
        ]

    steps = [
        (SECOND, hidden_blocks),
        (ATTEND_OUTPUT, blocks),
        (QUERIES, 1),
        (KEYS, 1),
        (FIRST, hidden_blocks),
        (MIXER_OUTPUT, blocks),
        (MIXER_INPUT, 3 * blocks // 2),
    ]
    first_step, total = {}, 0
    for name, number in steps:
        first_step[name] = total
        total += number
    order = [name for name, _ in steps]
    numbers = dict(steps)

    def tile_step(name, j):
        slot = (first_step[name] + j) % 2 if isinstance(j, int) else lax.rem(first_step[name] + j, 2)
        for copy in tile_copies(name, j, slot):
            copy.wait()

        @pl.when(j + 1 < numbers[name])
        def _():
            for copy in tile_copies(name, j + 1, 1 - slot):
                copy.start()

        if name != order[-1]:
            following = order[order.index(name) + 1]

            @pl.when(j + 1 == numbers[name])
            def _():
                for copy in tile_copies(following, 0, 1 - slot):
                    copy.start()

        return slot

    def load(place, source, target):
        return pltpu.make_async_copy(source, target, load_sem.at[place])

    count = len(entries)
    x_loads = [
        load(number, at.xs[number - 2], x_all.at[:, :, pl.ds(x_first, x_count)])
        for number, (x_first, x_count, _, _, _) in enumerate(entries)
        if 2 <= number < count - 1
    ]
    cotangent_load = load(count, at.cotangent, g_all.at[:, pl.ds(second_down, width)])
    middle_loads = [
        load(count + 1, at.queries_out, queries),
        load(count + 2, at.keys_values, keys_values),
        load(count + 5, at.keys_raw, keys_raw),
    ]
    raw_load = load(count + 4, at.queries_raw, queries_raw)
    staged = queries_raw
    late_loads = [
        load(count + 6, at.mixer_saved, keys_values.at[0]),
        load(count + 7, at.projected, keys_values.at[1, pl.ds(0, 3 * tokens)]),
    ]
    hidden_loads = [
        load(count + 8, source, hidden)
        for source in (at.hidden_three, at.hidden_two, at.hidden_one, at.hidden_zero)
    ]
    out_copy = load(count + 9, staged, token_out)
    mixed_copy = load(count + 9, staged, mixed_out)

    hidden_loads[0].start()
    cotangent_load.start()
    for copy in tile_copies(SECOND, 0, 0):
        copy.start()
    for copy in middle_loads + x_loads:
        copy.start()
    normed_grad[...] = jnp.zeros_like(normed_grad)
    small[...] = jnp.zeros_like(small)
    g_all[:, pl.ds(small_at, COLS)] = jnp.zeros((tokens, COLS), jnp.bfloat16)
    wide[...] = jnp.zeros_like(wide)
    hidden_loads[0].wait()
    normed = attended_grad
    x_two = entries[0][0]
    for first in range(0, tokens, 128):
        span = pl.ds(first, 128)
        value = hidden[span]
        inverse = lax.rsqrt(jnp.mean(value * value, axis=-1, keepdims=True) + EPS)
        value = value * inverse * at.vectors[0:1, :]
        normed[span] = value.astype(jnp.bfloat16)
        turned = value.T.astype(jnp.bfloat16)
        shape = x_all.shape[:2] + (2,) + x_all.shape[3:4] + (128,)
        x_all[:, :, x_two : x_two + 2, :, pl.ds(first, 128)] = turned.reshape(shape)
    cotangent_load.wait()
    gradient[...] = g_all[:, pl.ds(second_down, width)].astype(jnp.float32)

    def low_gradient(place):
        g_all[:, pl.ds(place, width)] = gradient[...].astype(jnp.bfloat16)

    def norm_back(number):
        if number > 0:
            hidden_loads[number].wait()
        gain = at.vectors[number : number + 1, :]
        sums = jnp.zeros((1, width), jnp.float32)
        piece = 64
        for first in range(0, tokens, piece):
            span = pl.ds(first, piece)
            value, upper = hidden[span], normed_grad[span]
            inverse = lax.rsqrt(jnp.mean(value * value, axis=-1, keepdims=True) + EPS)
            value = value * inverse
            sums = sums + jnp.sum(upper * value, axis=0, keepdims=True)
            upper = upper * gain
            shift = jnp.mean(upper * value, axis=-1, keepdims=True)
            gradient[span] = gradient[span] + inverse * (upper - value * shift)
        for block in range(blocks):
            place = blocks * number + block
            small[place : place + 1, :] = sums[:, block * COLS : (block + 1) * COLS]
        normed_grad[...] = jnp.zeros_like(normed_grad)
        if number + 1 < len(hidden_loads):
            hidden_loads[number + 1].start()

    def feed_tile(name, j, gradient_at, wide_at):
        slot = tile_step(name, j)
        low = g_all[:, pl.ds(gradient_at, width)]
        active_grad = dot_nt(low, tiles_a[slot])
        if name == SECOND:
            gate_value = jnp.dot(normed[...], tiles_b[slot], preferred_element_type=jnp.float32)
            up_value = jnp.dot(normed[...], tiles_c[slot], preferred_element_type=jnp.float32)
        else:
            gate_value = saved[slot, 0].astype(jnp.float32)
            up_value = saved[slot, 1].astype(jnp.float32)
        share = 1.0 / (1.0 + jnp.exp(-gate_value))
        if name == SECOND:
            active = gate_value * share * up_value
            wide[...] += jnp.dot(
                active.astype(jnp.bfloat16), tiles_a[slot], preferred_element_type=jnp.float32
            )
            turned = active.T.astype(jnp.bfloat16)
            x_down, x_count = entries[1][:2]
            block_rows = x_all.shape[3]
            for block in range(COLS // block_rows):
                place = j * (COLS // block_rows) + block
                shard = place // x_count
                part = turned[block * block_rows : (block + 1) * block_rows]
                x_all[shard // 2, lax.rem(shard, 2), x_down + lax.rem(place, x_count)] = part
        up_grad = (active_grad * gate_value * share).astype(jnp.bfloat16)
        gate_grad = active_grad * up_value * share * (1.0 + gate_value * (1.0 - share))
        gate_grad = gate_grad.astype(jnp.bfloat16)
        gate_place = pl.multiple_of(wide_at + j * COLS, COLS)
        up_place = pl.multiple_of(wide_at + (hidden_blocks + j) * COLS, COLS)
        g_all[:, pl.ds(gate_place, COLS)] = gate_grad
        g_all[:, pl.ds(up_place, COLS)] = up_grad
        normed_grad[...] += dot_nt(gate_grad, tiles_b[slot]) + dot_nt(up_grad, tiles_c[slot])

    def output_tile(name, j, gradient_at, target):
        slot = tile_step(name, j)
        low = g_all[:, pl.ds(gradient_at, width)]
        value = dot_nt(low, tiles_a[slot])
        target[:, j * COLS : (j + 1) * COLS] = value.astype(target.dtype)

    def attention_head(row_at, head):
        span = pl.ds(pl.multiple_of(row_at * length, length), length)
        columns = pl.ds(pl.multiple_of(head * 2 * HEAD_DIM, 2 * HEAD_DIM), 2 * HEAD_DIM)
        query = two_heads(queries[span, columns], True)
        upper = two_heads(attended_grad[span, columns], False)
        place = jnp.where(single_row(at.lengths, keys_values.shape[1]) == row_at, 0, 1)
        both = keys_values[place, :, columns]
        key_at = lax.broadcasted_iota(jnp.int32, (both.shape[0], length), 0)
        query_at = lax.broadcasted_iota(jnp.int32, (both.shape[0], length), 1) + seq * length
        start = segment_start(at.lengths, row_at, query_at[0:8])[0:1]
        allowed = jnp.logical_and(key_at >= start, key_at <= query_at)
        weights = jnp.exp(dot_nt(both, query))
        weights = jnp.where(jnp.concatenate([allowed, allowed], axis=1), weights, 0.0)
        weights = weights * (1.0 / jnp.sum(weights, axis=0, keepdims=True))
        weight_grad_value = dot_nt(both, upper)
        delta = jnp.sum(weights * weight_grad_value, axis=0, keepdims=True)
        score_grad = (weights * (weight_grad_value - delta)).astype(jnp.bfloat16)
        both_grad = jnp.dot(score_grad, query, preferred_element_type=jnp.float32)
        both_grad += jnp.dot(
            weights.astype(jnp.bfloat16), upper, preferred_element_type=jnp.float32
        )
        shape = key_grads.shape[1:5] + (2 * HEAD_DIM,)
        key_grads[row_at, :, :, :, :, columns] = both_grad.astype(jnp.bfloat16).reshape(shape)
        query_grad = dot_tn(score_grad, both) * HEAD_DIM ** (-0.5)
        first = lanes_below((length, 2 * HEAD_DIM), HEAD_DIM, 2 * HEAD_DIM)
        wide[span, columns] = jnp.where(
            first, query_grad[:length], pltpu.roll(query_grad[length:], HEAD_DIM, 1)
        )

    lane = 2 * HEAD_DIM
    head_mean, turn = head_tools(lane)

    def head_back(value, raw, gain):
        value = value * at.cosine[...] - turn(value) * at.sine[...]
        raw = raw.astype(jnp.float32)
        inverse = lax.rsqrt(head_mean(raw * raw) + EPS)
        raw = raw * inverse
        sums = jnp.sum(value * raw, axis=0, keepdims=True)
        value = value * gain
        return inverse * (value - raw * head_mean(value * raw)), sums

    head_row = 7 * blocks

    def query_heads():
        sums = jnp.zeros((1, lane), jnp.float32)
        for part_at in range(0, width, lane):
            columns = pl.ds(part_at, lane)
            value, more = head_back(wide[:, columns], queries_raw[:, columns], both_halves(at.vectors[7:8, pl.ds(0, lane)]))
            g_all[:, pl.ds(heads_at + part_at, lane)] = value.astype(jnp.bfloat16)
            sums = sums + more
        small[head_row : head_row + 1, 0:lane] = both_halves(sums)

    def key_heads():
        sums = jnp.zeros((1, lane), jnp.float32)
        first = lanes_below((tokens, lane), HEAD_DIM, lane)
        for pair in range(width // lane // 2):
            even, odd = [
                key_sums[:, :, :, pl.ds((2 * pair + which) * lane, lane)]
                .astype(jnp.float32)
                .reshape(tokens, lane)
                for which in range(2)
            ]
            key_value = jnp.where(first, even, pltpu.roll(odd, HEAD_DIM, 1))
            value_value = jnp.where(first, pltpu.roll(even, HEAD_DIM, 1), odd)
            columns = pl.ds(pair * lane, lane)
            value, more = head_back(key_value, keys_raw[:, columns], both_halves(at.vectors[8:9, pl.ds(0, lane)]))
            place = heads_at + width + pair * lane
            g_all[:, pl.ds(place, lane)] = value.astype(jnp.bfloat16)
            place += width // 2
            g_all[:, pl.ds(place, lane)] = value_value.astype(jnp.bfloat16)
            sums = sums + more
        small[head_row : head_row + 1, lane : 2 * lane] = both_halves(sums)

    def project_back(name, j, even_at, odd_at):
        slot = tile_step(name, j)
        normed_grad[...] += dot_nt(g_all[:, pl.ds(even_at, COLS)], tiles_b[slot]) + dot_nt(
            g_all[:, pl.ds(odd_at, COLS)], tiles_c[slot]
        )

    def halo_copy():
        return pltpu.make_async_remote_copy(
            src_ref=halo_out,
            dst_ref=halo_in,
            send_sem=halo_sem.at[0],
            recv_sem=halo_sem.at[1],
            device_id=(row, jnp.maximum(seq - 1, 0)),
            device_id_type=MESH,
        )

    def saved_part(number, columns):
        return keys_values[0, pl.ds(number * tokens, tokens), columns].astype(jnp.float32)

    def projected_part(number, columns):
        return keys_values[1, pl.ds(number * tokens, tokens), columns].astype(jnp.float32)

    def convolution_back():
        within = lax.rem(lax.broadcasted_iota(jnp.int32, (tokens, lane), 0), length)
        position = within + seq * length
        start = [
            segment_start(at.lengths, which, position[which * length : (which + 1) * length])
            for which in range(rows)
        ]
        start = jnp.concatenate(start, axis=0)
        keep_one = position - 1 >= start
        keep_two = position - 2 >= start
        edge = lax.broadcasted_iota(jnp.int32, (8, lane), 0)
        for part_at in range(0, width, lane):
            columns = pl.ds(part_at, lane)
            gated_grad = wide[:, columns]
            exit_grad = gated_grad * saved_part(0, columns)
            place = mixer_in_at + width + part_at
            g_all[:, pl.ds(place, lane)] = exit_grad.astype(jnp.bfloat16)
            conv_grad = gated_grad * projected_part(1, columns)
            block, inside = part_at // COLS, part_at % COLS
            for tap in range(3):
                sums = jnp.sum(conv_grad * saved_part(1 + tap, columns), axis=0, keepdims=True)
                place = blocks * (4 + tap) + block
                small[place : place + 1, inside : inside + lane] = sums
            two = jnp.where(keep_two, at.vectors[4:5, columns] * conv_grad, 0.0)
            one = jnp.where(keep_one, at.vectors[5:6, columns] * conv_grad, 0.0)
            here = at.vectors[6:7, columns] * conv_grad
            here += jnp.where(within < length - 1, pltpu.roll(one, tokens - 1, 0), 0.0)
            here += jnp.where(within < length - 2, pltpu.roll(two, tokens - 2, 0), 0.0)
            normed_grad[:, columns] = here
            for which in range(rows):
                span = slice(which * length, which * length + 8)
                sent = two[span] + jnp.where(edge == 1, pltpu.roll(one[span], 1, 0), 0.0)
                halo_out[which, :, columns] = jnp.where(edge < 2, sent, 0.0)

        @pl.when(seq > 0)
        def _():
            halo_copy().start()

    def product_back():
        @pl.when(seq < shards - 1)
        def _():
            halo_copy().wait_recv()
            for which in range(rows):
                span = pl.ds((which + 1) * length - 8, 8)
                normed_grad[span] = normed_grad[span] + pltpu.roll(halo_in[which], 6, 0)

        @pl.when(seq > 0)
        def _():
            halo_copy().wait_send()

        for part_at in range(0, width, lane):
            columns = pl.ds(part_at, lane)
            product_grad = normed_grad[:, columns]
            entry_grad = product_grad * projected_part(2, columns)
            carrier_grad = product_grad * projected_part(0, columns)
            g_all[:, pl.ds(mixer_in_at + part_at, lane)] = entry_grad.astype(jnp.bfloat16)
            place = mixer_in_at + 2 * width + part_at
            g_all[:, pl.ds(place, lane)] = carrier_grad.astype(jnp.bfloat16)
        normed_grad[...] = jnp.zeros_like(normed_grad)

    def task(i):
        def when(name, run, after=0, number=1):
            j = i - (starts[name] + after)

            @pl.when(jnp.logical_and(j >= 0, j < number))
            def _():
                run(j)

        when(
            SECOND,
            lambda j: feed_tile(SECOND, j + 1, second_down, second_wide),
            0,
            hidden_blocks - 1,
        )

        def waits(j):
            for copy in middle_loads + x_loads:
                copy.wait()

        when(ATTEND_OUTPUT, waits)

        def to_attended(j):
            staged[...] = (hidden[...] + wide[...]).astype(jnp.bfloat16)
            mixed_copy.start()
            norm_back(0)
            low_gradient(output_at)
            output_tile(ATTEND_OUTPUT, 0, output_at, attended_grad)

        when(ATTEND_OUTPUT, to_attended)
        when(ATTEND_OUTPUT, lambda j: output_tile(ATTEND_OUTPUT, 1, output_at, attended_grad), 1)

        def staged_free(j):
            mixed_copy.wait()
            raw_load.start()

        when(ATTENTION, staged_free)

        def attention(j):
            pairs = KV_HEADS // 2
            for which in range(2):
                attention_head(j // pairs, 2 * lax.rem(j, pairs) + which)

        when(ATTENTION, attention, 0, rows * KV_HEADS // 2)

        def to_queries(j):
            raw_load.wait()
            for copy in late_loads:
                copy.start()
            query_heads()

        when(QUERIES, to_queries)
        def pick_rows(j):
            block_rows = x_all.shape[3]
            shape = (shards * 2 * block_rows, tokens)
            place = lax.broadcasted_iota(jnp.int32, shape, 0)
            vector, shard = lax.rem(place, 2 * block_rows), place // (2 * block_rows)
            wanted = blocks * vector + jnp.where(vector < 7, shard * blocks // shards, 0)
            found = lax.broadcasted_iota(jnp.int32, shape, 1) == wanted
            found = jnp.logical_and(found, vector < 8).astype(jnp.float32).astype(jnp.bfloat16)
            x_first = entries[-1][0]
            target = x_all.shape[:2] + (2, block_rows, tokens)
            x_all[:, :, x_first : x_first + 2] = found.reshape(target)

        when(QUERIES, pick_rows, 2)
        when(QUERIES, lambda j: project_back(QUERIES, 0, heads_at, heads_at + COLS), 1)

        def to_keys(j):
            key_heads()
            project_back(KEYS, 0, heads_at + width, heads_at + width + COLS)
            norm_back(1)
            low_gradient(first_down)

        when(KEYS, to_keys)
        when(FIRST, lambda j: feed_tile(FIRST, j, first_down, first_wide), 0, hidden_blocks)

        def to_gated(j):
            norm_back(2)
            low_gradient(mixer_out_at)
            output_tile(MIXER_OUTPUT, 0, mixer_out_at, wide)
            for copy in late_loads:
                copy.wait()

        when(MIXER_OUTPUT, to_gated)

        def to_convolved(j):
            output_tile(MIXER_OUTPUT, 1, mixer_out_at, wide)
            convolution_back()

        when(MIXER_OUTPUT, to_convolved, 1)
        when(HALO, lambda j: product_back())

        def mixer_tile(j):
            even = pl.multiple_of(mixer_in_at + 2 * j * COLS, COLS)
            project_back(MIXER_INPUT, j, even, pl.multiple_of(even + COLS, COLS))

        when(MIXER_INPUT, mixer_tile, 0, numbers[MIXER_INPUT])

        def close(j):
            norm_back(3)
            staged[...] = gradient[...].astype(jnp.bfloat16)
            out_copy.start()
            g_all[pl.ds(0, small.shape[0]), pl.ds(small_at, COLS)] = small[...].astype(jnp.bfloat16)

        when(CLOSE, close)
        when(CLOSE, lambda j: out_copy.wait(), 1)

    exchange.meet()
    feed_tile(SECOND, 0, second_down, second_wide)
    exchange.run(task)


def backward(groups, arrays, resident, row_count, shards, collective_id):
    xs = [x for x, _ in groups if not isinstance(x, int)]
    block_rows, tokens = xs[0].shape[3:]
    width = arrays["cotangent"].shape[1]
    entries, x_blocks, g_blocks, chunks = reduce_entries(
        [(x if isinstance(x, int) else x.shape[2], columns // COLS) for x, columns in groups]
    )
    names = ["xs_%d" % number for number in range(len(xs))] + list(arrays)
    values = list(xs) + list(arrays.values())
    rows, total_length = arrays["keys_values"].shape[:2]
    any_space = pl.BlockSpec(memory_space=pl.ANY)
    spaces = dict.fromkeys(resident, pltpu.VMEM)
    spaces["lengths"] = pltpu.SMEM
    key_blocks = total_length // shards // block_rows

    def kernel(*refs):
        xs_refs, others = refs[: len(xs)], refs[len(xs) : len(values)]
        named = [("xs", xs_refs)] + list(zip(arrays, others))
        backward_kernel(
            [name for name, _ in named],
            entries,
            row_count,
            shards,
            *[ref for _, ref in named],
            *refs[len(values) :],
        )

    low, full = jnp.bfloat16, jnp.float32
    return pl.pallas_call(
        kernel,
        out_shape=[
            jax.ShapeDtypeStruct((x_count * block_rows, g_count * COLS), low)
            for _, x_count, _, g_count, _ in entries
        ]
        + [jax.ShapeDtypeStruct((tokens, width), low)] * 2,
        in_specs=[pl.BlockSpec(memory_space=spaces.get(name, pl.ANY)) for name in names],
        out_specs=[any_space] * (len(entries) + 2),
        scratch_shapes=[
            pltpu.VMEM((2, COLS, width), low),
            pltpu.VMEM((2, width, COLS), low),
            pltpu.VMEM((2, width, COLS), low),
            pltpu.VMEM((2, 2, tokens, COLS), low),
            pltpu.VMEM((rows, total_length, width), low),
            pltpu.VMEM((rows, shards // 2, 2, key_blocks, block_rows, width), low),
            pltpu.VMEM((rows, key_blocks, block_rows, width), low),
            pltpu.VMEM((tokens, width), low),
            pltpu.VMEM((tokens, width), low),
            pltpu.VMEM((tokens, width), full),
            pltpu.VMEM((tokens, width), low),
            pltpu.VMEM((tokens, width // 2), low),
            pltpu.VMEM((tokens, width), full),
            pltpu.VMEM((tokens, width), full),
            pltpu.VMEM((tokens, width), full),
            pltpu.VMEM((rows, 8, width), full),
            pltpu.VMEM((rows, 8, width), full),
            pltpu.VMEM((16, COLS), full),
            pltpu.SemaphoreType.DMA((2, 5)),
            pltpu.SemaphoreType.DMA((len(entries) + 10,)),
            pltpu.SemaphoreType.DMA((2,)),
            *fold_scratch(shards, block_rows),
            *exchange_scratch(row_count, shards, block_rows, x_blocks, g_blocks, tokens),
        ],
        compiler_params=pltpu.CompilerParams(
            collective_id=collective_id, has_side_effects=True, vmem_limit_bytes=63 * 2**20
        ),
        cost_estimate=pl.CostEstimate(
            flops=4 * chunks * shards * block_rows * COLS * tokens,
            bytes_accessed=2 * chunks * shards * block_rows * COLS,
            transcendentals=0,
        ),
    )(*values)


def fused_body(
    tokens,
    lengths,
    mixer_gain,
    mixer_input,
    mixer_kernel,
    mixer_output,
    first_gain,
    first_gate,
    first_up,
    first_down,
    attend_gain,
    query_weight,
    key_weight,
    value_weight,
    query_gain,
    key_gain,
    attend_output,
    second_gain,
    second_gate,
    second_up,
    second_down,
    cotangent,
):
    full, low = jnp.float32, jnp.bfloat16
    rows, length, width = tokens.shape
    token_count = rows * length
    lane = 2 * HEAD_DIM
    row_count, shards = lax.axis_size("row"), lax.axis_size("seq")
    seq = lax.axis_index("seq")
    tables = dict(
        lengths=lengths,
        mixer_kernel=mixer_kernel,
        mixer_gain=mixer_gain,
        first_gain=first_gain,
        attend_gain=attend_gain,
        second_gain=second_gain,
        query_gain=query_gain,
        key_gain=key_gain,
    )
    arrays = dict(
        tokens=tokens.reshape(token_count, width),
        mixer_input=mixer_input,
        mixer_output=mixer_output,
        first_gate=first_gate,
        first_up=first_up,
        first_down=first_down,
        query_weight=query_weight,
        key_weight=key_weight,
        value_weight=value_weight,
        attend_output=attend_output,
        **tables,
    )
    saved = types.SimpleNamespace(**forward(arrays, tuple(tables), rows, shards, 2))
    block_rows = saved.attended_x.shape[3]
    weights = dict(
        second_down=second_down,
        second_gate=second_gate,
        second_up=second_up,
        attend_output=attend_output,
        query_weight=query_weight,
        key_weight=key_weight,
        value_weight=value_weight,
        first_down=first_down,
        first_gate=first_gate,
        first_up=first_up,
        mixer_output=mixer_output,
        mixer_input=mixer_input,
    )
    tables = dict(vectors=saved.vectors_out, cosine=saved.cosine_out, sine=saved.sine_out)
    arrays = dict(
        lengths=lengths,
        cotangent=cotangent.reshape(token_count, width),
        gate_one=saved.gate_one,
        up_one=saved.up_one,
        hidden_three=saved.hidden_three,
        hidden_two=saved.hidden_two,
        hidden_one=saved.hidden_one,
        hidden_zero=saved.hidden_zero,
        queries_out=saved.queries_out,
        keys_values=saved.keys_values,
        queries_raw=saved.queries_raw,
        keys_raw=saved.keys_raw,
        mixer_saved=saved.mixer_saved,
        projected=saved.projected,
        **tables,
        **weights,
    )
    hidden_columns = first_gate.shape[1]
    head_columns = width + 2 * key_weight.shape[1]
    groups = [
        (width // shards // block_rows, 2 * hidden_columns),
        (hidden_columns // shards // block_rows, width),
        (saved.attended_x, width),
        (saved.attend_in_x, head_columns),
        (saved.active_x, width),
        (saved.first_in_x, 2 * hidden_columns),
        (saved.gated_x, width),
        (saved.mixer_in_x, 3 * width),
        (2, COLS),
    ]
    (
        second_both,
        grad_second_down,
        grad_attend_output,
        attend_three,
        grad_first_down,
        first_both,
        grad_mixer_output,
        grad_mixer_input,
        sums,
        token_grad,
        mixed,
    ) = backward(groups, arrays, tuple(tables), row_count, shards, 1)

    key_columns = key_weight.shape[1]
    lows = [second_both, first_both, grad_second_down, grad_first_down]
    lows += [attend_three, grad_attend_output, grad_mixer_output, grad_mixer_input]
    fulls, (mixed, token_grad), small = to_full(
        (mixed, token_grad),
        sums,
        lows,
        (
            (0, 0, hidden_columns),
            (0, hidden_columns, hidden_columns),
            (1, 0, hidden_columns),
            (1, hidden_columns, hidden_columns),
            (2, 0, width),
            (3, 0, width),
            (4, 0, width),
            (4, width, key_columns),
            (4, width + key_columns, key_columns),
            (5, 0, width),
            (6, 0, width),
            (7, 0, 3 * width),
        ),
        shards,
    )
    (
        second_gate_full,
        second_up_full,
        first_gate_full,
        first_up_full,
        second_down_full,
        first_down_full,
        query_full,
        key_full,
        value_full,
        attend_output_full,
        mixer_output_full,
        mixer_input_full,
    ) = fulls
    return (
        mixed.reshape(tokens.shape),
        token_grad.reshape(tokens.shape),
        small[3],
        mixer_input_full,
        small[4],
        mixer_output_full,
        small[2],
        first_gate_full,
        first_up_full,
        first_down_full,
        small[1],
        query_full,
        key_full,
        value_full,
        small[5],
        small[6],
        attend_output_full,
        small[0],
        second_gate_full,
        second_up_full,
        second_down_full,
    )


def fused_or_general(*args):
    tokens = args[0]
    rows, length, width = tokens.shape
    row_count, shards = lax.axis_size("row"), lax.axis_size("seq")
    key_bytes = 2 * rows * length * shards * width
    if key_bytes <= 4 * 2**20 and shards == 8 and 4 * rows == shards and row_count == 4:
        return fused_body(*args)
    return body(*args)


def solution(mesh):
    in_specs = (
        P("row", "seq", None),
        P("row", None),
        P(),
        P(),
        P(),
        P(),
        P(),
        P(),
        P(),
        P(),
        P(),
        P(),
        P(),
        P(),
        P(),
        P(),
        P(),
        P(),
        P(),
        P(),
        P(),
        P("row", "seq", None),
    )
    out_specs = (
        P("row", "seq", None),
        P("row", "seq", None),
        P("seq"),
        P("seq", None),
        P(None, "seq"),
        P("seq", None),
        P("seq"),
        P("seq", None),
        P("seq", None),
        P("seq", None),
        P("seq"),
        P("seq", None),
        P("seq", None),
        P("seq", None),
        P("seq"),
        P("seq"),
        P("seq", None),
        P("seq"),
        P("seq", None),
        P("seq", None),
        P("seq", None),
    )
    return jax.shard_map(fused_or_general, mesh=mesh, in_specs=in_specs, out_specs=out_specs, check_vma=False)
```
